32 devices in a mesh: seq: 8 (over y, x, core), fsdp: 4 (over z).
Axes of the slice: x: 2, y: 2, z: 4, core: 2. Of those that a mesh axis runs over, the one named last changes fastest.
Arguments:
- tokens: bfloat16 [4, 3072, 768], P('fsdp', 'seq'), may hold values from -18 to 18, as said below
- lengths: int32 [4], P('fsdp'), may hold values from 768 to 3072, as said below
- w_qkv: bfloat16 [768, 2304], P('fsdp'), may hold values from -1 to 1, as said below
- q_bias: bfloat16 [768], P('fsdp'), may hold values from -2.5 to 2.5
- v_bias: bfloat16 [768], P('fsdp'), may hold values from -2.5 to 2.5
- w_out: bfloat16 [768, 768], P('fsdp'), may hold values from -1.25 to 1.25
- out_bias: bfloat16 [768], P('fsdp'), may hold values from -4 to 4
- ln1_gain: bfloat16 [768], P('fsdp'), may hold values from 0.5 to 1.5
- ln1_bias: bfloat16 [768], P('fsdp'), may hold values from -2.5 to 2.5
- w_in: bfloat16 [768, 3072], P('fsdp'), may hold values from -0.21875 to 0.21875
- in_bias: bfloat16 [3072], P('fsdp'), may hold values from -2.5 to 2.5
- w_back: bfloat16 [3072, 768], P('fsdp'), may hold values from -0.15625 to 0.15625
- back_bias: bfloat16 [768], P('fsdp'), may hold values from -2.5 to 2.5
- ln2_gain: bfloat16 [768], P('fsdp'), may hold values from 0.5 to 1.5
- ln2_bias: bfloat16 [768], P('fsdp'), may hold values from -2.5 to 2.5
- cotangent: bfloat16 [4, 3072, 768], P('fsdp', 'seq'), may hold values from -6 to 6
Outputs:
- output: bfloat16 [4, 3072, 768], P('fsdp', 'seq')
- grad_tokens: bfloat16 [4, 3072, 768], P('fsdp', 'seq')
- g_w_qkv: float32 [768, 2304], P('fsdp')
- g_q_bias: float32 [768], P('fsdp')
- g_v_bias: float32 [768], P('fsdp')
- g_w_out: float32 [768, 768], P('fsdp')
- g_out_bias: float32 [768], P('fsdp')
- g_ln1_gain: float32 [768], P('fsdp')
- g_ln1_bias: float32 [768], P('fsdp')
- g_w_in: float32 [768, 3072], P('fsdp')
- g_in_bias: float32 [3072], P('fsdp')
- g_w_back: float32 [3072, 768], P('fsdp')
- g_back_bias: float32 [768], P('fsdp')
- g_ln2_gain: float32 [768], P('fsdp')
- g_ln2_bias: float32 [768], P('fsdp')
The draws below stay inside these ranges and needn't reach their ends.
Inputs may be any that keep to these rules, and one draw needn't show every extreme that they name: `lengths`: every sequence has at least 768 valid positions, and one sequence is full. `tokens`: real-valued entries of order one. `w_qkv`: real-valued entries of order 768 ** -0.5.
All inputs are finite; a program needn't handle non-finite values.
Results may differ from the reference program's by a relative error of at most 0.025.
Values may be sent and summed in bfloat16 or wider, within the bound.
A program may use at most 320 MiB of HBM per device.

```python
import math
import jax
import jax.numpy as jnp
from jax import lax

D = 768
HEADS = 12
HEAD_DIM = 64
FF = 3072
GROUPS = 4
SEQ_LEN = 3072


def draw_lengths(key, part):
    full_len = SEQ_LEN
    drawn_len = jax.random.randint(jax.random.fold_in(key, 1), (GROUPS,), full_len // 4, full_len + 1)
    chosen = jax.random.randint(jax.random.fold_in(key, 2), (), 0, GROUPS)
    return jnp.where(jnp.arange(GROUPS) == chosen, full_len, drawn_len).astype(jnp.int32)


def draw_tokens(key, part):
    key = jax.random.fold_in(key, 5)
    values = jax.random.truncated_normal(jax.random.fold_in(key, 1), -6.0, 6.0, (GROUPS, SEQ_LEN, D), jnp.float32)
    paired = jax.random.permutation(jax.random.fold_in(key, 2), GROUPS)
    column_block = jnp.arange(D) // (D // GROUPS)
    boost = jnp.where(column_block[None, :] == paired[:, None], 3.0, 1.0).astype(jnp.float32)
    return (values * boost[:, None, :]).astype(jnp.bfloat16)


def draw_w_qkv(key, part):
    key = jax.random.fold_in(key, 7)
    values = jax.random.truncated_normal(key, -3.0, 3.0, (D, 3 * D), jnp.float32)
    return (values * (2.0 / D) ** 0.5).astype(jnp.bfloat16)


def block_levels(rng, shape, shards, least, top_value):
    def one(dim, parts):
        draws = jax.random.uniform(jax.random.fold_in(jax.random.fold_in(rng, 6), dim), (parts,), jnp.float32, least / len(shards), top_value / len(shards))
        return jnp.repeat(jnp.exp(draws), shape[dim] // parts).reshape((-1,) + (1,) * (len(shape) - dim - 1))

    level = one(*shards[0])
    for cut in shards[1:]:
        level = level * one(*cut)
    return level


def gaussian(own_key, extent, spread, bound, pieces=(), kind=jnp.bfloat16):
    entries = jax.random.normal(own_key, extent, jnp.float32) * spread
    if len(pieces) > 0:
        entries = block_levels(own_key, extent, pieces, -0.22, 0.18) * entries
    return jnp.clip(entries, min=-bound, max=bound).astype(kind)


def setup_inputs(seed: int = 0) -> dict:
    arg_keys = jax.random.split(jax.random.key(seed), 17)
    return {
        "tokens": draw_tokens(jax.random.fold_in(arg_keys[16], 71), 0),
        "lengths": draw_lengths(jax.random.fold_in(arg_keys[16], 71), 0),
        "w_qkv": draw_w_qkv(jax.random.fold_in(arg_keys[16], 71), 0),
        "q_bias": gaussian(arg_keys[3], (D,), 0.3, 2.5, ((0, 4),)),
        "v_bias": gaussian(arg_keys[4], (D,), 0.3, 2.5, ((0, 4),)),
        "w_out": gaussian(arg_keys[5], (D, D), (D // 32) ** -0.5, 1.25, ((0, 4),)),
        "out_bias": gaussian(arg_keys[6], (D,), 1.0, 4.0, ((0, 4),)),
        "ln1_gain": jnp.clip(1.0 + 0.1 * jax.random.normal(arg_keys[7], (D,), jnp.float32), 0.5, 1.5).astype(jnp.bfloat16),
        "ln1_bias": gaussian(arg_keys[8], (D,), 0.3, 2.5, ((0, 4),)),
        "w_in": gaussian(arg_keys[9], (D, FF), D ** -0.5, 0.21875, ((0, 4),)),
        "in_bias": gaussian(arg_keys[10], (FF,), 0.3, 2.5, ((0, 4),)),
        "w_back": gaussian(arg_keys[11], (FF, D), (FF // 2) ** -0.5, 0.15625, ((0, 4),)),
        "back_bias": gaussian(arg_keys[12], (D,), 0.3, 2.5, ((0, 4),)),
        "ln2_gain": jnp.clip(1.0 + 0.1 * jax.random.normal(arg_keys[13], (D,), jnp.float32), 0.5, 1.5).astype(jnp.bfloat16),
        "ln2_bias": gaussian(arg_keys[14], (D,), 0.3, 2.5, ((0, 4),)),
        "cotangent": gaussian(arg_keys[15], (GROUPS, SEQ_LEN, D), 1.0, 6.0, ((0, 4), (1, 8))),
    }


@jax.custom_vjp
def low(v):
    return lax.optimization_barrier(v.astype(jnp.bfloat16)).astype(jnp.float32)

@jax.custom_vjp
def low_back(v):
    return v

def low_keep(v):
    return (low(v), None)

def low_pass(kept, grad):
    return (grad,)

def back_keep(v):
    return (v, None)

def back_low(kept, grad):
    return (low(grad),)
low.defvjp(low_keep, low_pass)
low_back.defvjp(back_keep, back_low)
masked_score = -1e+30
highest = lax.Precision.HIGHEST

def layer_norm(hidden, gain_vec, shift_vec):
    average = lax.optimization_barrier(jnp.mean(hidden, axis=-1, keepdims=True))
    centred = hidden - average
    variance = lax.optimization_barrier(jnp.mean(centred * centred, axis=-1, keepdims=True))
    return centred * lax.rsqrt(variance + 1e-05) * gain_vec + shift_vec

def attend_block(query_block, key_heads, value_heads, key_ok):
    scores = jnp.einsum('hqd,hkd->hqk', query_block, key_heads, precision=highest) * HEAD_DIM ** (-0.5)
    scores = low_back(scores)
    scores = jnp.where(key_ok[None, None, :], scores, masked_score)
    row_max = lax.optimization_barrier(jnp.max(scores, axis=2, keepdims=True))
    log_total = row_max + jnp.log(lax.optimization_barrier(jnp.sum(jnp.exp(scores - row_max), axis=2, keepdims=True)))
    prob_low = low(jnp.exp(scores - log_total))
    return jnp.einsum('hqk,hkd->hqd', prob_low, value_heads, precision=highest)

def forward_sequence(seq_tokens, seq_length, params):
    w_qkv, q_bias, v_bias, w_out, out_bias, ln1_gain, ln1_bias, w_in, in_bias, w_back, back_bias, ln2_gain, ln2_bias = params
    block_rows = math.gcd(SEQ_LEN, 512)
    key_ok = jnp.arange(SEQ_LEN, dtype=jnp.int32) < seq_length
    row_valid = key_ok.astype(seq_tokens.dtype)
    bias_all = jnp.concatenate([q_bias, jnp.zeros_like(q_bias), v_bias])
    projected = low_back(low(jnp.dot(seq_tokens, w_qkv, precision=highest) + bias_all))
    split_q = projected[:, :D].reshape(SEQ_LEN // block_rows, block_rows, HEADS, HEAD_DIM).transpose(0, 2, 1, 3)
    key_heads = projected[:, D:2 * D].reshape(SEQ_LEN, HEADS, HEAD_DIM).transpose(1, 0, 2)
    value_heads = projected[:, 2 * D:].reshape(SEQ_LEN, HEADS, HEAD_DIM).transpose(1, 0, 2)
    block_fn = jax.checkpoint(lambda query_block: attend_block(query_block, key_heads, value_heads, key_ok))
    attended = lax.map(block_fn, split_q).transpose(0, 2, 1, 3).reshape(SEQ_LEN, D)
    attended = low_back(low(attended))
    branch = low_back(jnp.dot(attended, w_out, precision=highest) + out_bias)
    first_norm = layer_norm(seq_tokens + branch, ln1_gain, ln1_bias)
    inner_act = low_back(jnp.dot(low(first_norm), w_in, precision=highest) + in_bias)
    activated = low(jax.nn.gelu(inner_act, approximate=False))
    second = low_back(jnp.dot(activated, w_back, precision=highest) + back_bias)
    return layer_norm(first_norm + second, ln2_gain, ln2_bias) * row_valid[:, None]

def reference(tokens, lengths, w_qkv, q_bias, v_bias, w_out, out_bias, ln1_gain, ln1_bias, w_in, in_bias, w_back, back_bias, ln2_gain, ln2_bias, cotangent):
    params = tuple((weight_arg.astype(jnp.float32) for weight_arg in (w_qkv, q_bias, v_bias, w_out, out_bias, ln1_gain, ln1_bias, w_in, in_bias, w_back, back_bias, ln2_gain, ln2_bias)))

    def one_sequence(totals, seq_items):
        seq_tokens, seq_length, seq_cot = seq_items
        output, pullback = jax.vjp(lambda tok_f, par_f: forward_sequence(tok_f, seq_length, par_f), seq_tokens.astype(jnp.float32), params)
        grad_input, grad_params = pullback(seq_cot.astype(jnp.float32))
        totals = jax.tree.map(jnp.add, totals, grad_params)
        return (totals, (output.astype(jnp.bfloat16), grad_input.astype(jnp.bfloat16)))
    zero_sums = jax.tree.map(jnp.zeros_like, params)
    totals, (outputs, grad_inputs) = lax.scan(one_sequence, zero_sums, (tokens, lengths, cotangent))
    return (outputs, grad_inputs, totals[0], totals[1], totals[2], totals[3], totals[4], totals[5], totals[6], totals[7], totals[8], totals[9], totals[10], totals[11], totals[12])
```

```python
import functools
import math

import jax
import jax.numpy as jnp
from jax import lax
from jax.experimental import pallas as pl
from jax.experimental.pallas import tpu as pltpu
from jax.sharding import PartitionSpec as P

HEADS = 12
bf16 = jnp.bfloat16
f32 = jnp.float32
MESH = pl.DeviceIdType.MESH
LOG2E = math.log2(math.e)
NT = (((1,), (1,)), ((), ()))
NN = (((1,), (0,)), ((), ()))

PLANES = 4
CHIPS = 4
GROUP_HEADS = 3
PACKED = (12, 24, 13, 25, 0, 1, 2, None, 14, 26)
KV_TILE = (0, 1, 4)
PACK = 640


def dot(a, b, dims=NN):
    return lax.dot_general(a, b, dims, preferred_element_type=f32)


class Net:
    def __init__(self, send_sems, recv_sems):
        self.send_sems, self.recv_sems = send_sems, recv_sems
        self.specs = {}

    def add(self, name, src, dst, device):
        self.specs[name] = (len(self.specs), src, dst, device)

    def get(self, name):
        k, src, dst, device = self.specs[name]
        return pltpu.make_async_remote_copy(
            src_ref=src(),
            dst_ref=dst(),
            send_sem=self.send_sems.at[k],
            recv_sem=self.recv_sems.at[k],
            device_id=device,
            device_id_type=MESH,
        )

    def start(self, *names):
        for name in names:
            self.get(name).start()

    def recv(self, *names):
        for name in names:
            self.get(name).wait_recv()

    def sent(self, *names):
        for name in names:
            self.get(name).wait_send()


class Local:
    def __init__(self, sems):
        self.sems = sems
        self.specs = {}

    def add(self, name, src, dst):
        self.specs[name] = (len(self.specs), src, dst)

    def get(self, name):
        k, src, dst = self.specs[name]
        return pltpu.make_async_copy(src(), dst(), self.sems.at[k])

    def start(self, *names):
        for name in names:
            self.get(name).start()

    def wait(self, *names):
        for name in names:
            self.get(name).wait()


def coordinates():
    s, z = lax.axis_index("seq"), lax.axis_index("fsdp")
    core = lax.rem(s, 2)
    chip = lax.div(s, 2)
    return s, z, core, chip


def flip(value, mask):
    low, high = lax.rem(value, 2), lax.div(value, 2)
    if mask & 1:
        low = 1 - low
    if mask & 2:
        high = 1 - high
    return high * 2 + low


def hello(devices):
    barrier = pltpu.get_barrier_semaphore()
    for device in devices:
        pl.semaphore_signal(barrier, inc=1, device_id=device, device_id_type=MESH)


def met(count):
    pl.semaphore_wait(pltpu.get_barrier_semaphore(), count)


def greet(devices):
    hello(devices)
    met(len(devices))


def lanes_of(rows=1):
    return lax.broadcasted_iota(jnp.int32, (rows, 128), 1)


def split3(column):
    hi = column.astype(bf16).astype(f32)
    mid = (column - hi).astype(bf16).astype(f32)
    return hi, mid, column - hi - mid


def forward_kernel(
    length_ref, tok_ref, wraw_ref, win_ref, wback_ref, wout_ref, small_ref,
    q_out, k_out, v_out, o_out, tok_out, att_out, small_out, win_full, wback_full, wout_full, wq_full,
    tok, wqv, q_s, k_s, v_s, o_s, att, atts, kvs, kvr, small, wraw, wq_ref, send_sems, recv_sems, local_sems,
):
    s, z, core, chip = coordinates()
    other = 1 - core
    rows = tok_ref.shape[0]
    half = rows // 2
    shard = wq_ref.shape[1]
    piece = shard // 2
    peer = [None] + [(flip(chip, j) * 2 + core, z) for j in (1, 2, 3)]
    mate = (chip * 2 + other, z)
    plane = [None] + [(s, flip(z, dz)) for dz in (1, 2, 3)]
    zs = [z] + [flip(z, dz) for dz in (1, 2, 3)]
    net, loc = Net(send_sems, recv_sems), Local(local_sems)
    width = win_full.shape[1] // 8
    back = wback_full.shape[0] // PLANES
    bpiece = back // 8
    arrays = ("out", "in", "back", "qkv")

    def part(a, zz, m, c):
        if a == "in":
            return win_full.at[pl.ds(pl.multiple_of(zz * shard, 16), shard), pl.ds(pl.multiple_of((m * 4 + c) * width, 128), width)]
        if a == "back":
            return wback_full.at[pl.ds(pl.multiple_of(zz * back + (m * 4 + c) * bpiece, 16), bpiece), :]
        if a == "out":
            return wout_full.at[pl.ds(pl.multiple_of(zz * shard + c * (shard // 4), 16), shard // 4), pl.ds(pl.multiple_of(m * width, 128), width)]
        return wq_full.at[zz, m * 2 + lax.div(c, 2), pl.ds(pl.multiple_of(lax.rem(c, 2) * piece, 16), piece), :]

    def own_part(a, m, c):
        if a == "in":
            return win_ref.at[:, pl.ds(pl.multiple_of((m * 4 + c) * width, 128), width)]
        if a == "back":
            return wback_ref.at[pl.ds(pl.multiple_of((m * 4 + c) * bpiece, 16), bpiece), :]
        if a == "out":
            return wout_ref.at[pl.ds(pl.multiple_of(c * (shard // 4), 16), shard // 4), pl.ds(pl.multiple_of(m * width, 128), width)]
        return wq_ref.at[m * 2 + lax.div(c, 2), pl.ds(pl.multiple_of(lax.rem(c, 2) * piece, 16), piece), :]

    def side(a, zz, m):
        if a == "in":
            return win_full.at[pl.ds(pl.multiple_of(zz * shard, 16), shard), pl.ds(pl.multiple_of(m * 4 * width, 128), 4 * width)]
        if a == "back":
            return wback_full.at[pl.ds(pl.multiple_of(zz * back + m * 4 * bpiece, 16), 4 * bpiece), :]
        if a == "out":
            return wout_full.at[pl.ds(pl.multiple_of(zz * shard, 16), shard), pl.ds(pl.multiple_of(m * width, 128), width)]
        return wq_full.at[zz, pl.ds(m * 2, 2)]

    for dz in (1, 2, 3):
        net.add(("wq", dz), lambda: wq_ref.at[chip, pl.ds(pl.multiple_of(core * piece, 16), piece), :],
                lambda: wqv.at[pl.ds(pl.multiple_of(z * shard + core * piece, 16), piece), :], plane[dz])
        net.add(("wqm", dz), lambda dz=dz: wqv.at[pl.ds(pl.multiple_of(zs[dz] * shard + core * piece, 16), piece), :],
                lambda dz=dz: wqv.at[pl.ds(pl.multiple_of(zs[dz] * shard + core * piece, 16), piece), :], mate)
        net.add(("small", dz), lambda: small_ref, lambda: small.at[z], plane[dz])
    top, bottom = slice(0, half), slice(half, rows)
    net.add("t1a", lambda: tok_ref.at[top], lambda: tok.at[1, top], peer[1])
    net.add("t1b", lambda: tok_ref.at[bottom], lambda: tok.at[1, bottom], peer[1])
    net.add("t2b", lambda: tok_ref.at[bottom], lambda: tok.at[2, bottom], peer[2])
    net.add("t2a", lambda: tok_ref.at[top], lambda: tok.at[2, top], peer[2])
    net.add("t3a", lambda: tok.at[1, top], lambda: tok.at[3, top], peer[2])
    net.add("t3b", lambda: tok.at[2, bottom], lambda: tok.at[3, bottom], peer[1])
    for j in range(4):
        net.add(("kv", j), lambda j=j: kvs.at[j], lambda j=j: kvr.at[j], mate)
    for j in (1, 2, 3):
        net.add(("att0", j), lambda j=j: atts.at[j, :, 0:128], lambda: att.at[chip, :, 0:128], peer[j])
        net.add(("att1", j), lambda j=j: atts.at[j, :, 128:256], lambda: att.at[chip, :, 128:256], peer[j])
    for a in arrays:
        via, last = (1, 2) if a in ("in", "qkv") else (2, 1)
        for dz in (1, 2, 3):
            net.add((a, "z", dz), lambda a=a: own_part(a, core, chip), lambda a=a: part(a, z, core, chip), plane[dz])
            for j in (1, 2):
                net.add((a, j, dz), lambda a=a, dz=dz: part(a, zs[dz], core, chip), lambda a=a, dz=dz: part(a, zs[dz], core, chip), peer[j])
            net.add((a, 3, dz), lambda a=a, dz=dz, via=via: part(a, zs[dz], core, flip(chip, via)),
                    lambda a=a, dz=dz, via=via: part(a, zs[dz], core, flip(chip, via)), peer[last])
            net.add((a, "m", dz), lambda a=a, dz=dz: side(a, zs[dz], core), lambda a=a, dz=dz: side(a, zs[dz], core), mate)
    loc.add("raw", lambda: wraw_ref, lambda: wraw)
    loc.add("tok", lambda: tok_ref, lambda: tok.at[0])
    loc.add("wq", lambda: wq_ref.at[chip], lambda: wqv.at[pl.ds(pl.multiple_of(z * shard, 16), shard), :])
    loc.add("small", lambda: small_ref, lambda: small.at[z])
    loc.add("in", lambda: win_ref, lambda: win_full.at[pl.ds(pl.multiple_of(z * shard, 16), shard), :])
    loc.add("back", lambda: wback_ref, lambda: wback_full.at[pl.ds(pl.multiple_of(z * back, 16), back), :])
    loc.add("out", lambda: wout_ref, lambda: wout_full.at[pl.ds(pl.multiple_of(z * shard, 16), shard), :])
    loc.add("qkv", lambda: wq_ref, lambda: wq_full.at[z])
    outs = (("k_o", k_s, k_out), ("v_o", v_s, v_out), ("q_o", q_s, q_out), ("o_o", o_s, o_out),
            ("tok_o", tok, tok_out), ("att_o", att, att_out), ("small_o", small, small_out))
    for name, src, dst in outs:
        loc.add(name, lambda src=src: src, lambda dst=dst: dst)

    loc.start("raw", "tok", "small")
    hello(peer[1:] + [mate] + plane[1:])
    lane = lanes_of()
    loc.wait("raw")
    for g in range(CHIPS):
        for t in range(PACK // 128):
            halves = []
            for upper in (0, 1):
                block = PACKED[2 * t + upper]
                if block is None:
                    halves.append(0.0)
                    continue
                block += GROUP_HEADS * g
                tile_of = lambda i: wraw[:, i * 128 : (i + 1) * 128].astype(f32)
                halves.append(half_tile(tile_of, block, upper))
            wq_ref[g, :, t * 128 : (t + 1) * 128] = jnp.where(lane < 64, halves[0], halves[1]).astype(bf16)
    loc.start("wq")
    met(len(peer[1:] + [mate] + plane[1:]))
    net.start(*[("wq", dz) for dz in (1, 2, 3)], *[("small", dz) for dz in (1, 2, 3)])
    net.start("t1a", "t2b", "t1b", "t2a")
    loc.start(*arrays)
    for dz in (1, 2, 3):
        net.recv(("wq", dz))
        net.start(("wqm", dz))
    for dz in (1, 2, 3):
        net.start(*[(a, "z", dz) for a in arrays])
    loc.wait("tok", "wq", "small")
    for dz in (1, 2, 3):
        net.recv(("small", dz), ("wqm", dz))

    length = length_ref[0]
    bias = small[chip, 7:8, 0:PACK].astype(f32)

    def keep(tile, h, slot, block):
        position = block * rows + lax.broadcasted_iota(jnp.int32, (rows, 1), 0)
        mask = jnp.where(position < length, 0.0, -1e30).astype(f32)
        ones = jnp.where((lane > 64) & (lane < 68), 1.0, 0.0)
        k_s[h, slot * rows : (slot + 1) * rows, :] = jnp.where(
            lane < 64, tile, jnp.where(lane == 64, mask, ones)
        ).astype(bf16)
        v_s[h, slot * rows : (slot + 1) * rows, :] = jnp.where(
            lane < 64, pltpu.roll(tile, 64, 1), jnp.where(lane < 67, 1.0, 0.0)
        ).astype(bf16)

    def project(j):
        proj = dot(tok[j], wqv[...]) + bias
        for h in range(GROUP_HEADS):
            tile = proj[:, KV_TILE[h] * 128 : (KV_TILE[h] + 1) * 128]
            keep(tile.astype(bf16).astype(f32), h, j, flip(chip, j) * 2 + core)
            kvs[j, :, h * 128 : (h + 1) * 128] = tile.astype(bf16)
            first = 256 + (h // 2) * 128
            tile = proj[:, first : first + 128].astype(bf16).astype(f32) * 0.125
            if h == 1:
                tile = pltpu.roll(tile, 64, 1)
            q_s[h, j * rows : (j + 1) * rows, :] = jnp.where(
                lane < 64, tile, jnp.where(lane == 64, 1.0, 0.0)
            ).astype(bf16)
        net.start(("kv", j))

    def keep_other(j):
        net.recv(("kv", j))
        for h in range(GROUP_HEADS):
            tile = kvr[j, :, h * 128 : (h + 1) * 128].astype(f32)
            keep(tile, h, 4 + j, flip(chip, j) * 2 + other)

    project(0)
    net.recv("t1a")
    net.start("t3a")
    net.recv("t2b")
    net.start("t3b")
    net.recv("t1b")
    project(1)
    net.recv("t2a")
    project(2)
    keep_other(0)
    keep_other(1)
    keep_other(2)
    net.recv("t3a", "t3b")
    project(3)
    keep_other(3)
    loc.start("k_o", "v_o", "tok_o", "small_o")

    query_tile, key_chunk = 512, 1024
    tiles = 4 * rows // query_tile
    chunks = 8 * rows // key_chunk

    def first_hop(dz):
        for a in arrays:
            net.recv((a, "z", dz))
            net.start((a, 1, dz), (a, 2, dz))

    def second_hop(dz):
        for a in arrays:
            net.recv((a, 1, dz), (a, 2, dz))
            net.start((a, 3, dz))

    def third_hop(dz):
        for a in arrays:
            net.recv((a, 3, dz))
            net.start((a, "m", dz))

    def attended_tile(which):
        for j in range(4):
            r = slice(j * rows, (j + 1) * rows)
            if which == 0:
                upper = pltpu.roll(o_s[1, r, :].astype(f32), 64, 1)
                value = jnp.where(lane < 64, o_s[0, r, :].astype(f32), upper)
            else:
                value = jnp.where(lane < 64, o_s[2, r, :].astype(f32), 0.0)
            place = slice(which * 128, (which + 1) * 128)
            if j == 0:
                att[chip, :, place] = value.astype(bf16)
            else:
                atts[j, :, place] = value.astype(bf16)
                net.start((f"att{which}", j))

    def visit(t, carry):
        h, i = lax.div(t, tiles), lax.rem(t, tiles)
        qrows = pl.ds(pl.multiple_of(i * query_tile, query_tile), query_tile)
        q = q_s[h, qrows, :]
        top_score = jnp.full((query_tile, 1), -1e30, f32)
        acc = jnp.zeros((query_tile, 128), f32)
        for c in range(chunks):
            krows = slice(c * key_chunk, (c + 1) * key_chunk)
            scores = dot(q, k_s[h, krows, :], NT)
            new_top = jnp.maximum(top_score, jnp.max(scores, axis=1, keepdims=True))
            probs = jnp.exp2((scores - new_top) * LOG2E)
            fade = jnp.exp2((top_score - new_top) * LOG2E)
            acc = acc * fade + dot(probs.astype(bf16), v_s[h, krows, :])
            top_score = new_top
        total = acc[:, 64:65]
        o_s[h, qrows, :] = (acc / total).astype(bf16)
        hi, mid, low = split3(-(top_score + jnp.log(total)))
        wide = q.astype(f32)
        wide = jnp.where(lane == 65, hi, jnp.where(lane == 66, mid, jnp.where(lane == 67, low, wide)))
        q_s[h, qrows, :] = wide.astype(bf16)

        for at, work in enumerate((
            lambda: first_hop(1), lambda: None, lambda: first_hop(2), lambda: second_hop(1),
            lambda: first_hop(3), lambda: (second_hop(2), attended_tile(0)), lambda: third_hop(1), lambda: second_hop(3),
            lambda: (attended_tile(1), third_hop(2)),
        )):
            pl.when(t == at)(lambda work=work: (work(), None)[1])
        return carry

    lax.fori_loop(0, GROUP_HEADS * tiles, visit, 0)
    third_hop(3)
    loc.start("q_o", "o_o")
    for j in (1, 2, 3):
        net.recv(("att0", j), ("att1", j))
    loc.start("att_o")
    for dz in (1, 2, 3):
        for a in arrays:
            net.recv((a, "m", dz))
    for name in net.specs:
        net.sent(name)
    loc.wait(*arrays, *[name for name, _, _ in outs])


def backward_kernel(
    do_ref, q_ref, k_ref, v_ref, o_ref, tok_ref, grads_ref, sums_ref,
    dproj_out, gw_out, fin_out, sums_out,
    do_s, q_s, k_s, v_s, o_s, doa, tok, tokt, dqs, dq_keep, kv_own, kvs, kvr, dall, dproj,
    gw, gwr, gz, gzr, gwf, acc, rb, rx, ry, rx2, ry2, rz, fin, sums, sums_r, sums_z, sums_f,
    send_sems, recv_sems, local_sems,
):
    s, z, core, chip = coordinates()
    other = 1 - core
    rows = do_ref.shape[1]
    peer = [None] + [(flip(chip, j) * 2 + core, z) for j in (1, 2, 3)]
    mate = (chip * 2 + other, z)
    plane = [None] + [(s, flip(z, dz)) for dz in (1, 2, 3)]
    zs = [z] + [flip(z, dz) for dz in (1, 2, 3)]
    ch = [chip] + [flip(chip, j) for j in (1, 2, 3)]
    net, loc = Net(send_sems, recv_sems), Local(local_sems)
    length = grads_ref.shape[3]
    cut = length // 32 * 16
    xs, ys = slice(0, cut), slice(cut, length)
    shard = tok.shape[2] // PLANES
    piece = shard // 2

    for j in (1, 2, 3):
        net.add(("do", j), lambda j=j: do_ref.at[ch[j]], lambda j=j: do_s.at[j], peer[j])
    for h in range(GROUP_HEADS):
        net.add(("kv", h), lambda h=h: kvs.at[h], lambda h=h: kvr.at[h], mate)
        place = ((0, 128), (128, 384), (384, 640))[h]
        for j in (1, 2, 3):
            net.add(("dp", h, j), lambda j=j, place=place: dall.at[j, :, place[0] : place[1]],
                    lambda place=place: dproj.at[chip, :, place[0] : place[1]], peer[j])
    order = (3, 2, 1, 0)
    for dz in order:
        net.add(("r1", dz), lambda dz=dz: grads_ref.at[other, zs[dz]], lambda dz=dz: rb.at[zs[dz]], mate)
        for n, j in enumerate((1, 3)):
            net.add(("x1", n, dz), lambda dz=dz, j=j: acc.at[zs[dz], ch[j], xs], lambda dz=dz, n=n: rx.at[zs[dz], n], peer[1])
        net.add(("x2", dz), lambda dz=dz: acc.at[zs[dz], ch[2], xs], lambda dz=dz: rx2.at[zs[dz]], peer[2])
        for n, j in enumerate((2, 3)):
            net.add(("y1", n, dz), lambda dz=dz, j=j: acc.at[zs[dz], ch[j], ys], lambda dz=dz, n=n: ry.at[zs[dz], n], peer[2])
        net.add(("y2", dz), lambda dz=dz: acc.at[zs[dz], ch[1], ys], lambda dz=dz: ry2.at[zs[dz]], peer[1])
        if dz:
            net.add(("rz", dz), lambda dz=dz: acc.at[zs[dz], chip], lambda dz=dz: rz.at[dz - 1], plane[dz])
    net.add("f1", lambda: fin.at[core, chip], lambda: fin.at[core, chip], peer[1])
    net.add("f2", lambda: fin.at[core, chip], lambda: fin.at[core, chip], peer[2])
    net.add("f3x", lambda: fin.at[core, ch[1], xs], lambda: fin.at[core, ch[1], xs], peer[2])
    net.add("f3y", lambda: fin.at[core, ch[2], ys], lambda: fin.at[core, ch[2], ys], peer[1])
    net.add("fm", lambda: fin.at[core], lambda: fin.at[core], mate)
    net.add("s0", lambda: sums_ref, lambda: sums_r.at[0], mate)
    net.add("s1", lambda: sums.at[1], lambda: sums_r.at[1], peer[1])
    net.add("s2", lambda: sums.at[2], lambda: sums_r.at[2], peer[2])
    for dz in (1, 2, 3):
        net.add(("sz", dz), lambda dz=dz: sums.at[3, zs[dz]], lambda dz=dz: sums_z.at[dz - 1], plane[dz])
    net.add("g0", lambda: gw.at[other], lambda: gwr, mate)
    for dz in (1, 2, 3):
        net.add(("gz", dz), lambda dz=dz: gz.at[zs[dz]], lambda dz=dz: gzr.at[dz - 1], plane[dz])
    for j in (1, 2, 3):
        net.add(("gf", j), lambda: gwf.at[core, chip], lambda: gwf.at[core, chip], peer[j])
    net.add("gm", lambda: gwf.at[core], lambda: gwf.at[core], mate)

    loads = (("do", lambda: do_ref.at[chip], lambda: do_s.at[0]), ("o", lambda: o_ref, lambda: o_s),
             ("tok", lambda: tok_ref, lambda: tok), ("q", lambda: q_ref, lambda: q_s),
             ("k", lambda: k_ref, lambda: k_s), ("v", lambda: v_ref, lambda: v_s),
             ("sums", lambda: sums_ref, lambda: sums.at[0]), ("acc", lambda: grads_ref.at[core], lambda: acc))
    for name, src, dst in loads:
        loc.add(name, src, dst)
    stores = (("dp_o", dproj, dproj_out), ("gw_o", gwf, gw_out), ("fin_o", fin, fin_out))
    for name, src, dst in stores:
        loc.add(name, lambda src=src: src, lambda dst=dst: dst)
    loc.add("sums_o", lambda: sums_f, lambda: sums_out)

    loc.start(*[name for name, _, _ in loads])
    greet(peer[1:] + [mate] + plane[1:])
    net.start(*[("do", j) for j in (1, 2, 3)])
    net.start("s0", *[("r1", dz) for dz in order])
    lane = lanes_of()
    loc.wait("tok")
    for j in range(4):
        tokt[:, j * rows : (j + 1) * rows] = tok[j].T
    loc.wait("do", "o", "q", "k", "v", "sums", "acc")
    for j in range(4):
        if j:
            net.recv(("do", j))
        for h in range(GROUP_HEADS):
            tile = do_s[j, :, (h // 2) * 128 : (h // 2) * 128 + 128].astype(f32)
            if h == 1:
                tile = pltpu.roll(tile, 64, 1)
            tile = jnp.where(lane < 64, tile, 0.0)
            r = slice(j * rows, (j + 1) * rows)
            delta = jnp.sum(tile * o_s[h, r, :].astype(f32), axis=1, keepdims=True)
            hi, mid, low = split3(-delta)
            tile = jnp.where(lane == 64, hi, jnp.where(lane == 65, mid, jnp.where(lane == 66, low, tile)))
            doa[h, r, :] = tile.astype(bf16)

    def add_into(ref, index, other_ref, other_index):
        ref[index] = (ref[index].astype(f32) + other_ref[other_index].astype(f32)).astype(bf16)

    def step_one(dz):
        net.recv(("r1", dz))
        def body(c, carry):
            add_into(acc, (zs[dz], c), rb, (zs[dz], c))
            return carry
        lax.fori_loop(0, CHIPS, body, 0)
        net.start(*[("x1", n, dz) for n in (0, 1)], *[("y1", n, dz) for n in (0, 1)])

    def step_two(dz):
        for n in range(2):
            net.recv(("x1", 1 - n, dz), ("y1", 1 - n, dz))
            jx, jy = (2, 1) if n == 0 else (0, 0)
            add_into(acc, (zs[dz], ch[jx], xs), rx, (zs[dz], 1 - n))
            add_into(acc, (zs[dz], ch[jy], ys), ry, (zs[dz], 1 - n))
            if n == 0:
                net.start(("x2", dz), ("y2", dz))

    def step_three(dz):
        net.recv(("x2", dz), ("y2", dz))
        add_into(acc, (zs[dz], chip, xs), rx2, zs[dz])
        add_into(acc, (zs[dz], chip, ys), ry2, zs[dz])
        if dz:
            net.start(("rz", dz))

    def sums_step(n):
        net.recv(f"s{n}")
        sums[n + 1] = (sums[n].astype(f32) + sums_r[n].astype(f32)).astype(bf16)
        if n < 2:
            net.start(f"s{n + 1}")
        else:
            net.start(*[("sz", dz) for dz in (1, 2, 3)])

    key_chunk, query_tile = 2 * rows, 256
    per_head = 4

    def head_end(h):
        net.recv(("kv", h))
        tile = KV_TILE[h]
        dst = (0, 1, 4)[h] * 128
        for j in range(4):
            r = slice(j * rows, (j + 1) * rows)
            both = kv_own[r, :] + kvr[h, r, :].astype(f32)
            dall[j, :, dst : dst + 128] = both.astype(bf16)
        dq = dqs[...].T * 0.125
        for j in range(4):
            r = slice(j * rows, (j + 1) * rows)
            mine = dq[r, :]
            if h == 0:
                dq_keep[r, :] = mine
            elif h == 1:
                dall[j, :, 256:384] = jnp.where(lane < 64, dq_keep[r, :], pltpu.roll(mine, 64, 1)).astype(bf16)
            else:
                dall[j, :, 384:512] = jnp.where(lane < 64, mine, 0.0).astype(bf16)
        for j in (1, 2, 3):
            net.start(("dp", h, j))

    stages = {
        0: lambda: (step_one(3), sums_step(0)),
        1: lambda: (step_one(2), sums_step(1)),
        2: lambda: (step_two(3), sums_step(2)),
        3: lambda: step_one(1),
        4: lambda: (step_three(3), step_two(2)),
        5: lambda: step_one(0),
        6: lambda: (step_three(2), step_two(1)),
        8: lambda: step_two(0),
        9: lambda: step_three(1),
        11: lambda: step_three(0),
    }

    def visit(t, carry):
        h, part = lax.div(t, per_head), lax.rem(t, per_head)
        start = pl.multiple_of(lax.rem(part + 2, 4) * key_chunk, key_chunk)
        krows = pl.ds(start, key_chunk)
        k, v = k_s[h, krows, :], v_s[h, krows, :]
        kt = k.T

        @pl.when(part == 0)
        def _():
            dqs[...] = jnp.zeros_like(dqs)

        dk = jnp.zeros((key_chunk, 128), f32)
        dv = jnp.zeros((key_chunk, 128), f32)
        for i in range(4 * rows // query_tile):
            r = slice(i * query_tile, (i + 1) * query_tile)
            q, do = q_s[h, r, :], doa[h, r, :]
            probs = jnp.exp2(dot(k, q, NT) * LOG2E)
            dscores = (probs * dot(v, do, NT)).astype(bf16)
            dv = dv + dot(probs.astype(bf16), do)
            dk = dk + dot(dscores, q)
            dqs[:, r] += dot(kt, dscores)
        packed = jnp.where(lane < 64, dk, pltpu.roll(dv, 64, 1))

        @pl.when(part < 2)
        def _():
            kvs[h, pl.ds(pl.multiple_of(part * key_chunk, key_chunk), key_chunk), :] = packed.astype(bf16)

        @pl.when(part >= 2)
        def _():
            kv_own[pl.ds(pl.multiple_of((part - 2) * key_chunk, key_chunk), key_chunk), :] = packed

        for hh in range(GROUP_HEADS):
            @pl.when(t == hh * per_head + 1)
            def _(hh=hh):
                net.start(("kv", hh))

            @pl.when(t == hh * per_head + 3)
            def _(hh=hh):
                head_end(hh)
        for at, work in stages.items():
            pl.when(t == at)(lambda work=work: (work(), None)[1])
        return carry

    lax.fori_loop(0, GROUP_HEADS * per_head, visit, 0)

    dproj[chip] = dall[0]
    d_cols = dall[...].reshape(4 * rows, PACK)
    column_sums = jnp.sum(d_cols.astype(f32), axis=0, keepdims=True)
    extra = jnp.where(lax.broadcasted_iota(jnp.int32, (16, 1), 0) == 0, column_sums, 0.0).astype(bf16)
    for zz in range(PLANES):
        part = dot(tokt[zz * shard : (zz + 1) * shard, :], d_cols)
        for m in range(2):
            gw[m, zz, 0:piece, :] = part[m * piece : (m + 1) * piece, :].astype(bf16)
            gw[m, zz, piece : piece + 16, :] = extra
    net.start("g0")

    for dz in (1, 2, 3):
        net.recv(("rz", dz), ("sz", dz))
    total = acc[z, chip].astype(f32) + rz[0].astype(f32) + rz[1].astype(f32) + rz[2].astype(f32)
    fin[core, chip] = total.astype(bf16)
    net.start("f1", "f2")
    total = sums[3, z].astype(f32)
    for n in range(3):
        total = total + sums_z[n].astype(f32)
    sums_f[...] = total.astype(bf16)
    loc.start("sums_o")

    net.recv("g0")
    for zz in range(PLANES):
        gz[zz] = (gw[core, zz].astype(f32) + gwr[zz].astype(f32)).astype(bf16)
    net.start(*[("gz", dz) for dz in (1, 2, 3)])
    for h in range(GROUP_HEADS):
        for j in (1, 2, 3):
            net.recv(("dp", h, j))
    loc.start("dp_o")
    net.recv("f1")
    net.start("f3x")
    net.recv("f2")
    net.start("f3y")
    total = gz[z].astype(f32)
    for dz in (1, 2, 3):
        net.recv(("gz", dz))
        total = total + gzr[dz - 1].astype(f32)
    gwf[core, chip] = total.astype(bf16)
    net.start(*[("gf", j) for j in (1, 2, 3)])
    net.recv("f3x", "f3y")
    net.start("fm")
    net.recv(*[("gf", j) for j in (1, 2, 3)])
    net.start("gm")
    net.recv("fm", "gm")
    loc.start("gw_o", "fin_o")
    for name in net.specs:
        net.sent(name)
    loc.wait("dp_o", "gw_o", "fin_o", "sums_o")


def gelu_parts(u):
    x = jnp.abs(u) * (0.5 ** 0.5)
    d = 1.0 + 0.3275911 * x
    t = pl.reciprocal(d, approx=True)
    t = t * (2.0 - d * t)
    poly = t * (0.254829592 + t * (-0.284496736 + t * (1.421413741 + t * (-1.453152027 + t * 1.061405429))))
    bell = jnp.exp2(u * u * (-0.5 * LOG2E))
    tail = 0.5 * poly * bell
    phi = jnp.where(u >= 0, 1.0 - tail, tail)
    return u * phi, phi + u * bell * (1.0 / math.sqrt(2.0 * math.pi))


def row_mean(a):
    return jnp.mean(a, axis=1, keepdims=True)


def wide_vectors(small):
    total = small[0].astype(f32)[0:8]
    step = small.shape[2] // PLANES
    lane = lax.broadcasted_iota(jnp.int32, total.shape, 1)
    total = jnp.where(lane < step, total, 0.0)
    for zz in range(1, PLANES):
        part = jnp.where(lane < step, small[zz].astype(f32)[0:8], 0.0)
        total = total + pltpu.roll(part, zz * step, 1)
    return total


def ffn_kernel(
    length_ref, att_ref, tok_ref, cot_ref, win_ref, wback_ref, wout_ref, small_ref,
    out_ref, gh1_ref, do_ref, grads_ref, sums_ref,
    winv, wbackv, woutv, act_s, gp_s, gi_s, acc, first_s, n1_s, low_s, lowt_s, gsec_s, gh2_s, isum, local_sems,
):
    s = lax.axis_index("seq")
    rows, width = tok_ref.shape
    step = width // PLANES
    ch = winv.shape[1] // 8
    loc = Local(local_sems)
    loc.add("out", lambda: wout_ref, lambda: woutv)
    for n in range(8):
        loc.add(("in", n), lambda n=n: win_ref.at[:, n * ch : (n + 1) * ch], lambda n=n: winv.at[:, n * ch : (n + 1) * ch])
        loc.add(("back", n), lambda n=n: wback_ref.at[n * ch : (n + 1) * ch, :], lambda n=n: wbackv.at[n * ch : (n + 1) * ch, :])
    loc.start("out")
    for n in range(8):
        loc.start(("in", n), ("back", n))
    vectors = wide_vectors(small_ref)
    vec = lambda i: vectors[i : i + 1, :]
    loc.wait("out")
    branch = vec(0)
    for g in range(4):
        branch = branch + dot(att_ref[g, :, 0:step], woutv[g * step : (g + 1) * step, :])
    hidden = tok_ref[...].astype(f32) + branch
    centred = hidden - row_mean(hidden)
    inverse1 = lax.rsqrt(row_mean(centred * centred) + 1e-5)
    normed = centred * inverse1
    n1_s[...] = normed
    first = normed * vec(1) + vec(2)
    first_s[...] = first
    low_s[...] = first.astype(bf16)
    lowt_s[...] = first.astype(bf16).T
    acc[...] = jnp.zeros_like(acc)
    for n in range(8):
        loc.wait(("in", n), ("back", n))

    def forward(n, carry):
        cols = pl.ds(pl.multiple_of(n * ch, 128), ch)
        bias = small_ref[lax.div(n, 2), 6:7, pl.ds(pl.multiple_of(lax.rem(n, 2) * ch, 128), ch)].astype(f32)
        inner = dot(low_s[...], winv[:, cols]) + bias
        value, slope = gelu_parts(inner)
        value = value.astype(bf16)
        act_s[n] = value
        gp_s[n] = slope
        acc[...] += dot(value, wbackv[cols, :])
        return carry

    lax.fori_loop(0, 8, forward, 0)
    position = s * rows + lax.broadcasted_iota(jnp.int32, (rows, 1), 0)
    valid = (position < length_ref[0]).astype(f32)
    hidden = first_s[...] + acc[...] + vec(3)
    centred = hidden - row_mean(hidden)
    inverse = lax.rsqrt(row_mean(centred * centred) + 1e-5)
    normed = centred * inverse
    out_ref[...] = ((normed * vec(4) + vec(5)) * valid).astype(bf16)
    grad = cot_ref[...].astype(f32) * valid
    sum_rows = lambda a: jnp.sum(a, axis=0, keepdims=True)
    g2_gain, g2_bias = sum_rows(grad * normed), sum_rows(grad)
    scaled = grad * vec(4)
    gh2 = inverse * (scaled - row_mean(scaled) - normed * row_mean(scaled * normed))
    gh2_s[...] = gh2
    second = gh2.astype(bf16)
    gsec_s[...] = second
    back_sum = sum_rows(second.astype(f32))
    acc[...] = jnp.zeros_like(acc)

    def backward(n, carry):
        cols = pl.ds(pl.multiple_of(n * ch, 128), ch)
        grad_inner = (dot(gsec_s[...], wbackv[cols, :], NT) * gp_s[n]).astype(bf16)
        gi_s[n] = grad_inner
        isum[n] = jnp.broadcast_to(sum_rows(grad_inner.astype(f32)), (8, ch))
        acc[...] += dot(grad_inner, winv[:, cols], NT)
        return carry

    lax.fori_loop(0, 8, backward, 0)
    grad = gh2_s[...] + acc[...]
    normed = n1_s[...]
    g1_gain, g1_bias = sum_rows(grad * normed), sum_rows(grad)
    scaled = grad * vec(1)
    gh1 = inverse1 * (scaled - row_mean(scaled) - normed * row_mean(scaled * normed))
    gh1_ref[...] = gh1
    gbranch = gh1.astype(bf16)
    out_sum = sum_rows(gbranch.astype(f32))
    for g in range(4):
        w = woutv[g * step : (g + 1) * step, :]
        do_ref[g, :, 0:step] = dot(gbranch, w, NT).astype(bf16)
        do_ref[g, :, step:] = jnp.zeros((rows, do_ref.shape[2] - step), bf16)
        gw = dot(att_ref[g, :, 0:step].T, gbranch).astype(bf16)
        part = step // 4
        for c in range(4):
            for m in range(2):
                grads_ref[m, g, c, step + 2 * 96 :, :] = gw[c * part : (c + 1) * part, m * ch : (m + 1) * ch]

    def weights(n, carry):
        gback = dot(act_s[n].T, gsec_s[...]).astype(bf16)
        part = ch // 4
        for k in range(4):
            for x in range(2):
                grads_ref[lax.rem(n, 2), lax.div(n, 2), k, step + x * part : step + (x + 1) * part, :] = gback[
                    k * part : (k + 1) * part, x * ch : (x + 1) * ch
                ]
        for zz in range(PLANES):
            gin = dot(lowt_s[zz * step : (zz + 1) * step, :], gi_s[n])
            grads_ref[lax.div(n, 4), zz, lax.rem(n, 4), 0:step, :] = gin.astype(bf16)
        return carry

    lax.fori_loop(0, 8, weights, 0)
    lane = lax.broadcasted_iota(jnp.int32, (8, width), 1)
    place = lax.broadcasted_iota(jnp.int32, (8, width), 0)
    total = jnp.zeros((8, width), f32)
    for i, v in enumerate((out_sum, g1_gain, g1_bias, back_sum, g2_gain, g2_bias)):
        total = jnp.where(place == i, v, total)
    for zz in range(PLANES):
        part = total if zz == 0 else pltpu.roll(total, width - zz * step, 1)
        part = jnp.where(lane < step, part, 0.0)
        both = jnp.concatenate([isum[2 * zz], isum[2 * zz + 1]], axis=1)
        part = jnp.where(place == 6, both, part)
        sums_ref[zz, 0:16, :] = jnp.concatenate([part, jnp.zeros((8, width), f32)], axis=0).astype(bf16)


Q_PLACE, K_PLACE, V_PLACE = (4, 5, 6), (0, 2, 8), (1, 3, 9)


def half_tile(tile_of, block, upper):
    tile = tile_of(block // 2)
    return tile if block % 2 == upper else pltpu.roll(tile, 64, 1)


def final_kernel(
    dproj_ref, wq_ref, gh1_ref, gw_ref, fin_ref, sums_ref,
    gt_ref, gqkv_ref, gin_ref, gback_ref, gout_ref, qb_ref, vb_ref, o0, o1, o2, o3, o4, o5, ib_ref,
    wv, local_sems,
):
    z = lax.axis_index("fsdp")
    loc = Local(local_sems)
    shard = wq_ref.shape[2]
    for zz in range(PLANES):
        loc.add(zz, lambda zz=zz: wq_ref.at[zz], lambda zz=zz: wv.at[:, zz * shard : (zz + 1) * shard, :])
    loc.start(*range(PLANES))
    lane = lanes_of()
    up = lambda a: a.astype(f32)
    ch = fin_ref.shape[3]
    for m in range(2):
        for c in range(4):
            n = m * 4 + c
            gin_ref[:, n * ch : (n + 1) * ch] = up(fin_ref[m, c, 0:shard, :])
            part = ch // 4
            for x in range(2):
                gback_ref[n * part : (n + 1) * part, x * ch : (x + 1) * ch] = up(
                    fin_ref[m, c, shard + x * part : shard + (x + 1) * part, :]
                )
            gout_ref[c * (shard // 4) : (c + 1) * (shard // 4), m * ch : (m + 1) * ch] = up(fin_ref[m, c, shard + 2 * part :, :])
    piece = shard // 2
    for m in range(2):
        r = slice(m * piece, (m + 1) * piece)
        for kind, places in enumerate((Q_PLACE, K_PLACE, V_PLACE)):
            for i in range(HEADS // 2):
                halves = []
                for upper in (0, 1):
                    g, h = divmod(2 * i + upper, GROUP_HEADS)
                    tile_of = lambda t, g=g: up(gw_ref[m, g, 0:piece, t * 128 : (t + 1) * 128])
                    halves.append(half_tile(tile_of, places[h], upper))
                at = kind * HEADS * 64 + i * 128
                gqkv_ref[r, at : at + 128] = jnp.where(lane < 64, halves[0], halves[1])
    tile_of = lambda t: up(gw_ref[0, z, piece : piece + 16, t * 128 : (t + 1) * 128])
    for ref, places in ((qb_ref, Q_PLACE), (vb_ref, V_PLACE)):
        first = jnp.where(lane < 64, half_tile(tile_of, places[0], 0), half_tile(tile_of, places[1], 1))
        ref[:, 0:128] = first[0:1]
        ref[:, 128:192] = half_tile(tile_of, places[2], 0)[0:1, 0:64]
    for i, ref in enumerate((o0, o1, o2, o3, o4, o5)):
        ref[...] = up(sums_ref[...])[i : i + 1, 0:shard]
    ib_ref[...] = up(sums_ref[...])[6:7, :]
    loc.wait(*range(PLANES))
    total = gh1_ref[...]
    for g in range(4):
        total = total + dot(dproj_ref[g], wv[g], NT)
    gt_ref[...] = total.astype(bf16)


def vmem(shape, dtype=bf16):
    return pltpu.VMEM(shape, dtype)


ANY = pl.BlockSpec(memory_space=pl.ANY)
SMEM = pl.BlockSpec(memory_space=pltpu.SMEM)
VMEM = pl.BlockSpec(memory_space=pltpu.VMEM)
VMEM_BYTES = 60 * 2**20
SEMS = 96


def semaphores():
    return [pltpu.SemaphoreType.DMA((SEMS,)), pltpu.SemaphoreType.DMA((SEMS,)), pltpu.SemaphoreType.DMA((16,))]


def params(collective_id):
    return pltpu.CompilerParams(
        collective_id=collective_id, has_side_effects=True, vmem_limit_bytes=VMEM_BYTES
    )


def run_forward(lengths, tokens, w_qkv, w_in, w_back, w_out, small):
    rows, width = tokens.shape
    shard = w_qkv.shape[0]
    hidden = w_in.shape[1]
    S = jax.ShapeDtypeStruct
    q_shape, kv_shape = (GROUP_HEADS, 4 * rows, 128), (GROUP_HEADS, 8 * rows, 128)
    return pl.pallas_call(
        forward_kernel,
        out_shape=(
            S(q_shape, bf16), S(kv_shape, bf16), S(kv_shape, bf16), S(q_shape, bf16),
            S((4, rows, width), bf16), S((4, rows, 256), bf16), S((PLANES, 16, width), bf16),
            S((PLANES * shard, hidden), bf16), S((hidden, width), bf16), S((width, width), bf16),
            S((PLANES, CHIPS, shard, PACK), bf16),
        ),
        in_specs=[SMEM] + [ANY] * 6,
        out_specs=[ANY] * 11,
        scratch_shapes=[
            vmem((4, rows, width)), vmem((width, PACK)), vmem(q_shape), vmem(kv_shape), vmem(kv_shape), vmem(q_shape),
            vmem((4, rows, 256)), vmem((4, rows, 256)), vmem((4, rows, 384)), vmem((4, rows, 384)),
            vmem((PLANES, 16, width)), vmem((shard, w_qkv.shape[1])), vmem((CHIPS, shard, PACK)),
        ] + semaphores(),
        compiler_params=params(1),
    )(lengths, tokens, w_qkv, w_in, w_back, w_out, small)


def run_backward(do, q, k, v, o, tok, grads, sums):
    rows = do.shape[1]
    width = tok.shape[2]
    shard = width // PLANES
    length, cols = grads.shape[3:]
    cut = length // 32 * 16
    S = jax.ShapeDtypeStruct
    ext = shard // 2 + 16
    return pl.pallas_call(
        backward_kernel,
        out_shape=(
            S((4, rows, PACK), bf16), S((2, 4, ext, PACK), bf16), S((2, 4, length, cols), bf16), S((16, width), bf16),
        ),
        in_specs=[ANY] * 8,
        out_specs=[ANY] * 4,
        scratch_shapes=[
            vmem((4, rows, 256)), vmem(q.shape), vmem(k.shape), vmem(v.shape), vmem(o.shape), vmem(q.shape),
            vmem(tok.shape), vmem((width, 4 * rows)), vmem((128, 4 * rows), f32), vmem((4 * rows, 128), f32),
            vmem((4 * rows, 128), f32), vmem((3, 4 * rows, 128)), vmem((3, 4 * rows, 128)),
            vmem((4, rows, PACK)), vmem((4, rows, PACK)),
            vmem((2, 4, ext, PACK)), vmem((4, ext, PACK)), vmem((4, ext, PACK)), vmem((3, ext, PACK)), vmem((2, 4, ext, PACK)),
            vmem((4, 4, length, cols)), vmem((4, 4, length, cols)),
            vmem((4, 2, cut, cols)), vmem((4, 2, length - cut, cols)), vmem((4, cut, cols)), vmem((4, length - cut, cols)),
            vmem((3, length, cols)), vmem((2, 4, length, cols)),
            vmem((4, 4, 16, width)), vmem((3, 4, 16, width)), vmem((3, 16, width)), vmem((16, width)),
        ] + semaphores(),
        compiler_params=params(2),
    )(do, q, k, v, o, tok, grads, sums)


def run_ffn(lengths, att, tokens, cotangent, w_in, w_back, w_out, small):
    rows, width = tokens.shape
    hidden = w_in.shape[1]
    ch = hidden // 8
    S = jax.ShapeDtypeStruct
    one = S((rows, width), bf16)
    return pl.pallas_call(
        ffn_kernel,
        out_shape=(one, S((rows, width), f32), S((4, rows, 256), bf16), S((2, 4, 4, width // 4 + 192 + 48, ch), bf16), S((4, 16, width), bf16)),
        in_specs=[SMEM] + [VMEM] * 3 + [ANY] * 3 + [VMEM],
        out_specs=[VMEM] * 5,
        scratch_shapes=[
            vmem((width, hidden)), vmem((hidden, width)), vmem((width, width)),
            vmem((8, rows, ch)), vmem((8, rows, ch), f32), vmem((8, rows, ch)),
            vmem((rows, width), f32), vmem((rows, width), f32), vmem((rows, width), f32),
            vmem((rows, width)), vmem((width, rows)), vmem((rows, width)), vmem((rows, width), f32), vmem((8, 8, ch), f32),
            pltpu.SemaphoreType.DMA((24,)),
        ],
        compiler_params=pltpu.CompilerParams(vmem_limit_bytes=VMEM_BYTES),
    )(lengths, att, tokens, cotangent, w_in, w_back, w_out, small)


def run_final(dproj, wq_full, gh1, gw, fin, sums):
    rows, width = gh1.shape
    shard = width // PLANES
    S = jax.ShapeDtypeStruct
    one = S((1, shard), f32)
    return pl.pallas_call(
        final_kernel,
        out_shape=(
            S((rows, width), bf16), S((shard, 3 * width), f32), S((shard, 8 * fin.shape[3]), f32),
            S((2 * fin.shape[3], width), f32), S((shard, width), f32), one, one, one, one, one, one, one, one, S((1, width), f32),
        ),
        in_specs=[VMEM, ANY] + [VMEM] * 4,
        out_specs=[VMEM] * 14,
        scratch_shapes=[vmem((4, width, PACK)), pltpu.SemaphoreType.DMA((4,))],
        compiler_params=pltpu.CompilerParams(vmem_limit_bytes=VMEM_BYTES),
    )(dproj, wq_full, gh1, gw, fin, sums)


def planned(
    tokens, lengths, w_qkv, q_bias, v_bias, w_out, out_bias, ln1_gain, ln1_bias,
    w_in, in_bias, w_back, back_bias, ln2_gain, ln2_bias, cotangent,
):
    width = tokens.shape[2]
    shard = q_bias.shape[0]
    gap, half = jnp.zeros((width - shard,), bf16), jnp.zeros((64,), bf16)
    vectors = []
    for a in (out_bias, ln1_gain, ln1_bias, back_bias, ln2_gain, ln2_bias):
        vectors += [a, gap]
    vectors += [in_bias, half, v_bias[0:64], half, v_bias[64:128], q_bias, half, half, v_bias[128:192]]
    vectors += [jnp.zeros((width - PACK + 8 * width,), bf16)]
    small = jnp.concatenate(vectors).reshape(16, width)
    q, k, v, o, tok_all, att, small_all, full_in, full_back, full_out, wq_full = run_forward(
        lengths, tokens[0], w_qkv, w_in, w_back, w_out, small
    )
    output, gh1, do, grads, sums = run_ffn(
        lengths, att, tokens[0], cotangent[0], full_in, full_back, full_out, small_all
    )
    dproj, gw, fin, sums_f = run_backward(do, q, k, v, o, tok_all, grads, sums)
    gt, gqkv, gin, gback, gout, qb, vb, ob, g1, b1, bb, g2, b2, ib = run_final(dproj, wq_full, gh1, gw, fin, sums_f)
    flat = lambda a: a.reshape(a.shape[1])
    return (
        output[None], gt[None], gqkv, flat(qb), flat(vb), gout, flat(ob), flat(g1), flat(b1), gin, flat(ib),
        gback, flat(bb), flat(g2), flat(b2),
    )


masked_score = -1e30


def passed_along(block, axis, distance):
    devices = range(lax.axis_size(axis))
    route = [((i - distance) % len(devices), i) for i in devices]
    return lax.ppermute(block, axis, route)


def norm_forward(hidden, gain_vec, shift_vec):
    average = jnp.mean(hidden, axis=-1, keepdims=True)
    centred = hidden - average
    variance = jnp.mean(centred * centred, axis=-1, keepdims=True)
    inverse = lax.rsqrt(variance + 1e-05)
    normed = centred * inverse
    return (normed * gain_vec + shift_vec, normed, inverse)


def norm_backward(grad_norm, normed, inverse, gain_vec):
    scaled = grad_norm * gain_vec
    grad_input = inverse * (
        scaled
        - jnp.mean(scaled, axis=-1, keepdims=True)
        - normed * jnp.mean(scaled * normed, axis=-1, keepdims=True)
    )
    return (grad_input, jnp.sum(grad_norm * normed, axis=0), jnp.sum(grad_norm, axis=0))


def forward_tile(state_in, query_heads, key_pair, length):
    old_max, old_sum, old_acc = state_in
    key_rows = key_pair.shape[0]
    head_count = query_heads.shape[1]
    head_size = query_heads.shape[2]
    key_heads = key_pair[:, 0].reshape(key_rows, head_count, head_size)
    value_heads = key_pair[:, 1].reshape(key_rows, head_count, head_size)
    key_ok = jnp.arange(key_rows, dtype=jnp.int32) < length
    scores = jnp.einsum(
        "qhd,khd->hqk", query_heads, key_heads, preferred_element_type=jnp.float32
    ) * head_size ** (-0.5)
    scores = jnp.where(key_ok[None, None, :], scores, masked_score)
    new_max = jnp.maximum(old_max, jnp.max(scores, axis=2))
    prob_tile = jnp.where(key_ok[None, None, :], jnp.exp(scores - new_max[:, :, None]), 0.0)
    new_sum = jnp.sum(prob_tile, axis=2)
    new_acc = jnp.einsum(
        "hqk,khd->hqd",
        prob_tile.astype(jnp.bfloat16),
        value_heads,
        preferred_element_type=jnp.float32,
    )
    return (new_max, new_sum, new_acc)


def backward_tile(query_pair, log_total, delta, key_pair, key_start, length):
    query_rows = query_pair.shape[0]
    key_rows = key_pair.shape[0]
    model_width = query_pair.shape[2]
    head_count = log_total.shape[0]
    head_size = model_width // head_count
    score_scale = head_size ** (-0.5)
    query_heads = query_pair[:, 0].reshape(query_rows, head_count, head_size)
    grad_heads = query_pair[:, 1].reshape(query_rows, head_count, head_size)
    key_heads = key_pair[:, 0].reshape(key_rows, head_count, head_size)
    value_heads = key_pair[:, 1].reshape(key_rows, head_count, head_size)
    key_ok = key_start + jnp.arange(key_rows, dtype=jnp.int32) < length
    scores = (
        jnp.einsum("qhd,khd->hqk", query_heads, key_heads, preferred_element_type=jnp.float32)
        * score_scale
    )
    prob_tile = jnp.where(key_ok[None, None, :], jnp.exp(scores - log_total[:, :, None]), 0.0)
    grad_values = jnp.einsum(
        "hqk,qhd->khd",
        prob_tile.astype(jnp.bfloat16),
        grad_heads,
        preferred_element_type=jnp.float32,
    )
    grad_probs = jnp.einsum(
        "qhd,khd->hqk", grad_heads, value_heads, preferred_element_type=jnp.float32
    )
    grad_scores = (prob_tile * (grad_probs - delta[:, :, None])).astype(jnp.bfloat16)
    grad_queries = (
        jnp.einsum("hqk,khd->qhd", grad_scores, key_heads, preferred_element_type=jnp.float32)
        * score_scale
    )
    grad_keys = (
        jnp.einsum("hqk,qhd->khd", grad_scores, query_heads, preferred_element_type=jnp.float32)
        * score_scale
    )
    grad_pair = jnp.stack([grad_keys, grad_values], axis=1).reshape(key_rows, 2, model_width)
    return (grad_queries.reshape(query_rows, model_width), grad_pair)


def on_device(
    tokens,
    lengths,
    w_qkv,
    q_bias,
    v_bias,
    w_out,
    out_bias,
    ln1_gain,
    ln1_bias,
    w_in,
    in_bias,
    w_back,
    back_bias,
    ln2_gain,
    ln2_bias,
    cotangent,
):
    gathered = (
        lax.all_gather(w_qkv, "fsdp", axis=0, tiled=True),
        lax.all_gather(q_bias, "fsdp", axis=0, tiled=True),
        lax.all_gather(v_bias, "fsdp", axis=0, tiled=True),
        lax.all_gather(w_out, "fsdp", axis=0, tiled=True),
        lax.all_gather(out_bias, "fsdp", axis=0, tiled=True),
        lax.all_gather(ln1_gain, "fsdp", axis=0, tiled=True),
        lax.all_gather(ln1_bias, "fsdp", axis=0, tiled=True),
        lax.all_gather(w_in, "fsdp", axis=0, tiled=True),
        lax.all_gather(in_bias, "fsdp", axis=0, tiled=True),
        lax.all_gather(w_back, "fsdp", axis=0, tiled=True),
        lax.all_gather(back_bias, "fsdp", axis=0, tiled=True),
        lax.all_gather(ln2_gain, "fsdp", axis=0, tiled=True),
        lax.all_gather(ln2_bias, "fsdp", axis=0, tiled=True),
    )
    (
        full_qkv,
        full_qbias,
        full_vbias,
        full_out,
        full_obias,
        full_g1,
        full_n1,
        full_in,
        full_ibias,
        full_back,
        full_bbias,
        full_g2,
        full_n2,
    ) = gathered
    f32 = jnp.float32
    seq_index = lax.axis_index("seq")
    seq_count = lax.axis_size("seq")
    token_rows = tokens.shape[1]
    model_width = tokens.shape[2]
    head_count = HEADS
    head_size = model_width // head_count
    length = lengths[0]
    my_start = seq_index * token_rows
    row_valid = (my_start + jnp.arange(token_rows, dtype=jnp.int32) < length).astype(f32)
    inputs_b = tokens[0]
    inputs_f = inputs_b.astype(f32)
    bias_all = jnp.concatenate(
        [full_qbias.astype(f32), jnp.zeros((model_width,), f32), full_vbias.astype(f32)]
    )
    projected = (jnp.dot(inputs_b, full_qkv, preferred_element_type=f32) + bias_all).astype(
        jnp.bfloat16
    )
    query_heads = projected[:, :model_width].reshape(token_rows, head_count, head_size)
    key_pair = projected[:, model_width:].reshape(token_rows, 2, model_width)
    init_state = (
        jnp.full((head_count, token_rows), masked_score, f32),
        jnp.zeros((head_count, token_rows), f32),
        jnp.zeros((head_count, token_rows, head_size), f32),
    )
    pieces = lax.all_gather(key_pair, "seq", axis=0, tiled=True)
    run_max, run_sum, run_acc = forward_tile(init_state, query_heads, pieces, length)
    positive = run_sum > 0.0
    safe_sum = jnp.where(positive, run_sum, 1.0)
    attended_heads = jnp.where(positive[:, :, None], run_acc / safe_sum[:, :, None], 0.0)
    log_total = jnp.where(positive, run_max + jnp.log(safe_sum), 0.0)
    attended_f = attended_heads.transpose(1, 0, 2).reshape(token_rows, model_width)
    attended_b = attended_f.astype(jnp.bfloat16)
    branch_f = jnp.dot(attended_b, full_out, preferred_element_type=f32) + full_obias.astype(f32)
    first_norm, normed_one, inverse_one = norm_forward(
        inputs_f + branch_f, full_g1.astype(f32), full_n1.astype(f32)
    )
    first_low = first_norm.astype(jnp.bfloat16)
    inner_act = jnp.dot(first_low, full_in, preferred_element_type=f32) + full_ibias.astype(f32)
    activated_b = jax.nn.gelu(inner_act, approximate=False).astype(jnp.bfloat16)
    second = jnp.dot(activated_b, full_back, preferred_element_type=f32) + full_bbias.astype(f32)
    result, normed_two, inverse_two = norm_forward(
        first_norm + second, full_g2.astype(f32), full_n2.astype(f32)
    )
    output = (result * row_valid[:, None]).astype(jnp.bfloat16)
    grad_result = cotangent[0].astype(f32) * row_valid[:, None]
    grad_h2, g_ln2_gain, g_ln2_bias = norm_backward(
        grad_result, normed_two, inverse_two, full_g2.astype(f32)
    )
    grad_second = grad_h2.astype(jnp.bfloat16)
    g_w_back = jnp.einsum("tf,td->fd", activated_b, grad_second, preferred_element_type=f32)
    g_back_bias = jnp.sum(grad_second.astype(f32), axis=0)
    grad_act = jnp.einsum("td,fd->tf", grad_second, full_back, preferred_element_type=f32)
    gelu_value, gelu_pull = jax.vjp(
        lambda values_in: jax.nn.gelu(values_in, approximate=False), inner_act
    )
    grad_inner = gelu_pull(grad_act)[0].astype(jnp.bfloat16)
    g_w_in = jnp.einsum("td,tf->df", first_low, grad_inner, preferred_element_type=f32)
    g_in_bias = jnp.sum(grad_inner.astype(f32), axis=0)
    grad_first = grad_h2 + jnp.einsum("tf,df->td", grad_inner, full_in, preferred_element_type=f32)
    grad_h1, g_ln1_gain, g_ln1_bias = norm_backward(
        grad_first, normed_one, inverse_one, full_g1.astype(f32)
    )
    grad_branch = grad_h1.astype(jnp.bfloat16)
    g_w_out = jnp.einsum("tc,td->cd", attended_b, grad_branch, preferred_element_type=f32)
    g_out_bias = jnp.sum(grad_branch.astype(f32), axis=0)
    grad_attended = jnp.einsum(
        "td,cd->tc", grad_branch, full_out, preferred_element_type=f32
    ).astype(jnp.bfloat16)
    delta = jnp.sum(
        (grad_attended.astype(f32) * attended_f).reshape(token_rows, head_count, head_size), axis=2
    ).T
    query_pair = jnp.stack([projected[:, :model_width], grad_attended], axis=1)
    zero_rows = jnp.zeros((token_rows, model_width), f32)
    zero_pair = jnp.zeros((token_rows, 2, model_width), f32)

    def visit_keys(hop_index, grad_q, moving_pair, grad_pair):
        anchor = (seq_index - hop_index) % seq_count
        add_q, add_pair = backward_tile(
            query_pair, log_total, delta, moving_pair, anchor * token_rows, length
        )
        return (grad_q + add_q, grad_pair + add_pair)

    def return_key_grads(grad_pair):
        return passed_along(grad_pair.astype(jnp.bfloat16), "seq", 1).astype(grad_pair.dtype)

    def key_hop(hop_index, loop_state):
        grad_q, moving_pair, grad_pair = loop_state
        grad_q, grad_pair = visit_keys(hop_index, grad_q, moving_pair, grad_pair)
        moved = passed_along(moving_pair, "seq", 1)
        return (grad_q, moved, return_key_grads(grad_pair))

    grad_q, moving_pair, grad_pair = lax.fori_loop(
        0, seq_count - 1, key_hop, (zero_rows, key_pair, zero_pair)
    )
    grad_q, grad_pair = visit_keys(seq_count - 1, grad_q, moving_pair, grad_pair)
    grad_pair = return_key_grads(grad_pair)
    grad_projected = jnp.concatenate(
        [grad_q, grad_pair.reshape(token_rows, 2 * model_width)], axis=1
    ).astype(jnp.bfloat16)
    g_w_qkv = jnp.einsum("td,te->de", inputs_b, grad_projected, preferred_element_type=f32)
    grad_proj_f = grad_projected.astype(f32)
    g_q_bias = jnp.sum(grad_proj_f[:, :model_width], axis=0)
    g_v_bias = jnp.sum(grad_proj_f[:, 2 * model_width :], axis=0)
    grad_input = grad_h1 + jnp.einsum(
        "te,de->td", grad_projected, full_qkv, preferred_element_type=f32
    )
    local_grads = (
        g_w_qkv,
        g_q_bias,
        g_v_bias,
        g_w_out,
        g_out_bias,
        g_ln1_gain,
        g_ln1_bias,
        g_w_in,
        g_in_bias,
        g_w_back,
        g_back_bias,
        g_ln2_gain,
        g_ln2_bias,
    )
    owned = (
        lax.psum_scatter(
            local_grads[0].astype(jnp.bfloat16), "fsdp", scatter_dimension=0, tiled=True
        ).astype(jnp.float32),
        lax.psum_scatter(
            local_grads[1].astype(jnp.bfloat16), "fsdp", scatter_dimension=0, tiled=True
        ).astype(jnp.float32),
        lax.psum_scatter(
            local_grads[2].astype(jnp.bfloat16), "fsdp", scatter_dimension=0, tiled=True
        ).astype(jnp.float32),
        lax.psum_scatter(
            local_grads[3].astype(jnp.bfloat16), "fsdp", scatter_dimension=0, tiled=True
        ).astype(jnp.float32),
        lax.psum_scatter(
            local_grads[4].astype(jnp.bfloat16), "fsdp", scatter_dimension=0, tiled=True
        ).astype(jnp.float32),
        lax.psum_scatter(
            local_grads[5].astype(jnp.bfloat16), "fsdp", scatter_dimension=0, tiled=True
        ).astype(jnp.float32),
        lax.psum_scatter(
            local_grads[6].astype(jnp.bfloat16), "fsdp", scatter_dimension=0, tiled=True
        ).astype(jnp.float32),
        lax.psum_scatter(
            local_grads[7].astype(jnp.bfloat16), "fsdp", scatter_dimension=0, tiled=True
        ).astype(jnp.float32),
        lax.psum_scatter(
            local_grads[8].astype(jnp.bfloat16), "fsdp", scatter_dimension=0, tiled=True
        ).astype(jnp.float32),
        lax.psum_scatter(
            local_grads[9].astype(jnp.bfloat16), "fsdp", scatter_dimension=0, tiled=True
        ).astype(jnp.float32),
        lax.psum_scatter(
            local_grads[10].astype(jnp.bfloat16), "fsdp", scatter_dimension=0, tiled=True
        ).astype(jnp.float32),
        lax.psum_scatter(
            local_grads[11].astype(jnp.bfloat16), "fsdp", scatter_dimension=0, tiled=True
        ).astype(jnp.float32),
        lax.psum_scatter(
            local_grads[12].astype(jnp.bfloat16), "fsdp", scatter_dimension=0, tiled=True
        ).astype(jnp.float32),
    )
    totals = (
        lax.psum(owned[0].astype(jnp.bfloat16), "seq").astype(jnp.float32),
        lax.psum(owned[1].astype(jnp.bfloat16), "seq").astype(jnp.float32),
        lax.psum(owned[2].astype(jnp.bfloat16), "seq").astype(jnp.float32),
        lax.psum(owned[3].astype(jnp.bfloat16), "seq").astype(jnp.float32),
        lax.psum(owned[4].astype(jnp.bfloat16), "seq").astype(jnp.float32),
        lax.psum(owned[5].astype(jnp.bfloat16), "seq").astype(jnp.float32),
        lax.psum(owned[6].astype(jnp.bfloat16), "seq").astype(jnp.float32),
        lax.psum(owned[7].astype(jnp.bfloat16), "seq").astype(jnp.float32),
        lax.psum(owned[8].astype(jnp.bfloat16), "seq").astype(jnp.float32),
        lax.psum(owned[9].astype(jnp.bfloat16), "seq").astype(jnp.float32),
        lax.psum(owned[10].astype(jnp.bfloat16), "seq").astype(jnp.float32),
        lax.psum(owned[11].astype(jnp.bfloat16), "seq").astype(jnp.float32),
        lax.psum(owned[12].astype(jnp.bfloat16), "seq").astype(jnp.float32),
    )
    return (output[None], grad_input.astype(jnp.bfloat16)[None]) + tuple(totals)


def solution(mesh):
    fits = mesh.shape["seq"] == 2 * CHIPS and mesh.shape["fsdp"] == PLANES
    return jax.shard_map(
        planned if fits else on_device,
        mesh=mesh,
        in_specs=(
            P("fsdp", "seq", None),
            P("fsdp"),
            P("fsdp", None),
            P("fsdp"),
            P("fsdp"),
            P("fsdp", None),
            P("fsdp"),
            P("fsdp"),
            P("fsdp"),
            P("fsdp", None),
            P("fsdp"),
            P("fsdp", None),
            P("fsdp"),
            P("fsdp"),
            P("fsdp"),
            P("fsdp", "seq", None),
        ),
        out_specs=(
            P("fsdp", "seq", None),
            P("fsdp", "seq", None),
            P("fsdp", None),
            P("fsdp"),
            P("fsdp"),
            P("fsdp", None),
            P("fsdp"),
            P("fsdp"),
            P("fsdp"),
            P("fsdp", None),
            P("fsdp"),
            P("fsdp", None),
            P("fsdp"),
            P("fsdp"),
            P("fsdp"),
        ),
        check_vma=False,
    )
```

```python
import functools
import math

import jax
import jax.numpy as jnp
from jax import lax
from jax.experimental import pallas as pl
from jax.experimental.pallas import tpu as pltpu
from jax.sharding import PartitionSpec as P

HEADS = 12
bf16 = jnp.bfloat16
f32 = jnp.float32
MESH = pl.DeviceIdType.MESH
LOG2E = math.log2(math.e)
NT = (((1,), (1,)), ((), ()))
NN = (((1,), (0,)), ((), ()))

PLANES = 4
CHIPS = 4
GROUP_HEADS = 3
PACKED = (12, 24, 13, 25, 0, 1, 2, None, 14, 26)
KV_TILE = (0, 1, 4)
PACK = 640


def dot(a, b, dims=NN):
    return lax.dot_general(a, b, dims, preferred_element_type=f32)


class Net:
    def __init__(self, send_sems, recv_sems):
        self.send_sems, self.recv_sems = send_sems, recv_sems
        self.specs = {}

    def add(self, name, src, dst, device):
        self.specs[name] = (len(self.specs), src, dst, device)

    def get(self, name):
        k, src, dst, device = self.specs[name]
        return pltpu.make_async_remote_copy(
            src_ref=src(),
            dst_ref=dst(),
            send_sem=self.send_sems.at[k],
            recv_sem=self.recv_sems.at[k],
            device_id=device,
            device_id_type=MESH,
        )

    def start(self, *names):
        for name in names:
            self.get(name).start()

    def recv(self, *names):
        for name in names:
            self.get(name).wait_recv()

    def sent(self, *names):
        for name in names:
            self.get(name).wait_send()


class Local:
    def __init__(self, sems):
        self.sems = sems
        self.specs = {}

    def add(self, name, src, dst):
        self.specs[name] = (len(self.specs), src, dst)

    def get(self, name):
        k, src, dst = self.specs[name]
        return pltpu.make_async_copy(src(), dst(), self.sems.at[k])

    def start(self, *names):
        for name in names:
            self.get(name).start()

    def wait(self, *names):
        for name in names:
            self.get(name).wait()


def coordinates():
    s, z = lax.axis_index("seq"), lax.axis_index("fsdp")
    core = lax.rem(s, 2)
    chip = lax.div(s, 2)
    return s, z, core, chip


def flip(value, mask):
    low, high = lax.rem(value, 2), lax.div(value, 2)
    if mask & 1:
        low = 1 - low
    if mask & 2:
        high = 1 - high
    return high * 2 + low


def hello(devices):
    barrier = pltpu.get_barrier_semaphore()
    for device in devices:
        pl.semaphore_signal(barrier, inc=1, device_id=device, device_id_type=MESH)


def met(count):
    pl.semaphore_wait(pltpu.get_barrier_semaphore(), count)


def greet(devices):
    hello(devices)
    met(len(devices))


def lanes_of(rows=1):
    return lax.broadcasted_iota(jnp.int32, (rows, 128), 1)


def split3(column):
    hi = column.astype(bf16).astype(f32)
    mid = (column - hi).astype(bf16).astype(f32)
    return hi, mid, column - hi - mid


def forward_kernel(
    length_ref, tok_ref, wraw_ref, win_ref, wback_ref, wout_ref, small_ref,
    q_out, k_out, v_out, o_out, tok_out, att_out, small_out, win_full, wout_full, wq_out, wback_full, wq_full,
    tok, wqv, q_s, k_s, v_s, o_s, att, atts, kvs, kvr, small, wraw, wq_ref, send_sems, recv_sems, local_sems,
):
    s, z, core, chip = coordinates()
    other = 1 - core
    rows = tok_ref.shape[0]
    half = rows // 2
    shard = wq_ref.shape[1]
    piece = shard // 2
    peer = [None] + [(flip(chip, j) * 2 + core, z) for j in (1, 2, 3)]
    mate = (chip * 2 + other, z)
    plane = [None] + [(s, flip(z, dz)) for dz in (1, 2, 3)]
    zs = [z] + [flip(z, dz) for dz in (1, 2, 3)]
    net, loc = Net(send_sems, recv_sems), Local(local_sems)
    width = win_full.shape[1] // 8
    back = wback_ref.shape[0]
    bpiece = back // 8
    arrays = ("out", "in", "back")
    at = lambda start, size, unit=16: pl.ds(pl.multiple_of(start, unit), size)

    def part(a, zz, m, c):
        if a == "in":
            return win_full.at[at(zz * shard, shard), at((m * 4 + c) * width, width, 128)]
        if a == "back":
            return wback_full.at[at(zz * back + (m * 4 + c) * bpiece, bpiece), :]
        return wout_full.at[at(zz * shard + c * (shard // 4), shard // 4), at(m * width, width, 128)]

    def own_part(a, m, c):
        if a == "in":
            return win_ref.at[:, at((m * 4 + c) * width, width, 128)]
        if a == "back":
            return wback_ref.at[at((m * 4 + c) * bpiece, bpiece), :]
        return wout_ref.at[at(c * (shard // 4), shard // 4), at(m * width, width, 128)]

    def side(a, zz, m):
        if a == "in":
            return win_full.at[at(zz * shard, shard), at(m * 4 * width, 4 * width, 128)]
        if a == "back":
            return wback_full.at[at(zz * back + m * 4 * bpiece, 4 * bpiece), :]
        return wout_full.at[at(zz * shard, shard), at(m * width, width, 128)]

    for dz in (1, 2, 3):
        net.add(("wq", dz), lambda: wq_ref.at[chip, pl.ds(pl.multiple_of(core * piece, 16), piece), :],
                lambda: wqv.at[pl.ds(pl.multiple_of(z * shard + core * piece, 16), piece), :], plane[dz])
        net.add(("wqm", dz), lambda dz=dz: wqv.at[pl.ds(pl.multiple_of(zs[dz] * shard + core * piece, 16), piece), :],
                lambda dz=dz: wqv.at[pl.ds(pl.multiple_of(zs[dz] * shard + core * piece, 16), piece), :], mate)
        net.add(("small", dz), lambda: small_ref, lambda: small.at[z], plane[dz])
    top, bottom = slice(0, half), slice(half, rows)
    net.add("t1a", lambda: tok_ref.at[top], lambda: tok.at[1, top], peer[1])
    net.add("t1b", lambda: tok_ref.at[bottom], lambda: tok.at[1, bottom], peer[1])
    net.add("t2b", lambda: tok_ref.at[bottom], lambda: tok.at[2, bottom], peer[2])
    net.add("t2a", lambda: tok_ref.at[top], lambda: tok.at[2, top], peer[2])
    net.add("t3a", lambda: tok.at[1, top], lambda: tok.at[3, top], peer[2])
    net.add("t3b", lambda: tok.at[2, bottom], lambda: tok.at[3, bottom], peer[1])
    for j in range(4):
        net.add(("kv", j), lambda j=j: kvs.at[j], lambda j=j: kvr.at[j], mate)
    for j in (1, 2, 3):
        net.add(("att0", j), lambda j=j: atts.at[j, :, 0:128], lambda: att.at[chip, :, 0:128], peer[j])
        net.add(("att1", j), lambda j=j: atts.at[j, :, 128:256], lambda: att.at[chip, :, 128:256], peer[j])
    for a in arrays:
        via, last = (1, 2) if a == "in" else (2, 1)
        for dz in (1, 2, 3):
            net.add((a, "z", dz), lambda a=a: own_part(a, core, chip), lambda a=a: part(a, z, core, chip), plane[dz])
            for j in (1, 2):
                net.add((a, j, dz), lambda a=a, dz=dz: part(a, zs[dz], core, chip), lambda a=a, dz=dz: part(a, zs[dz], core, chip), peer[j])
            net.add((a, 3, dz), lambda a=a, dz=dz, via=via: part(a, zs[dz], core, flip(chip, via)),
                    lambda a=a, dz=dz, via=via: part(a, zs[dz], core, flip(chip, via)), peer[last])
            net.add((a, "m", dz), lambda a=a, dz=dz: side(a, zs[dz], core), lambda a=a, dz=dz: side(a, zs[dz], core), mate)
    for dz in (1, 2, 3):
        net.add(("qkv", "z", dz), lambda: wq_ref.at[core * 2 + lax.div(chip, 2), pl.ds(pl.multiple_of(lax.rem(chip, 2) * piece, 16), piece), :],
                lambda: wq_full.at[z, core * 2 + lax.div(chip, 2), pl.ds(pl.multiple_of(lax.rem(chip, 2) * piece, 16), piece), :], plane[dz])
    loc.add("raw", lambda: wraw_ref, lambda: wraw)
    loc.add("tok", lambda: tok_ref, lambda: tok.at[0])
    loc.add("wq", lambda: wq_ref.at[chip], lambda: wqv.at[pl.ds(pl.multiple_of(z * shard, 16), shard), :])
    loc.add("small", lambda: small_ref, lambda: small.at[z])
    outs = (("wq_o", wq_ref, wq_out), ("k_o", k_s, k_out), ("v_o", v_s, v_out), ("q_o", q_s, q_out), ("o_o", o_s, o_out),
            ("tok_o", tok, tok_out), ("att_o", att, att_out), ("small_o", small, small_out))
    for name, src, dst in outs:
        loc.add(name, lambda src=src: src, lambda dst=dst: dst)

    loc.start("raw", "tok", "small")
    hello(peer[1:] + [mate] + plane[1:])
    lane = lanes_of()
    loc.wait("raw")
    for g in range(CHIPS):
        for t in range(PACK // 128):
            halves = []
            for upper in (0, 1):
                block = PACKED[2 * t + upper]
                if block is None:
                    halves.append(0.0)
                    continue
                block += GROUP_HEADS * g
                tile_of = lambda i: wraw[:, i * 128 : (i + 1) * 128].astype(f32)
                halves.append(half_tile(tile_of, block, upper))
            wq_ref[g, :, t * 128 : (t + 1) * 128] = jnp.where(lane < 64, halves[0], halves[1]).astype(bf16)
    loc.start("wq", "wq_o")
    met(len(peer[1:] + [mate] + plane[1:]))
    net.start(*[("wq", dz) for dz in (1, 2, 3)], *[("small", dz) for dz in (1, 2, 3)])
    net.start("t1a", "t2b", "t1b", "t2a")
    for dz in (1, 2, 3):
        net.recv(("wq", dz))
        net.start(("wqm", dz))
    for dz in (1, 2, 3):
        net.start(*[(a, "z", dz) for a in arrays])
    loc.wait("tok", "wq", "small")
    for dz in (1, 2, 3):
        net.recv(("small", dz), ("wqm", dz))

    length = length_ref[0]
    bias = small[chip, 3:4, 0:PACK].astype(f32)

    def keep(tile, h, slot, block):
        position = block * rows + lax.broadcasted_iota(jnp.int32, (rows, 1), 0)
        mask = jnp.where(position < length, 0.0, -1e30).astype(f32)
        ones = jnp.where((lane > 64) & (lane < 68), 1.0, 0.0)
        k_s[h, slot * rows : (slot + 1) * rows, :] = jnp.where(
            lane < 64, tile, jnp.where(lane == 64, mask, ones)
        ).astype(bf16)
        v_s[h, slot * rows : (slot + 1) * rows, :] = jnp.where(
            lane < 64, pltpu.roll(tile, 64, 1), jnp.where(lane < 67, 1.0, 0.0)
        ).astype(bf16)

    def project(j):
        proj = dot(tok[j], wqv[...]) + bias
        for h in range(GROUP_HEADS):
            tile = proj[:, KV_TILE[h] * 128 : (KV_TILE[h] + 1) * 128]
            keep(tile.astype(bf16).astype(f32), h, j, flip(chip, j) * 2 + core)
            kvs[j, :, h * 128 : (h + 1) * 128] = tile.astype(bf16)
            first = 256 + (h // 2) * 128
            tile = proj[:, first : first + 128].astype(bf16).astype(f32) * 0.125
            if h == 1:
                tile = pltpu.roll(tile, 64, 1)
            q_s[h, j * rows : (j + 1) * rows, :] = jnp.where(
                lane < 64, tile, jnp.where(lane == 64, 1.0, 0.0)
            ).astype(bf16)
        net.start(("kv", j))

    def keep_other(j):
        net.recv(("kv", j))
        for h in range(GROUP_HEADS):
            tile = kvr[j, :, h * 128 : (h + 1) * 128].astype(f32)
            keep(tile, h, 4 + j, flip(chip, j) * 2 + other)

    project(0)
    net.recv("t1a")
    net.start("t3a")
    net.recv("t2b")
    net.start("t3b")
    net.recv("t1b")
    project(1)
    net.recv("t2a")
    project(2)
    keep_other(0)
    keep_other(1)
    keep_other(2)
    net.recv("t3a", "t3b")
    project(3)
    keep_other(3)
    loc.start("k_o", "v_o", "tok_o", "small_o")

    query_tile, key_chunk = 2 * rows, 4 * rows
    tiles = 4 * rows // query_tile
    chunks = 8 * rows // key_chunk

    def first_hop(dz):
        for a in arrays:
            net.recv((a, "z", dz))
            net.start((a, 1, dz), (a, 2, dz))

    def second_hop(dz):
        for a in arrays:
            net.recv((a, 1, dz), (a, 2, dz))
            net.start((a, 3, dz))

    def third_hop(dz):
        for a in arrays:
            net.recv((a, 3, dz))
            net.start((a, "m", dz))

    def attended_tile(which):
        for j in range(4):
            r = slice(j * rows, (j + 1) * rows)
            if which == 0:
                upper = pltpu.roll(o_s[1, r, :].astype(f32), 64, 1)
                value = jnp.where(lane < 64, o_s[0, r, :].astype(f32), upper)
            else:
                value = jnp.where(lane < 64, o_s[2, r, :].astype(f32), 0.0)
            place = slice(which * 128, (which + 1) * 128)
            if j == 0:
                att[chip, :, place] = value.astype(bf16)
            else:
                atts[j, :, place] = value.astype(bf16)
                net.start((f"att{which}", j))

    def visit(t, carry):
        h, i = lax.div(t, tiles), lax.rem(t, tiles)
        qrows = pl.ds(pl.multiple_of(i * query_tile, query_tile), query_tile)
        q = q_s[h, qrows, :]
        top_score = jnp.full((query_tile, 1), -1e30, f32)
        acc = jnp.zeros((query_tile, 128), f32)
        for c in range(chunks):
            krows = slice(c * key_chunk, (c + 1) * key_chunk)
            scores = dot(q, k_s[h, krows, :], NT)
            new_top = jnp.maximum(top_score, jnp.max(scores, axis=1, keepdims=True))
            probs = jnp.exp2((scores - new_top) * LOG2E)
            fade = jnp.exp2((top_score - new_top) * LOG2E)
            acc = acc * fade + dot(probs.astype(bf16), v_s[h, krows, :])
            top_score = new_top
        total = acc[:, 64:65]
        o_s[h, qrows, :] = (acc / total).astype(bf16)
        hi, mid, low = split3(-(top_score + jnp.log(total)))
        wide = q.astype(f32)
        wide = jnp.where(lane == 65, hi, jnp.where(lane == 66, mid, jnp.where(lane == 67, low, wide)))
        q_s[h, qrows, :] = wide.astype(bf16)

        for at, work in enumerate((
            lambda: first_hop(1),
            lambda: (first_hop(2), second_hop(1)),
            lambda: (first_hop(3), net.start(*[("qkv", "z", dz) for dz in (1, 2, 3)]), second_hop(2), third_hop(1)),
            lambda: (attended_tile(0), second_hop(3)),
            lambda: third_hop(2),
            lambda: attended_tile(1),
        )):
            pl.when(t == at)(lambda work=work: (work(), None)[1])
        return carry

    lax.fori_loop(0, GROUP_HEADS * tiles, visit, 0)
    third_hop(3)
    loc.start("q_o", "o_o")
    for j in (1, 2, 3):
        net.recv(("att0", j), ("att1", j))
    loc.start("att_o")
    for dz in (1, 2, 3):
        for a in arrays:
            net.recv((a, "m", dz))
        net.recv(("qkv", "z", dz))
    for name in net.specs:
        net.sent(name)
    loc.wait(*[name for name, _, _ in outs])


def backward_kernel(
    do_ref, q_ref, k_ref, v_ref, o_ref, tok_ref, grads_ref, sums_ref, back_ref,
    dproj_out, gw_out, hw_out, fin_out, finb_out, sums_out,
    do_s, q_s, k_s, v_s, o_s, doa, tok, tokt, dqs, dq_keep, kv_own, kvs, kvr, dall, dproj,
    gw, gwr, gz, gzr, gwf, hw, hwr, hz, hzr, hwf, acc, rb, rx, ry, rx2, ry2, rz, rzb, fin, finb, sums, sums_r, sums_z, sums_f,
    send_sems, recv_sems, local_sems,
):
    s, z, core, chip = coordinates()
    other = 1 - core
    rows = do_ref.shape[1]
    peer = [None] + [(flip(chip, j) * 2 + core, z) for j in (1, 2, 3)]
    mate = (chip * 2 + other, z)
    plane = [None] + [(s, flip(z, dz)) for dz in (1, 2, 3)]
    zs = [z] + [flip(z, dz) for dz in (1, 2, 3)]
    ch = [chip] + [flip(chip, j) for j in (1, 2, 3)]
    net, loc = Net(send_sems, recv_sems), Local(local_sems)
    length = grads_ref.shape[3]
    cut = length // 32 * 16
    xs, ys = slice(0, cut), slice(cut, length)
    shard = tok.shape[2] // PLANES
    piece = shard // 2

    for h in range(GROUP_HEADS):
        net.add(("kv", h), lambda h=h: kvs.at[h], lambda h=h: kvr.at[h], mate)
        place = ((0, 128), (128, 384), (384, 640))[h]
        for j in (1, 2, 3):
            net.add(("dp", h, j), lambda j=j, place=place: dall.at[j, :, place[0] : place[1]],
                    lambda place=place: dproj.at[chip, :, place[0] : place[1]], peer[j])
    order = (3, 2, 1, 0)
    for dz in order:
        net.add(("r1", dz), lambda dz=dz: grads_ref.at[other, zs[dz]], lambda dz=dz: rb.at[zs[dz]], mate)
        for n, j in enumerate((1, 3)):
            net.add(("x1", n, dz), lambda dz=dz, j=j: acc.at[zs[dz], ch[j], xs], lambda dz=dz, n=n: rx.at[zs[dz], n], peer[1])
        net.add(("x2", dz), lambda dz=dz: acc.at[zs[dz], ch[2], xs], lambda dz=dz: rx2.at[zs[dz]], peer[2])
        for n, j in enumerate((2, 3)):
            net.add(("y1", n, dz), lambda dz=dz, j=j: acc.at[zs[dz], ch[j], ys], lambda dz=dz, n=n: ry.at[zs[dz], n], peer[2])
        net.add(("y2", dz), lambda dz=dz: acc.at[zs[dz], ch[1], ys], lambda dz=dz: ry2.at[zs[dz]], peer[1])
        if dz:
            net.add(("rz", dz), lambda dz=dz: acc.at[zs[dz], chip], lambda dz=dz: rz.at[dz - 1], plane[dz])
    for dz in (1, 2, 3):
        net.add(("rzb", dz), lambda dz=dz: back_ref.at[zs[dz]], lambda dz=dz: rzb.at[dz], plane[dz])
    bh = finb.shape[2] // 2
    bx, by = slice(0, bh), slice(bh, 2 * bh)
    net.add("b1", lambda: finb.at[core, chip], lambda: finb.at[core, chip], peer[1])
    net.add("b2", lambda: finb.at[core, chip], lambda: finb.at[core, chip], peer[2])
    net.add("b3x", lambda: finb.at[core, ch[1], bx], lambda: finb.at[core, ch[1], bx], peer[2])
    net.add("b3y", lambda: finb.at[core, ch[2], by], lambda: finb.at[core, ch[2], by], peer[1])
    net.add("bm", lambda: finb.at[core], lambda: finb.at[core], mate)
    net.add("f1", lambda: fin.at[core, chip], lambda: fin.at[core, chip], peer[1])
    net.add("f2", lambda: fin.at[core, chip], lambda: fin.at[core, chip], peer[2])
    net.add("f3x", lambda: fin.at[core, ch[1], xs], lambda: fin.at[core, ch[1], xs], peer[2])
    net.add("f3y", lambda: fin.at[core, ch[2], ys], lambda: fin.at[core, ch[2], ys], peer[1])
    net.add("fm", lambda: fin.at[core], lambda: fin.at[core], mate)
    net.add("s0", lambda: sums_ref, lambda: sums_r.at[0], mate)
    net.add("s1", lambda: sums.at[1], lambda: sums_r.at[1], peer[1])
    net.add("s2", lambda: sums.at[2], lambda: sums_r.at[2], peer[2])
    for dz in (1, 2, 3):
        net.add(("sz", dz), lambda dz=dz: sums.at[3, zs[dz]], lambda dz=dz: sums_z.at[dz - 1], plane[dz])
    for a, w, wr, g, gr, f in (("g", gw, gwr, gz, gzr, gwf), ("h", hw, hwr, hz, hzr, hwf)):
        net.add((a, 0), lambda w=w: w.at[other], lambda wr=wr: wr, mate)
        for dz in (1, 2, 3):
            net.add((a, "z", dz), lambda g=g, dz=dz: g.at[zs[dz]], lambda gr=gr, dz=dz: gr.at[dz - 1], plane[dz])
        for j in (1, 2, 3):
            net.add((a, "f", j), lambda f=f: f.at[core, chip], lambda f=f: f.at[core, chip], peer[j])
        net.add((a, "m"), lambda f=f: f.at[core], lambda f=f: f.at[core], mate)

    loads = (("do", lambda: do_ref, lambda: do_s), ("o", lambda: o_ref, lambda: o_s),
             ("tok", lambda: tok_ref, lambda: tok), ("q", lambda: q_ref, lambda: q_s),
             ("k", lambda: k_ref, lambda: k_s), ("v", lambda: v_ref, lambda: v_s),
             ("sums", lambda: sums_ref, lambda: sums.at[0]), ("back", lambda: back_ref.at[z], lambda: rzb.at[0]), ("acc", lambda: grads_ref.at[core], lambda: acc))
    for name, src, dst in loads:
        loc.add(name, src, dst)
    stores = (("dp_o", dproj, dproj_out), ("gw_o", gwf, gw_out), ("hw_o", hwf, hw_out), ("fin_o", fin, fin_out), ("finb_o", finb, finb_out))
    for name, src, dst in stores:
        loc.add(name, lambda src=src: src, lambda dst=dst: dst)
    loc.add("sums_o", lambda: sums_f, lambda: sums_out)

    loc.start(*[name for name, _, _ in loads])
    greet(peer[1:] + [mate] + plane[1:])
    net.start("s0", *[("r1", dz) for dz in order])
    net.start(*[("rzb", dz) for dz in (1, 2, 3)])
    lane = lanes_of()
    loc.wait("tok")
    for j in range(4):
        tokt[:, j * rows : (j + 1) * rows] = tok[j].T
    loc.wait("do", "o", "q", "k", "v", "sums", "back", "acc")
    for j in range(4):
        for h in range(GROUP_HEADS):
            tile = do_s[j, :, (h // 2) * 128 : (h // 2) * 128 + 128].astype(f32)
            if h == 1:
                tile = pltpu.roll(tile, 64, 1)
            tile = jnp.where(lane < 64, tile, 0.0)
            r = slice(j * rows, (j + 1) * rows)
            delta = jnp.sum(tile * o_s[h, r, :].astype(f32), axis=1, keepdims=True)
            hi, mid, low = split3(-delta)
            tile = jnp.where(lane == 64, hi, jnp.where(lane == 65, mid, jnp.where(lane == 66, low, tile)))
            doa[h, r, :] = tile.astype(bf16)

    def add_into(ref, index, other_ref, other_index):
        ref[index] = (ref[index].astype(f32) + other_ref[other_index].astype(f32)).astype(bf16)

    def step_one(dz):
        net.recv(("r1", dz))
        def body(c, carry):
            add_into(acc, (zs[dz], c), rb, (zs[dz], c))
            return carry
        lax.fori_loop(0, CHIPS, body, 0)
        net.start(*[("x1", n, dz) for n in (0, 1)], *[("y1", n, dz) for n in (0, 1)])

    def step_two(dz):
        for n in range(2):
            net.recv(("x1", 1 - n, dz), ("y1", 1 - n, dz))
            jx, jy = (2, 1) if n == 0 else (0, 0)
            add_into(acc, (zs[dz], ch[jx], xs), rx, (zs[dz], 1 - n))
            add_into(acc, (zs[dz], ch[jy], ys), ry, (zs[dz], 1 - n))
            if n == 0:
                net.start(("x2", dz), ("y2", dz))

    def step_three(dz):
        net.recv(("x2", dz), ("y2", dz))
        add_into(acc, (zs[dz], chip, xs), rx2, zs[dz])
        add_into(acc, (zs[dz], chip, ys), ry2, zs[dz])
        if dz:
            net.start(("rz", dz))

    def sums_step(n):
        net.recv(f"s{n}")
        sums[n + 1] = (sums[n].astype(f32) + sums_r[n].astype(f32)).astype(bf16)
        if n < 2:
            net.start(f"s{n + 1}")
        else:
            net.start(*[("sz", dz) for dz in (1, 2, 3)])

    def back_total():
        net.recv(*[("rzb", dz) for dz in (1, 2, 3)])
        total = rzb[0].astype(f32) + rzb[1].astype(f32) + rzb[2].astype(f32) + rzb[3].astype(f32)
        finb[core, chip] = total.astype(bf16)
        net.start("b1", "b2")

    def back_forward():
        net.recv("b1")
        net.start("b3x")
        net.recv("b2")
        net.start("b3y")

    def back_mate():
        net.recv("b3x", "b3y")
        net.start("bm")

    def fin_total():
        for dz in (1, 2, 3):
            net.recv(("rz", dz), ("sz", dz))
        total = acc[z, chip].astype(f32) + rz[0].astype(f32) + rz[1].astype(f32) + rz[2].astype(f32)
        fin[core, chip] = total.astype(bf16)
        net.start("f1", "f2")
        total = sums[3, z].astype(f32)
        for n in range(3):
            total = total + sums_z[n].astype(f32)
        sums_f[...] = total.astype(bf16)
        loc.start("sums_o")

    def fin_forward():
        net.recv("f1")
        net.start("f3x")
        net.recv("f2")
        net.start("f3y")

    def weight_part(a, w, first, last):
        cols = dall[:, :, first:last].reshape(4 * rows, last - first)
        column_sums = jnp.sum(cols.astype(f32), axis=0, keepdims=True)
        extra = jnp.where(lax.broadcasted_iota(jnp.int32, (16, 1), 0) == 0, column_sums, 0.0).astype(bf16)
        for zz in range(PLANES):
            part = dot(tokt[zz * shard : (zz + 1) * shard, :], cols)
            for m in range(2):
                w[m, zz, 0:piece, :] = part[m * piece : (m + 1) * piece, :].astype(bf16)
                w[m, zz, piece : piece + 16, :] = extra
        net.start((a, 0))

    def weight_pair(a, w, wr, g):
        net.recv((a, 0))
        for zz in range(PLANES):
            g[zz] = (w[core, zz].astype(f32) + wr[zz].astype(f32)).astype(bf16)
        net.start(*[(a, "z", dz) for dz in (1, 2, 3)])

    def weight_total(a, g, gr, f):
        total = g[z].astype(f32)
        for dz in (1, 2, 3):
            net.recv((a, "z", dz))
            total = total + gr[dz - 1].astype(f32)
        f[core, chip] = total.astype(bf16)
        net.start(*[(a, "f", j) for j in (1, 2, 3)])

    def weight_mate(a):
        net.recv(*[(a, "f", j) for j in (1, 2, 3)])
        net.start((a, "m"))

    key_chunk, query_tile = 2 * rows, 256
    per_head = 4

    def head_end(h):
        net.recv(("kv", h))
        tile = KV_TILE[h]
        dst = (0, 1, 4)[h] * 128
        for j in range(4):
            r = slice(j * rows, (j + 1) * rows)
            both = kv_own[r, :] + kvr[h, r, :].astype(f32)
            dall[j, :, dst : dst + 128] = both.astype(bf16)
        dq = dqs[...].T * 0.125
        for j in range(4):
            r = slice(j * rows, (j + 1) * rows)
            mine = dq[r, :]
            if h == 0:
                dq_keep[r, :] = mine
            elif h == 1:
                dall[j, :, 256:384] = jnp.where(lane < 64, dq_keep[r, :], pltpu.roll(mine, 64, 1)).astype(bf16)
            else:
                dall[j, :, 384:512] = jnp.where(lane < 64, mine, 0.0).astype(bf16)
        for j in (1, 2, 3):
            net.start(("dp", h, j))

    stages = {
        0: lambda: (step_one(3), sums_step(0)),
        1: lambda: (step_one(2), sums_step(1)),
        2: lambda: (step_two(3), step_one(1), sums_step(2)),
        3: lambda: (step_three(3), step_two(2)),
        4: lambda: (step_one(0), back_total()),
        5: lambda: (step_three(2), step_two(1)),
        6: lambda: (step_two(0), back_forward()),
        7: lambda: (step_three(1), weight_part("g", gw, 0, 384)),
        8: lambda: (step_three(0), back_mate()),
        9: lambda: (fin_total(), weight_pair("g", gw, gwr, gz)),
        11: lambda: (fin_forward(), weight_total("g", gz, gzr, gwf)),
    }

    def visit(t, carry):
        h, part = lax.div(t, per_head), lax.rem(t, per_head)
        start = pl.multiple_of(lax.rem(part + 2, 4) * key_chunk, key_chunk)
        krows = pl.ds(start, key_chunk)
        k, v = k_s[h, krows, :], v_s[h, krows, :]
        kt = k.T

        @pl.when(part == 0)
        def _():
            dqs[...] = jnp.zeros_like(dqs)

        dk = jnp.zeros((key_chunk, 128), f32)
        dv = jnp.zeros((key_chunk, 128), f32)
        for i in range(4 * rows // query_tile):
            r = slice(i * query_tile, (i + 1) * query_tile)
            q, do = q_s[h, r, :], doa[h, r, :]
            probs = jnp.exp2(dot(k, q, NT) * LOG2E)
            dscores = (probs * dot(v, do, NT)).astype(bf16)
            dv = dv + dot(probs.astype(bf16), do)
            dk = dk + dot(dscores, q)
            dqs[:, r] += dot(kt, dscores)
        packed = jnp.where(lane < 64, dk, pltpu.roll(dv, 64, 1))

        @pl.when(part < 2)
        def _():
            kvs[h, pl.ds(pl.multiple_of(part * key_chunk, key_chunk), key_chunk), :] = packed.astype(bf16)

        @pl.when(part >= 2)
        def _():
            kv_own[pl.ds(pl.multiple_of((part - 2) * key_chunk, key_chunk), key_chunk), :] = packed

        for hh in range(GROUP_HEADS):
            @pl.when(t == hh * per_head + 1)
            def _(hh=hh):
                net.start(("kv", hh))

            @pl.when(t == hh * per_head + 3)
            def _(hh=hh):
                head_end(hh)
        for at, work in stages.items():
            pl.when(t == at)(lambda work=work: (work(), None)[1])
        return carry

    lax.fori_loop(0, GROUP_HEADS * per_head, visit, 0)

    weight_part("h", hw, 384, PACK)
    dproj[chip] = dall[0]
    weight_pair("h", hw, hwr, hz)
    weight_mate("g")
    net.recv("f3x", "f3y")
    net.start("fm")
    weight_total("h", hz, hzr, hwf)
    for h in range(GROUP_HEADS):
        for j in (1, 2, 3):
            net.recv(("dp", h, j))
    net.recv("fm", "bm", ("g", "m"))
    loc.start("dp_o", "gw_o", "fin_o", "finb_o")
    weight_mate("h")
    net.recv(("h", "m"))
    loc.start("hw_o")
    for name in net.specs:
        net.sent(name)
    loc.wait("dp_o", "gw_o", "hw_o", "fin_o", "finb_o", "sums_o")


def gelu_parts(u):
    x = jnp.abs(u) * (0.5 ** 0.5)
    d = 1.0 + 0.3275911 * x
    t = pl.reciprocal(d, approx=True)
    t = t * (2.0 - d * t)
    poly = t * (0.254829592 + t * (-0.284496736 + t * (1.421413741 + t * (-1.453152027 + t * 1.061405429))))
    bell = jnp.exp2(u * u * (-0.5 * LOG2E))
    tail = 0.5 * poly * bell
    phi = jnp.where(u >= 0, 1.0 - tail, tail)
    return u * phi, phi + u * bell * (1.0 / math.sqrt(2.0 * math.pi))


def row_mean(a):
    return jnp.mean(a, axis=1, keepdims=True)


def wide_vectors(small):
    step = small.shape[2] // PLANES
    lane = lax.broadcasted_iota(jnp.int32, (8, small.shape[2]), 1)
    total = [0.0] * PLANES
    for zz in range(PLANES):
        value = small[zz].astype(f32)[0:8]
        for k in range(PLANES):
            part = jnp.where((lane >= k * step) & (lane < (k + 1) * step), value, 0.0)
            turn = (zz - k) % PLANES * step
            total[k] = total[k] + (pltpu.roll(part, turn, 1) if turn else part)
    return total


def ffn_kernel(
    length_ref, att_ref, tok_ref, cot_ref, win_ref, win_own, wout_ref, wout_own, small_ref, wback_ref, wback_own, wq_in,
    out_ref, gh1_ref, do_out, grads_ref, sums_ref, wq_full, back_out,
    winv, wbackv, woutv, act_s, gp_s, gi_s, acc, first_s, n1_s, low_s, lowt_s, gsec_s, gh2_s, isum,
    gb, rb, rx, ry, rx2, ry2, do_ref, do_in, send_sems, recv_sems, local_sems,
):
    s, z, core, chip = coordinates()
    other = 1 - core
    rows, width = tok_ref.shape
    step = width // PLANES
    ch = winv.shape[1] // 8
    wide = 2 * ch
    back = wback_own.shape[0]
    shard = win_own.shape[0]
    piece = shard // 2
    peer = [None] + [(flip(chip, j) * 2 + core, z) for j in (1, 2, 3)]
    mate = (chip * 2 + other, z)
    zs = [z] + [flip(z, dz) for dz in (1, 2, 3)]
    ch_of = [chip] + [flip(chip, j) for j in (1, 2, 3)]
    net, loc = Net(send_sems, recv_sems), Local(local_sems)

    def region(zz, m, c):
        return wq_full.at[zz, m * 2 + lax.div(c, 2), pl.ds(pl.multiple_of(lax.rem(c, 2) * piece, 16), piece), :]

    for dz in (1, 2, 3):
        for j in (1, 2):
            net.add((j, dz), lambda dz=dz: region(zs[dz], core, chip), lambda dz=dz: region(zs[dz], core, chip), peer[j])
        net.add((3, dz), lambda dz=dz: region(zs[dz], core, ch_of[2]), lambda dz=dz: region(zs[dz], core, ch_of[2]), peer[1])
        net.add(("m", dz), lambda dz=dz: wq_full.at[zs[dz], pl.ds(core * 2, 2)], lambda dz=dz: wq_full.at[zs[dz], pl.ds(core * 2, 2)], mate)
    half = gb.shape[3] // 2
    xs, ys = slice(0, half), slice(half, 2 * half)
    for zz in range(PLANES):
        net.add(("r1", zz), lambda zz=zz: gb.at[other, zz], lambda zz=zz: rb.at[zz], mate)
        for n, j in enumerate((1, 3)):
            net.add(("x1", n, zz), lambda zz=zz, j=j: gb.at[core, zz, ch_of[j], xs], lambda zz=zz, n=n: rx.at[zz, n], peer[1])
        net.add(("x2", zz), lambda zz=zz: gb.at[core, zz, ch_of[2], xs], lambda zz=zz: rx2.at[zz], peer[2])
        for n, j in enumerate((2, 3)):
            net.add(("y1", n, zz), lambda zz=zz, j=j: gb.at[core, zz, ch_of[j], ys], lambda zz=zz, n=n: ry.at[zz, n], peer[2])
        net.add(("y2", zz), lambda zz=zz: gb.at[core, zz, ch_of[1], ys], lambda zz=zz: ry2.at[zz], peer[1])
    for j in (1, 2, 3):
        net.add(("do", j), lambda j=j: do_ref.at[ch_of[j]], lambda j=j: do_in.at[j], peer[j])
    loc.add("do_o", lambda: do_in, lambda: do_out)
    loc.add("back_o", lambda: gb.at[core, :, chip], lambda: back_out)
    for dz in range(4):
        for name, own, full, dst in (("out", wout_own, wout_ref, woutv), ("in", win_own, win_ref, winv), ("back", wback_own, wback_ref, wbackv)):
            n = own.shape[0]
            place = lambda dz=dz, n=n: pl.ds(pl.multiple_of(zs[dz] * n, 16), n)
            loc.add((name, dz), lambda own=own, full=full, dz=dz, place=place: own if dz == 0 else full.at[place(), :],
                    lambda dst=dst, place=place: dst.at[place(), :])
    for name in ("out", "in", "back"):
        loc.start(*[(name, dz) for dz in range(4)])
    hello(peer[1:] + [mate])

    def hop_two(dz):
        net.recv((1, dz), (2, dz))
        net.start((3, dz))

    def hop_three(dz):
        net.recv((3, dz))
        net.start(("m", dz))

    def add_into(ref, index, other_ref, other_index):
        ref[index] = (ref[index].astype(f32) + other_ref[other_index].astype(f32)).astype(bf16)

    def step_one(zz):
        net.recv(("r1", zz))
        for c in range(CHIPS):
            add_into(gb, (core, zz, c), rb, (zz, c))
        net.start(*[("x1", n, zz) for n in (0, 1)], *[("y1", n, zz) for n in (0, 1)])

    def step_two(zz):
        net.recv(("x1", 1, zz), ("y1", 1, zz))
        add_into(gb, (core, zz, ch_of[2], xs), rx, (zz, 1))
        add_into(gb, (core, zz, ch_of[1], ys), ry, (zz, 1))
        net.start(("x2", zz), ("y2", zz))
        net.recv(("x1", 0, zz), ("y1", 0, zz))
        add_into(gb, (core, zz, chip, xs), rx, (zz, 0))
        add_into(gb, (core, zz, chip, ys), ry, (zz, 0))

    def step_three(zz):
        net.recv(("x2", zz), ("y2", zz))
        add_into(gb, (core, zz, chip, xs), rx2, zz)
        add_into(gb, (core, zz, chip, ys), ry2, zz)

    def during(n, works):
        for at, work in works.items():
            pl.when(n == at)(lambda work=work: (work(), None)[1])

    vectors = wide_vectors(small_ref)
    vec = lambda i: vectors[i % 4][i // 4 : i // 4 + 1, :]
    loc.wait(*[("out", dz) for dz in range(4)])
    branch = vec(0)
    for g in range(4):
        branch = branch + dot(att_ref[g, :, 0:step], woutv[g * step : (g + 1) * step, :])
    hidden = tok_ref[...].astype(f32) + branch
    centred = hidden - row_mean(hidden)
    inverse1 = lax.rsqrt(row_mean(centred * centred) + 1e-5)
    normed = centred * inverse1
    n1_s[...] = normed
    first = normed * vec(1) + vec(2)
    first_s[...] = first
    low_s[...] = first.astype(bf16)
    lowt_s[...] = first.astype(bf16).T
    acc[...] = jnp.zeros_like(acc)
    met(4)
    for dz in (1, 2, 3):
        net.start((1, dz), (2, dz))
    loc.wait(*[("in", dz) for dz in range(4)])
    loc.wait(*[("back", dz) for dz in range(4)])

    def forward(n, carry):
        cols = pl.ds(pl.multiple_of(n * wide, 128), wide)
        inner = dot(low_s[...], winv[:, cols]) + small_ref[n, 2:3, :].astype(f32)
        value, slope = gelu_parts(inner)
        value = value.astype(bf16)
        act_s[n] = value
        gp_s[n] = slope
        acc[...] += dot(value, wbackv[cols, :])
        return carry

    lax.fori_loop(0, PLANES, forward, 0)
    for dz in (1, 2, 3):
        hop_two(dz)
    position = s * rows + lax.broadcasted_iota(jnp.int32, (rows, 1), 0)
    valid = (position < length_ref[0]).astype(f32)
    hidden = first_s[...] + acc[...] + vec(3)
    centred = hidden - row_mean(hidden)
    inverse = lax.rsqrt(row_mean(centred * centred) + 1e-5)
    normed = centred * inverse
    out_ref[...] = ((normed * vec(4) + vec(5)) * valid).astype(bf16)
    grad = cot_ref[...].astype(f32) * valid
    sum_rows = lambda a: jnp.sum(a, axis=0, keepdims=True)
    g2_gain, g2_bias = sum_rows(grad * normed), sum_rows(grad)
    scaled = grad * vec(4)
    gh2 = inverse * (scaled - row_mean(scaled) - normed * row_mean(scaled * normed))
    gh2_s[...] = gh2
    second = gh2.astype(bf16)
    gsec_s[...] = second
    back_sum = sum_rows(second.astype(f32))
    acc[...] = jnp.zeros_like(acc)

    def back_weights(n, carry):
        gback = dot(act_s[n].T, gsec_s[...]).astype(bf16)
        part = wide // 8
        for m in range(2):
            for k in range(4):
                for x in range(2):
                    gb[m, n, k, x * part : (x + 1) * part, :] = gback[
                        (m * 4 + k) * part : (m * 4 + k + 1) * part, x * ch : (x + 1) * ch
                    ]
        during(n, {
            0: lambda: net.start(("r1", 0)), 1: lambda: (net.start(("r1", 1)), hop_three(1)),
            2: lambda: (net.start(("r1", 2)), hop_three(2)), 3: lambda: (net.start(("r1", 3)), hop_three(3)),
        })
        return carry

    lax.fori_loop(0, PLANES, back_weights, 0)

    def backward(n, carry):
        cols = pl.ds(pl.multiple_of(n * wide, 128), wide)
        grad_inner = (dot(gsec_s[...], wbackv[cols, :], NT) * gp_s[n]).astype(bf16)
        gi_s[n] = grad_inner
        isum[n] = jnp.broadcast_to(sum_rows(grad_inner.astype(f32)), (8, wide))
        acc[...] += dot(grad_inner, winv[:, cols], NT)
        during(n, {
            0: lambda: step_one(0), 1: lambda: step_one(1),
            2: lambda: (step_one(2), step_two(0)), 3: lambda: step_one(3),
        })
        return carry

    lax.fori_loop(0, PLANES, backward, 0)
    grad = gh2_s[...] + acc[...]
    normed = n1_s[...]
    g1_gain, g1_bias = sum_rows(grad * normed), sum_rows(grad)
    scaled = grad * vec(1)
    gh1 = inverse1 * (scaled - row_mean(scaled) - normed * row_mean(scaled * normed))
    gh1_ref[...] = gh1
    gbranch = gh1.astype(bf16)
    out_sum = sum_rows(gbranch.astype(f32))
    for g in range(4):
        w = woutv[g * step : (g + 1) * step, :]
        do_ref[g, :, 0:step] = dot(gbranch, w, NT).astype(bf16)
        do_ref[g, :, step:] = jnp.zeros((rows, do_ref.shape[2] - step), bf16)
    net.start(*[("do", j) for j in (1, 2, 3)])
    do_in[0] = do_ref[chip]
    for g in range(4):
        gw = dot(att_ref[g, :, 0:step].T, gbranch).astype(bf16)
        part = step // 4
        for c in range(4):
            for m in range(2):
                grads_ref[m, g, c, step:, :] = gw[c * part : (c + 1) * part, m * ch : (m + 1) * ch]

    def weights(n, carry):
        for zz in range(PLANES):
            gin = dot(lowt_s[zz * step : (zz + 1) * step, :], gi_s[n]).astype(bf16)
            for x in range(2):
                grads_ref[lax.div(n, 2), zz, lax.rem(n, 2) * 2 + x, 0:step, :] = gin[:, x * ch : (x + 1) * ch]
        during(n, {
            0: lambda: (step_two(1), step_three(0)), 1: lambda: step_two(2),
            2: lambda: (step_two(3), step_three(1)), 3: lambda: step_three(2),
        })
        return carry

    lax.fori_loop(0, PLANES, weights, 0)
    lane = lax.broadcasted_iota(jnp.int32, (8, width), 1)
    place = lax.broadcasted_iota(jnp.int32, (8, width), 0)
    total = jnp.zeros((8, width), f32)
    for i, v in enumerate((out_sum, g1_gain, g1_bias, back_sum, g2_gain, g2_bias)):
        total = jnp.where(place == i, v, total)
    for zz in range(PLANES):
        part = total if zz == 0 else pltpu.roll(total, width - zz * step, 1)
        part = jnp.where(lane < step, part, 0.0)
        part = jnp.where(place == 6, isum[zz], part)
        sums_ref[zz, 0:16, :] = jnp.concatenate([part, jnp.zeros((8, width), f32)], axis=0).astype(bf16)
    step_three(3)
    net.recv(*[("do", j) for j in (1, 2, 3)])
    loc.start("back_o", "do_o")
    net.recv(*[("m", dz) for dz in (1, 2, 3)])
    for name in net.specs:
        net.sent(name)
    loc.wait("back_o", "do_o")


Q_PLACE, K_PLACE, V_PLACE = (4, 5, 6), (0, 2, 8), (1, 3, 9)


def half_tile(tile_of, block, upper):
    tile = tile_of(block // 2)
    return tile if block % 2 == upper else pltpu.roll(tile, 64, 1)


def final_kernel(
    dproj_ref, wq_ref, wq_own, gh1_ref, gw_ref, hw_ref, fin_ref, finb_ref, sums_ref,
    gt_ref, gqkv_ref, gin_ref, gback_ref, gout_ref, qb_ref, vb_ref, o0, o1, o2, o3, o4, o5, ib_ref,
    wv, local_sems,
):
    z = lax.axis_index("fsdp")
    loc = Local(local_sems)
    shard = wq_ref.shape[2]
    for dz in range(PLANES):
        zz = flip(z, dz)
        loc.add(dz, lambda zz=zz, dz=dz: wq_own if dz == 0 else wq_ref.at[zz],
                lambda zz=zz: wv.at[:, pl.ds(pl.multiple_of(zz * shard, 16), shard), :])
    loc.start(*range(PLANES))
    lane = lanes_of()
    up = lambda a: a.astype(f32)
    ch = fin_ref.shape[3]
    for m in range(2):
        for c in range(4):
            n = m * 4 + c
            gin_ref[:, n * ch : (n + 1) * ch] = up(fin_ref[m, c, 0:shard, :])
            part = ch // 4
            for x in range(2):
                gback_ref[n * part : (n + 1) * part, x * ch : (x + 1) * ch] = up(
                    finb_ref[m, c, x * part : (x + 1) * part, :]
                )
            gout_ref[c * (shard // 4) : (c + 1) * (shard // 4), m * ch : (m + 1) * ch] = up(fin_ref[m, c, shard:, :])
    piece = shard // 2

    def packed_tile(m, g, r, t):
        if t < 3:
            return up(gw_ref[m, g, r, t * 128 : (t + 1) * 128])
        return up(hw_ref[m, g, r, (t - 3) * 128 : (t - 2) * 128])

    for m in range(2):
        r = slice(m * piece, (m + 1) * piece)
        for kind, places in enumerate((Q_PLACE, K_PLACE, V_PLACE)):
            for i in range(HEADS // 2):
                halves = []
                for upper in (0, 1):
                    g, h = divmod(2 * i + upper, GROUP_HEADS)
                    tile_of = lambda t, g=g: packed_tile(m, g, slice(0, piece), t)
                    halves.append(half_tile(tile_of, places[h], upper))
                at = kind * HEADS * 64 + i * 128
                gqkv_ref[r, at : at + 128] = jnp.where(lane < 64, halves[0], halves[1])
    tile_of = lambda t: packed_tile(0, z, slice(piece, piece + 16), t)
    for ref, places in ((qb_ref, Q_PLACE), (vb_ref, V_PLACE)):
        first = jnp.where(lane < 64, half_tile(tile_of, places[0], 0), half_tile(tile_of, places[1], 1))
        ref[:, 0:128] = first[0:1]
        ref[:, 128:192] = half_tile(tile_of, places[2], 0)[0:1, 0:64]
    for i, ref in enumerate((o0, o1, o2, o3, o4, o5)):
        ref[...] = up(sums_ref[...])[i : i + 1, 0:shard]
    ib_ref[...] = up(sums_ref[...])[6:7, :]
    loc.wait(*range(PLANES))
    total = gh1_ref[...]
    for g in range(4):
        total = total + dot(dproj_ref[g], wv[g], NT)
    gt_ref[...] = total.astype(bf16)


def vmem(shape, dtype=bf16):
    return pltpu.VMEM(shape, dtype)


ANY = pl.BlockSpec(memory_space=pl.ANY)
SMEM = pl.BlockSpec(memory_space=pltpu.SMEM)
VMEM = pl.BlockSpec(memory_space=pltpu.VMEM)
VMEM_BYTES = 60 * 2**20
SEMS = 96


def semaphores():
    return [pltpu.SemaphoreType.DMA((SEMS,)), pltpu.SemaphoreType.DMA((SEMS,)), pltpu.SemaphoreType.DMA((16,))]


def params(collective_id):
    return pltpu.CompilerParams(
        collective_id=collective_id, has_side_effects=True, vmem_limit_bytes=VMEM_BYTES
    )


def run_forward(lengths, tokens, w_qkv, w_in, w_back, w_out, small):
    rows, width = tokens.shape
    shard = w_qkv.shape[0]
    hidden = w_in.shape[1]
    S = jax.ShapeDtypeStruct
    q_shape, kv_shape = (GROUP_HEADS, 4 * rows, 128), (GROUP_HEADS, 8 * rows, 128)
    return pl.pallas_call(
        forward_kernel,
        out_shape=(
            S(q_shape, bf16), S(kv_shape, bf16), S(kv_shape, bf16), S(q_shape, bf16),
            S((4, rows, width), bf16), S((4, rows, 256), bf16), S((PLANES, 16, width), bf16),
            S((PLANES * shard, hidden), bf16), S((width, width), bf16),
            S((CHIPS, shard, PACK), bf16), S((hidden, width), bf16), S((PLANES, CHIPS, shard, PACK), bf16),
        ),
        in_specs=[SMEM] + [ANY] * 6,
        out_specs=[ANY] * 12,
        scratch_shapes=[
            vmem((4, rows, width)), vmem((width, PACK)), vmem(q_shape), vmem(kv_shape), vmem(kv_shape), vmem(q_shape),
            vmem((4, rows, 256)), vmem((4, rows, 256)), vmem((4, rows, 384)), vmem((4, rows, 384)),
            vmem((PLANES, 16, width)), vmem((shard, w_qkv.shape[1])), vmem((CHIPS, shard, PACK)),
        ] + semaphores(),
        compiler_params=params(1),
    )(lengths, tokens, w_qkv, w_in, w_back, w_out, small)


def run_backward(do, q, k, v, o, tok, grads, sums, back):
    rows = do.shape[1]
    width = tok.shape[2]
    shard = width // PLANES
    length, cols = grads.shape[3:]
    cut = length // 32 * 16
    S = jax.ShapeDtypeStruct
    ext = shard // 2 + 16
    return pl.pallas_call(
        backward_kernel,
        out_shape=(
            S((4, rows, PACK), bf16), S((2, 4, ext, 384), bf16), S((2, 4, ext, 256), bf16), S((2, 4, length, cols), bf16), S((2, 4) + back.shape[1:], bf16), S((16, width), bf16),
        ),
        in_specs=[ANY] * 9,
        out_specs=[ANY] * 6,
        scratch_shapes=[
            vmem((4, rows, 256)), vmem(q.shape), vmem(k.shape), vmem(v.shape), vmem(o.shape), vmem(q.shape),
            vmem(tok.shape), vmem((width, 4 * rows)), vmem((128, 4 * rows), f32), vmem((4 * rows, 128), f32),
            vmem((4 * rows, 128), f32), vmem((3, 4 * rows, 128)), vmem((3, 4 * rows, 128)),
            vmem((4, rows, PACK)), vmem((4, rows, PACK)),
            *[vmem(lead + (ext, n)) for n in (384, 256) for lead in ((2, 4), (4,), (4,), (3,), (2, 4))],
            vmem((4, 4, length, cols)), vmem((4, 4, length, cols)),
            vmem((4, 2, cut, cols)), vmem((4, 2, length - cut, cols)), vmem((4, cut, cols)), vmem((4, length - cut, cols)),
            vmem((3, length, cols)), vmem((4,) + back.shape[1:]), vmem((2, 4, length, cols)), vmem((2, 4) + back.shape[1:]),
            vmem((4, 4, 16, width)), vmem((3, 4, 16, width)), vmem((3, 16, width)), vmem((16, width)),
        ] + semaphores(),
        compiler_params=params(2),
    )(do, q, k, v, o, tok, grads, sums, back)


def run_ffn(lengths, att, tokens, cotangent, full_in, w_in, full_out, w_out, small, full_back, w_back, wq_full):
    rows, width = tokens.shape
    hidden = w_in.shape[1]
    ch = hidden // 8
    S = jax.ShapeDtypeStruct
    one = S((rows, width), bf16)
    bp = w_back.shape[0] // 8
    return pl.pallas_call(
        ffn_kernel,
        out_shape=(
            one, S((rows, width), f32), S((4, rows, 256), bf16), S((2, 4, 4, width // 4 + 48, ch), bf16), S((4, 16, width), bf16),
            S(wq_full.shape, bf16), S((4, 2 * bp, ch), bf16),
        ),
        in_specs=[SMEM] + [VMEM] * 3 + [ANY] * 4 + [VMEM] + [ANY] * 3,
        input_output_aliases={11: 5},
        out_specs=[VMEM] * 2 + [ANY] + [VMEM] * 2 + [ANY] * 2,
        scratch_shapes=[
            vmem((width, hidden)), vmem((hidden, width)), vmem((width, width)),
            vmem((4, rows, 2 * ch)), vmem((4, rows, 2 * ch), f32), vmem((4, rows, 2 * ch)),
            vmem((rows, width), f32), vmem((rows, width), f32), vmem((rows, width), f32),
            vmem((rows, width)), vmem((width, rows)), vmem((rows, width)), vmem((rows, width), f32), vmem((4, 8, 2 * ch), f32),
            vmem((2, 4, 4, 2 * bp, ch)), vmem((4, 4, 2 * bp, ch)), vmem((4, 2, bp, ch)), vmem((4, 2, bp, ch)), vmem((4, bp, ch)), vmem((4, bp, ch)),
            vmem((4, rows, 256)), vmem((4, rows, 256)),
            pltpu.SemaphoreType.DMA((SEMS,)), pltpu.SemaphoreType.DMA((SEMS,)), pltpu.SemaphoreType.DMA((24,)),
        ],
        compiler_params=params(3),
    )(lengths, att, tokens, cotangent, full_in, w_in, full_out, w_out, small, full_back, w_back, wq_full)


def run_final(dproj, wq_full, wq, gh1, gw, hw, fin, finb, sums):
    rows, width = gh1.shape
    shard = width // PLANES
    S = jax.ShapeDtypeStruct
    one = S((1, shard), f32)
    return pl.pallas_call(
        final_kernel,
        out_shape=(
            S((rows, width), bf16), S((shard, 3 * width), f32), S((shard, 8 * fin.shape[3]), f32),
            S((2 * fin.shape[3], width), f32), S((shard, width), f32), one, one, one, one, one, one, one, one, S((1, width), f32),
        ),
        in_specs=[VMEM, ANY, ANY] + [VMEM] * 6,
        out_specs=[VMEM] * 14,
        scratch_shapes=[vmem((4, width, PACK)), pltpu.SemaphoreType.DMA((4,))],
        compiler_params=pltpu.CompilerParams(vmem_limit_bytes=VMEM_BYTES),
    )(dproj, wq_full, wq, gh1, gw, hw, fin, finb, sums)


def planned(
    tokens, lengths, w_qkv, q_bias, v_bias, w_out, out_bias, ln1_gain, ln1_bias,
    w_in, in_bias, w_back, back_bias, ln2_gain, ln2_bias, cotangent,
):
    width = tokens.shape[2]
    line = lambda *a: jnp.concatenate(a + (jnp.zeros((width - sum(x.shape[0] for x in a),), bf16),))
    gap = jnp.zeros((64,), bf16)
    small = jnp.stack([
        jnp.concatenate([out_bias, ln1_gain, ln1_bias, back_bias]), line(ln2_gain, ln2_bias), in_bias,
        line(gap, v_bias[0:64], gap, v_bias[64:128], q_bias, gap, gap, v_bias[128:192]),
    ] + [jnp.zeros((width,), bf16)] * 12)
    q, k, v, o, tok_all, att, small_all, full_in, full_out, wq, full_back, wq_full = run_forward(
        lengths, tokens[0], w_qkv, w_in, w_back, w_out, small
    )
    output, gh1, do, grads, sums, wq_full, back = run_ffn(
        lengths, att, tokens[0], cotangent[0], full_in, w_in, full_out, w_out, small_all, full_back, w_back, wq_full
    )
    dproj, gw, hw, fin, finb, sums_f = run_backward(do, q, k, v, o, tok_all, grads, sums, back)
    gt, gqkv, gin, gback, gout, qb, vb, ob, g1, b1, bb, g2, b2, ib = run_final(dproj, wq_full, wq, gh1, gw, hw, fin, finb, sums_f)
    flat = lambda a: a.reshape(a.shape[1])
    return (
        output[None], gt[None], gqkv, flat(qb), flat(vb), gout, flat(ob), flat(g1), flat(b1), gin, flat(ib),
        gback, flat(bb), flat(g2), flat(b2),
    )


masked_score = -1e30


def passed_along(block, axis, distance):
    devices = range(lax.axis_size(axis))
    route = [((i - distance) % len(devices), i) for i in devices]
    return lax.ppermute(block, axis, route)


def norm_forward(hidden, gain_vec, shift_vec):
    average = jnp.mean(hidden, axis=-1, keepdims=True)
    centred = hidden - average
    variance = jnp.mean(centred * centred, axis=-1, keepdims=True)
    inverse = lax.rsqrt(variance + 1e-05)
    normed = centred * inverse
    return (normed * gain_vec + shift_vec, normed, inverse)


def norm_backward(grad_norm, normed, inverse, gain_vec):
    scaled = grad_norm * gain_vec
    grad_input = inverse * (
        scaled
        - jnp.mean(scaled, axis=-1, keepdims=True)
        - normed * jnp.mean(scaled * normed, axis=-1, keepdims=True)
    )
    return (grad_input, jnp.sum(grad_norm * normed, axis=0), jnp.sum(grad_norm, axis=0))


def forward_tile(state_in, query_heads, key_pair, length):
    old_max, old_sum, old_acc = state_in
    key_rows = key_pair.shape[0]
    head_count = query_heads.shape[1]
    head_size = query_heads.shape[2]
    key_heads = key_pair[:, 0].reshape(key_rows, head_count, head_size)
    value_heads = key_pair[:, 1].reshape(key_rows, head_count, head_size)
    key_ok = jnp.arange(key_rows, dtype=jnp.int32) < length
    scores = jnp.einsum(
        "qhd,khd->hqk", query_heads, key_heads, preferred_element_type=jnp.float32
    ) * head_size ** (-0.5)
    scores = jnp.where(key_ok[None, None, :], scores, masked_score)
    new_max = jnp.maximum(old_max, jnp.max(scores, axis=2))
    prob_tile = jnp.where(key_ok[None, None, :], jnp.exp(scores - new_max[:, :, None]), 0.0)
    new_sum = jnp.sum(prob_tile, axis=2)
    new_acc = jnp.einsum(
        "hqk,khd->hqd",
        prob_tile.astype(jnp.bfloat16),
        value_heads,
        preferred_element_type=jnp.float32,
    )
    return (new_max, new_sum, new_acc)


def backward_tile(query_pair, log_total, delta, key_pair, key_start, length):
    query_rows = query_pair.shape[0]
    key_rows = key_pair.shape[0]
    model_width = query_pair.shape[2]
    head_count = log_total.shape[0]
    head_size = model_width // head_count
    score_scale = head_size ** (-0.5)
    query_heads = query_pair[:, 0].reshape(query_rows, head_count, head_size)
    grad_heads = query_pair[:, 1].reshape(query_rows, head_count, head_size)
    key_heads = key_pair[:, 0].reshape(key_rows, head_count, head_size)
    value_heads = key_pair[:, 1].reshape(key_rows, head_count, head_size)
    key_ok = key_start + jnp.arange(key_rows, dtype=jnp.int32) < length
    scores = (
        jnp.einsum("qhd,khd->hqk", query_heads, key_heads, preferred_element_type=jnp.float32)
        * score_scale
    )
    prob_tile = jnp.where(key_ok[None, None, :], jnp.exp(scores - log_total[:, :, None]), 0.0)
    grad_values = jnp.einsum(
        "hqk,qhd->khd",
        prob_tile.astype(jnp.bfloat16),
        grad_heads,
        preferred_element_type=jnp.float32,
    )
    grad_probs = jnp.einsum(
        "qhd,khd->hqk", grad_heads, value_heads, preferred_element_type=jnp.float32
    )
    grad_scores = (prob_tile * (grad_probs - delta[:, :, None])).astype(jnp.bfloat16)
    grad_queries = (
        jnp.einsum("hqk,khd->qhd", grad_scores, key_heads, preferred_element_type=jnp.float32)
        * score_scale
    )
    grad_keys = (
        jnp.einsum("hqk,qhd->khd", grad_scores, query_heads, preferred_element_type=jnp.float32)
        * score_scale
    )
    grad_pair = jnp.stack([grad_keys, grad_values], axis=1).reshape(key_rows, 2, model_width)
    return (grad_queries.reshape(query_rows, model_width), grad_pair)


def on_device(
    tokens,
    lengths,
    w_qkv,
    q_bias,
    v_bias,
    w_out,
    out_bias,
    ln1_gain,
    ln1_bias,
    w_in,
    in_bias,
    w_back,
    back_bias,
    ln2_gain,
    ln2_bias,
    cotangent,
):
    gathered = (
        lax.all_gather(w_qkv, "fsdp", axis=0, tiled=True),
        lax.all_gather(q_bias, "fsdp", axis=0, tiled=True),
        lax.all_gather(v_bias, "fsdp", axis=0, tiled=True),
        lax.all_gather(w_out, "fsdp", axis=0, tiled=True),
        lax.all_gather(out_bias, "fsdp", axis=0, tiled=True),
        lax.all_gather(ln1_gain, "fsdp", axis=0, tiled=True),
        lax.all_gather(ln1_bias, "fsdp", axis=0, tiled=True),
        lax.all_gather(w_in, "fsdp", axis=0, tiled=True),
        lax.all_gather(in_bias, "fsdp", axis=0, tiled=True),
        lax.all_gather(w_back, "fsdp", axis=0, tiled=True),
        lax.all_gather(back_bias, "fsdp", axis=0, tiled=True),
        lax.all_gather(ln2_gain, "fsdp", axis=0, tiled=True),
        lax.all_gather(ln2_bias, "fsdp", axis=0, tiled=True),
    )
    (
        full_qkv,
        full_qbias,
        full_vbias,
        full_out,
        full_obias,
        full_g1,
        full_n1,
        full_in,
        full_ibias,
        full_back,
        full_bbias,
        full_g2,
        full_n2,
    ) = gathered
    f32 = jnp.float32
    seq_index = lax.axis_index("seq")
    seq_count = lax.axis_size("seq")
    token_rows = tokens.shape[1]
    model_width = tokens.shape[2]
    head_count = HEADS
    head_size = model_width // head_count
    length = lengths[0]
    my_start = seq_index * token_rows
    row_valid = (my_start + jnp.arange(token_rows, dtype=jnp.int32) < length).astype(f32)
    inputs_b = tokens[0]
    inputs_f = inputs_b.astype(f32)
    bias_all = jnp.concatenate(
        [full_qbias.astype(f32), jnp.zeros((model_width,), f32), full_vbias.astype(f32)]
    )
    projected = (jnp.dot(inputs_b, full_qkv, preferred_element_type=f32) + bias_all).astype(
        jnp.bfloat16
    )
    query_heads = projected[:, :model_width].reshape(token_rows, head_count, head_size)
    key_pair = projected[:, model_width:].reshape(token_rows, 2, model_width)
    init_state = (
        jnp.full((head_count, token_rows), masked_score, f32),
        jnp.zeros((head_count, token_rows), f32),
        jnp.zeros((head_count, token_rows, head_size), f32),
    )
    pieces = lax.all_gather(key_pair, "seq", axis=0, tiled=True)
    run_max, run_sum, run_acc = forward_tile(init_state, query_heads, pieces, length)
    positive = run_sum > 0.0
    safe_sum = jnp.where(positive, run_sum, 1.0)
    attended_heads = jnp.where(positive[:, :, None], run_acc / safe_sum[:, :, None], 0.0)
    log_total = jnp.where(positive, run_max + jnp.log(safe_sum), 0.0)
    attended_f = attended_heads.transpose(1, 0, 2).reshape(token_rows, model_width)
    attended_b = attended_f.astype(jnp.bfloat16)
    branch_f = jnp.dot(attended_b, full_out, preferred_element_type=f32) + full_obias.astype(f32)
    first_norm, normed_one, inverse_one = norm_forward(
        inputs_f + branch_f, full_g1.astype(f32), full_n1.astype(f32)
    )
    first_low = first_norm.astype(jnp.bfloat16)
    inner_act = jnp.dot(first_low, full_in, preferred_element_type=f32) + full_ibias.astype(f32)
    activated_b = jax.nn.gelu(inner_act, approximate=False).astype(jnp.bfloat16)
    second = jnp.dot(activated_b, full_back, preferred_element_type=f32) + full_bbias.astype(f32)
    result, normed_two, inverse_two = norm_forward(
        first_norm + second, full_g2.astype(f32), full_n2.astype(f32)
    )
    output = (result * row_valid[:, None]).astype(jnp.bfloat16)
    grad_result = cotangent[0].astype(f32) * row_valid[:, None]
    grad_h2, g_ln2_gain, g_ln2_bias = norm_backward(
        grad_result, normed_two, inverse_two, full_g2.astype(f32)
    )
    grad_second = grad_h2.astype(jnp.bfloat16)
    g_w_back = jnp.einsum("tf,td->fd", activated_b, grad_second, preferred_element_type=f32)
    g_back_bias = jnp.sum(grad_second.astype(f32), axis=0)
    grad_act = jnp.einsum("td,fd->tf", grad_second, full_back, preferred_element_type=f32)
    gelu_value, gelu_pull = jax.vjp(
        lambda values_in: jax.nn.gelu(values_in, approximate=False), inner_act
    )
    grad_inner = gelu_pull(grad_act)[0].astype(jnp.bfloat16)
    g_w_in = jnp.einsum("td,tf->df", first_low, grad_inner, preferred_element_type=f32)
    g_in_bias = jnp.sum(grad_inner.astype(f32), axis=0)
    grad_first = grad_h2 + jnp.einsum("tf,df->td", grad_inner, full_in, preferred_element_type=f32)
    grad_h1, g_ln1_gain, g_ln1_bias = norm_backward(
        grad_first, normed_one, inverse_one, full_g1.astype(f32)
    )
    grad_branch = grad_h1.astype(jnp.bfloat16)
    g_w_out = jnp.einsum("tc,td->cd", attended_b, grad_branch, preferred_element_type=f32)
    g_out_bias = jnp.sum(grad_branch.astype(f32), axis=0)
    grad_attended = jnp.einsum(
        "td,cd->tc", grad_branch, full_out, preferred_element_type=f32
    ).astype(jnp.bfloat16)
    delta = jnp.sum(
        (grad_attended.astype(f32) * attended_f).reshape(token_rows, head_count, head_size), axis=2
    ).T
    query_pair = jnp.stack([projected[:, :model_width], grad_attended], axis=1)
    zero_rows = jnp.zeros((token_rows, model_width), f32)
    zero_pair = jnp.zeros((token_rows, 2, model_width), f32)

    def visit_keys(hop_index, grad_q, moving_pair, grad_pair):
        anchor = (seq_index - hop_index) % seq_count
        add_q, add_pair = backward_tile(
            query_pair, log_total, delta, moving_pair, anchor * token_rows, length
        )
        return (grad_q + add_q, grad_pair + add_pair)

    def return_key_grads(grad_pair):
        return passed_along(grad_pair.astype(jnp.bfloat16), "seq", 1).astype(grad_pair.dtype)

    def key_hop(hop_index, loop_state):
        grad_q, moving_pair, grad_pair = loop_state
        grad_q, grad_pair = visit_keys(hop_index, grad_q, moving_pair, grad_pair)
        moved = passed_along(moving_pair, "seq", 1)
        return (grad_q, moved, return_key_grads(grad_pair))

    grad_q, moving_pair, grad_pair = lax.fori_loop(
        0, seq_count - 1, key_hop, (zero_rows, key_pair, zero_pair)
    )
    grad_q, grad_pair = visit_keys(seq_count - 1, grad_q, moving_pair, grad_pair)
    grad_pair = return_key_grads(grad_pair)
    grad_projected = jnp.concatenate(
        [grad_q, grad_pair.reshape(token_rows, 2 * model_width)], axis=1
    ).astype(jnp.bfloat16)
    g_w_qkv = jnp.einsum("td,te->de", inputs_b, grad_projected, preferred_element_type=f32)
    grad_proj_f = grad_projected.astype(f32)
    g_q_bias = jnp.sum(grad_proj_f[:, :model_width], axis=0)
    g_v_bias = jnp.sum(grad_proj_f[:, 2 * model_width :], axis=0)
    grad_input = grad_h1 + jnp.einsum(
        "te,de->td", grad_projected, full_qkv, preferred_element_type=f32
    )
    local_grads = (
        g_w_qkv,
        g_q_bias,
        g_v_bias,
        g_w_out,
        g_out_bias,
        g_ln1_gain,
        g_ln1_bias,
        g_w_in,
        g_in_bias,
        g_w_back,
        g_back_bias,
        g_ln2_gain,
        g_ln2_bias,
    )
    owned = (
        lax.psum_scatter(
            local_grads[0].astype(jnp.bfloat16), "fsdp", scatter_dimension=0, tiled=True
        ).astype(jnp.float32),
        lax.psum_scatter(
            local_grads[1].astype(jnp.bfloat16), "fsdp", scatter_dimension=0, tiled=True
        ).astype(jnp.float32),
        lax.psum_scatter(
            local_grads[2].astype(jnp.bfloat16), "fsdp", scatter_dimension=0, tiled=True
        ).astype(jnp.float32),
        lax.psum_scatter(
            local_grads[3].astype(jnp.bfloat16), "fsdp", scatter_dimension=0, tiled=True
        ).astype(jnp.float32),
        lax.psum_scatter(
            local_grads[4].astype(jnp.bfloat16), "fsdp", scatter_dimension=0, tiled=True
        ).astype(jnp.float32),
        lax.psum_scatter(
            local_grads[5].astype(jnp.bfloat16), "fsdp", scatter_dimension=0, tiled=True
        ).astype(jnp.float32),
        lax.psum_scatter(
            local_grads[6].astype(jnp.bfloat16), "fsdp", scatter_dimension=0, tiled=True
        ).astype(jnp.float32),
        lax.psum_scatter(
            local_grads[7].astype(jnp.bfloat16), "fsdp", scatter_dimension=0, tiled=True
        ).astype(jnp.float32),
        lax.psum_scatter(
            local_grads[8].astype(jnp.bfloat16), "fsdp", scatter_dimension=0, tiled=True
        ).astype(jnp.float32),
        lax.psum_scatter(
            local_grads[9].astype(jnp.bfloat16), "fsdp", scatter_dimension=0, tiled=True
        ).astype(jnp.float32),
        lax.psum_scatter(
            local_grads[10].astype(jnp.bfloat16), "fsdp", scatter_dimension=0, tiled=True
        ).astype(jnp.float32),
        lax.psum_scatter(
            local_grads[11].astype(jnp.bfloat16), "fsdp", scatter_dimension=0, tiled=True
        ).astype(jnp.float32),
        lax.psum_scatter(
            local_grads[12].astype(jnp.bfloat16), "fsdp", scatter_dimension=0, tiled=True
        ).astype(jnp.float32),
    )
    totals = (
        lax.psum(owned[0].astype(jnp.bfloat16), "seq").astype(jnp.float32),
        lax.psum(owned[1].astype(jnp.bfloat16), "seq").astype(jnp.float32),
        lax.psum(owned[2].astype(jnp.bfloat16), "seq").astype(jnp.float32),
        lax.psum(owned[3].astype(jnp.bfloat16), "seq").astype(jnp.float32),
        lax.psum(owned[4].astype(jnp.bfloat16), "seq").astype(jnp.float32),
        lax.psum(owned[5].astype(jnp.bfloat16), "seq").astype(jnp.float32),
        lax.psum(owned[6].astype(jnp.bfloat16), "seq").astype(jnp.float32),
        lax.psum(owned[7].astype(jnp.bfloat16), "seq").astype(jnp.float32),
        lax.psum(owned[8].astype(jnp.bfloat16), "seq").astype(jnp.float32),
        lax.psum(owned[9].astype(jnp.bfloat16), "seq").astype(jnp.float32),
        lax.psum(owned[10].astype(jnp.bfloat16), "seq").astype(jnp.float32),
        lax.psum(owned[11].astype(jnp.bfloat16), "seq").astype(jnp.float32),
        lax.psum(owned[12].astype(jnp.bfloat16), "seq").astype(jnp.float32),
    )
    return (output[None], grad_input.astype(jnp.bfloat16)[None]) + tuple(totals)


def solution(mesh):
    fits = mesh.shape["seq"] == 2 * CHIPS and mesh.shape["fsdp"] == PLANES
    return jax.shard_map(
        planned if fits else on_device,
        mesh=mesh,
        in_specs=(
            P("fsdp", "seq", None),
            P("fsdp"),
            P("fsdp", None),
            P("fsdp"),
            P("fsdp"),
            P("fsdp", None),
            P("fsdp"),
            P("fsdp"),
            P("fsdp"),
            P("fsdp", None),
            P("fsdp"),
            P("fsdp", None),
            P("fsdp"),
            P("fsdp"),
            P("fsdp"),
            P("fsdp", "seq", None),
        ),
        out_specs=(
            P("fsdp", "seq", None),
            P("fsdp", "seq", None),
            P("fsdp", None),
            P("fsdp"),
            P("fsdp"),
            P("fsdp", None),
            P("fsdp"),
            P("fsdp"),
            P("fsdp"),
            P("fsdp", None),
            P("fsdp"),
            P("fsdp", None),
            P("fsdp"),
            P("fsdp"),
            P("fsdp"),
        ),
        check_vma=False,
    )
```

```python
import functools
import math

import jax
import jax.numpy as jnp
from jax import lax
from jax.experimental import pallas as pl
from jax.experimental.pallas import tpu as pltpu
from jax.sharding import PartitionSpec as P

HEADS = 12
bf16 = jnp.bfloat16
f32 = jnp.float32
MESH = pl.DeviceIdType.MESH
LOG2E = math.log2(math.e)
NT = (((1,), (1,)), ((), ()))
NN = (((1,), (0,)), ((), ()))

PLANES = 4
CHIPS = 4
GROUP_HEADS = 3
PACKED = (12, 24, 13, 25, 0, 1, 2, None, 14, 26)
KV_TILE = (0, 1, 4)
PACK = 640


(
    K_ACC, K_ATT0, K_ATT1, K_ATT_O, K_B1, K_B2, K_B3X, K_B3Y, K_BACK, K_BACK_O, K_BM, K_DO, K_DO_O, K_DP,
    K_DP_O, K_F, K_F1, K_F2, K_F3X, K_F3Y, K_FINB_O, K_FIN_O, K_FM, K_G, K_GW_O, K_H, K_HW_O, K_IN, K_K, K_KV,
    K_K_O, K_M, K_O, K_OUT, K_O_O, K_Q, K_QKV, K_Q_O, K_R1, K_RAW, K_RZ, K_RZB, K_S0, K_S1, K_S2, K_SMALL,
    K_SMALL_O, K_SUMS, K_SUMS_O, K_SZ, K_T1A, K_T1B, K_T2A, K_T2B, K_T3A, K_T3B, K_TOK, K_TOK_O, K_V, K_V_O,
    K_WQ, K_WQM, K_WQ_O, K_X1, K_X2, K_Y1, K_Y2, K_Z,
) = range(100, 168)


def dot(a, b, dims=NN):
    return lax.dot_general(a, b, dims, preferred_element_type=f32)


class Net:
    def __init__(self, send_sems, recv_sems):
        self.send_sems, self.recv_sems = send_sems, recv_sems
        self.specs = {}

    def add(self, name, src, dst, device):
        self.specs[name] = (len(self.specs), src, dst, device)

    def get(self, name):
        k, src, dst, device = self.specs[name]
        return pltpu.make_async_remote_copy(
            src_ref=src(),
            dst_ref=dst(),
            send_sem=self.send_sems.at[k],
            recv_sem=self.recv_sems.at[k],
            device_id=device,
            device_id_type=MESH,
        )

    def start(self, *names):
        for name in names:
            self.get(name).start()

    def recv(self, *names):
        for name in names:
            self.get(name).wait_recv()

    def sent(self, *names):
        for name in names:
            self.get(name).wait_send()


class Local:
    def __init__(self, sems):
        self.sems = sems
        self.specs = {}

    def add(self, name, src, dst):
        self.specs[name] = (len(self.specs), src, dst)

    def get(self, name):
        k, src, dst = self.specs[name]
        return pltpu.make_async_copy(src(), dst(), self.sems.at[k])

    def start(self, *names):
        for name in names:
            self.get(name).start()

    def wait(self, *names):
        for name in names:
            self.get(name).wait()


class Line:
    def __init__(self, s, z, send_sems, recv_sems):
        high = lax.div(z, 2)
        self.s, self.z = s, z
        self.order = [z, 1 - z + 4 * high, 2 - high, 3 - 3 * high]
        self.has_right, self.has_left = z < PLANES - 1, z > 0
        self.right, self.left = jnp.minimum(z + 1, PLANES - 1), jnp.maximum(z - 1, 0)
        self.middle = jnp.logical_and(self.has_right, self.has_left)
        self.end = jnp.logical_not(self.middle)
        self.send_sems, self.recv_sems = send_sems, recv_sems
        self.specs = {}

    def add(self, name, own, place):
        self.specs[name] = (len(self.specs), own, place)

    def copy(self, name, i, to_right=False):
        n, own, place = self.specs[name]
        zz = self.order[i]
        if i:
            target = jnp.where(zz < self.z, self.right, self.left)
        else:
            target = self.right if to_right else self.left
        return pltpu.make_async_remote_copy(
            src_ref=place(zz) if i else own(),
            dst_ref=place(zz),
            send_sem=self.send_sems.at[n * 5 + (i + 1 if i else int(to_right))],
            recv_sem=self.recv_sems.at[n * PLANES + zz],
            device_id=(self.s, target),
            device_id_type=MESH,
        )

    def start(self, *names):
        for name in names:
            pl.when(self.has_right)(lambda: self.copy(name, 0, True).start())
            pl.when(self.has_left)(lambda: self.copy(name, 0).start())

    def pass_on(self, name, i):
        self.copy(name, i).wait_recv()
        self.copy(name, i).start()

    def step(self, n, *names):
        for name in names:
            if n == 1:
                @pl.when(self.middle)
                def _():
                    self.pass_on(name, 1)
                    self.pass_on(name, 2)

                pl.when(self.end)(lambda: self.copy(name, 1).wait_recv())
            elif n == 2:
                pl.when(self.middle)(lambda: self.pass_on(name, 3))
                pl.when(self.end)(lambda: self.copy(name, 2).wait_recv())
            else:
                pl.when(self.end)(lambda: self.copy(name, 3).wait_recv())

    def sent(self):
        for name in self.specs:
            pl.when(self.has_right)(lambda: self.copy(name, 0, True).wait_send())
            pl.when(self.has_left)(lambda: self.copy(name, 0).wait_send())

            @pl.when(self.middle)
            def _():
                for i in (1, 2, 3):
                    self.copy(name, i).wait_send()


def coordinates():
    s, z = lax.axis_index("seq"), lax.axis_index("fsdp")
    core = lax.rem(s, 2)
    chip = lax.div(s, 2)
    return s, z, core, chip


def flip(value, mask):
    low, high = lax.rem(value, 2), lax.div(value, 2)
    if mask & 1:
        low = 1 - low
    if mask & 2:
        high = 1 - high
    return high * 2 + low


def hello(devices):
    barrier = pltpu.get_barrier_semaphore()
    for device in devices:
        pl.semaphore_signal(barrier, inc=1, device_id=device, device_id_type=MESH)


def met(count):
    pl.semaphore_wait(pltpu.get_barrier_semaphore(), count)


def greet(devices):
    hello(devices)
    met(len(devices))


def lanes_of(rows=1):
    return lax.broadcasted_iota(jnp.int32, (rows, 128), 1)


def split3(column):
    hi = column.astype(bf16).astype(f32)
    mid = (column - hi).astype(bf16).astype(f32)
    return hi, mid, column - hi - mid


def forward_kernel(
    length_ref, tok_ref, wraw_ref, win_ref, wback_ref, wout_ref, small_ref,
    q_out, k_out, v_out, o_out, tok_out, att_out, small_out, win_full, wout_full, wq_out, wback_full,
    tok, wqv, q_s, k_s, v_s, o_s, att, atts, kvs, kvr, small, wraw, wq_ref, send_sems, recv_sems, line_send, line_recv, local_sems,
):
    s, z, core, chip = coordinates()
    other = 1 - core
    rows = tok_ref.shape[0]
    half = rows // 2
    shard = wq_ref.shape[1]
    piece = shard // 2
    peer = [None] + [(flip(chip, j) * 2 + core, z) for j in (1, 2, 3)]
    mate = (chip * 2 + other, z)
    plane = [None] + [(s, flip(z, dz)) for dz in (1, 2, 3)]
    zs = [z] + [flip(z, dz) for dz in (1, 2, 3)]
    net, loc = Net(send_sems, recv_sems), Local(local_sems)
    width = win_full.shape[1] // 8
    back = wback_ref.shape[0]
    bpiece = back // 8
    hops = [(K_IN, 1), (K_IN, 2), (K_IN, 3), (K_BACK, 1)]
    at = lambda start, size, unit=16: pl.ds(pl.multiple_of(start, unit), size)

    def part(a, zz, m, c):
        if a == K_IN:
            return win_full.at[at(zz * shard, shard), at((m * 4 + c) * width, width, 128)]
        if a == K_BACK:
            return wback_full.at[at(zz * back + (m * 4 + c) * bpiece, bpiece), :]
        return wout_full.at[at(zz * shard + c * (shard // 4), shard // 4), at(m * width, width, 128)]

    def own_part(a, m, c):
        if a == K_IN:
            return win_ref.at[:, at((m * 4 + c) * width, width, 128)]
        if a == K_BACK:
            return wback_ref.at[at((m * 4 + c) * bpiece, bpiece), :]
        return wout_ref.at[at(c * (shard // 4), shard // 4), at(m * width, width, 128)]

    def side(a, zz, m):
        if a == K_IN:
            return win_full.at[at(zz * shard, shard), at(m * 4 * width, 4 * width, 128)]
        if a == K_BACK:
            return wback_full.at[at(zz * back + m * 4 * bpiece, 4 * bpiece), :]
        return wout_full.at[at(zz * shard, shard), at(m * width, width, 128)]

    line = Line(s, z, line_send, line_recv)
    lines = line.order
    for a in (K_IN, K_BACK):
        line.add(a, lambda a=a: own_part(a, core, chip), lambda zz, a=a: part(a, zz, core, chip))
    line.add(K_OUT, lambda: wout_ref.at[:, at(core * width, width, 128)], lambda zz: side(K_OUT, zz, core))

    for dz in (1, 2, 3):
        net.add((K_WQ, dz), lambda: wq_ref.at[chip, pl.ds(pl.multiple_of(core * piece, 16), piece), :],
                lambda: wqv.at[pl.ds(pl.multiple_of(z * shard + core * piece, 16), piece), :], plane[dz])
        net.add((K_WQM, dz), lambda dz=dz: wqv.at[pl.ds(pl.multiple_of(zs[dz] * shard + core * piece, 16), piece), :],
                lambda dz=dz: wqv.at[pl.ds(pl.multiple_of(zs[dz] * shard + core * piece, 16), piece), :], mate)
        net.add((K_SMALL, dz), lambda: small_ref, lambda: small.at[z], plane[dz])
    top, bottom = slice(0, half), slice(half, rows)
    net.add(K_T1A, lambda: tok_ref.at[top], lambda: tok.at[1, top], peer[1])
    net.add(K_T1B, lambda: tok_ref.at[bottom], lambda: tok.at[1, bottom], peer[1])
    net.add(K_T2B, lambda: tok_ref.at[bottom], lambda: tok.at[2, bottom], peer[2])
    net.add(K_T2A, lambda: tok_ref.at[top], lambda: tok.at[2, top], peer[2])
    net.add(K_T3A, lambda: tok.at[1, top], lambda: tok.at[3, top], peer[2])
    net.add(K_T3B, lambda: tok.at[2, bottom], lambda: tok.at[3, bottom], peer[1])
    for j in range(4):
        net.add((K_KV, j), lambda j=j: kvs.at[j], lambda j=j: kvr.at[j], mate)
    for j in (1, 2, 3):
        net.add((K_ATT0, j), lambda j=j: atts.at[j, :, 0:128], lambda: att.at[chip, :, 0:128], peer[j])
        net.add((K_ATT1, j), lambda j=j: atts.at[j, :, 128:256], lambda: att.at[chip, :, 128:256], peer[j])
    for a, dz in hops:
        via, last = (1, 2) if a == K_IN else (2, 1)
        for j in (1, 2):
            net.add((a, j, dz), lambda a=a, dz=dz: part(a, lines[dz], core, chip), lambda a=a, dz=dz: part(a, lines[dz], core, chip), peer[j])
        net.add((a, 3, dz), lambda a=a, dz=dz, via=via: part(a, lines[dz], core, flip(chip, via)),
                lambda a=a, dz=dz, via=via: part(a, lines[dz], core, flip(chip, via)), peer[last])
    mates = hops + [(K_OUT, dz) for dz in (1, 2, 3)]
    for a, dz in mates:
        net.add((a, K_M, dz), lambda a=a, dz=dz: side(a, lines[dz], core), lambda a=a, dz=dz: side(a, lines[dz], core), mate)
    loc.add(K_RAW, lambda: wraw_ref, lambda: wraw)
    loc.add(K_TOK, lambda: tok_ref, lambda: tok.at[0])
    loc.add(K_WQ, lambda: wq_ref.at[chip], lambda: wqv.at[pl.ds(pl.multiple_of(z * shard, 16), shard), :])
    loc.add(K_SMALL, lambda: small_ref, lambda: small.at[z])
    outs = ((K_WQ_O, wq_ref, wq_out), (K_K_O, k_s, k_out), (K_V_O, v_s, v_out), (K_Q_O, q_s, q_out), (K_O_O, o_s, o_out),
            (K_TOK_O, tok, tok_out), (K_ATT_O, att, att_out), (K_SMALL_O, small, small_out))
    for name, src, dst in outs:
        loc.add(name, lambda src=src: src, lambda dst=dst: dst)

    loc.start(K_RAW, K_TOK, K_SMALL)
    greet(peer[1:] + [mate] + plane[1:])
    net.start(K_T1A, K_T2B, K_T1B, K_T2A)
    lane = lanes_of()
    loc.wait(K_RAW)
    for g in range(CHIPS):
        for t in range(PACK // 128):
            halves = []
            for upper in (0, 1):
                block = PACKED[2 * t + upper]
                if block is None:
                    halves.append(0.0)
                    continue
                block += GROUP_HEADS * g
                tile_of = lambda i: wraw[:, i * 128 : (i + 1) * 128].astype(f32)
                halves.append(half_tile(tile_of, block, upper))
            wq_ref[g, :, t * 128 : (t + 1) * 128] = jnp.where(lane < 64, halves[0], halves[1]).astype(bf16)
    loc.start(K_WQ, K_WQ_O)
    net.start(*[(K_WQ, dz) for dz in (1, 2, 3)], *[(K_SMALL, dz) for dz in (1, 2, 3)])
    for dz in (1, 2, 3):
        net.recv((K_WQ, dz))
        net.start((K_WQM, dz))
    line.start(K_OUT, K_IN)
    loc.wait(K_TOK, K_WQ, K_SMALL)
    for dz in (1, 2, 3):
        net.recv((K_SMALL, dz), (K_WQM, dz))

    length = length_ref[0]
    bias = small[chip, 3:4, 0:PACK].astype(f32)

    def keep(tile, h, slot, block):
        position = block * rows + lax.broadcasted_iota(jnp.int32, (rows, 1), 0)
        mask = jnp.where(position < length, 0.0, -1e30).astype(f32)
        ones = jnp.where((lane > 64) & (lane < 68), 1.0, 0.0)
        k_s[h, slot * rows : (slot + 1) * rows, :] = jnp.where(
            lane < 64, tile, jnp.where(lane == 64, mask, ones)
        ).astype(bf16)
        v_s[h, slot * rows : (slot + 1) * rows, :] = jnp.where(
            lane < 64, pltpu.roll(tile, 64, 1), jnp.where(lane < 67, 1.0, 0.0)
        ).astype(bf16)

    def project(j):
        proj = dot(tok[j], wqv[...]) + bias
        for h in range(GROUP_HEADS):
            tile = proj[:, KV_TILE[h] * 128 : (KV_TILE[h] + 1) * 128]
            keep(tile.astype(bf16).astype(f32), h, j, flip(chip, j) * 2 + core)
            kvs[j, :, h * 128 : (h + 1) * 128] = tile.astype(bf16)
            first = 256 + (h // 2) * 128
            tile = proj[:, first : first + 128].astype(bf16).astype(f32) * 0.125
            if h == 1:
                tile = pltpu.roll(tile, 64, 1)
            q_s[h, j * rows : (j + 1) * rows, :] = jnp.where(
                lane < 64, tile, jnp.where(lane == 64, 1.0, 0.0)
            ).astype(bf16)
        net.start((K_KV, j))

    def keep_other(j):
        net.recv((K_KV, j))
        for h in range(GROUP_HEADS):
            tile = kvr[j, :, h * 128 : (h + 1) * 128].astype(f32)
            keep(tile, h, 4 + j, flip(chip, j) * 2 + other)

    def first_hop(a, dz):
        net.start((a, 1, dz), (a, 2, dz))

    def second_hop(a, dz):
        net.recv((a, 1, dz), (a, 2, dz))
        net.start((a, 3, dz))

    def third_hop(a, dz):
        net.recv((a, 3, dz))
        net.start((a, K_M, dz))

    project(0)
    net.recv(K_T1A)
    net.start(K_T3A)
    net.recv(K_T2B)
    net.start(K_T3B)
    net.recv(K_T1B)
    project(1)
    net.recv(K_T2A)
    project(2)
    keep_other(0)
    keep_other(1)
    keep_other(2)
    line.step(1, K_OUT, K_IN)
    line.start(K_BACK)
    first_hop(K_IN, 1)
    net.recv(K_T3A, K_T3B)
    project(3)
    keep_other(3)
    loc.start(K_K_O, K_V_O, K_TOK_O, K_SMALL_O)

    query_tile, key_chunk = 2 * rows, 4 * rows
    tiles = 4 * rows // query_tile
    chunks = 8 * rows // key_chunk

    def attended_tile(which):
        for j in range(4):
            r = slice(j * rows, (j + 1) * rows)
            if which == 0:
                upper = pltpu.roll(o_s[1, r, :].astype(f32), 64, 1)
                value = jnp.where(lane < 64, o_s[0, r, :].astype(f32), upper)
            else:
                value = jnp.where(lane < 64, o_s[2, r, :].astype(f32), 0.0)
            place = slice(which * 128, (which + 1) * 128)
            if j == 0:
                att[chip, :, place] = value.astype(bf16)
            else:
                atts[j, :, place] = value.astype(bf16)
                net.start(((K_ATT0, K_ATT1)[which], j))

    stages = {
        0: lambda: (line.step(2, K_OUT, K_IN), first_hop(K_IN, 2), line.step(1, K_BACK)),
        2: lambda: second_hop(K_IN, 1),
        3: lambda: (line.step(3, K_OUT, K_IN), first_hop(K_IN, 3), [net.start((K_OUT, K_M, dz)) for dz in (1, 2, 3)]),
        4: lambda: (line.step(2, K_BACK), second_hop(K_IN, 2), first_hop(K_BACK, 1)),
        5: lambda: third_hop(K_IN, 1),
        6: lambda: third_hop(K_IN, 2),
        7: lambda: attended_tile(0),
        8: lambda: (second_hop(K_IN, 3), line.step(3, K_BACK)),
        9: lambda: second_hop(K_BACK, 1),
        10: lambda: third_hop(K_IN, 3),
        11: lambda: (attended_tile(1), third_hop(K_BACK, 1)),
    }

    def progress(n):
        for at, work in stages.items():
            pl.when(n == at)(lambda work=work: (work(), None)[1])

    def visit(t, carry):
        h, i = lax.div(t, tiles), lax.rem(t, tiles)
        qrows = pl.ds(pl.multiple_of(i * query_tile, query_tile), query_tile)
        q = q_s[h, qrows, :]
        top_score = jnp.full((query_tile, 1), -1e30, f32)
        acc = jnp.zeros((query_tile, 128), f32)
        for c in range(chunks):
            krows = slice(c * key_chunk, (c + 1) * key_chunk)
            scores = dot(q, k_s[h, krows, :], NT)
            new_top = jnp.maximum(top_score, jnp.max(scores, axis=1, keepdims=True))
            probs = jnp.exp2((scores - new_top) * LOG2E)
            fade = jnp.exp2((top_score - new_top) * LOG2E)
            acc = acc * fade + dot(probs.astype(bf16), v_s[h, krows, :])
            top_score = new_top
            if c < chunks - 1:
                progress(t * chunks + c)
        total = acc[:, 64:65]
        o_s[h, qrows, :] = (acc / total).astype(bf16)
        hi, mid, low = split3(-(top_score + jnp.log(total)))
        wide = q.astype(f32)
        wide = jnp.where(lane == 65, hi, jnp.where(lane == 66, mid, jnp.where(lane == 67, low, wide)))
        q_s[h, qrows, :] = wide.astype(bf16)
        progress(t * chunks + chunks - 1)
        return carry

    lax.fori_loop(0, GROUP_HEADS * tiles, visit, 0)
    loc.start(K_Q_O, K_O_O)
    for j in (1, 2, 3):
        net.recv((K_ATT0, j), (K_ATT1, j))
    loc.start(K_ATT_O)
    net.recv(*[(a, K_M, dz) for a, dz in mates])
    for name in net.specs:
        net.sent(name)
    line.sent()
    loc.wait(*[name for name, _, _ in outs])


def backward_kernel(
    do_ref, q_ref, k_ref, v_ref, o_ref, tok_ref, grads_ref, sums_ref, back_ref,
    dproj_out, gw_out, hw_out, fin_out, finb_out, sums_out,
    do_s, q_s, k_s, v_s, o_s, doa, tok, tokt, dqs, dq_keep, kv_own, kvs, kvr, dall, dproj,
    gw, gwr, gz, gzr, gwf, hw, hwr, hz, hzr, hwf, acc, rb, rx, ry, rx2, ry2, rz, rzb, fin, finb, sums, sums_r, sums_z, sums_f,
    send_sems, recv_sems, local_sems,
):
    s, z, core, chip = coordinates()
    other = 1 - core
    rows = do_ref.shape[1]
    peer = [None] + [(flip(chip, j) * 2 + core, z) for j in (1, 2, 3)]
    mate = (chip * 2 + other, z)
    plane = [None] + [(s, flip(z, dz)) for dz in (1, 2, 3)]
    zs = [z] + [flip(z, dz) for dz in (1, 2, 3)]
    ch = [chip] + [flip(chip, j) for j in (1, 2, 3)]
    net, loc = Net(send_sems, recv_sems), Local(local_sems)
    length = grads_ref.shape[3]
    cut = length // 32 * 16
    xs, ys = slice(0, cut), slice(cut, length)
    shard = tok.shape[2] // PLANES
    piece = shard // 2

    for h in range(GROUP_HEADS):
        net.add((K_KV, h), lambda h=h: kvs.at[h], lambda h=h: kvr.at[h], mate)
        place = ((0, 128), (128, 384), (384, 640))[h]
        for j in (1, 2, 3):
            net.add((K_DP, h, j), lambda j=j, place=place: dall.at[j, :, place[0] : place[1]],
                    lambda place=place: dproj.at[chip, :, place[0] : place[1]], peer[j])
    order = (3, 2, 1, 0)
    for dz in order:
        net.add((K_R1, dz), lambda dz=dz: grads_ref.at[other, zs[dz]], lambda dz=dz: rb.at[zs[dz]], mate)
        for n, j in enumerate((1, 3)):
            net.add((K_X1, n, dz), lambda dz=dz, j=j: acc.at[zs[dz], ch[j], xs], lambda dz=dz, n=n: rx.at[zs[dz], n], peer[1])
        net.add((K_X2, dz), lambda dz=dz: acc.at[zs[dz], ch[2], xs], lambda dz=dz: rx2.at[zs[dz]], peer[2])
        for n, j in enumerate((2, 3)):
            net.add((K_Y1, n, dz), lambda dz=dz, j=j: acc.at[zs[dz], ch[j], ys], lambda dz=dz, n=n: ry.at[zs[dz], n], peer[2])
        net.add((K_Y2, dz), lambda dz=dz: acc.at[zs[dz], ch[1], ys], lambda dz=dz: ry2.at[zs[dz]], peer[1])
        if dz:
            net.add((K_RZ, dz), lambda dz=dz: acc.at[zs[dz], chip], lambda dz=dz: rz.at[dz - 1], plane[dz])
    for dz in (1, 2, 3):
        net.add((K_RZB, dz), lambda dz=dz: back_ref.at[zs[dz]], lambda dz=dz: rzb.at[dz], plane[dz])
    bh = finb.shape[2] // 2
    bx, by = slice(0, bh), slice(bh, 2 * bh)
    net.add(K_B1, lambda: finb.at[core, chip], lambda: finb.at[core, chip], peer[1])
    net.add(K_B2, lambda: finb.at[core, chip], lambda: finb.at[core, chip], peer[2])
    net.add(K_B3X, lambda: finb.at[core, ch[1], bx], lambda: finb.at[core, ch[1], bx], peer[2])
    net.add(K_B3Y, lambda: finb.at[core, ch[2], by], lambda: finb.at[core, ch[2], by], peer[1])
    net.add(K_BM, lambda: finb.at[core], lambda: finb.at[core], mate)
    net.add(K_F1, lambda: fin.at[core, chip], lambda: fin.at[core, chip], peer[1])
    net.add(K_F2, lambda: fin.at[core, chip], lambda: fin.at[core, chip], peer[2])
    net.add(K_F3X, lambda: fin.at[core, ch[1], xs], lambda: fin.at[core, ch[1], xs], peer[2])
    net.add(K_F3Y, lambda: fin.at[core, ch[2], ys], lambda: fin.at[core, ch[2], ys], peer[1])
    net.add(K_FM, lambda: fin.at[core], lambda: fin.at[core], mate)
    net.add(K_S0, lambda: sums_ref, lambda: sums_r.at[0], mate)
    net.add(K_S1, lambda: sums.at[1], lambda: sums_r.at[1], peer[1])
    net.add(K_S2, lambda: sums.at[2], lambda: sums_r.at[2], peer[2])
    for dz in (1, 2, 3):
        net.add((K_SZ, dz), lambda dz=dz: sums.at[3, zs[dz]], lambda dz=dz: sums_z.at[dz - 1], plane[dz])
    for a, w, wr, g, gr, f in ((K_G, gw, gwr, gz, gzr, gwf), (K_H, hw, hwr, hz, hzr, hwf)):
        net.add((a, 0), lambda w=w: w.at[other], lambda wr=wr: wr, mate)
        for dz in (1, 2, 3):
            net.add((a, K_Z, dz), lambda g=g, dz=dz: g.at[zs[dz]], lambda gr=gr, dz=dz: gr.at[dz - 1], plane[dz])
        for j in (1, 2, 3):
            net.add((a, K_F, j), lambda f=f: f.at[core, chip], lambda f=f: f.at[core, chip], peer[j])
        net.add((a, K_M), lambda f=f: f.at[core], lambda f=f: f.at[core], mate)

    loads = ((K_DO, lambda: do_ref, lambda: do_s), (K_O, lambda: o_ref, lambda: o_s),
             (K_TOK, lambda: tok_ref, lambda: tok), (K_Q, lambda: q_ref, lambda: q_s),
             (K_K, lambda: k_ref, lambda: k_s), (K_V, lambda: v_ref, lambda: v_s),
             (K_SUMS, lambda: sums_ref, lambda: sums.at[0]), (K_BACK, lambda: back_ref.at[z], lambda: rzb.at[0]), (K_ACC, lambda: grads_ref.at[core], lambda: acc))
    for name, src, dst in loads:
        loc.add(name, src, dst)
    stores = ((K_DP_O, dproj, dproj_out), (K_GW_O, gwf, gw_out), (K_HW_O, hwf, hw_out), (K_FIN_O, fin, fin_out), (K_FINB_O, finb, finb_out))
    for name, src, dst in stores:
        loc.add(name, lambda src=src: src, lambda dst=dst: dst)
    loc.add(K_SUMS_O, lambda: sums_f, lambda: sums_out)

    loc.start(*[name for name, _, _ in loads])
    greet(peer[1:] + [mate] + plane[1:])
    net.start(K_S0, *[(K_R1, dz) for dz in order])
    net.start(*[(K_RZB, dz) for dz in (1, 2, 3)])
    lane = lanes_of()
    loc.wait(K_TOK)
    for j in range(4):
        tokt[:, j * rows : (j + 1) * rows] = tok[j].T
    loc.wait(K_DO, K_O, K_Q, K_K, K_V, K_SUMS, K_BACK, K_ACC)
    for j in range(4):
        for h in range(GROUP_HEADS):
            tile = do_s[j, :, (h // 2) * 128 : (h // 2) * 128 + 128].astype(f32)
            if h == 1:
                tile = pltpu.roll(tile, 64, 1)
            tile = jnp.where(lane < 64, tile, 0.0)
            r = slice(j * rows, (j + 1) * rows)
            delta = jnp.sum(tile * o_s[h, r, :].astype(f32), axis=1, keepdims=True)
            hi, mid, low = split3(-delta)
            tile = jnp.where(lane == 64, hi, jnp.where(lane == 65, mid, jnp.where(lane == 66, low, tile)))
            doa[h, r, :] = tile.astype(bf16)

    def add_into(ref, index, other_ref, other_index):
        ref[index] = (ref[index].astype(f32) + other_ref[other_index].astype(f32)).astype(bf16)

    def step_one(dz):
        net.recv((K_R1, dz))
        def body(c, carry):
            add_into(acc, (zs[dz], c), rb, (zs[dz], c))
            return carry
        lax.fori_loop(0, CHIPS, body, 0)
        net.start(*[(K_X1, n, dz) for n in (0, 1)], *[(K_Y1, n, dz) for n in (0, 1)])

    def step_two(dz):
        for n in range(2):
            net.recv((K_X1, 1 - n, dz), (K_Y1, 1 - n, dz))
            jx, jy = (2, 1) if n == 0 else (0, 0)
            add_into(acc, (zs[dz], ch[jx], xs), rx, (zs[dz], 1 - n))
            add_into(acc, (zs[dz], ch[jy], ys), ry, (zs[dz], 1 - n))
            if n == 0:
                net.start((K_X2, dz), (K_Y2, dz))

    def step_three(dz):
        net.recv((K_X2, dz), (K_Y2, dz))
        add_into(acc, (zs[dz], chip, xs), rx2, zs[dz])
        add_into(acc, (zs[dz], chip, ys), ry2, zs[dz])
        if dz:
            net.start((K_RZ, dz))

    def sums_step(n):
        net.recv((K_S0, K_S1, K_S2)[n])
        sums[n + 1] = (sums[n].astype(f32) + sums_r[n].astype(f32)).astype(bf16)
        if n < 2:
            net.start((K_S1, K_S2)[n])
        else:
            net.start(*[(K_SZ, dz) for dz in (1, 2, 3)])

    def back_total():
        net.recv(*[(K_RZB, dz) for dz in (1, 2, 3)])
        total = rzb[0].astype(f32) + rzb[1].astype(f32) + rzb[2].astype(f32) + rzb[3].astype(f32)
        finb[core, chip] = total.astype(bf16)
        net.start(K_B1, K_B2)

    def back_forward():
        net.recv(K_B1)
        net.start(K_B3X)
        net.recv(K_B2)
        net.start(K_B3Y)

    def back_mate():
        net.recv(K_B3X, K_B3Y)
        net.start(K_BM)

    def fin_total():
        for dz in (1, 2, 3):
            net.recv((K_RZ, dz), (K_SZ, dz))
        total = acc[z, chip].astype(f32) + rz[0].astype(f32) + rz[1].astype(f32) + rz[2].astype(f32)
        fin[core, chip] = total.astype(bf16)
        net.start(K_F1, K_F2)
        total = sums[3, z].astype(f32)
        for n in range(3):
            total = total + sums_z[n].astype(f32)
        sums_f[...] = total.astype(bf16)
        loc.start(K_SUMS_O)

    def fin_forward():
        net.recv(K_F1)
        net.start(K_F3X)
        net.recv(K_F2)
        net.start(K_F3Y)

    def weight_part(a, w, first, last):
        cols = dall[:, :, first:last].reshape(4 * rows, last - first)
        column_sums = jnp.sum(cols.astype(f32), axis=0, keepdims=True)
        extra = jnp.where(lax.broadcasted_iota(jnp.int32, (16, 1), 0) == 0, column_sums, 0.0).astype(bf16)
        for zz in range(PLANES):
            part = dot(tokt[zz * shard : (zz + 1) * shard, :], cols)
            for m in range(2):
                w[m, zz, 0:piece, :] = part[m * piece : (m + 1) * piece, :].astype(bf16)
                w[m, zz, piece : piece + 16, :] = extra
        net.start((a, 0))

    def weight_pair(a, w, wr, g):
        net.recv((a, 0))
        for zz in range(PLANES):
            g[zz] = (w[core, zz].astype(f32) + wr[zz].astype(f32)).astype(bf16)
        net.start(*[(a, K_Z, dz) for dz in (1, 2, 3)])

    def weight_total(a, g, gr, f):
        total = g[z].astype(f32)
        for dz in (1, 2, 3):
            net.recv((a, K_Z, dz))
            total = total + gr[dz - 1].astype(f32)
        f[core, chip] = total.astype(bf16)
        net.start(*[(a, K_F, j) for j in (1, 2, 3)])

    def weight_mate(a):
        net.recv(*[(a, K_F, j) for j in (1, 2, 3)])
        net.start((a, K_M))

    key_chunk, query_tile = 2 * rows, 256
    per_head = 4

    def head_end(h):
        net.recv((K_KV, h))
        tile = KV_TILE[h]
        dst = (0, 1, 4)[h] * 128
        for j in range(4):
            r = slice(j * rows, (j + 1) * rows)
            both = kv_own[r, :] + kvr[h, r, :].astype(f32)
            dall[j, :, dst : dst + 128] = both.astype(bf16)
        dq = dqs[...].T * 0.125
        for j in range(4):
            r = slice(j * rows, (j + 1) * rows)
            mine = dq[r, :]
            if h == 0:
                dq_keep[r, :] = mine
            elif h == 1:
                dall[j, :, 256:384] = jnp.where(lane < 64, dq_keep[r, :], pltpu.roll(mine, 64, 1)).astype(bf16)
            else:
                dall[j, :, 384:512] = jnp.where(lane < 64, mine, 0.0).astype(bf16)
        for j in (1, 2, 3):
            net.start((K_DP, h, j))

    stages = {
        0: lambda: (step_one(3), sums_step(0)),
        1: lambda: (step_one(2), sums_step(1)),
        2: lambda: (step_two(3), step_one(1), sums_step(2)),
        3: lambda: (step_three(3), step_two(2)),
        4: lambda: (step_one(0), back_total()),
        5: lambda: (step_three(2), step_two(1)),
        6: lambda: (step_two(0), back_forward()),
        7: lambda: (step_three(1), weight_part(K_G, gw, 0, 384)),
        8: lambda: (step_three(0), back_mate()),
        9: lambda: (fin_total(), weight_pair(K_G, gw, gwr, gz)),
        11: lambda: (fin_forward(), weight_total(K_G, gz, gzr, gwf)),
    }

    def visit(t, carry):
        h, part = lax.div(t, per_head), lax.rem(t, per_head)
        start = pl.multiple_of(lax.rem(part + 2, 4) * key_chunk, key_chunk)
        krows = pl.ds(start, key_chunk)
        k, v = k_s[h, krows, :], v_s[h, krows, :]
        kt = k.T

        @pl.when(part == 0)
        def _():
            dqs[...] = jnp.zeros_like(dqs)

        dk = jnp.zeros((key_chunk, 128), f32)
        dv = jnp.zeros((key_chunk, 128), f32)
        for i in range(4 * rows // query_tile):
            r = slice(i * query_tile, (i + 1) * query_tile)
            q, do = q_s[h, r, :], doa[h, r, :]
            probs = jnp.exp2(dot(k, q, NT) * LOG2E)
            dscores = (probs * dot(v, do, NT)).astype(bf16)
            dv = dv + dot(probs.astype(bf16), do)
            dk = dk + dot(dscores, q)
            dqs[:, r] += dot(kt, dscores)
        packed = jnp.where(lane < 64, dk, pltpu.roll(dv, 64, 1))

        @pl.when(part < 2)
        def _():
            kvs[h, pl.ds(pl.multiple_of(part * key_chunk, key_chunk), key_chunk), :] = packed.astype(bf16)

        @pl.when(part >= 2)
        def _():
            kv_own[pl.ds(pl.multiple_of((part - 2) * key_chunk, key_chunk), key_chunk), :] = packed

        for hh in range(GROUP_HEADS):
            @pl.when(t == hh * per_head + 1)
            def _(hh=hh):
                net.start((K_KV, hh))

            @pl.when(t == hh * per_head + 3)
            def _(hh=hh):
                head_end(hh)
        for at, work in stages.items():
            pl.when(t == at)(lambda work=work: (work(), None)[1])
        return carry

    lax.fori_loop(0, GROUP_HEADS * per_head, visit, 0)

    weight_part(K_H, hw, 384, PACK)
    dproj[chip] = dall[0]
    weight_pair(K_H, hw, hwr, hz)
    weight_mate(K_G)
    net.recv(K_F3X, K_F3Y)
    net.start(K_FM)
    weight_total(K_H, hz, hzr, hwf)
    for h in range(GROUP_HEADS):
        for j in (1, 2, 3):
            net.recv((K_DP, h, j))
    net.recv(K_FM, K_BM, (K_G, K_M))
    loc.start(K_DP_O, K_GW_O, K_FIN_O, K_FINB_O)
    weight_mate(K_H)
    net.recv((K_H, K_M))
    loc.start(K_HW_O)
    for name in net.specs:
        net.sent(name)
    loc.wait(K_DP_O, K_GW_O, K_HW_O, K_FIN_O, K_FINB_O, K_SUMS_O)


def gelu_parts(u):
    x = jnp.abs(u) * (0.5 ** 0.5)
    d = 1.0 + 0.3275911 * x
    t = pl.reciprocal(d, approx=True)
    t = t * (2.0 - d * t)
    poly = t * (0.254829592 + t * (-0.284496736 + t * (1.421413741 + t * (-1.453152027 + t * 1.061405429))))
    bell = jnp.exp2(u * u * (-0.5 * LOG2E))
    tail = 0.5 * poly * bell
    phi = jnp.where(u >= 0, 1.0 - tail, tail)
    return u * phi, phi + u * bell * (1.0 / math.sqrt(2.0 * math.pi))


def row_mean(a):
    return jnp.mean(a, axis=1, keepdims=True)


def wide_vectors(small):
    step = small.shape[2] // PLANES
    lane = lax.broadcasted_iota(jnp.int32, (8, small.shape[2]), 1)
    total = [0.0] * PLANES
    for zz in range(PLANES):
        value = small[zz].astype(f32)[0:8]
        for k in range(PLANES):
            part = jnp.where((lane >= k * step) & (lane < (k + 1) * step), value, 0.0)
            turn = (zz - k) % PLANES * step
            total[k] = total[k] + (pltpu.roll(part, turn, 1) if turn else part)
    return total


def ffn_kernel(
    length_ref, att_ref, tok_ref, cot_ref, win_ref, win_own, wout_ref, wout_own, small_ref, wback_ref, wback_own, wq_own,
    out_ref, gh1_ref, do_out, grads_ref, sums_ref, wq_full, back_out,
    winv, wbackv, woutv, act_s, gp_s, gi_s, acc, first_s, n1_s, low_s, lowt_s, gsec_s, gh2_s, isum,
    gb, rb, rx, ry, rx2, ry2, do_ref, do_in, send_sems, recv_sems, line_send, line_recv, local_sems,
):
    s, z, core, chip = coordinates()
    other = 1 - core
    rows, width = tok_ref.shape
    step = width // PLANES
    ch = winv.shape[1] // 8
    wide = 2 * ch
    back = wback_own.shape[0]
    shard = win_own.shape[0]
    piece = shard // 2
    peer = [None] + [(flip(chip, j) * 2 + core, z) for j in (1, 2, 3)]
    mate = (chip * 2 + other, z)
    plane = [(s, flip(z, dz)) for dz in (1, 2, 3)]
    ch_of = [chip] + [flip(chip, j) for j in (1, 2, 3)]
    net, loc = Net(send_sems, recv_sems), Local(local_sems)

    bpiece = back // 8
    line = Line(s, z, line_send, line_recv)
    lines = line.order
    line.add(K_QKV, lambda: wq_own.at[pl.ds(core * 2, 2)], lambda zz: wq_full.at[zz, pl.ds(core * 2, 2)])
    for dz in (1, 2, 3):
        net.add((K_QKV, dz), lambda dz=dz: wq_full.at[lines[dz], pl.ds(core * 2, 2)], lambda dz=dz: wq_full.at[lines[dz], pl.ds(core * 2, 2)], mate)

    def region(ref, zz, c):
        return ref.at[pl.ds(pl.multiple_of(zz * back + (core * 4 + c) * bpiece, 16), bpiece), :]

    def side(zz):
        return wbackv.at[pl.ds(pl.multiple_of(zz * back + core * 4 * bpiece, 16), 4 * bpiece), :]

    for dz in (2, 3):
        for j in (1, 2):
            net.add((j, dz), lambda dz=dz: region(wback_ref, lines[dz], chip), lambda dz=dz: region(wbackv, lines[dz], chip), peer[j])
        via, last = ((1, 2), (2, 1))[dz - 2]
        net.add((3, dz), lambda dz=dz, via=via: region(wbackv, lines[dz], ch_of[via]), lambda dz=dz, via=via: region(wbackv, lines[dz], ch_of[via]), peer[last])
        net.add((K_M, dz), lambda dz=dz: side(lines[dz]), lambda dz=dz: side(lines[dz]), mate)
        loc.add((K_M, dz), lambda dz=dz: region(wback_ref, lines[dz], chip), lambda dz=dz: region(wbackv, lines[dz], chip))
    half = gb.shape[3] // 2
    xs, ys = slice(0, half), slice(half, 2 * half)
    for zz in range(PLANES):
        net.add((K_R1, zz), lambda zz=zz: gb.at[other, zz], lambda zz=zz: rb.at[zz], mate)
        for n, j in enumerate((1, 3)):
            net.add((K_X1, n, zz), lambda zz=zz, j=j: gb.at[core, zz, ch_of[j], xs], lambda zz=zz, n=n: rx.at[zz, n], peer[1])
        net.add((K_X2, zz), lambda zz=zz: gb.at[core, zz, ch_of[2], xs], lambda zz=zz: rx2.at[zz], peer[2])
        for n, j in enumerate((2, 3)):
            net.add((K_Y1, n, zz), lambda zz=zz, j=j: gb.at[core, zz, ch_of[j], ys], lambda zz=zz, n=n: ry.at[zz, n], peer[2])
        net.add((K_Y2, zz), lambda zz=zz: gb.at[core, zz, ch_of[1], ys], lambda zz=zz: ry2.at[zz], peer[1])
    for j in (1, 2, 3):
        net.add((K_DO, j), lambda j=j: do_ref.at[ch_of[j]], lambda j=j: do_in.at[j], peer[j])
    loc.add(K_DO_O, lambda: do_in, lambda: do_out)
    loc.add(K_BACK_O, lambda: gb.at[core, :, chip], lambda: back_out)
    shards = {K_OUT: (wout_own, wout_ref, woutv), K_IN: (win_own, win_ref, winv), K_BACK: (wback_own, wback_ref, wbackv)}
    loads = [(name, i) for name in shards for i in range(4) if name != K_BACK or i < 2]
    for name, i in loads:
        own, full, dst = shards[name]
        n = own.shape[0]
        place = lambda i=i, n=n: pl.ds(pl.multiple_of(lines[i] * n, 16), n)
        loc.add((name, i), lambda own=own, full=full, i=i, place=place: full.at[place(), :] if i else own,
                lambda dst=dst, place=place: dst.at[place(), :])
    loc.start(*loads, (K_M, 2), (K_M, 3))
    greet(peer[1:] + [mate] + plane)
    net.start((1, 2), (2, 2), (1, 3), (2, 3))
    line.start(K_QKV)

    def hop_two(dz):
        net.recv((1, dz), (2, dz))
        net.start((3, dz))

    def hop_three(dz):
        net.recv((3, dz))
        loc.wait((K_M, dz))
        net.start((K_M, dz))

    def add_into(ref, index, other_ref, other_index):
        ref[index] = (ref[index].astype(f32) + other_ref[other_index].astype(f32)).astype(bf16)

    def step_one(zz):
        net.recv((K_R1, zz))
        for c in range(CHIPS):
            add_into(gb, (core, zz, c), rb, (zz, c))
        net.start(*[(K_X1, n, zz) for n in (0, 1)], *[(K_Y1, n, zz) for n in (0, 1)])

    def step_two(zz):
        net.recv((K_X1, 1, zz), (K_Y1, 1, zz))
        add_into(gb, (core, zz, ch_of[2], xs), rx, (zz, 1))
        add_into(gb, (core, zz, ch_of[1], ys), ry, (zz, 1))
        net.start((K_X2, zz), (K_Y2, zz))
        net.recv((K_X1, 0, zz), (K_Y1, 0, zz))
        add_into(gb, (core, zz, chip, xs), rx, (zz, 0))
        add_into(gb, (core, zz, chip, ys), ry, (zz, 0))

    def step_three(zz):
        net.recv((K_X2, zz), (K_Y2, zz))
        add_into(gb, (core, zz, chip, xs), rx2, zz)
        add_into(gb, (core, zz, chip, ys), ry2, zz)

    def during(n, works):
        for at, work in works.items():
            pl.when(n == at)(lambda work=work: (work(), None)[1])

    vectors = wide_vectors(small_ref)
    vec = lambda i: vectors[i % 4][i // 4 : i // 4 + 1, :]
    loc.wait(*[(K_OUT, dz) for dz in range(4)])
    branch = vec(0)
    for g in range(4):
        branch = branch + dot(att_ref[g, :, 0:step], woutv[g * step : (g + 1) * step, :])
    hidden = tok_ref[...].astype(f32) + branch
    centred = hidden - row_mean(hidden)
    inverse1 = lax.rsqrt(row_mean(centred * centred) + 1e-5)
    normed = centred * inverse1
    n1_s[...] = normed
    first = normed * vec(1) + vec(2)
    first_s[...] = first
    low_s[...] = first.astype(bf16)
    lowt_s[...] = first.astype(bf16).T
    loc.wait(*[(name, i) for name, i in loads if name != K_OUT])

    def forward(n, carry):
        cols = pl.ds(pl.multiple_of(n * wide, 128), wide)
        inner = dot(low_s[...], winv[:, cols]) + small_ref[n, 2:3, :].astype(f32)
        value, slope = gelu_parts(inner)
        value = value.astype(bf16)
        act_s[n] = value
        gp_s[n] = slope
        during(n, {2: lambda: hop_two(2), 3: lambda: hop_two(3)})
        return carry

    lax.fori_loop(0, PLANES, forward, 0)

    def second_layer(i):
        zz = lines[i]
        return dot(act_s[zz], wbackv[pl.ds(pl.multiple_of(zz * back, 16), back), :])

    acc[...] = second_layer(0)
    acc[...] += second_layer(1)
    hop_three(2)
    hop_three(3)
    line.step(1, K_QKV)
    net.recv((K_M, 2))
    acc[...] += second_layer(2)
    net.recv((K_M, 3))
    acc[...] += second_layer(3)
    position = s * rows + lax.broadcasted_iota(jnp.int32, (rows, 1), 0)
    valid = (position < length_ref[0]).astype(f32)
    hidden = first_s[...] + acc[...] + vec(3)
    centred = hidden - row_mean(hidden)
    inverse = lax.rsqrt(row_mean(centred * centred) + 1e-5)
    normed = centred * inverse
    out_ref[...] = ((normed * vec(4) + vec(5)) * valid).astype(bf16)
    grad = cot_ref[...].astype(f32) * valid
    sum_rows = lambda a: jnp.sum(a, axis=0, keepdims=True)
    g2_gain, g2_bias = sum_rows(grad * normed), sum_rows(grad)
    scaled = grad * vec(4)
    gh2 = inverse * (scaled - row_mean(scaled) - normed * row_mean(scaled * normed))
    gh2_s[...] = gh2
    second = gh2.astype(bf16)
    gsec_s[...] = second
    back_sum = sum_rows(second.astype(f32))
    acc[...] = jnp.zeros_like(acc)

    def back_weights(n, carry):
        gback = dot(act_s[n].T, gsec_s[...]).astype(bf16)
        part = wide // 8
        for m in range(2):
            for k in range(4):
                for x in range(2):
                    gb[m, n, k, x * part : (x + 1) * part, :] = gback[
                        (m * 4 + k) * part : (m * 4 + k + 1) * part, x * ch : (x + 1) * ch
                    ]
        during(n, {
            0: lambda: net.start((K_R1, 0)), 1: lambda: net.start((K_R1, 1)),
            2: lambda: net.start((K_R1, 2)), 3: lambda: net.start((K_R1, 3)),
        })
        return carry

    lax.fori_loop(0, PLANES, back_weights, 0)

    def backward(n, carry):
        cols = pl.ds(pl.multiple_of(n * wide, 128), wide)
        grad_inner = (dot(gsec_s[...], wbackv[cols, :], NT) * gp_s[n]).astype(bf16)
        gi_s[n] = grad_inner
        isum[n] = jnp.broadcast_to(sum_rows(grad_inner.astype(f32)), (8, wide))
        acc[...] += dot(grad_inner, winv[:, cols], NT)
        during(n, {
            0: lambda: step_one(0), 1: lambda: step_one(1),
            2: lambda: (step_one(2), step_two(0)), 3: lambda: step_one(3),
        })
        return carry

    lax.fori_loop(0, PLANES, backward, 0)
    grad = gh2_s[...] + acc[...]
    normed = n1_s[...]
    g1_gain, g1_bias = sum_rows(grad * normed), sum_rows(grad)
    scaled = grad * vec(1)
    gh1 = inverse1 * (scaled - row_mean(scaled) - normed * row_mean(scaled * normed))
    gh1_ref[...] = gh1
    gbranch = gh1.astype(bf16)
    out_sum = sum_rows(gbranch.astype(f32))
    for g in range(4):
        w = woutv[g * step : (g + 1) * step, :]
        do_ref[g, :, 0:step] = dot(gbranch, w, NT).astype(bf16)
        do_ref[g, :, step:] = jnp.zeros((rows, do_ref.shape[2] - step), bf16)
    net.start(*[(K_DO, j) for j in (1, 2, 3)])
    line.step(2, K_QKV)
    net.start((K_QKV, 1), (K_QKV, 2))
    do_in[0] = do_ref[chip]
    for g in range(4):
        gw = dot(att_ref[g, :, 0:step].T, gbranch).astype(bf16)
        part = step // 4
        for c in range(4):
            for m in range(2):
                grads_ref[m, g, c, step:, :] = gw[c * part : (c + 1) * part, m * ch : (m + 1) * ch]

    def weights(n, carry):
        for zz in range(PLANES):
            gin = dot(lowt_s[zz * step : (zz + 1) * step, :], gi_s[n]).astype(bf16)
            for x in range(2):
                grads_ref[lax.div(n, 2), zz, lax.rem(n, 2) * 2 + x, 0:step, :] = gin[:, x * ch : (x + 1) * ch]
        during(n, {
            0: lambda: (step_two(1), step_three(0)), 1: lambda: step_two(2),
            2: lambda: (step_two(3), step_three(1)), 3: lambda: step_three(2),
        })
        return carry

    lax.fori_loop(0, PLANES, weights, 0)
    lane = lax.broadcasted_iota(jnp.int32, (8, width), 1)
    place = lax.broadcasted_iota(jnp.int32, (8, width), 0)
    total = jnp.zeros((8, width), f32)
    for i, v in enumerate((out_sum, g1_gain, g1_bias, back_sum, g2_gain, g2_bias)):
        total = jnp.where(place == i, v, total)
    for zz in range(PLANES):
        part = total if zz == 0 else pltpu.roll(total, width - zz * step, 1)
        part = jnp.where(lane < step, part, 0.0)
        part = jnp.where(place == 6, isum[zz], part)
        sums_ref[zz, 0:16, :] = jnp.concatenate([part, jnp.zeros((8, width), f32)], axis=0).astype(bf16)
    step_three(3)
    net.recv(*[(K_DO, j) for j in (1, 2, 3)])
    loc.start(K_BACK_O, K_DO_O)
    line.step(3, K_QKV)
    net.start((K_QKV, 3))
    net.recv(*[(K_QKV, dz) for dz in (1, 2, 3)])
    for name in net.specs:
        net.sent(name)
    line.sent()
    loc.wait(K_BACK_O, K_DO_O)


Q_PLACE, K_PLACE, V_PLACE = (4, 5, 6), (0, 2, 8), (1, 3, 9)


def half_tile(tile_of, block, upper):
    tile = tile_of(block // 2)
    return tile if block % 2 == upper else pltpu.roll(tile, 64, 1)


def final_kernel(
    dproj_ref, wq_ref, wq_own, gh1_ref, gw_ref, hw_ref, fin_ref, finb_ref, sums_ref,
    gt_ref, gqkv_ref, gin_ref, gback_ref, gout_ref, qb_ref, vb_ref, o0, o1, o2, o3, o4, o5, ib_ref,
    wv, local_sems,
):
    z = lax.axis_index("fsdp")
    loc = Local(local_sems)
    shard = wq_ref.shape[2]
    for dz in range(PLANES):
        zz = flip(z, dz)
        loc.add(dz, lambda zz=zz, dz=dz: wq_own if dz == 0 else wq_ref.at[zz],
                lambda zz=zz: wv.at[:, pl.ds(pl.multiple_of(zz * shard, 16), shard), :])
    loc.start(*range(PLANES))
    lane = lanes_of()
    up = lambda a: a.astype(f32)
    ch = fin_ref.shape[3]
    for m in range(2):
        for c in range(4):
            n = m * 4 + c
            gin_ref[:, n * ch : (n + 1) * ch] = up(fin_ref[m, c, 0:shard, :])
            part = ch // 4
            for x in range(2):
                gback_ref[n * part : (n + 1) * part, x * ch : (x + 1) * ch] = up(
                    finb_ref[m, c, x * part : (x + 1) * part, :]
                )
            gout_ref[c * (shard // 4) : (c + 1) * (shard // 4), m * ch : (m + 1) * ch] = up(fin_ref[m, c, shard:, :])
    piece = shard // 2

    def packed_tile(m, g, r, t):
        if t < 3:
            return up(gw_ref[m, g, r, t * 128 : (t + 1) * 128])
        return up(hw_ref[m, g, r, (t - 3) * 128 : (t - 2) * 128])

    for m in range(2):
        r = slice(m * piece, (m + 1) * piece)
        for kind, places in enumerate((Q_PLACE, K_PLACE, V_PLACE)):
            for i in range(HEADS // 2):
                halves = []
                for upper in (0, 1):
                    g, h = divmod(2 * i + upper, GROUP_HEADS)
                    tile_of = lambda t, g=g: packed_tile(m, g, slice(0, piece), t)
                    halves.append(half_tile(tile_of, places[h], upper))
                at = kind * HEADS * 64 + i * 128
                gqkv_ref[r, at : at + 128] = jnp.where(lane < 64, halves[0], halves[1])
    tile_of = lambda t: packed_tile(0, z, slice(piece, piece + 16), t)
    for ref, places in ((qb_ref, Q_PLACE), (vb_ref, V_PLACE)):
        first = jnp.where(lane < 64, half_tile(tile_of, places[0], 0), half_tile(tile_of, places[1], 1))
        ref[:, 0:128] = first[0:1]
        ref[:, 128:192] = half_tile(tile_of, places[2], 0)[0:1, 0:64]
    for i, ref in enumerate((o0, o1, o2, o3, o4, o5)):
        ref[...] = up(sums_ref[...])[i : i + 1, 0:shard]
    ib_ref[...] = up(sums_ref[...])[6:7, :]
    loc.wait(*range(PLANES))
    total = gh1_ref[...]
    for g in range(4):
        total = total + dot(dproj_ref[g], wv[g], NT)
    gt_ref[...] = total.astype(bf16)


def vmem(shape, dtype=bf16):
    return pltpu.VMEM(shape, dtype)


ANY = pl.BlockSpec(memory_space=pl.ANY)
SMEM = pl.BlockSpec(memory_space=pltpu.SMEM)
VMEM = pl.BlockSpec(memory_space=pltpu.VMEM)
VMEM_BYTES = 60 * 2**20
SEMS = 96


def semaphores(line=False):
    counts = (SEMS, SEMS) + ((5 * 3, PLANES * 3) if line else ()) + (16,)
    return [pltpu.SemaphoreType.DMA((n,)) for n in counts]


def params(collective_id):
    return pltpu.CompilerParams(
        collective_id=collective_id, has_side_effects=True, vmem_limit_bytes=VMEM_BYTES
    )


def run_forward(lengths, tokens, w_qkv, w_in, w_back, w_out, small):
    rows, width = tokens.shape
    shard = w_qkv.shape[0]
    hidden = w_in.shape[1]
    S = jax.ShapeDtypeStruct
    q_shape, kv_shape = (GROUP_HEADS, 4 * rows, 128), (GROUP_HEADS, 8 * rows, 128)
    return pl.pallas_call(
        forward_kernel,
        out_shape=(
            S(q_shape, bf16), S(kv_shape, bf16), S(kv_shape, bf16), S(q_shape, bf16),
            S((4, rows, width), bf16), S((4, rows, 256), bf16), S((PLANES, 16, width), bf16),
            S((PLANES * shard, hidden), bf16), S((width, width), bf16),
            S((CHIPS, shard, PACK), bf16), S((hidden, width), bf16),
        ),
        in_specs=[SMEM] + [ANY] * 6,
        out_specs=[ANY] * 11,
        scratch_shapes=[
            vmem((4, rows, width)), vmem((width, PACK)), vmem(q_shape), vmem(kv_shape), vmem(kv_shape), vmem(q_shape),
            vmem((4, rows, 256)), vmem((4, rows, 256)), vmem((4, rows, 384)), vmem((4, rows, 384)),
            vmem((PLANES, 16, width)), vmem((shard, w_qkv.shape[1])), vmem((CHIPS, shard, PACK)),
        ] + semaphores(line=True),
        compiler_params=params(1),
    )(lengths, tokens, w_qkv, w_in, w_back, w_out, small)


def run_backward(do, q, k, v, o, tok, grads, sums, back):
    rows = do.shape[1]
    width = tok.shape[2]
    shard = width // PLANES
    length, cols = grads.shape[3:]
    cut = length // 32 * 16
    S = jax.ShapeDtypeStruct
    ext = shard // 2 + 16
    return pl.pallas_call(
        backward_kernel,
        out_shape=(
            S((4, rows, PACK), bf16), S((2, 4, ext, 384), bf16), S((2, 4, ext, 256), bf16), S((2, 4, length, cols), bf16), S((2, 4) + back.shape[1:], bf16), S((16, width), bf16),
        ),
        in_specs=[ANY] * 9,
        out_specs=[ANY] * 6,
        scratch_shapes=[
            vmem((4, rows, 256)), vmem(q.shape), vmem(k.shape), vmem(v.shape), vmem(o.shape), vmem(q.shape),
            vmem(tok.shape), vmem((width, 4 * rows)), vmem((128, 4 * rows), f32), vmem((4 * rows, 128), f32),
            vmem((4 * rows, 128), f32), vmem((3, 4 * rows, 128)), vmem((3, 4 * rows, 128)),
            vmem((4, rows, PACK)), vmem((4, rows, PACK)),
            *[vmem(lead + (ext, n)) for n in (384, 256) for lead in ((2, 4), (4,), (4,), (3,), (2, 4))],
            vmem((4, 4, length, cols)), vmem((4, 4, length, cols)),
            vmem((4, 2, cut, cols)), vmem((4, 2, length - cut, cols)), vmem((4, cut, cols)), vmem((4, length - cut, cols)),
            vmem((3, length, cols)), vmem((4,) + back.shape[1:]), vmem((2, 4, length, cols)), vmem((2, 4) + back.shape[1:]),
            vmem((4, 4, 16, width)), vmem((3, 4, 16, width)), vmem((3, 16, width)), vmem((16, width)),
        ] + semaphores(),
        compiler_params=params(2),
    )(do, q, k, v, o, tok, grads, sums, back)


def run_ffn(lengths, att, tokens, cotangent, full_in, w_in, full_out, w_out, small, full_back, w_back, wq):
    rows, width = tokens.shape
    hidden = w_in.shape[1]
    ch = hidden // 8
    S = jax.ShapeDtypeStruct
    one = S((rows, width), bf16)
    bp = w_back.shape[0] // 8
    return pl.pallas_call(
        ffn_kernel,
        out_shape=(
            one, S((rows, width), f32), S((4, rows, 256), bf16), S((2, 4, 4, width // 4 + 48, ch), bf16), S((4, 16, width), bf16),
            S((PLANES,) + wq.shape, bf16), S((4, 2 * bp, ch), bf16),
        ),
        in_specs=[SMEM] + [VMEM] * 3 + [ANY] * 4 + [VMEM] + [ANY] * 3,
        out_specs=[VMEM] * 2 + [ANY] + [VMEM] * 2 + [ANY] * 2,
        scratch_shapes=[
            vmem((width, hidden)), vmem((hidden, width)), vmem((width, width)),
            vmem((4, rows, 2 * ch)), vmem((4, rows, 2 * ch), f32), vmem((4, rows, 2 * ch)),
            vmem((rows, width), f32), vmem((rows, width), f32), vmem((rows, width), f32),
            vmem((rows, width)), vmem((width, rows)), vmem((rows, width)), vmem((rows, width), f32), vmem((4, 8, 2 * ch), f32),
            vmem((2, 4, 4, 2 * bp, ch)), vmem((4, 4, 2 * bp, ch)), vmem((4, 2, bp, ch)), vmem((4, 2, bp, ch)), vmem((4, bp, ch)), vmem((4, bp, ch)),
            vmem((4, rows, 256)), vmem((4, rows, 256)),
            pltpu.SemaphoreType.DMA((SEMS,)), pltpu.SemaphoreType.DMA((SEMS,)),
            pltpu.SemaphoreType.DMA((5,)), pltpu.SemaphoreType.DMA((PLANES,)), pltpu.SemaphoreType.DMA((24,)),
        ],
        compiler_params=params(3),
    )(lengths, att, tokens, cotangent, full_in, w_in, full_out, w_out, small, full_back, w_back, wq)


def run_final(dproj, wq_full, wq, gh1, gw, hw, fin, finb, sums):
    rows, width = gh1.shape
    shard = width // PLANES
    S = jax.ShapeDtypeStruct
    one = S((1, shard), f32)
    return pl.pallas_call(
        final_kernel,
        out_shape=(
            S((rows, width), bf16), S((shard, 3 * width), f32), S((shard, 8 * fin.shape[3]), f32),
            S((2 * fin.shape[3], width), f32), S((shard, width), f32), one, one, one, one, one, one, one, one, S((1, width), f32),
        ),
        in_specs=[VMEM, ANY, ANY] + [VMEM] * 6,
        out_specs=[VMEM] * 14,
        scratch_shapes=[vmem((4, width, PACK)), pltpu.SemaphoreType.DMA((4,))],
        compiler_params=pltpu.CompilerParams(vmem_limit_bytes=VMEM_BYTES),
    )(dproj, wq_full, wq, gh1, gw, hw, fin, finb, sums)


def planned(
    tokens, lengths, w_qkv, q_bias, v_bias, w_out, out_bias, ln1_gain, ln1_bias,
    w_in, in_bias, w_back, back_bias, ln2_gain, ln2_bias, cotangent,
):
    width = tokens.shape[2]
    line = lambda *a: jnp.concatenate(a + (jnp.zeros((width - sum(x.shape[0] for x in a),), bf16),))
    gap = jnp.zeros((64,), bf16)
    small = jnp.stack([
        jnp.concatenate([out_bias, ln1_gain, ln1_bias, back_bias]), line(ln2_gain, ln2_bias), in_bias,
        line(gap, v_bias[0:64], gap, v_bias[64:128], q_bias, gap, gap, v_bias[128:192]),
    ] + [jnp.zeros((width,), bf16)] * 12)
    q, k, v, o, tok_all, att, small_all, full_in, full_out, wq, full_back = run_forward(
        lengths, tokens[0], w_qkv, w_in, w_back, w_out, small
    )
    output, gh1, do, grads, sums, wq_full, back = run_ffn(
        lengths, att, tokens[0], cotangent[0], full_in, w_in, full_out, w_out, small_all, full_back, w_back, wq
    )
    dproj, gw, hw, fin, finb, sums_f = run_backward(do, q, k, v, o, tok_all, grads, sums, back)
    gt, gqkv, gin, gback, gout, qb, vb, ob, g1, b1, bb, g2, b2, ib = run_final(dproj, wq_full, wq, gh1, gw, hw, fin, finb, sums_f)
    flat = lambda a: a.reshape(a.shape[1])
    return (
        output[None], gt[None], gqkv, flat(qb), flat(vb), gout, flat(ob), flat(g1), flat(b1), gin, flat(ib),
        gback, flat(bb), flat(g2), flat(b2),
    )


masked_score = -1e30


def passed_along(block, axis, distance):
    devices = range(lax.axis_size(axis))
    route = [((i - distance) % len(devices), i) for i in devices]
    return lax.ppermute(block, axis, route)


def norm_forward(hidden, gain_vec, shift_vec):
    average = jnp.mean(hidden, axis=-1, keepdims=True)
    centred = hidden - average
    variance = jnp.mean(centred * centred, axis=-1, keepdims=True)
    inverse = lax.rsqrt(variance + 1e-05)
    normed = centred * inverse
    return (normed * gain_vec + shift_vec, normed, inverse)


def norm_backward(grad_norm, normed, inverse, gain_vec):
    scaled = grad_norm * gain_vec
    grad_input = inverse * (
        scaled
        - jnp.mean(scaled, axis=-1, keepdims=True)
        - normed * jnp.mean(scaled * normed, axis=-1, keepdims=True)
    )
    return (grad_input, jnp.sum(grad_norm * normed, axis=0), jnp.sum(grad_norm, axis=0))


def forward_tile(state_in, query_heads, key_pair, length):
    old_max, old_sum, old_acc = state_in
    key_rows = key_pair.shape[0]
    head_count = query_heads.shape[1]
    head_size = query_heads.shape[2]
    key_heads = key_pair[:, 0].reshape(key_rows, head_count, head_size)
    value_heads = key_pair[:, 1].reshape(key_rows, head_count, head_size)
    key_ok = jnp.arange(key_rows, dtype=jnp.int32) < length
    scores = jnp.einsum(
        "qhd,khd->hqk", query_heads, key_heads, preferred_element_type=jnp.float32
    ) * head_size ** (-0.5)
    scores = jnp.where(key_ok[None, None, :], scores, masked_score)
    new_max = jnp.maximum(old_max, jnp.max(scores, axis=2))
    prob_tile = jnp.where(key_ok[None, None, :], jnp.exp(scores - new_max[:, :, None]), 0.0)
    new_sum = jnp.sum(prob_tile, axis=2)
    new_acc = jnp.einsum(
        "hqk,khd->hqd",
        prob_tile.astype(jnp.bfloat16),
        value_heads,
        preferred_element_type=jnp.float32,
    )
    return (new_max, new_sum, new_acc)


def backward_tile(query_pair, log_total, delta, key_pair, key_start, length):
    query_rows = query_pair.shape[0]
    key_rows = key_pair.shape[0]
    model_width = query_pair.shape[2]
    head_count = log_total.shape[0]
    head_size = model_width // head_count
    score_scale = head_size ** (-0.5)
    query_heads = query_pair[:, 0].reshape(query_rows, head_count, head_size)
    grad_heads = query_pair[:, 1].reshape(query_rows, head_count, head_size)
    key_heads = key_pair[:, 0].reshape(key_rows, head_count, head_size)
    value_heads = key_pair[:, 1].reshape(key_rows, head_count, head_size)
    key_ok = key_start + jnp.arange(key_rows, dtype=jnp.int32) < length
    scores = (
        jnp.einsum("qhd,khd->hqk", query_heads, key_heads, preferred_element_type=jnp.float32)
        * score_scale
    )
    prob_tile = jnp.where(key_ok[None, None, :], jnp.exp(scores - log_total[:, :, None]), 0.0)
    grad_values = jnp.einsum(
        "hqk,qhd->khd",
        prob_tile.astype(jnp.bfloat16),
        grad_heads,
        preferred_element_type=jnp.float32,
    )
    grad_probs = jnp.einsum(
        "qhd,khd->hqk", grad_heads, value_heads, preferred_element_type=jnp.float32
    )
    grad_scores = (prob_tile * (grad_probs - delta[:, :, None])).astype(jnp.bfloat16)
    grad_queries = (
        jnp.einsum("hqk,khd->qhd", grad_scores, key_heads, preferred_element_type=jnp.float32)
        * score_scale
    )
    grad_keys = (
        jnp.einsum("hqk,qhd->khd", grad_scores, query_heads, preferred_element_type=jnp.float32)
        * score_scale
    )
    grad_pair = jnp.stack([grad_keys, grad_values], axis=1).reshape(key_rows, 2, model_width)
    return (grad_queries.reshape(query_rows, model_width), grad_pair)


def on_device(
    tokens,
    lengths,
    w_qkv,
    q_bias,
    v_bias,
    w_out,
    out_bias,
    ln1_gain,
    ln1_bias,
    w_in,
    in_bias,
    w_back,
    back_bias,
    ln2_gain,
    ln2_bias,
    cotangent,
):
    gathered = tuple(
        lax.all_gather(a, "fsdp", axis=0, tiled=True)
        for a in (
            w_qkv, q_bias, v_bias, w_out, out_bias, ln1_gain, ln1_bias, w_in, in_bias, w_back, back_bias, ln2_gain, ln2_bias
        )
    )
    (
        full_qkv,
        full_qbias,
        full_vbias,
        full_out,
        full_obias,
        full_g1,
        full_n1,
        full_in,
        full_ibias,
        full_back,
        full_bbias,
        full_g2,
        full_n2,
    ) = gathered
    f32 = jnp.float32
    seq_index = lax.axis_index("seq")
    seq_count = lax.axis_size("seq")
    token_rows = tokens.shape[1]
    model_width = tokens.shape[2]
    head_count = HEADS
    head_size = model_width // head_count
    length = lengths[0]
    my_start = seq_index * token_rows
    row_valid = (my_start + jnp.arange(token_rows, dtype=jnp.int32) < length).astype(f32)
    inputs_b = tokens[0]
    inputs_f = inputs_b.astype(f32)
    bias_all = jnp.concatenate(
        [full_qbias.astype(f32), jnp.zeros((model_width,), f32), full_vbias.astype(f32)]
    )
    projected = (jnp.dot(inputs_b, full_qkv, preferred_element_type=f32) + bias_all).astype(
        jnp.bfloat16
    )
    query_heads = projected[:, :model_width].reshape(token_rows, head_count, head_size)
    key_pair = projected[:, model_width:].reshape(token_rows, 2, model_width)
    init_state = (
        jnp.full((head_count, token_rows), masked_score, f32),
        jnp.zeros((head_count, token_rows), f32),
        jnp.zeros((head_count, token_rows, head_size), f32),
    )
    pieces = lax.all_gather(key_pair, "seq", axis=0, tiled=True)
    run_max, run_sum, run_acc = forward_tile(init_state, query_heads, pieces, length)
    positive = run_sum > 0.0
    safe_sum = jnp.where(positive, run_sum, 1.0)
    attended_heads = jnp.where(positive[:, :, None], run_acc / safe_sum[:, :, None], 0.0)
    log_total = jnp.where(positive, run_max + jnp.log(safe_sum), 0.0)
    attended_f = attended_heads.transpose(1, 0, 2).reshape(token_rows, model_width)
    attended_b = attended_f.astype(jnp.bfloat16)
    branch_f = jnp.dot(attended_b, full_out, preferred_element_type=f32) + full_obias.astype(f32)
    first_norm, normed_one, inverse_one = norm_forward(
        inputs_f + branch_f, full_g1.astype(f32), full_n1.astype(f32)
    )
    first_low = first_norm.astype(jnp.bfloat16)
    inner_act = jnp.dot(first_low, full_in, preferred_element_type=f32) + full_ibias.astype(f32)
    activated_b = jax.nn.gelu(inner_act, approximate=False).astype(jnp.bfloat16)
    second = jnp.dot(activated_b, full_back, preferred_element_type=f32) + full_bbias.astype(f32)
    result, normed_two, inverse_two = norm_forward(
        first_norm + second, full_g2.astype(f32), full_n2.astype(f32)
    )
    output = (result * row_valid[:, None]).astype(jnp.bfloat16)
    grad_result = cotangent[0].astype(f32) * row_valid[:, None]
    grad_h2, g_ln2_gain, g_ln2_bias = norm_backward(
        grad_result, normed_two, inverse_two, full_g2.astype(f32)
    )
    grad_second = grad_h2.astype(jnp.bfloat16)
    g_w_back = jnp.einsum("tf,td->fd", activated_b, grad_second, preferred_element_type=f32)
    g_back_bias = jnp.sum(grad_second.astype(f32), axis=0)
    grad_act = jnp.einsum("td,fd->tf", grad_second, full_back, preferred_element_type=f32)
    gelu_value, gelu_pull = jax.vjp(
        lambda values_in: jax.nn.gelu(values_in, approximate=False), inner_act
    )
    grad_inner = gelu_pull(grad_act)[0].astype(jnp.bfloat16)
    g_w_in = jnp.einsum("td,tf->df", first_low, grad_inner, preferred_element_type=f32)
    g_in_bias = jnp.sum(grad_inner.astype(f32), axis=0)
    grad_first = grad_h2 + jnp.einsum("tf,df->td", grad_inner, full_in, preferred_element_type=f32)
    grad_h1, g_ln1_gain, g_ln1_bias = norm_backward(
        grad_first, normed_one, inverse_one, full_g1.astype(f32)
    )
    grad_branch = grad_h1.astype(jnp.bfloat16)
    g_w_out = jnp.einsum("tc,td->cd", attended_b, grad_branch, preferred_element_type=f32)
    g_out_bias = jnp.sum(grad_branch.astype(f32), axis=0)
    grad_attended = jnp.einsum(
        "td,cd->tc", grad_branch, full_out, preferred_element_type=f32
    ).astype(jnp.bfloat16)
    delta = jnp.sum(
        (grad_attended.astype(f32) * attended_f).reshape(token_rows, head_count, head_size), axis=2
    ).T
    query_pair = jnp.stack([projected[:, :model_width], grad_attended], axis=1)
    zero_rows = jnp.zeros((token_rows, model_width), f32)
    zero_pair = jnp.zeros((token_rows, 2, model_width), f32)

    def visit_keys(hop_index, grad_q, moving_pair, grad_pair):
        anchor = (seq_index - hop_index) % seq_count
        add_q, add_pair = backward_tile(
            query_pair, log_total, delta, moving_pair, anchor * token_rows, length
        )
        return (grad_q + add_q, grad_pair + add_pair)

    def return_key_grads(grad_pair):
        return passed_along(grad_pair.astype(jnp.bfloat16), "seq", 1).astype(grad_pair.dtype)

    def key_hop(hop_index, loop_state):
        grad_q, moving_pair, grad_pair = loop_state
        grad_q, grad_pair = visit_keys(hop_index, grad_q, moving_pair, grad_pair)
        moved = passed_along(moving_pair, "seq", 1)
        return (grad_q, moved, return_key_grads(grad_pair))

    grad_q, moving_pair, grad_pair = lax.fori_loop(
        0, seq_count - 1, key_hop, (zero_rows, key_pair, zero_pair)
    )
    grad_q, grad_pair = visit_keys(seq_count - 1, grad_q, moving_pair, grad_pair)
    grad_pair = return_key_grads(grad_pair)
    grad_projected = jnp.concatenate(
        [grad_q, grad_pair.reshape(token_rows, 2 * model_width)], axis=1
    ).astype(jnp.bfloat16)
    g_w_qkv = jnp.einsum("td,te->de", inputs_b, grad_projected, preferred_element_type=f32)
    grad_proj_f = grad_projected.astype(f32)
    g_q_bias = jnp.sum(grad_proj_f[:, :model_width], axis=0)
    g_v_bias = jnp.sum(grad_proj_f[:, 2 * model_width :], axis=0)
    grad_input = grad_h1 + jnp.einsum(
        "te,de->td", grad_projected, full_qkv, preferred_element_type=f32
    )
    local_grads = (
        g_w_qkv,
        g_q_bias,
        g_v_bias,
        g_w_out,
        g_out_bias,
        g_ln1_gain,
        g_ln1_bias,
        g_w_in,
        g_in_bias,
        g_w_back,
        g_back_bias,
        g_ln2_gain,
        g_ln2_bias,
    )
    owned = [
        lax.psum_scatter(a.astype(jnp.bfloat16), "fsdp", scatter_dimension=0, tiled=True).astype(jnp.float32)
        for a in local_grads
    ]
    totals = [lax.psum(a.astype(jnp.bfloat16), "seq").astype(jnp.float32) for a in owned]
    return (output[None], grad_input.astype(jnp.bfloat16)[None]) + tuple(totals)


def solution(mesh):
    spread, vector, matrix = P("fsdp", "seq", None), P("fsdp"), P("fsdp", None)
    fits = mesh.shape["seq"] == 2 * CHIPS and mesh.shape["fsdp"] == PLANES
    return jax.shard_map(
        planned if fits else on_device,
        mesh=mesh,
        in_specs=(spread, vector, matrix, vector, vector, matrix) + (vector,) * 3
        + (matrix, vector, matrix) + (vector,) * 3 + (spread,),
        out_specs=(spread, spread, matrix, vector, vector, matrix) + (vector,) * 3
        + (matrix, vector, matrix) + (vector,) * 3,
        check_vma=False,
    )
```

```python
import functools
import math

import jax
import jax.numpy as jnp
from jax import lax
from jax.experimental import pallas as pl
from jax.experimental.pallas import tpu as pltpu
from jax.sharding import PartitionSpec as P

HEADS = 12
bf16 = jnp.bfloat16
f32 = jnp.float32
MESH = pl.DeviceIdType.MESH
LOG2E = math.log2(math.e)
NT = (((1,), (1,)), ((), ()))
NN = (((1,), (0,)), ((), ()))

PLANES = 4
CHIPS = 4
GROUP_HEADS = 3
PACKED = (12, 24, 13, 25, 0, 1, 2, None, 14, 26)
KV_TILE = (0, 1, 4)
PACK = 640


(
    K_ACC, K_ATT0, K_ATT1, K_ATT_O, K_B1, K_B2, K_B3X, K_B3Y, K_BACK, K_BACK_O, K_BM, K_DO, K_DO_O, K_DP,
    K_DP_O, K_F, K_F1, K_F2, K_F3X, K_F3Y, K_FINB_O, K_FIN_O, K_FM, K_G, K_GW_O, K_H, K_HW_O, K_IN, K_K, K_KV,
    K_K_O, K_M, K_O, K_OUT, K_O_O, K_Q, K_QKV, K_Q_O, K_R1, K_RAW, K_RZ, K_RZB, K_S0, K_S1, K_S2, K_SMALL,
    K_SMALL_O, K_SUMS, K_SUMS_O, K_SZ, K_T1A, K_T1B, K_T2A, K_T2B, K_T3A, K_T3B, K_TOK, K_TOK_O, K_V, K_V_O,
    K_WQ, K_WQM, K_WQ_O, K_X1, K_X2, K_Y1, K_Y2, K_Z,
) = range(100, 168)


def dot(a, b, dims=NN):
    return lax.dot_general(a, b, dims, preferred_element_type=f32)


class Net:
    def __init__(self, send_sems, recv_sems):
        self.send_sems, self.recv_sems = send_sems, recv_sems
        self.specs = {}

    def add(self, name, src, dst, device):
        self.specs[name] = (len(self.specs), src, dst, device)

    def get(self, name):
        k, src, dst, device = self.specs[name]
        return pltpu.make_async_remote_copy(
            src_ref=src(),
            dst_ref=dst(),
            send_sem=self.send_sems.at[k],
            recv_sem=self.recv_sems.at[k],
            device_id=device,
            device_id_type=MESH,
        )

    def start(self, *names):
        for name in names:
            self.get(name).start()

    def recv(self, *names):
        for name in names:
            self.get(name).wait_recv()

    def sent(self, *names):
        for name in names:
            self.get(name).wait_send()


class Local:
    def __init__(self, sems):
        self.sems = sems
        self.specs = {}

    def add(self, name, src, dst):
        self.specs[name] = (len(self.specs), src, dst)

    def get(self, name):
        k, src, dst = self.specs[name]
        return pltpu.make_async_copy(src(), dst(), self.sems.at[k])

    def start(self, *names):
        for name in names:
            self.get(name).start()

    def wait(self, *names):
        for name in names:
            self.get(name).wait()


class Line:
    def __init__(self, s, z, send_sems, recv_sems):
        high = lax.div(z, 2)
        self.s, self.z = s, z
        self.order = [z, 1 - z + 4 * high, 2 - high, 3 - 3 * high]
        self.has_right, self.has_left = z < PLANES - 1, z > 0
        self.right, self.left = jnp.minimum(z + 1, PLANES - 1), jnp.maximum(z - 1, 0)
        self.middle = jnp.logical_and(self.has_right, self.has_left)
        self.end = jnp.logical_not(self.middle)
        self.send_sems, self.recv_sems = send_sems, recv_sems
        self.specs = {}

    def add(self, name, own, place):
        self.specs[name] = (len(self.specs), own, place)

    def copy(self, name, i, to_right=False):
        n, own, place = self.specs[name]
        zz = self.order[i]
        if i:
            target = jnp.where(zz < self.z, self.right, self.left)
        else:
            target = self.right if to_right else self.left
        return pltpu.make_async_remote_copy(
            src_ref=place(zz) if i else own(),
            dst_ref=place(zz),
            send_sem=self.send_sems.at[n * 5 + (i + 1 if i else int(to_right))],
            recv_sem=self.recv_sems.at[n * PLANES + zz],
            device_id=(self.s, target),
            device_id_type=MESH,
        )

    def start(self, *names):
        for name in names:
            pl.when(self.has_right)(lambda: self.copy(name, 0, True).start())
            pl.when(self.has_left)(lambda: self.copy(name, 0).start())

    def pass_on(self, name, i):
        self.copy(name, i).wait_recv()
        self.copy(name, i).start()

    def step(self, n, *names):
        for name in names:
            if n == 1:
                @pl.when(self.middle)
                def _():
                    self.pass_on(name, 1)
                    self.pass_on(name, 2)

                pl.when(self.end)(lambda: self.copy(name, 1).wait_recv())
            elif n == 2:
                pl.when(self.middle)(lambda: self.pass_on(name, 3))
                pl.when(self.end)(lambda: self.copy(name, 2).wait_recv())
            else:
                pl.when(self.end)(lambda: self.copy(name, 3).wait_recv())

    def sent(self):
        for name in self.specs:
            pl.when(self.has_right)(lambda: self.copy(name, 0, True).wait_send())
            pl.when(self.has_left)(lambda: self.copy(name, 0).wait_send())

            @pl.when(self.middle)
            def _():
                for i in (1, 2, 3):
                    self.copy(name, i).wait_send()


def coordinates():
    s, z = lax.axis_index("seq"), lax.axis_index("fsdp")
    core = lax.rem(s, 2)
    chip = lax.div(s, 2)
    return s, z, core, chip


def flip(value, mask):
    low, high = lax.rem(value, 2), lax.div(value, 2)
    if mask & 1:
        low = 1 - low
    if mask & 2:
        high = 1 - high
    return high * 2 + low


def hello(devices):
    barrier = pltpu.get_barrier_semaphore()
    for device in devices:
        pl.semaphore_signal(barrier, inc=1, device_id=device, device_id_type=MESH)


def met(count):
    pl.semaphore_wait(pltpu.get_barrier_semaphore(), count)


def greet(devices):
    hello(devices)
    met(len(devices))


def lanes_of(rows=1):
    return lax.broadcasted_iota(jnp.int32, (rows, 128), 1)


def split3(column):
    hi = column.astype(bf16).astype(f32)
    mid = (column - hi).astype(bf16).astype(f32)
    return hi, mid, column - hi - mid


def forward_kernel(
    length_ref, tok_ref, wraw_ref, win_ref, wback_ref, wout_ref,
    ob_ref, g1_ref, n1_ref, bb_ref, g2_ref, n2_ref, ib_ref, qb_ref, vb_ref,
    q_out, k_out, v_out, o_out, tok_out, att_out, small_out, win_full, wout_full, wq_out, wback_full,
    tok, wqv, q_s, k_s, v_s, o_s, att, atts, kvs, kvr, small, wraw, wq_ref, vec_s, vec_v, send_sems, recv_sems, line_send, line_recv, local_sems,
):
    s, z, core, chip = coordinates()
    other = 1 - core
    rows = tok_ref.shape[0]
    half = rows // 2
    shard = wq_ref.shape[1]
    piece = shard // 2
    peer = [None] + [(flip(chip, j) * 2 + core, z) for j in (1, 2, 3)]
    mate = (chip * 2 + other, z)
    plane = [None] + [(s, flip(z, dz)) for dz in (1, 2, 3)]
    zs = [z] + [flip(z, dz) for dz in (1, 2, 3)]
    net, loc = Net(send_sems, recv_sems), Local(local_sems)
    width = win_full.shape[1] // 8
    back = wback_ref.shape[0]
    bpiece = back // 8
    hops = [(K_IN, 1), (K_IN, 2), (K_IN, 3), (K_BACK, 1)]
    at = lambda start, size, unit=16: pl.ds(pl.multiple_of(start, unit), size)

    def part(a, zz, m, c):
        if a == K_IN:
            return win_full.at[at(zz * shard, shard), at((m * 4 + c) * width, width, 128)]
        if a == K_BACK:
            return wback_full.at[at(zz * back + (m * 4 + c) * bpiece, bpiece), :]
        return wout_full.at[at(zz * shard + c * (shard // 4), shard // 4), at(m * width, width, 128)]

    def own_part(a, m, c):
        if a == K_IN:
            return win_ref.at[:, at((m * 4 + c) * width, width, 128)]
        if a == K_BACK:
            return wback_ref.at[at((m * 4 + c) * bpiece, bpiece), :]
        return wout_ref.at[at(c * (shard // 4), shard // 4), at(m * width, width, 128)]

    def side(a, zz, m):
        if a == K_IN:
            return win_full.at[at(zz * shard, shard), at(m * 4 * width, 4 * width, 128)]
        if a == K_BACK:
            return wback_full.at[at(zz * back + m * 4 * bpiece, 4 * bpiece), :]
        return wout_full.at[at(zz * shard, shard), at(m * width, width, 128)]

    line = Line(s, z, line_send, line_recv)
    lines = line.order
    line.add(K_BACK, lambda: own_part(K_BACK, core, chip), lambda zz: part(K_BACK, zz, core, chip))
    line.add(K_OUT, lambda: wout_ref.at[:, at(core * width, width, 128)], lambda zz: side(K_OUT, zz, core))

    for dz in (1, 2, 3):
        net.add((K_WQ, dz), lambda: wq_ref.at[chip, pl.ds(pl.multiple_of(core * piece, 16), piece), :],
                lambda: wqv.at[pl.ds(pl.multiple_of(z * shard + core * piece, 16), piece), :], plane[dz])
        net.add((K_WQM, dz), lambda dz=dz: wqv.at[pl.ds(pl.multiple_of(zs[dz] * shard + core * piece, 16), piece), :],
                lambda dz=dz: wqv.at[pl.ds(pl.multiple_of(zs[dz] * shard + core * piece, 16), piece), :], mate)
        net.add((K_SMALL, dz), lambda: small.at[z], lambda: small.at[z], plane[dz])
    top, bottom = slice(0, half), slice(half, rows)
    net.add(K_T1A, lambda: tok_ref.at[top], lambda: tok.at[1, top], peer[1])
    net.add(K_T1B, lambda: tok_ref.at[bottom], lambda: tok.at[1, bottom], peer[1])
    net.add(K_T2B, lambda: tok_ref.at[bottom], lambda: tok.at[2, bottom], peer[2])
    net.add(K_T2A, lambda: tok_ref.at[top], lambda: tok.at[2, top], peer[2])
    net.add(K_T3A, lambda: tok.at[1, top], lambda: tok.at[3, top], peer[2])
    net.add(K_T3B, lambda: tok.at[2, bottom], lambda: tok.at[3, bottom], peer[1])
    for j in range(4):
        net.add((K_KV, j), lambda j=j: kvs.at[j], lambda j=j: kvr.at[j], mate)
    for j in (1, 2, 3):
        net.add((K_ATT0, j), lambda j=j: atts.at[j, :, 0:128], lambda: att.at[chip, :, 0:128], peer[j])
        net.add((K_ATT1, j), lambda j=j: atts.at[j, :, 128:256], lambda: att.at[chip, :, 128:256], peer[j])
    where = {K_IN: zs, K_BACK: lines, K_OUT: lines}
    for a, dz in hops:
        place = lambda c, a=a, dz=dz: part(a, where[a][dz], core, c)

        def half_place(c, n, a=a, dz=dz):
            zz = where[a][dz]
            if a == K_IN:
                return win_full.at[at(zz * shard + n * piece, piece), at((core * 4 + c) * width, width, 128)]
            return wback_full.at[at(zz * back + (core * 4 + c) * bpiece + n * (bpiece // 2), bpiece // 2), :]

        for j in (1, 2):
            net.add((a, j, dz), lambda place=place: place(chip), lambda place=place: place(chip), peer[j])
        for n, via, last in ((0, 1, 2), (1, 2, 1)):
            there = lambda half_place=half_place, n=n, via=via: half_place(flip(chip, via), n)
            net.add((a, 3 + n, dz), there, there, peer[last])
    for dz in (1, 2, 3):
        net.add((K_IN, K_Z, dz), lambda: own_part(K_IN, core, chip), lambda: part(K_IN, z, core, chip), plane[dz])
    mates = hops + [(K_OUT, dz) for dz in (1, 2, 3)]
    for a, dz in mates:
        net.add((a, K_M, dz), lambda a=a, dz=dz: side(a, where[a][dz], core), lambda a=a, dz=dz: side(a, where[a][dz], core), mate)
    loc.add(K_RAW, lambda: wraw_ref, lambda: wraw)
    loc.add(K_TOK, lambda: tok_ref, lambda: tok.at[0])
    loc.add(K_WQ, lambda: wq_ref.at[chip], lambda: wqv.at[pl.ds(pl.multiple_of(z * shard, 16), shard), :])
    outs = ((K_WQ_O, wq_ref, wq_out), (K_K_O, k_s, k_out), (K_V_O, v_s, v_out), (K_Q_O, q_s, q_out), (K_O_O, o_s, o_out),
            (K_TOK_O, tok, tok_out), (K_ATT_O, att, att_out), (K_SMALL_O, small, small_out))
    for name, src, dst in outs:
        loc.add(name, lambda src=src: src, lambda dst=dst: dst)

    loc.start(K_RAW, K_TOK)
    greet(peer[1:] + [mate] + plane[1:])
    net.start(K_T1A, K_T2B, K_T1B, K_T2A)
    lane = lanes_of()
    vec_s[...] = jnp.zeros_like(vec_s)
    vec_v[...] = jnp.zeros_like(vec_v)
    for i, ref in enumerate((ob_ref, g1_ref, n1_ref, bb_ref, g2_ref, n2_ref)):
        vec_s[i : i + 1, 0:shard] = ref[...].astype(f32).reshape(1, shard)
    vec_s[6:7, :] = ib_ref[...].astype(f32).reshape(1, ib_ref.shape[0])
    vec_s[7:8, 256 : 256 + shard] = qb_ref[...].astype(f32).reshape(1, shard)
    vec_v[0:1, 0:shard] = vb_ref[...].astype(f32).reshape(1, shard)
    first, last = vec_v[:, 0:128], vec_v[:, 128:256]
    for t, tile in ((0, pltpu.roll(first, 64, 1)), (1, first), (4, pltpu.roll(last, 64, 1))):
        vec_s[7:8, t * 128 : (t + 1) * 128] = jnp.where(lane < 64, 0.0, tile[0:1])
    small[z] = jnp.concatenate([vec_s[...], jnp.zeros_like(vec_s)], axis=0).astype(bf16)
    loc.wait(K_RAW)
    for g in range(CHIPS):
        for t in range(PACK // 128):
            halves = []
            for upper in (0, 1):
                block = PACKED[2 * t + upper]
                if block is None:
                    halves.append(0.0)
                    continue
                block += GROUP_HEADS * g
                tile_of = lambda i: wraw[:, i * 128 : (i + 1) * 128].astype(f32)
                halves.append(half_tile(tile_of, block, upper))
            wq_ref[g, :, t * 128 : (t + 1) * 128] = jnp.where(lane < 64, halves[0], halves[1]).astype(bf16)
    loc.start(K_WQ, K_WQ_O)
    net.start(*[(K_WQ, dz) for dz in (1, 2, 3)], *[(K_SMALL, dz) for dz in (1, 2, 3)])
    for dz in (1, 2, 3):
        net.recv((K_WQ, dz))
        net.start((K_WQM, dz))
    net.start(*[(K_IN, K_Z, dz) for dz in (1, 2, 3)])
    loc.wait(K_TOK, K_WQ)
    for dz in (1, 2, 3):
        net.recv((K_SMALL, dz), (K_WQM, dz))

    length = length_ref[0]
    bias = small[chip, 7:8, 0:PACK].astype(f32)

    def keep(tile, h, slot, block):
        position = block * rows + lax.broadcasted_iota(jnp.int32, (rows, 1), 0)
        mask = jnp.where(position < length, 0.0, -1e30).astype(f32)
        ones = jnp.where((lane > 64) & (lane < 68), 1.0, 0.0)
        k_s[h, slot * rows : (slot + 1) * rows, :] = jnp.where(
            lane < 64, tile, jnp.where(lane == 64, mask, ones)
        ).astype(bf16)
        v_s[h, slot * rows : (slot + 1) * rows, :] = jnp.where(
            lane < 64, pltpu.roll(tile, 64, 1), jnp.where(lane < 67, 1.0, 0.0)
        ).astype(bf16)

    def project(j):
        proj = dot(tok[j], wqv[...]) + bias
        for h in range(GROUP_HEADS):
            tile = proj[:, KV_TILE[h] * 128 : (KV_TILE[h] + 1) * 128]
            keep(tile.astype(bf16).astype(f32), h, j, flip(chip, j) * 2 + core)
            kvs[j, :, h * 128 : (h + 1) * 128] = tile.astype(bf16)
            first = 256 + (h // 2) * 128
            tile = proj[:, first : first + 128].astype(bf16).astype(f32) * 0.125
            if h == 1:
                tile = pltpu.roll(tile, 64, 1)
            q_s[h, j * rows : (j + 1) * rows, :] = jnp.where(
                lane < 64, tile, jnp.where(lane == 64, 1.0, 0.0)
            ).astype(bf16)
        net.start((K_KV, j))

    def keep_other(j):
        net.recv((K_KV, j))
        for h in range(GROUP_HEADS):
            tile = kvr[j, :, h * 128 : (h + 1) * 128].astype(f32)
            keep(tile, h, 4 + j, flip(chip, j) * 2 + other)

    def first_hop(a, dz):
        net.start((a, 1, dz), (a, 2, dz))

    def second_hop(a, dz):
        net.recv((a, 1, dz))
        net.start((a, 3, dz))
        net.recv((a, 2, dz))
        net.start((a, 4, dz))

    def third_hop(a, dz):
        net.recv((a, 3, dz), (a, 4, dz))
        net.start((a, K_M, dz))

    project(0)
    net.recv(K_T1A)
    net.start(K_T3A)
    net.recv(K_T2B)
    net.start(K_T3B)
    net.recv(K_T1B)
    project(1)
    net.recv(K_T2A)
    project(2)
    keep_other(0)
    keep_other(1)
    keep_other(2)
    net.recv((K_IN, K_Z, 1))
    first_hop(K_IN, 1)
    line.start(K_BACK, K_OUT)
    net.recv(K_T3A, K_T3B)
    project(3)
    keep_other(3)
    loc.start(K_K_O, K_V_O, K_TOK_O, K_SMALL_O)

    query_tile, key_chunk = 2 * rows, 4 * rows
    tiles = 4 * rows // query_tile
    chunks = 8 * rows // key_chunk

    def attended_tile(which):
        for j in range(4):
            r = slice(j * rows, (j + 1) * rows)
            if which == 0:
                upper = pltpu.roll(o_s[1, r, :].astype(f32), 64, 1)
                value = jnp.where(lane < 64, o_s[0, r, :].astype(f32), upper)
            else:
                value = jnp.where(lane < 64, o_s[2, r, :].astype(f32), 0.0)
            place = slice(which * 128, (which + 1) * 128)
            if j == 0:
                att[chip, :, place] = value.astype(bf16)
            else:
                atts[j, :, place] = value.astype(bf16)
                net.start(((K_ATT0, K_ATT1)[which], j))

    def in_hop(dz):
        net.recv((K_IN, K_Z, dz))
        first_hop(K_IN, dz)

    stages = {
        0: lambda: (in_hop(2), in_hop(3)),
        1: lambda: line.step(1, K_BACK, K_OUT),
        2: lambda: (second_hop(K_IN, 1), first_hop(K_BACK, 1)),
        4: lambda: (second_hop(K_IN, 2), third_hop(K_IN, 1)),
        5: lambda: line.step(2, K_BACK, K_OUT),
        6: lambda: (second_hop(K_IN, 3), third_hop(K_IN, 2)),
        7: lambda: (attended_tile(0), second_hop(K_BACK, 1)),
        8: lambda: third_hop(K_IN, 3),
        9: lambda: (line.step(3, K_BACK, K_OUT), [net.start((K_OUT, K_M, dz)) for dz in (1, 2, 3)]),
        10: lambda: third_hop(K_BACK, 1),
        11: lambda: attended_tile(1),
    }

    def progress(n):
        for at, work in stages.items():
            pl.when(n == at)(lambda work=work: (work(), None)[1])

    def visit(t, carry):
        h, i = lax.div(t, tiles), lax.rem(t, tiles)
        qrows = pl.ds(pl.multiple_of(i * query_tile, query_tile), query_tile)
        q = q_s[h, qrows, :]
        top_score = jnp.full((query_tile, 1), -1e30, f32)
        acc = jnp.zeros((query_tile, 128), f32)
        for c in range(chunks):
            krows = slice(c * key_chunk, (c + 1) * key_chunk)
            scores = dot(q, k_s[h, krows, :], NT)
            new_top = jnp.maximum(top_score, jnp.max(scores, axis=1, keepdims=True))
            probs = jnp.exp2((scores - new_top) * LOG2E)
            fade = jnp.exp2((top_score - new_top) * LOG2E)
            acc = acc * fade + dot(probs.astype(bf16), v_s[h, krows, :])
            top_score = new_top
            if c < chunks - 1:
                progress(t * chunks + c)
        total = acc[:, 64:65]
        o_s[h, qrows, :] = (acc / total).astype(bf16)
        hi, mid, low = split3(-(top_score + jnp.log(total)))
        wide = q.astype(f32)
        wide = jnp.where(lane == 65, hi, jnp.where(lane == 66, mid, jnp.where(lane == 67, low, wide)))
        q_s[h, qrows, :] = wide.astype(bf16)
        progress(t * chunks + chunks - 1)
        return carry

    lax.fori_loop(0, GROUP_HEADS * tiles, visit, 0)
    loc.start(K_Q_O, K_O_O)
    for j in (1, 2, 3):
        net.recv((K_ATT0, j), (K_ATT1, j))
    loc.start(K_ATT_O)
    net.recv(*[(a, K_M, dz) for a, dz in mates])
    for name in net.specs:
        net.sent(name)
    line.sent()
    loc.wait(*[name for name, _, _ in outs])


def backward_kernel(
    do_ref, q_ref, k_ref, v_ref, o_ref, tok_ref, grads_ref, sums_ref, back_ref,
    dproj_out, gw_out, hw_out, fin_out, finb_out, sums_out,
    do_s, q_s, k_s, v_s, o_s, doa, tok, tokt, dqs, dq_keep, kv_own, kvs, kvr, dall, dproj,
    gw, gwr, gz, gzr, gwf, hw, hwr, hz, hzr, hwf, acc, rb, rx, ry, rx2, ry2, rz, rzb, backv, bx2, by2, fin, finb, sums, sums_r, sums_z, sums_f,
    send_sems, recv_sems, local_sems,
):
    s, z, core, chip = coordinates()
    other = 1 - core
    rows = do_ref.shape[1]
    peer = [None] + [(flip(chip, j) * 2 + core, z) for j in (1, 2, 3)]
    mate = (chip * 2 + other, z)
    plane = [None] + [(s, flip(z, dz)) for dz in (1, 2, 3)]
    zs = [z] + [flip(z, dz) for dz in (1, 2, 3)]
    ch = [chip] + [flip(chip, j) for j in (1, 2, 3)]
    net, loc = Net(send_sems, recv_sems), Local(local_sems)
    length = grads_ref.shape[3]
    cut = length // 32 * 16
    xs, ys = slice(0, cut), slice(cut, length)
    shard = tok.shape[2] // PLANES
    piece = shard // 2

    for h in range(GROUP_HEADS):
        net.add((K_KV, h), lambda h=h: kvs.at[h], lambda h=h: kvr.at[h], mate)
        place = ((0, 128), (128, 384), (384, 640))[h]
        for j in (1, 2, 3):
            net.add((K_DP, h, j), lambda j=j, place=place: dall.at[j, :, place[0] : place[1]],
                    lambda place=place: dproj.at[chip, :, place[0] : place[1]], peer[j])
    order = (3, 2, 1, 0)
    for dz in order:
        net.add((K_R1, dz), lambda dz=dz: grads_ref.at[other, zs[dz]], lambda dz=dz: rb.at[zs[dz]], mate)
        for n, j in enumerate((1, 3)):
            net.add((K_X1, n, dz), lambda dz=dz, j=j: acc.at[zs[dz], ch[j], xs], lambda dz=dz, n=n: rx.at[zs[dz], n], peer[1])
        net.add((K_X2, dz), lambda dz=dz: acc.at[zs[dz], ch[2], xs], lambda dz=dz: rx2.at[zs[dz]], peer[2])
        for n, j in enumerate((2, 3)):
            net.add((K_Y1, n, dz), lambda dz=dz, j=j: acc.at[zs[dz], ch[j], ys], lambda dz=dz, n=n: ry.at[zs[dz], n], peer[2])
        net.add((K_Y2, dz), lambda dz=dz: acc.at[zs[dz], ch[1], ys], lambda dz=dz: ry2.at[zs[dz]], peer[1])
        if dz:
            net.add((K_RZ, dz), lambda dz=dz: acc.at[zs[dz], chip], lambda dz=dz: rz.at[dz - 1], plane[dz])
    for dz in (1, 2, 3):
        net.add((K_RZB, dz), lambda dz=dz: backv.at[zs[dz]], lambda dz=dz: rzb.at[dz - 1], plane[dz])
    bh = finb.shape[2] // 2
    bx, by = slice(0, bh), slice(bh, 2 * bh)
    net.add((K_X2, K_BACK), lambda: back_ref.at[2, :, bx], lambda: bx2, peer[2])
    net.add((K_Y2, K_BACK), lambda: back_ref.at[1, :, by], lambda: by2, peer[1])
    net.add(K_B1, lambda: finb.at[core, chip], lambda: finb.at[core, chip], peer[1])
    net.add(K_B2, lambda: finb.at[core, chip], lambda: finb.at[core, chip], peer[2])
    net.add(K_B3X, lambda: finb.at[core, ch[1], bx], lambda: finb.at[core, ch[1], bx], peer[2])
    net.add(K_B3Y, lambda: finb.at[core, ch[2], by], lambda: finb.at[core, ch[2], by], peer[1])
    net.add(K_BM, lambda: finb.at[core], lambda: finb.at[core], mate)
    net.add(K_F1, lambda: fin.at[core, chip], lambda: fin.at[core, chip], peer[1])
    net.add(K_F2, lambda: fin.at[core, chip], lambda: fin.at[core, chip], peer[2])
    net.add(K_F3X, lambda: fin.at[core, ch[1], xs], lambda: fin.at[core, ch[1], xs], peer[2])
    net.add(K_F3Y, lambda: fin.at[core, ch[2], ys], lambda: fin.at[core, ch[2], ys], peer[1])
    net.add(K_FM, lambda: fin.at[core], lambda: fin.at[core], mate)
    net.add(K_S0, lambda: sums_ref, lambda: sums_r.at[0], mate)
    net.add(K_S1, lambda: sums.at[1], lambda: sums_r.at[1], peer[1])
    net.add(K_S2, lambda: sums.at[2], lambda: sums_r.at[2], peer[2])
    for dz in (1, 2, 3):
        net.add((K_SZ, dz), lambda dz=dz: sums.at[3, zs[dz]], lambda dz=dz: sums_z.at[dz - 1], plane[dz])
    for a, w, wr, g, gr, f in ((K_G, gw, gwr, gz, gzr, gwf), (K_H, hw, hwr, hz, hzr, hwf)):
        net.add((a, 0), lambda w=w: w.at[other], lambda wr=wr: wr, mate)
        for dz in (1, 2, 3):
            net.add((a, K_Z, dz), lambda g=g, dz=dz: g.at[zs[dz]], lambda gr=gr, dz=dz: gr.at[dz - 1], plane[dz])
        for j in (1, 2, 3):
            net.add((a, K_F, j), lambda f=f: f.at[core, chip], lambda f=f: f.at[core, chip], peer[j])
        net.add((a, K_M), lambda f=f: f.at[core], lambda f=f: f.at[core], mate)

    loads = ((K_DO, lambda: do_ref, lambda: do_s), (K_O, lambda: o_ref, lambda: o_s),
             (K_TOK, lambda: tok_ref, lambda: tok), (K_Q, lambda: q_ref, lambda: q_s),
             (K_K, lambda: k_ref, lambda: k_s), (K_V, lambda: v_ref, lambda: v_s),
             (K_SUMS, lambda: sums_ref, lambda: sums.at[0]), (K_BACK, lambda: back_ref.at[0], lambda: backv), (K_ACC, lambda: grads_ref.at[core], lambda: acc))
    for name, src, dst in loads:
        loc.add(name, src, dst)
    stores = ((K_DP_O, dproj, dproj_out), (K_GW_O, gwf, gw_out), (K_HW_O, hwf, hw_out), (K_FIN_O, fin, fin_out), (K_FINB_O, finb, finb_out))
    for name, src, dst in stores:
        loc.add(name, lambda src=src: src, lambda dst=dst: dst)
    loc.add(K_SUMS_O, lambda: sums_f, lambda: sums_out)

    loc.start(*[name for name, _, _ in loads])
    greet(peer[1:] + [mate] + plane[1:])
    net.start(K_S0, *[(K_R1, dz) for dz in order])
    net.start((K_X2, K_BACK), (K_Y2, K_BACK))
    lane = lanes_of()
    loc.wait(K_TOK)
    for j in range(4):
        tokt[:, j * rows : (j + 1) * rows] = tok[j].T
    loc.wait(K_DO, K_O, K_Q, K_K, K_V, K_SUMS, K_BACK, K_ACC)
    for j in range(4):
        for h in range(GROUP_HEADS):
            tile = do_s[j, :, (h // 2) * 128 : (h // 2) * 128 + 128].astype(f32)
            if h == 1:
                tile = pltpu.roll(tile, 64, 1)
            tile = jnp.where(lane < 64, tile, 0.0)
            r = slice(j * rows, (j + 1) * rows)
            delta = jnp.sum(tile * o_s[h, r, :].astype(f32), axis=1, keepdims=True)
            hi, mid, low = split3(-delta)
            tile = jnp.where(lane == 64, hi, jnp.where(lane == 65, mid, jnp.where(lane == 66, low, tile)))
            doa[h, r, :] = tile.astype(bf16)

    def add_into(ref, index, other_ref, other_index):
        ref[index] = (ref[index].astype(f32) + other_ref[other_index].astype(f32)).astype(bf16)

    def step_one(dz):
        net.recv((K_R1, dz))
        def body(c, carry):
            add_into(acc, (zs[dz], c), rb, (zs[dz], c))
            return carry
        lax.fori_loop(0, CHIPS, body, 0)
        net.start(*[(K_X1, n, dz) for n in (0, 1)], *[(K_Y1, n, dz) for n in (0, 1)])

    def step_two(dz):
        for n in range(2):
            net.recv((K_X1, 1 - n, dz), (K_Y1, 1 - n, dz))
            jx, jy = (2, 1) if n == 0 else (0, 0)
            add_into(acc, (zs[dz], ch[jx], xs), rx, (zs[dz], 1 - n))
            add_into(acc, (zs[dz], ch[jy], ys), ry, (zs[dz], 1 - n))
            if n == 0:
                net.start((K_X2, dz), (K_Y2, dz))

    def step_three(dz):
        net.recv((K_X2, dz), (K_Y2, dz))
        add_into(acc, (zs[dz], chip, xs), rx2, zs[dz])
        add_into(acc, (zs[dz], chip, ys), ry2, zs[dz])
        if dz:
            net.start((K_RZ, dz))

    def sums_step(n):
        net.recv((K_S0, K_S1, K_S2)[n])
        sums[n + 1] = (sums[n].astype(f32) + sums_r[n].astype(f32)).astype(bf16)
        if n < 2:
            net.start((K_S1, K_S2)[n])
        else:
            net.start(*[(K_SZ, dz) for dz in (1, 2, 3)])

    def back_plane():
        net.recv((K_X2, K_BACK), (K_Y2, K_BACK))
        for zz in range(PLANES):
            add_into(backv, (zz, bx), bx2, zz)
            add_into(backv, (zz, by), by2, zz)
        net.start(*[(K_RZB, dz) for dz in (1, 2, 3)])

    def back_total():
        net.recv(*[(K_RZB, dz) for dz in (1, 2, 3)])
        total = backv[z].astype(f32) + rzb[0].astype(f32) + rzb[1].astype(f32) + rzb[2].astype(f32)
        finb[core, chip] = total.astype(bf16)
        net.start(K_B1, K_B2)

    def back_forward():
        net.recv(K_B1)
        net.start(K_B3X)
        net.recv(K_B2)
        net.start(K_B3Y)

    def back_mate():
        net.recv(K_B3X, K_B3Y)
        net.start(K_BM)

    def fin_total():
        for dz in (1, 2, 3):
            net.recv((K_RZ, dz), (K_SZ, dz))
        total = acc[z, chip].astype(f32) + rz[0].astype(f32) + rz[1].astype(f32) + rz[2].astype(f32)
        fin[core, chip] = total.astype(bf16)
        net.start(K_F1, K_F2)
        total = sums[3, z].astype(f32)
        for n in range(3):
            total = total + sums_z[n].astype(f32)
        sums_f[...] = total.astype(bf16)
        loc.start(K_SUMS_O)

    def fin_forward():
        net.recv(K_F1)
        net.start(K_F3X)
        net.recv(K_F2)
        net.start(K_F3Y)

    def weight_part(a, w, first, last):
        cols = dall[:, :, first:last].reshape(4 * rows, last - first)
        column_sums = jnp.sum(cols.astype(f32), axis=0, keepdims=True)
        extra = jnp.where(lax.broadcasted_iota(jnp.int32, (16, 1), 0) == 0, column_sums, 0.0).astype(bf16)
        for zz in range(PLANES):
            part = dot(tokt[zz * shard : (zz + 1) * shard, :], cols)
            for m in range(2):
                w[m, zz, 0:piece, :] = part[m * piece : (m + 1) * piece, :].astype(bf16)
                w[m, zz, piece : piece + 16, :] = extra
        net.start((a, 0))

    def weight_pair(a, w, wr, g):
        net.recv((a, 0))
        for zz in range(PLANES):
            g[zz] = (w[core, zz].astype(f32) + wr[zz].astype(f32)).astype(bf16)
        net.start(*[(a, K_Z, dz) for dz in (1, 2, 3)])

    def weight_total(a, g, gr, f):
        total = g[z].astype(f32)
        for dz in (1, 2, 3):
            net.recv((a, K_Z, dz))
            total = total + gr[dz - 1].astype(f32)
        f[core, chip] = total.astype(bf16)
        net.start(*[(a, K_F, j) for j in (1, 2, 3)])

    def weight_mate(a):
        net.recv(*[(a, K_F, j) for j in (1, 2, 3)])
        net.start((a, K_M))

    key_chunk, query_tile = 2 * rows, 256
    per_head = 4

    def head_end(h):
        net.recv((K_KV, h))
        tile = KV_TILE[h]
        dst = (0, 1, 4)[h] * 128
        for j in range(4):
            r = slice(j * rows, (j + 1) * rows)
            both = kv_own[r, :] + kvr[h, r, :].astype(f32)
            dall[j, :, dst : dst + 128] = both.astype(bf16)
        dq = dqs[...].T * 0.125
        for j in range(4):
            r = slice(j * rows, (j + 1) * rows)
            mine = dq[r, :]
            if h == 0:
                dq_keep[r, :] = mine
            elif h == 1:
                dall[j, :, 256:384] = jnp.where(lane < 64, dq_keep[r, :], pltpu.roll(mine, 64, 1)).astype(bf16)
            else:
                dall[j, :, 384:512] = jnp.where(lane < 64, mine, 0.0).astype(bf16)
        for j in (1, 2, 3):
            net.start((K_DP, h, j))

    stages = {
        0: lambda: (step_one(3), back_plane(), sums_step(0)),
        1: lambda: (step_one(2), sums_step(1)),
        2: lambda: (step_two(3), step_one(1), sums_step(2)),
        3: lambda: (step_three(3), step_two(2)),
        4: lambda: (step_one(0), back_total()),
        5: lambda: (step_three(2), step_two(1)),
        6: lambda: (step_two(0), back_forward()),
        7: lambda: (step_three(1), weight_part(K_G, gw, 0, 384)),
        8: lambda: (step_three(0), back_mate()),
        9: lambda: (fin_total(), weight_pair(K_G, gw, gwr, gz)),
        11: lambda: (fin_forward(), weight_total(K_G, gz, gzr, gwf)),
    }

    def visit(t, carry):
        h, part = lax.div(t, per_head), lax.rem(t, per_head)
        start = pl.multiple_of(lax.rem(part + 2, 4) * key_chunk, key_chunk)
        krows = pl.ds(start, key_chunk)
        k, v = k_s[h, krows, :], v_s[h, krows, :]
        kt = k.T

        @pl.when(part == 0)
        def _():
            dqs[...] = jnp.zeros_like(dqs)

        dk = jnp.zeros((key_chunk, 128), f32)
        dv = jnp.zeros((key_chunk, 128), f32)
        for i in range(4 * rows // query_tile):
            r = slice(i * query_tile, (i + 1) * query_tile)
            q, do = q_s[h, r, :], doa[h, r, :]
            probs = jnp.exp2(dot(k, q, NT) * LOG2E)
            dscores = (probs * dot(v, do, NT)).astype(bf16)
            dv = dv + dot(probs.astype(bf16), do)
            dk = dk + dot(dscores, q)
            dqs[:, r] += dot(kt, dscores)
        packed = jnp.where(lane < 64, dk, pltpu.roll(dv, 64, 1))

        @pl.when(part < 2)
        def _():
            kvs[h, pl.ds(pl.multiple_of(part * key_chunk, key_chunk), key_chunk), :] = packed.astype(bf16)

        @pl.when(part >= 2)
        def _():
            kv_own[pl.ds(pl.multiple_of((part - 2) * key_chunk, key_chunk), key_chunk), :] = packed

        for hh in range(GROUP_HEADS):
            @pl.when(t == hh * per_head + 1)
            def _(hh=hh):
                net.start((K_KV, hh))

            @pl.when(t == hh * per_head + 3)
            def _(hh=hh):
                head_end(hh)
        for at, work in stages.items():
            pl.when(t == at)(lambda work=work: (work(), None)[1])
        return carry

    lax.fori_loop(0, GROUP_HEADS * per_head, visit, 0)

    weight_part(K_H, hw, 384, PACK)
    dproj[chip] = dall[0]
    weight_pair(K_H, hw, hwr, hz)
    weight_mate(K_G)
    net.recv(K_F3X, K_F3Y)
    net.start(K_FM)
    weight_total(K_H, hz, hzr, hwf)
    for h in range(GROUP_HEADS):
        for j in (1, 2, 3):
            net.recv((K_DP, h, j))
    net.recv(K_FM, K_BM, (K_G, K_M))
    loc.start(K_DP_O, K_GW_O, K_FIN_O, K_FINB_O)
    weight_mate(K_H)
    net.recv((K_H, K_M))
    loc.start(K_HW_O)
    for name in net.specs:
        net.sent(name)
    loc.wait(K_DP_O, K_GW_O, K_HW_O, K_FIN_O, K_FINB_O, K_SUMS_O)


def gelu_parts(u):
    x = jnp.abs(u) * (0.5 ** 0.5)
    d = 1.0 + 0.3275911 * x
    t = pl.reciprocal(d, approx=True)
    t = t * (2.0 - d * t)
    poly = t * (0.254829592 + t * (-0.284496736 + t * (1.421413741 + t * (-1.453152027 + t * 1.061405429))))
    bell = jnp.exp2(u * u * (-0.5 * LOG2E))
    tail = 0.5 * poly * bell
    phi = jnp.where(u >= 0, 1.0 - tail, tail)
    return u * phi, phi + u * bell * (1.0 / math.sqrt(2.0 * math.pi))


def row_mean(a):
    return jnp.mean(a, axis=1, keepdims=True)


def wide_vectors(small):
    step = small.shape[2] // PLANES
    lane = lax.broadcasted_iota(jnp.int32, (8, small.shape[2]), 1)
    total = 0.0
    for zz in range(PLANES):
        part = jnp.where(lane < step, small[zz].astype(f32)[0:8], 0.0)
        total = total + (pltpu.roll(part, zz * step, 1) if zz else part)
    return total


def ffn_kernel(
    length_ref, att_ref, tok_ref, cot_ref, win_ref, win_own, wout_ref, wout_own, small_ref, wback_ref, wback_own, wq_own,
    out_ref, gh1_ref, do_out, grads_ref, sums_ref, wq_full, back_out,
    winv, wbackv, woutv, act_s, gp_s, gi_s, acc, first_s, n1_s, low_s, lowt_s, gsec_s, gh2_s, isum,
    gb, rb, rx, ry, do_ref, do_in, send_sems, recv_sems, line_send, line_recv, local_sems,
):
    s, z, core, chip = coordinates()
    other = 1 - core
    rows, width = tok_ref.shape
    step = width // PLANES
    ch = winv.shape[1] // 8
    wide = 2 * ch
    back = wback_own.shape[0]
    shard = win_own.shape[0]
    piece = shard // 2
    peer = [None] + [(flip(chip, j) * 2 + core, z) for j in (1, 2, 3)]
    mate = (chip * 2 + other, z)
    plane = [(s, flip(z, dz)) for dz in (1, 2, 3)]
    ch_of = [chip] + [flip(chip, j) for j in (1, 2, 3)]
    net, loc = Net(send_sems, recv_sems), Local(local_sems)

    bpiece = back // 8
    line = Line(s, z, line_send, line_recv)
    lines = line.order
    line.add(K_QKV, lambda: wq_own.at[pl.ds(core * 2, 2)], lambda zz: wq_full.at[zz, pl.ds(core * 2, 2)])
    for dz in (1, 2, 3):
        net.add((K_QKV, dz), lambda dz=dz: wq_full.at[lines[dz], pl.ds(core * 2, 2)], lambda dz=dz: wq_full.at[lines[dz], pl.ds(core * 2, 2)], mate)

    def region(ref, zz, c):
        return ref.at[pl.ds(pl.multiple_of(zz * back + (core * 4 + c) * bpiece, 16), bpiece), :]

    def side(zz):
        return wbackv.at[pl.ds(pl.multiple_of(zz * back + core * 4 * bpiece, 16), 4 * bpiece), :]

    for dz in (2, 3):
        for j in (1, 2):
            net.add((j, dz), lambda dz=dz: region(wback_ref, lines[dz], chip), lambda dz=dz: region(wbackv, lines[dz], chip), peer[j])
        via, last = ((1, 2), (2, 1))[dz - 2]
        net.add((3, dz), lambda dz=dz, via=via: region(wbackv, lines[dz], ch_of[via]), lambda dz=dz, via=via: region(wbackv, lines[dz], ch_of[via]), peer[last])
        net.add((K_M, dz), lambda dz=dz: side(lines[dz]), lambda dz=dz: side(lines[dz]), mate)
        loc.add((K_M, dz), lambda dz=dz: region(wback_ref, lines[dz], chip), lambda dz=dz: region(wbackv, lines[dz], chip))
    half = gb.shape[3] // 2
    xs, ys = slice(0, half), slice(half, 2 * half)
    for zz in range(PLANES):
        net.add((K_R1, zz), lambda zz=zz: gb.at[other, zz], lambda zz=zz: rb.at[zz], mate)
        for n, j in enumerate((1, 3)):
            net.add((K_X1, n, zz), lambda zz=zz, j=j: gb.at[core, zz, ch_of[j], xs], lambda zz=zz, n=n: rx.at[zz, n], peer[1])
        for n, j in enumerate((2, 3)):
            net.add((K_Y1, n, zz), lambda zz=zz, j=j: gb.at[core, zz, ch_of[j], ys], lambda zz=zz, n=n: ry.at[zz, n], peer[2])
    for j in (1, 2, 3):
        net.add((K_DO, j), lambda j=j: do_ref.at[ch_of[j]], lambda j=j: do_in.at[j], peer[j])
    loc.add(K_DO_O, lambda: do_in, lambda: do_out)
    for j in range(3):
        loc.add((K_BACK_O, j), lambda j=j: gb.at[core, :, ch_of[j]], lambda j=j: back_out.at[j])
    shards = {K_OUT: (wout_own, wout_ref, woutv), K_IN: (win_own, win_ref, winv), K_BACK: (wback_own, wback_ref, wbackv)}
    loads = [(name, i) for name in shards for i in range(4) if name != K_BACK or i < 2]
    for name, i in loads:
        own, full, dst = shards[name]
        n = own.shape[0]
        place = lambda i=i, n=n: pl.ds(pl.multiple_of(lines[i] * n, 16), n)
        loc.add((name, i), lambda own=own, full=full, i=i, place=place: full.at[place(), :] if i else own,
                lambda dst=dst, place=place: dst.at[place(), :])
    loc.start(*loads, (K_M, 2), (K_M, 3))
    greet(peer[1:] + [mate] + plane)
    net.start((1, 2), (2, 2), (1, 3), (2, 3))
    line.start(K_QKV)

    def hop_two(dz):
        net.recv((1, dz), (2, dz))
        net.start((3, dz))

    def hop_three(dz):
        net.recv((3, dz))
        loc.wait((K_M, dz))
        net.start((K_M, dz))

    def add_into(ref, index, other_ref, other_index):
        ref[index] = (ref[index].astype(f32) + other_ref[other_index].astype(f32)).astype(bf16)

    def step_one(zz):
        net.recv((K_R1, zz))
        for c in range(CHIPS):
            add_into(gb, (core, zz, c), rb, (zz, c))
        net.start(*[(K_X1, n, zz) for n in (0, 1)], *[(K_Y1, n, zz) for n in (0, 1)])

    def step_two(zz):
        net.recv((K_X1, 1, zz), (K_Y1, 1, zz))
        add_into(gb, (core, zz, ch_of[2], xs), rx, (zz, 1))
        add_into(gb, (core, zz, ch_of[1], ys), ry, (zz, 1))
        net.recv((K_X1, 0, zz), (K_Y1, 0, zz))
        add_into(gb, (core, zz, chip, xs), rx, (zz, 0))
        add_into(gb, (core, zz, chip, ys), ry, (zz, 0))

    def during(n, works):
        for at, work in works.items():
            pl.when(n == at)(lambda work=work: (work(), None)[1])

    vectors = wide_vectors(small_ref)
    vec = lambda i: vectors[i : i + 1, :]
    loc.wait(*[(K_OUT, dz) for dz in range(4)])
    branch = vec(0)
    for g in range(4):
        branch = branch + dot(att_ref[g, :, 0:step], woutv[g * step : (g + 1) * step, :])
    hidden = tok_ref[...].astype(f32) + branch
    centred = hidden - row_mean(hidden)
    inverse1 = lax.rsqrt(row_mean(centred * centred) + 1e-5)
    normed = centred * inverse1
    n1_s[...] = normed
    first = normed * vec(1) + vec(2)
    first_s[...] = first
    low_s[...] = first.astype(bf16)
    lowt_s[...] = first.astype(bf16).T
    loc.wait(*[(name, i) for name, i in loads if name != K_OUT])

    def forward(n, carry):
        cols = pl.ds(pl.multiple_of(n * wide, 128), wide)
        inner = dot(low_s[...], winv[:, cols]) + small_ref[n, 6:7, :].astype(f32)
        value, slope = gelu_parts(inner)
        value = value.astype(bf16)
        act_s[n] = value
        gp_s[n] = slope
        during(n, {2: lambda: hop_two(2), 3: lambda: hop_two(3)})
        return carry

    lax.fori_loop(0, PLANES, forward, 0)

    def second_layer(i):
        zz = lines[i]
        return dot(act_s[zz], wbackv[pl.ds(pl.multiple_of(zz * back, 16), back), :])

    acc[...] = second_layer(0)
    acc[...] += second_layer(1)
    hop_three(2)
    hop_three(3)
    line.step(1, K_QKV)
    net.recv((K_M, 2))
    acc[...] += second_layer(2)
    net.recv((K_M, 3))
    acc[...] += second_layer(3)
    position = s * rows + lax.broadcasted_iota(jnp.int32, (rows, 1), 0)
    valid = (position < length_ref[0]).astype(f32)
    hidden = first_s[...] + acc[...] + vec(3)
    centred = hidden - row_mean(hidden)
    inverse = lax.rsqrt(row_mean(centred * centred) + 1e-5)
    normed = centred * inverse
    out_ref[...] = ((normed * vec(4) + vec(5)) * valid).astype(bf16)
    grad = cot_ref[...].astype(f32) * valid
    sum_rows = lambda a: jnp.sum(a, axis=0, keepdims=True)
    g2_gain, g2_bias = sum_rows(grad * normed), sum_rows(grad)
    scaled = grad * vec(4)
    gh2 = inverse * (scaled - row_mean(scaled) - normed * row_mean(scaled * normed))
    gh2_s[...] = gh2
    second = gh2.astype(bf16)
    gsec_s[...] = second
    back_sum = sum_rows(second.astype(f32))
    acc[...] = jnp.zeros_like(acc)

    def back_weights(n, carry):
        gback = dot(act_s[n].T, gsec_s[...]).astype(bf16)
        part = wide // 8
        for m in range(2):
            for k in range(4):
                for x in range(2):
                    gb[m, n, k, x * part : (x + 1) * part, :] = gback[
                        (m * 4 + k) * part : (m * 4 + k + 1) * part, x * ch : (x + 1) * ch
                    ]
        during(n, {
            0: lambda: net.start((K_R1, 0)), 1: lambda: net.start((K_R1, 1)),
            2: lambda: net.start((K_R1, 2)), 3: lambda: net.start((K_R1, 3)),
        })
        return carry

    lax.fori_loop(0, PLANES, back_weights, 0)

    def backward(n, carry):
        cols = pl.ds(pl.multiple_of(n * wide, 128), wide)
        grad_inner = (dot(gsec_s[...], wbackv[cols, :], NT) * gp_s[n]).astype(bf16)
        gi_s[n] = grad_inner
        isum[n] = jnp.broadcast_to(sum_rows(grad_inner.astype(f32)), (8, wide))
        acc[...] += dot(grad_inner, winv[:, cols], NT)
        during(n, {
            0: lambda: step_one(0), 1: lambda: step_one(1),
            2: lambda: (step_one(2), step_two(0)), 3: lambda: step_one(3),
        })
        return carry

    lax.fori_loop(0, PLANES, backward, 0)
    grad = gh2_s[...] + acc[...]
    normed = n1_s[...]
    g1_gain, g1_bias = sum_rows(grad * normed), sum_rows(grad)
    scaled = grad * vec(1)
    gh1 = inverse1 * (scaled - row_mean(scaled) - normed * row_mean(scaled * normed))
    gh1_ref[...] = gh1
    gbranch = gh1.astype(bf16)
    out_sum = sum_rows(gbranch.astype(f32))
    for g in range(4):
        w = woutv[g * step : (g + 1) * step, :]
        do_ref[g, :, 0:step] = dot(gbranch, w, NT).astype(bf16)
        do_ref[g, :, step:] = jnp.zeros((rows, do_ref.shape[2] - step), bf16)
    net.start(*[(K_DO, j) for j in (1, 2, 3)])
    line.step(2, K_QKV)
    net.start((K_QKV, 1), (K_QKV, 2))
    do_in[0] = do_ref[chip]
    for g in range(4):
        gw = dot(att_ref[g, :, 0:step].T, gbranch).astype(bf16)
        part = step // 4
        for c in range(4):
            for m in range(2):
                grads_ref[m, g, c, step:, :] = gw[c * part : (c + 1) * part, m * ch : (m + 1) * ch]

    def weights(n, carry):
        for zz in range(PLANES):
            gin = dot(lowt_s[zz * step : (zz + 1) * step, :], gi_s[n]).astype(bf16)
            for x in range(2):
                grads_ref[lax.div(n, 2), zz, lax.rem(n, 2) * 2 + x, 0:step, :] = gin[:, x * ch : (x + 1) * ch]
        during(n, {
            0: lambda: step_two(1), 1: lambda: step_two(2), 2: lambda: step_two(3),
        })
        return carry

    lax.fori_loop(0, PLANES, weights, 0)
    lane = lax.broadcasted_iota(jnp.int32, (8, width), 1)
    place = lax.broadcasted_iota(jnp.int32, (8, width), 0)
    total = jnp.zeros((8, width), f32)
    for i, v in enumerate((out_sum, g1_gain, g1_bias, back_sum, g2_gain, g2_bias)):
        total = jnp.where(place == i, v, total)
    for zz in range(PLANES):
        part = total if zz == 0 else pltpu.roll(total, width - zz * step, 1)
        part = jnp.where(lane < step, part, 0.0)
        part = jnp.where(place == 6, isum[zz], part)
        sums_ref[zz, 0:16, :] = jnp.concatenate([part, jnp.zeros((8, width), f32)], axis=0).astype(bf16)
    net.recv(*[(K_DO, j) for j in (1, 2, 3)])
    loc.start(*[(K_BACK_O, j) for j in range(3)], K_DO_O)
    line.step(3, K_QKV)
    net.start((K_QKV, 3))
    net.recv(*[(K_QKV, dz) for dz in (1, 2, 3)])
    for name in net.specs:
        net.sent(name)
    line.sent()
    loc.wait(*[(K_BACK_O, j) for j in range(3)], K_DO_O)


Q_PLACE, K_PLACE, V_PLACE = (4, 5, 6), (0, 2, 8), (1, 3, 9)


def half_tile(tile_of, block, upper):
    tile = tile_of(block // 2)
    return tile if block % 2 == upper else pltpu.roll(tile, 64, 1)


def final_kernel(
    dproj_ref, wq_ref, wq_own, gh1_ref, gw_ref, hw_ref, fin_ref, finb_ref, sums_ref,
    gt_ref, gqkv_ref, gin_ref, gback_ref, gout_ref, qb_ref, vb_ref, o0, o1, o2, o3, o4, o5, ib_ref,
    wv, row, local_sems,
):
    z = lax.axis_index("fsdp")
    loc = Local(local_sems)
    shard = wq_ref.shape[2]
    for dz in range(PLANES):
        zz = flip(z, dz)
        loc.add(dz, lambda zz=zz, dz=dz: wq_own if dz == 0 else wq_ref.at[zz],
                lambda zz=zz: wv.at[:, pl.ds(pl.multiple_of(zz * shard, 16), shard), :])
    loc.start(*range(PLANES))
    lane = lanes_of()
    up = lambda a: a.astype(f32)
    ch = fin_ref.shape[3]
    for m in range(2):
        for c in range(4):
            n = m * 4 + c
            gin_ref[:, n * ch : (n + 1) * ch] = up(fin_ref[m, c, 0:shard, :])
            part = ch // 4
            for x in range(2):
                gback_ref[n * part : (n + 1) * part, x * ch : (x + 1) * ch] = up(
                    finb_ref[m, c, x * part : (x + 1) * part, :]
                )
            gout_ref[c * (shard // 4) : (c + 1) * (shard // 4), m * ch : (m + 1) * ch] = up(fin_ref[m, c, shard:, :])
    piece = shard // 2

    def packed_tile(m, g, r, t):
        if t < 3:
            return up(gw_ref[m, g, r, t * 128 : (t + 1) * 128])
        return up(hw_ref[m, g, r, (t - 3) * 128 : (t - 2) * 128])

    for m in range(2):
        r = slice(m * piece, (m + 1) * piece)
        for kind, places in enumerate((Q_PLACE, K_PLACE, V_PLACE)):
            for i in range(HEADS // 2):
                halves = []
                for upper in (0, 1):
                    g, h = divmod(2 * i + upper, GROUP_HEADS)
                    tile_of = lambda t, g=g: packed_tile(m, g, slice(0, piece), t)
                    halves.append(half_tile(tile_of, places[h], upper))
                at = kind * HEADS * 64 + i * 128
                gqkv_ref[r, at : at + 128] = jnp.where(lane < 64, halves[0], halves[1])
    tile_of = lambda t: packed_tile(0, z, slice(piece, piece + 16), t)
    for ref, places in ((qb_ref, Q_PLACE), (vb_ref, V_PLACE)):
        first = jnp.where(lane < 64, half_tile(tile_of, places[0], 0), half_tile(tile_of, places[1], 1))
        row[0:1, 0:128] = first[0:1]
        row[0:1, 128:256] = half_tile(tile_of, places[2], 0)[0:1]
        ref[...] = row[0:1, 0:shard].reshape(shard)
    for i, ref in enumerate((o0, o1, o2, o3, o4, o5)):
        ref[...] = up(sums_ref[...])[i : i + 1, 0:shard].reshape(shard)
    ib_ref[...] = up(sums_ref[...])[6:7, :].reshape(ib_ref.shape[0])
    loc.wait(*range(PLANES))
    total = gh1_ref[...]
    for g in range(4):
        total = total + dot(dproj_ref[g], wv[g], NT)
    gt_ref[...] = total.astype(bf16)


def vmem(shape, dtype=bf16):
    return pltpu.VMEM(shape, dtype)


ANY = pl.BlockSpec(memory_space=pl.ANY)
SMEM = pl.BlockSpec(memory_space=pltpu.SMEM)
VMEM = pl.BlockSpec(memory_space=pltpu.VMEM)
VMEM_BYTES = 60 * 2**20
SEMS = 96


def semaphores(line=False):
    counts = (SEMS, SEMS) + ((5 * 2, PLANES * 2) if line else ()) + (16,)
    return [pltpu.SemaphoreType.DMA((n,)) for n in counts]


def params(collective_id):
    return pltpu.CompilerParams(
        collective_id=collective_id, has_side_effects=True, vmem_limit_bytes=VMEM_BYTES
    )


def run_forward(lengths, tokens, w_qkv, w_in, w_back, w_out, *vectors):
    rows, width = tokens.shape
    shard = w_qkv.shape[0]
    hidden = w_in.shape[1]
    S = jax.ShapeDtypeStruct
    q_shape, kv_shape = (GROUP_HEADS, 4 * rows, 128), (GROUP_HEADS, 8 * rows, 128)
    return pl.pallas_call(
        forward_kernel,
        out_shape=(
            S(q_shape, bf16), S(kv_shape, bf16), S(kv_shape, bf16), S(q_shape, bf16),
            S((4, rows, width), bf16), S((4, rows, 256), bf16), S((PLANES, 16, width), bf16),
            S((PLANES * shard, hidden), bf16), S((width, width), bf16),
            S((CHIPS, shard, PACK), bf16), S((hidden, width), bf16),
        ),
        in_specs=[SMEM] + [ANY] * 5 + [VMEM] * 9,
        out_specs=[ANY] * 11,
        scratch_shapes=[
            vmem((4, rows, width)), vmem((width, PACK)), vmem(q_shape), vmem(kv_shape), vmem(kv_shape), vmem(q_shape),
            vmem((4, rows, 256)), vmem((4, rows, 256)), vmem((4, rows, 384)), vmem((4, rows, 384)),
            vmem((PLANES, 16, width)), vmem((shard, w_qkv.shape[1])), vmem((CHIPS, shard, PACK)),
            vmem((8, width), f32), vmem((8, 256), f32),
        ] + semaphores(line=True),
        compiler_params=params(1),
    )(lengths, tokens, w_qkv, w_in, w_back, w_out, *vectors)


def run_backward(do, q, k, v, o, tok, grads, sums, back):
    rows = do.shape[1]
    width = tok.shape[2]
    shard = width // PLANES
    length, cols = grads.shape[3:]
    cut = length // 32 * 16
    S = jax.ShapeDtypeStruct
    ext = shard // 2 + 16
    return pl.pallas_call(
        backward_kernel,
        out_shape=(
            S((4, rows, PACK), bf16), S((2, 4, ext, 384), bf16), S((2, 4, ext, 256), bf16), S((2, 4, length, cols), bf16), S((2, 4) + back.shape[2:], bf16), S((16, width), bf16),
        ),
        in_specs=[ANY] * 9,
        out_specs=[ANY] * 6,
        scratch_shapes=[
            vmem((4, rows, 256)), vmem(q.shape), vmem(k.shape), vmem(v.shape), vmem(o.shape), vmem(q.shape),
            vmem(tok.shape), vmem((width, 4 * rows)), vmem((128, 4 * rows), f32), vmem((4 * rows, 128), f32),
            vmem((4 * rows, 128), f32), vmem((3, 4 * rows, 128)), vmem((3, 4 * rows, 128)),
            vmem((4, rows, PACK)), vmem((4, rows, PACK)),
            *[vmem(lead + (ext, n)) for n in (384, 256) for lead in ((2, 4), (4,), (4,), (3,), (2, 4))],
            vmem((4, 4, length, cols)), vmem((4, 4, length, cols)),
            vmem((4, 2, cut, cols)), vmem((4, 2, length - cut, cols)), vmem((4, cut, cols)), vmem((4, length - cut, cols)),
            vmem((3, length, cols)), vmem((3,) + back.shape[2:]), vmem(back.shape[1:]),
            vmem((4, back.shape[2] // 2, cols)), vmem((4, back.shape[2] // 2, cols)), vmem((2, 4, length, cols)), vmem((2, 4) + back.shape[2:]),
            vmem((4, 4, 16, width)), vmem((3, 4, 16, width)), vmem((3, 16, width)), vmem((16, width)),
        ] + semaphores(),
        compiler_params=params(2),
    )(do, q, k, v, o, tok, grads, sums, back)


def run_ffn(lengths, att, tokens, cotangent, full_in, w_in, full_out, w_out, small, full_back, w_back, wq):
    rows, width = tokens.shape
    hidden = w_in.shape[1]
    ch = hidden // 8
    S = jax.ShapeDtypeStruct
    one = S((rows, width), bf16)
    bp = w_back.shape[0] // 8
    return pl.pallas_call(
        ffn_kernel,
        out_shape=(
            one, S((rows, width), f32), S((4, rows, 256), bf16), S((2, 4, 4, width // 4 + 48, ch), bf16), S((4, 16, width), bf16),
            S((PLANES,) + wq.shape, bf16), S((3, 4, 2 * bp, ch), bf16),
        ),
        in_specs=[SMEM] + [VMEM] * 3 + [ANY] * 4 + [VMEM] + [ANY] * 3,
        out_specs=[VMEM] * 2 + [ANY] + [VMEM] * 2 + [ANY] * 2,
        scratch_shapes=[
            vmem((width, hidden)), vmem((hidden, width)), vmem((width, width)),
            vmem((4, rows, 2 * ch)), vmem((4, rows, 2 * ch), f32), vmem((4, rows, 2 * ch)),
            vmem((rows, width), f32), vmem((rows, width), f32), vmem((rows, width), f32),
            vmem((rows, width)), vmem((width, rows)), vmem((rows, width)), vmem((rows, width), f32), vmem((4, 8, 2 * ch), f32),
            vmem((2, 4, 4, 2 * bp, ch)), vmem((4, 4, 2 * bp, ch)), vmem((4, 2, bp, ch)), vmem((4, 2, bp, ch)),
            vmem((4, rows, 256)), vmem((4, rows, 256)),
            pltpu.SemaphoreType.DMA((SEMS,)), pltpu.SemaphoreType.DMA((SEMS,)),
            pltpu.SemaphoreType.DMA((5,)), pltpu.SemaphoreType.DMA((PLANES,)), pltpu.SemaphoreType.DMA((24,)),
        ],
        compiler_params=params(3),
    )(lengths, att, tokens, cotangent, full_in, w_in, full_out, w_out, small, full_back, w_back, wq)


def run_final(dproj, wq_full, wq, gh1, gw, hw, fin, finb, sums):
    rows, width = gh1.shape
    shard = width // PLANES
    S = jax.ShapeDtypeStruct
    one = S((shard,), f32)
    return pl.pallas_call(
        final_kernel,
        out_shape=(
            S((rows, width), bf16), S((shard, 3 * width), f32), S((shard, 8 * fin.shape[3]), f32),
            S((2 * fin.shape[3], width), f32), S((shard, width), f32), one, one, one, one, one, one, one, one, S((width,), f32),
        ),
        in_specs=[VMEM, ANY, ANY] + [VMEM] * 6,
        out_specs=[VMEM] * 14,
        scratch_shapes=[vmem((4, width, PACK)), vmem((8, 256), f32), pltpu.SemaphoreType.DMA((4,))],
        compiler_params=pltpu.CompilerParams(vmem_limit_bytes=VMEM_BYTES),
    )(dproj, wq_full, wq, gh1, gw, hw, fin, finb, sums)


def planned(
    tokens, lengths, w_qkv, q_bias, v_bias, w_out, out_bias, ln1_gain, ln1_bias,
    w_in, in_bias, w_back, back_bias, ln2_gain, ln2_bias, cotangent,
):
    vectors = (out_bias, ln1_gain, ln1_bias, back_bias, ln2_gain, ln2_bias, in_bias, q_bias, v_bias)
    q, k, v, o, tok_all, att, small_all, full_in, full_out, wq, full_back = run_forward(
        lengths, tokens[0], w_qkv, w_in, w_back, w_out, *vectors
    )
    output, gh1, do, grads, sums, wq_full, back = run_ffn(
        lengths, att, tokens[0], cotangent[0], full_in, w_in, full_out, w_out, small_all, full_back, w_back, wq
    )
    dproj, gw, hw, fin, finb, sums_f = run_backward(do, q, k, v, o, tok_all, grads, sums, back)
    gt, gqkv, gin, gback, gout, qb, vb, ob, g1, b1, bb, g2, b2, ib = run_final(dproj, wq_full, wq, gh1, gw, hw, fin, finb, sums_f)
    return (output[None], gt[None], gqkv, qb, vb, gout, ob, g1, b1, gin, ib, gback, bb, g2, b2)


masked_score = -1e30


def passed_along(block, axis, distance):
    devices = range(lax.axis_size(axis))
    route = [((i - distance) % len(devices), i) for i in devices]
    return lax.ppermute(block, axis, route)


def norm_forward(hidden, gain_vec, shift_vec):
    average = jnp.mean(hidden, axis=-1, keepdims=True)
    centred = hidden - average
    variance = jnp.mean(centred * centred, axis=-1, keepdims=True)
    inverse = lax.rsqrt(variance + 1e-05)
    normed = centred * inverse
    return (normed * gain_vec + shift_vec, normed, inverse)


def norm_backward(grad_norm, normed, inverse, gain_vec):
    scaled = grad_norm * gain_vec
    grad_input = inverse * (
        scaled
        - jnp.mean(scaled, axis=-1, keepdims=True)
        - normed * jnp.mean(scaled * normed, axis=-1, keepdims=True)
    )
    return (grad_input, jnp.sum(grad_norm * normed, axis=0), jnp.sum(grad_norm, axis=0))


def forward_tile(state_in, query_heads, key_pair, length):
    old_max, old_sum, old_acc = state_in
    key_rows = key_pair.shape[0]
    head_count = query_heads.shape[1]
    head_size = query_heads.shape[2]
    key_heads = key_pair[:, 0].reshape(key_rows, head_count, head_size)
    value_heads = key_pair[:, 1].reshape(key_rows, head_count, head_size)
    key_ok = jnp.arange(key_rows, dtype=jnp.int32) < length
    scores = jnp.einsum(
        "qhd,khd->hqk", query_heads, key_heads, preferred_element_type=jnp.float32
    ) * head_size ** (-0.5)
    scores = jnp.where(key_ok[None, None, :], scores, masked_score)
    new_max = jnp.maximum(old_max, jnp.max(scores, axis=2))
    prob_tile = jnp.where(key_ok[None, None, :], jnp.exp(scores - new_max[:, :, None]), 0.0)
    new_sum = jnp.sum(prob_tile, axis=2)
    new_acc = jnp.einsum(
        "hqk,khd->hqd",
        prob_tile.astype(jnp.bfloat16),
        value_heads,
        preferred_element_type=jnp.float32,
    )
    return (new_max, new_sum, new_acc)


def backward_tile(query_pair, log_total, delta, key_pair, key_start, length):
    query_rows = query_pair.shape[0]
    key_rows = key_pair.shape[0]
    model_width = query_pair.shape[2]
    head_count = log_total.shape[0]
    head_size = model_width // head_count
    score_scale = head_size ** (-0.5)
    query_heads = query_pair[:, 0].reshape(query_rows, head_count, head_size)
    grad_heads = query_pair[:, 1].reshape(query_rows, head_count, head_size)
    key_heads = key_pair[:, 0].reshape(key_rows, head_count, head_size)
    value_heads = key_pair[:, 1].reshape(key_rows, head_count, head_size)
    key_ok = key_start + jnp.arange(key_rows, dtype=jnp.int32) < length
    scores = (
        jnp.einsum("qhd,khd->hqk", query_heads, key_heads, preferred_element_type=jnp.float32)
        * score_scale
    )
    prob_tile = jnp.where(key_ok[None, None, :], jnp.exp(scores - log_total[:, :, None]), 0.0)
    grad_values = jnp.einsum(
        "hqk,qhd->khd",
        prob_tile.astype(jnp.bfloat16),
        grad_heads,
        preferred_element_type=jnp.float32,
    )
    grad_probs = jnp.einsum(
        "qhd,khd->hqk", grad_heads, value_heads, preferred_element_type=jnp.float32
    )
    grad_scores = (prob_tile * (grad_probs - delta[:, :, None])).astype(jnp.bfloat16)
    grad_queries = (
        jnp.einsum("hqk,khd->qhd", grad_scores, key_heads, preferred_element_type=jnp.float32)
        * score_scale
    )
    grad_keys = (
        jnp.einsum("hqk,qhd->khd", grad_scores, query_heads, preferred_element_type=jnp.float32)
        * score_scale
    )
    grad_pair = jnp.stack([grad_keys, grad_values], axis=1).reshape(key_rows, 2, model_width)
    return (grad_queries.reshape(query_rows, model_width), grad_pair)


def on_device(
    tokens,
    lengths,
    w_qkv,
    q_bias,
    v_bias,
    w_out,
    out_bias,
    ln1_gain,
    ln1_bias,
    w_in,
    in_bias,
    w_back,
    back_bias,
    ln2_gain,
    ln2_bias,
    cotangent,
):
    gathered = tuple(
        lax.all_gather(a, "fsdp", axis=0, tiled=True)
        for a in (
            w_qkv, q_bias, v_bias, w_out, out_bias, ln1_gain, ln1_bias, w_in, in_bias, w_back, back_bias, ln2_gain, ln2_bias
        )
    )
    (
        full_qkv,
        full_qbias,
        full_vbias,
        full_out,
        full_obias,
        full_g1,
        full_n1,
        full_in,
        full_ibias,
        full_back,
        full_bbias,
        full_g2,
        full_n2,
    ) = gathered
    f32 = jnp.float32
    seq_index = lax.axis_index("seq")
    seq_count = lax.axis_size("seq")
    token_rows = tokens.shape[1]
    model_width = tokens.shape[2]
    head_count = HEADS
    head_size = model_width // head_count
    length = lengths[0]
    my_start = seq_index * token_rows
    row_valid = (my_start + jnp.arange(token_rows, dtype=jnp.int32) < length).astype(f32)
    inputs_b = tokens[0]
    inputs_f = inputs_b.astype(f32)
    bias_all = jnp.concatenate(
        [full_qbias.astype(f32), jnp.zeros((model_width,), f32), full_vbias.astype(f32)]
    )
    projected = (jnp.dot(inputs_b, full_qkv, preferred_element_type=f32) + bias_all).astype(
        jnp.bfloat16
    )
    query_heads = projected[:, :model_width].reshape(token_rows, head_count, head_size)
    key_pair = projected[:, model_width:].reshape(token_rows, 2, model_width)
    init_state = (
        jnp.full((head_count, token_rows), masked_score, f32),
        jnp.zeros((head_count, token_rows), f32),
        jnp.zeros((head_count, token_rows, head_size), f32),
    )
    pieces = lax.all_gather(key_pair, "seq", axis=0, tiled=True)
    run_max, run_sum, run_acc = forward_tile(init_state, query_heads, pieces, length)
    positive = run_sum > 0.0
    safe_sum = jnp.where(positive, run_sum, 1.0)
    attended_heads = jnp.where(positive[:, :, None], run_acc / safe_sum[:, :, None], 0.0)
    log_total = jnp.where(positive, run_max + jnp.log(safe_sum), 0.0)
    attended_f = attended_heads.transpose(1, 0, 2).reshape(token_rows, model_width)
    attended_b = attended_f.astype(jnp.bfloat16)
    branch_f = jnp.dot(attended_b, full_out, preferred_element_type=f32) + full_obias.astype(f32)
    first_norm, normed_one, inverse_one = norm_forward(
        inputs_f + branch_f, full_g1.astype(f32), full_n1.astype(f32)
    )
    first_low = first_norm.astype(jnp.bfloat16)
    inner_act = jnp.dot(first_low, full_in, preferred_element_type=f32) + full_ibias.astype(f32)
    activated_b = jax.nn.gelu(inner_act, approximate=False).astype(jnp.bfloat16)
    second = jnp.dot(activated_b, full_back, preferred_element_type=f32) + full_bbias.astype(f32)
    result, normed_two, inverse_two = norm_forward(
        first_norm + second, full_g2.astype(f32), full_n2.astype(f32)
    )
    output = (result * row_valid[:, None]).astype(jnp.bfloat16)
    grad_result = cotangent[0].astype(f32) * row_valid[:, None]
    grad_h2, g_ln2_gain, g_ln2_bias = norm_backward(
        grad_result, normed_two, inverse_two, full_g2.astype(f32)
    )
    grad_second = grad_h2.astype(jnp.bfloat16)
    g_w_back = jnp.einsum("tf,td->fd", activated_b, grad_second, preferred_element_type=f32)
    g_back_bias = jnp.sum(grad_second.astype(f32), axis=0)
    grad_act = jnp.einsum("td,fd->tf", grad_second, full_back, preferred_element_type=f32)
    gelu_value, gelu_pull = jax.vjp(
        lambda values_in: jax.nn.gelu(values_in, approximate=False), inner_act
    )
    grad_inner = gelu_pull(grad_act)[0].astype(jnp.bfloat16)
    g_w_in = jnp.einsum("td,tf->df", first_low, grad_inner, preferred_element_type=f32)
    g_in_bias = jnp.sum(grad_inner.astype(f32), axis=0)
    grad_first = grad_h2 + jnp.einsum("tf,df->td", grad_inner, full_in, preferred_element_type=f32)
    grad_h1, g_ln1_gain, g_ln1_bias = norm_backward(
        grad_first, normed_one, inverse_one, full_g1.astype(f32)
    )
    grad_branch = grad_h1.astype(jnp.bfloat16)
    g_w_out = jnp.einsum("tc,td->cd", attended_b, grad_branch, preferred_element_type=f32)
    g_out_bias = jnp.sum(grad_branch.astype(f32), axis=0)
    grad_attended = jnp.einsum(
        "td,cd->tc", grad_branch, full_out, preferred_element_type=f32
    ).astype(jnp.bfloat16)
    delta = jnp.sum(
        (grad_attended.astype(f32) * attended_f).reshape(token_rows, head_count, head_size), axis=2
    ).T
    query_pair = jnp.stack([projected[:, :model_width], grad_attended], axis=1)
    zero_rows = jnp.zeros((token_rows, model_width), f32)
    zero_pair = jnp.zeros((token_rows, 2, model_width), f32)

    def visit_keys(hop_index, grad_q, moving_pair, grad_pair):
        anchor = (seq_index - hop_index) % seq_count
        add_q, add_pair = backward_tile(
            query_pair, log_total, delta, moving_pair, anchor * token_rows, length
        )
        return (grad_q + add_q, grad_pair + add_pair)

    def return_key_grads(grad_pair):
        return passed_along(grad_pair.astype(jnp.bfloat16), "seq", 1).astype(grad_pair.dtype)

    def key_hop(hop_index, loop_state):
        grad_q, moving_pair, grad_pair = loop_state
        grad_q, grad_pair = visit_keys(hop_index, grad_q, moving_pair, grad_pair)
        moved = passed_along(moving_pair, "seq", 1)
        return (grad_q, moved, return_key_grads(grad_pair))

    grad_q, moving_pair, grad_pair = lax.fori_loop(
        0, seq_count - 1, key_hop, (zero_rows, key_pair, zero_pair)
    )
    grad_q, grad_pair = visit_keys(seq_count - 1, grad_q, moving_pair, grad_pair)
    grad_pair = return_key_grads(grad_pair)
    grad_projected = jnp.concatenate(
        [grad_q, grad_pair.reshape(token_rows, 2 * model_width)], axis=1
    ).astype(jnp.bfloat16)
    g_w_qkv = jnp.einsum("td,te->de", inputs_b, grad_projected, preferred_element_type=f32)
    grad_proj_f = grad_projected.astype(f32)
    g_q_bias = jnp.sum(grad_proj_f[:, :model_width], axis=0)
    g_v_bias = jnp.sum(grad_proj_f[:, 2 * model_width :], axis=0)
    grad_input = grad_h1 + jnp.einsum(
        "te,de->td", grad_projected, full_qkv, preferred_element_type=f32
    )
    local_grads = (
        g_w_qkv,
        g_q_bias,
        g_v_bias,
        g_w_out,
        g_out_bias,
        g_ln1_gain,
        g_ln1_bias,
        g_w_in,
        g_in_bias,
        g_w_back,
        g_back_bias,
        g_ln2_gain,
        g_ln2_bias,
    )
    owned = [
        lax.psum_scatter(a.astype(jnp.bfloat16), "fsdp", scatter_dimension=0, tiled=True).astype(jnp.float32)
        for a in local_grads
    ]
    totals = [lax.psum(a.astype(jnp.bfloat16), "seq").astype(jnp.float32) for a in owned]
    return (output[None], grad_input.astype(jnp.bfloat16)[None]) + tuple(totals)


def solution(mesh):
    spread, vector, matrix = P("fsdp", "seq", None), P("fsdp"), P("fsdp", None)
    fits = mesh.shape["seq"] == 2 * CHIPS and mesh.shape["fsdp"] == PLANES
    return jax.shard_map(
        planned if fits else on_device,
        mesh=mesh,
        in_specs=(spread, vector, matrix, vector, vector, matrix) + (vector,) * 3
        + (matrix, vector, matrix) + (vector,) * 3 + (spread,),
        out_specs=(spread, spread, matrix, vector, vector, matrix) + (vector,) * 3
        + (matrix, vector, matrix) + (vector,) * 3,
        check_vma=False,
    )
```

```python
import functools
import math

import jax
import jax.numpy as jnp
from jax import lax
from jax.experimental import pallas as pl
from jax.experimental.pallas import tpu as pltpu
from jax.sharding import PartitionSpec as P

HEADS = 12
bf16 = jnp.bfloat16
f32 = jnp.float32
MESH = pl.DeviceIdType.MESH
LOG2E = math.log2(math.e)
NT = (((1,), (1,)), ((), ()))
NN = (((1,), (0,)), ((), ()))

PLANES = 4
CHIPS = 4
GROUP_HEADS = 3
PACKED = (12, 24, 13, 25, 0, 1, 2, None, 14, 26)
KV_TILE = (0, 1, 4)
PACK = 640


(
    K_ACC, K_ATT0, K_ATT1, K_ATT_O, K_B1, K_B2, K_B3X, K_B3Y, K_BACK, K_BACK_O, K_BM, K_DO, K_DO_O, K_DP,
    K_DP_O, K_F, K_F1, K_F2, K_F3X, K_F3Y, K_FINB_O, K_FIN_O, K_FM, K_G, K_GW_O, K_H, K_HW_O, K_IN, K_K, K_KV,
    K_K_O, K_M, K_O, K_OUT, K_O_O, K_Q, K_QKV, K_Q_O, K_R1, K_RAW, K_RZ, K_RZB, K_S0, K_S1, K_S2, K_SMALL,
    K_SMALL_O, K_SUMS, K_SUMS_O, K_SZ, K_T1A, K_T1B, K_T2A, K_T2B, K_T3A, K_T3B, K_TOK, K_TOK_O, K_V, K_V_O,
    K_WQ, K_WQM, K_WQ_O, K_X1, K_X2, K_Y1, K_Y2, K_Z,
    K_GH1, K_RES, K_GR, K_DO1,
) = range(100, 172)


def dot(a, b, dims=NN):
    return lax.dot_general(a, b, dims, preferred_element_type=f32)


class Net:
    def __init__(self, send_sems, recv_sems):
        self.send_sems, self.recv_sems = send_sems, recv_sems
        self.specs = {}

    def add(self, name, src, dst, device):
        self.specs[name] = (len(self.specs), src, dst, device)

    def get(self, name):
        k, src, dst, device = self.specs[name]
        return pltpu.make_async_remote_copy(
            src_ref=src(),
            dst_ref=dst(),
            send_sem=self.send_sems.at[k],
            recv_sem=self.recv_sems.at[k],
            device_id=device,
            device_id_type=MESH,
        )

    def start(self, *names):
        for name in names:
            self.get(name).start()

    def recv(self, *names):
        for name in names:
            self.get(name).wait_recv()

    def sent(self, *names):
        for name in names:
            self.get(name).wait_send()


class Local:
    def __init__(self, sems):
        self.sems = sems
        self.specs = {}

    def add(self, name, src, dst):
        self.specs[name] = (len(self.specs), src, dst)

    def get(self, name):
        k, src, dst = self.specs[name]
        return pltpu.make_async_copy(src(), dst(), self.sems.at[k])

    def start(self, *names):
        for name in names:
            self.get(name).start()

    def wait(self, *names):
        for name in names:
            self.get(name).wait()


class Line:
    def __init__(self, s, z, send_sems, recv_sems):
        high = lax.div(z, 2)
        self.s, self.z = s, z
        self.order = [z, 1 - z + 4 * high, 2 - high, 3 - 3 * high]
        self.has_right, self.has_left = z < PLANES - 1, z > 0
        self.right, self.left = jnp.minimum(z + 1, PLANES - 1), jnp.maximum(z - 1, 0)
        self.middle = jnp.logical_and(self.has_right, self.has_left)
        self.end = jnp.logical_not(self.middle)
        self.send_sems, self.recv_sems = send_sems, recv_sems
        self.specs = {}

    def add(self, name, own, place):
        self.specs[name] = (len(self.specs), own, place)

    def copy(self, name, i, to_right=False):
        n, own, place = self.specs[name]
        zz = self.order[i]
        if i:
            target = jnp.where(zz < self.z, self.right, self.left)
        else:
            target = self.right if to_right else self.left
        return pltpu.make_async_remote_copy(
            src_ref=place(zz) if i else own(),
            dst_ref=place(zz),
            send_sem=self.send_sems.at[n * 5 + (i + 1 if i else int(to_right))],
            recv_sem=self.recv_sems.at[n * PLANES + zz],
            device_id=(self.s, target),
            device_id_type=MESH,
        )

    def start(self, *names):
        for name in names:
            pl.when(self.has_right)(lambda: self.copy(name, 0, True).start())
            pl.when(self.has_left)(lambda: self.copy(name, 0).start())

    def pass_on(self, name, i):
        self.copy(name, i).wait_recv()
        self.copy(name, i).start()

    def step(self, n, *names):
        for name in names:
            if n == 1:
                @pl.when(self.middle)
                def _():
                    self.pass_on(name, 1)
                    self.pass_on(name, 2)

                pl.when(self.end)(lambda: self.copy(name, 1).wait_recv())
            elif n == 2:
                pl.when(self.middle)(lambda: self.pass_on(name, 3))
                pl.when(self.end)(lambda: self.copy(name, 2).wait_recv())
            else:
                pl.when(self.end)(lambda: self.copy(name, 3).wait_recv())

    def sent(self):
        for name in self.specs:
            pl.when(self.has_right)(lambda: self.copy(name, 0, True).wait_send())
            pl.when(self.has_left)(lambda: self.copy(name, 0).wait_send())

            @pl.when(self.middle)
            def _():
                for i in (1, 2, 3):
                    self.copy(name, i).wait_send()


def coordinates():
    s, z = lax.axis_index("seq"), lax.axis_index("fsdp")
    core = lax.rem(s, 2)
    chip = lax.div(s, 2)
    return s, z, core, chip


def flip(value, mask):
    low, high = lax.rem(value, 2), lax.div(value, 2)
    if mask & 1:
        low = 1 - low
    if mask & 2:
        high = 1 - high
    return high * 2 + low


def hello(devices):
    barrier = pltpu.get_barrier_semaphore()
    for device in devices:
        pl.semaphore_signal(barrier, inc=1, device_id=device, device_id_type=MESH)


def met(count):
    pl.semaphore_wait(pltpu.get_barrier_semaphore(), count)


def greet(devices):
    hello(devices)
    met(len(devices))


def lanes_of(rows=1):
    return lax.broadcasted_iota(jnp.int32, (rows, 128), 1)


def split3(column):
    hi = column.astype(bf16).astype(f32)
    mid = (column - hi).astype(bf16).astype(f32)
    return hi, mid, column - hi - mid


def forward_kernel(
    length_ref, tok_ref, wraw_ref, win_ref, wback_ref, wout_ref,
    ob_ref, g1_ref, n1_ref, bb_ref, g2_ref, n2_ref, ib_ref, qb_ref, vb_ref,
    q_out, k_out, v_out, o_out, tok_out, att_out, small_out, win_full, wout_full, wq_out, wback_full,
    tok, wqv, q_s, k_s, v_s, o_s, att, atts, kvs, kvr, small, wraw, wq_ref, vec_s, vec_v, send_sems, recv_sems, line_send, line_recv, local_sems,
):
    s, z, core, chip = coordinates()
    other = 1 - core
    rows = tok_ref.shape[0]
    half = rows // 2
    shard = wq_ref.shape[1]
    piece = shard // 2
    peer = [None] + [(flip(chip, j) * 2 + core, z) for j in (1, 2, 3)]
    mate = (chip * 2 + other, z)
    plane = [None] + [(s, flip(z, dz)) for dz in (1, 2, 3)]
    zs = [z] + [flip(z, dz) for dz in (1, 2, 3)]
    net, loc = Net(send_sems, recv_sems), Local(local_sems)
    width = win_full.shape[1] // 8
    back = wback_ref.shape[0]
    bpiece = back // 8
    hops = [(K_IN, 1), (K_IN, 2), (K_IN, 3), (K_BACK, 1)]
    at = lambda start, size, unit=16: pl.ds(pl.multiple_of(start, unit), size)

    def part(a, zz, m, c):
        if a == K_IN:
            return win_full.at[at(zz * shard, shard), at((m * 4 + c) * width, width, 128)]
        if a == K_BACK:
            return wback_full.at[at(zz * back + (m * 4 + c) * bpiece, bpiece), :]
        return wout_full.at[at(zz * shard + c * (shard // 4), shard // 4), at(m * width, width, 128)]

    def own_part(a, m, c):
        if a == K_IN:
            return win_ref.at[:, at((m * 4 + c) * width, width, 128)]
        if a == K_BACK:
            return wback_ref.at[at((m * 4 + c) * bpiece, bpiece), :]
        return wout_ref.at[at(c * (shard // 4), shard // 4), at(m * width, width, 128)]

    def side(a, zz, m):
        if a == K_IN:
            return win_full.at[at(zz * shard, shard), at(m * 4 * width, 4 * width, 128)]
        if a == K_BACK:
            return wback_full.at[at(zz * back + m * 4 * bpiece, 4 * bpiece), :]
        return wout_full.at[at(zz * shard, shard), at(m * width, width, 128)]

    line = Line(s, z, line_send, line_recv)
    lines = line.order
    line.add(K_BACK, lambda: own_part(K_BACK, core, chip), lambda zz: part(K_BACK, zz, core, chip))
    line.add(K_OUT, lambda: wout_ref.at[:, at(core * width, width, 128)], lambda zz: side(K_OUT, zz, core))

    for dz in (1, 2, 3):
        net.add((K_WQ, dz), lambda: wq_ref.at[chip, pl.ds(pl.multiple_of(core * piece, 16), piece), :],
                lambda: wqv.at[pl.ds(pl.multiple_of(z * shard + core * piece, 16), piece), :], plane[dz])
        net.add((K_WQM, dz), lambda dz=dz: wqv.at[pl.ds(pl.multiple_of(zs[dz] * shard + core * piece, 16), piece), :],
                lambda dz=dz: wqv.at[pl.ds(pl.multiple_of(zs[dz] * shard + core * piece, 16), piece), :], mate)
        net.add((K_SMALL, dz), lambda: small.at[z], lambda: small.at[z], plane[dz])
    top, bottom = slice(0, half), slice(half, rows)
    net.add(K_T1A, lambda: tok_ref.at[top], lambda: tok.at[1, top], peer[1])
    net.add(K_T1B, lambda: tok_ref.at[bottom], lambda: tok.at[1, bottom], peer[1])
    net.add(K_T2B, lambda: tok_ref.at[bottom], lambda: tok.at[2, bottom], peer[2])
    net.add(K_T2A, lambda: tok_ref.at[top], lambda: tok.at[2, top], peer[2])
    net.add(K_T3A, lambda: tok.at[1, top], lambda: tok.at[3, top], peer[2])
    net.add(K_T3B, lambda: tok.at[2, bottom], lambda: tok.at[3, bottom], peer[1])
    for j in range(4):
        net.add((K_KV, j), lambda j=j: kvs.at[j], lambda j=j: kvr.at[j], mate)
    for j in (1, 2, 3):
        net.add((K_ATT0, j), lambda j=j: atts.at[j, :, 0:128], lambda: att.at[chip, :, 0:128], peer[j])
        net.add((K_ATT1, j), lambda j=j: atts.at[j, :, 128:256], lambda: att.at[chip, :, 128:256], peer[j])
    where = {K_IN: zs, K_BACK: lines, K_OUT: lines}
    for a, dz in hops:
        place = lambda c, a=a, dz=dz: part(a, where[a][dz], core, c)

        def half_place(c, n, a=a, dz=dz):
            zz = where[a][dz]
            if a == K_IN:
                return win_full.at[at(zz * shard + n * piece, piece), at((core * 4 + c) * width, width, 128)]
            return wback_full.at[at(zz * back + (core * 4 + c) * bpiece + n * (bpiece // 2), bpiece // 2), :]

        for j in (1, 2):
            net.add((a, j, dz), lambda place=place: place(chip), lambda place=place: place(chip), peer[j])
        for n, via, last in ((0, 1, 2), (1, 2, 1)):
            there = lambda half_place=half_place, n=n, via=via: half_place(flip(chip, via), n)
            net.add((a, 3 + n, dz), there, there, peer[last])
    for dz in (1, 2, 3):
        net.add((K_IN, K_Z, dz), lambda: own_part(K_IN, core, chip), lambda: part(K_IN, z, core, chip), plane[dz])
    mates = hops + [(K_OUT, dz) for dz in (1, 2, 3)]
    for a, dz in mates:
        net.add((a, K_M, dz), lambda a=a, dz=dz: side(a, where[a][dz], core), lambda a=a, dz=dz: side(a, where[a][dz], core), mate)
    loc.add(K_RAW, lambda: wraw_ref, lambda: wraw)
    loc.add(K_TOK, lambda: tok_ref, lambda: tok.at[0])
    loc.add(K_WQ, lambda: wq_ref.at[chip], lambda: wqv.at[pl.ds(pl.multiple_of(z * shard, 16), shard), :])
    outs = ((K_WQ_O, wq_ref, wq_out), (K_K_O, k_s, k_out), (K_V_O, v_s, v_out), (K_Q_O, q_s, q_out), (K_O_O, o_s, o_out),
            (K_TOK_O, tok, tok_out), (K_ATT_O, att, att_out), (K_SMALL_O, small, small_out))
    for name, src, dst in outs:
        loc.add(name, lambda src=src: src, lambda dst=dst: dst)

    loc.start(K_RAW, K_TOK)
    greet(peer[1:] + [mate] + plane[1:])
    net.start(K_T1A, K_T2B, K_T1B, K_T2A)
    lane = lanes_of()
    loc.wait(K_RAW)
    for g in range(CHIPS):
        for t in range(PACK // 128):
            halves = []
            for upper in (0, 1):
                block = PACKED[2 * t + upper]
                if block is None:
                    halves.append(0.0)
                    continue
                block += GROUP_HEADS * g
                tile_of = lambda i: wraw[:, i * 128 : (i + 1) * 128].astype(f32)
                halves.append(half_tile(tile_of, block, upper))
            wq_ref[g, :, t * 128 : (t + 1) * 128] = jnp.where(lane < 64, halves[0], halves[1]).astype(bf16)
    loc.start(K_WQ, K_WQ_O)
    net.start(*[(K_WQ, dz) for dz in (1, 2, 3)])
    vec_s[...] = jnp.zeros_like(vec_s)
    vec_v[...] = jnp.zeros_like(vec_v)
    for i, ref in enumerate((ob_ref, g1_ref, n1_ref, bb_ref, g2_ref, n2_ref)):
        vec_s[i : i + 1, 0:shard] = ref[...].astype(f32).reshape(1, shard)
    vec_s[6:7, :] = ib_ref[...].astype(f32).reshape(1, ib_ref.shape[0])
    vec_s[7:8, 256 : 256 + shard] = qb_ref[...].astype(f32).reshape(1, shard)
    vec_v[0:1, 0:shard] = vb_ref[...].astype(f32).reshape(1, shard)
    first, last = vec_v[:, 0:128], vec_v[:, 128:256]
    for t, tile in ((0, pltpu.roll(first, 64, 1)), (1, first), (4, pltpu.roll(last, 64, 1))):
        vec_s[7:8, t * 128 : (t + 1) * 128] = jnp.where(lane < 64, 0.0, tile[0:1])
    small[z] = jnp.concatenate([vec_s[...], jnp.zeros_like(vec_s)], axis=0).astype(bf16)
    net.start(*[(K_SMALL, dz) for dz in (1, 2, 3)])
    for dz in (1, 2, 3):
        net.recv((K_WQ, dz))
        net.start((K_WQM, dz))
    net.start(*[(K_IN, K_Z, dz) for dz in (1, 2, 3)])
    loc.wait(K_TOK, K_WQ)
    for dz in (1, 2, 3):
        net.recv((K_SMALL, dz), (K_WQM, dz))

    length = length_ref[0]
    bias = small[chip, 7:8, 0:PACK].astype(f32)

    def keep(tile, h, slot, block):
        position = block * rows + lax.broadcasted_iota(jnp.int32, (rows, 1), 0)
        mask = jnp.where(position < length, 0.0, -1e30).astype(f32)
        ones = jnp.where((lane > 64) & (lane < 68), 1.0, 0.0)
        k_s[h, slot * rows : (slot + 1) * rows, :] = jnp.where(
            lane < 64, tile, jnp.where(lane == 64, mask, ones)
        ).astype(bf16)
        v_s[h, slot * rows : (slot + 1) * rows, :] = jnp.where(
            lane < 64, pltpu.roll(tile, 64, 1), jnp.where(lane < 67, 1.0, 0.0)
        ).astype(bf16)

    def project(j):
        proj = dot(tok[j], wqv[...]) + bias
        for h in range(GROUP_HEADS):
            tile = proj[:, KV_TILE[h] * 128 : (KV_TILE[h] + 1) * 128]
            keep(tile.astype(bf16).astype(f32), h, j, flip(chip, j) * 2 + core)
            kvs[j, :, h * 128 : (h + 1) * 128] = tile.astype(bf16)
            first = 256 + (h // 2) * 128
            tile = proj[:, first : first + 128].astype(bf16).astype(f32) * 0.125
            if h == 1:
                tile = pltpu.roll(tile, 64, 1)
            q_s[h, j * rows : (j + 1) * rows, :] = jnp.where(
                lane < 64, tile, jnp.where(lane == 64, 1.0, 0.0)
            ).astype(bf16)
        net.start((K_KV, j))

    def keep_other(j):
        net.recv((K_KV, j))
        for h in range(GROUP_HEADS):
            tile = kvr[j, :, h * 128 : (h + 1) * 128].astype(f32)
            keep(tile, h, 4 + j, flip(chip, j) * 2 + other)

    def first_hop(a, dz):
        net.start((a, 1, dz), (a, 2, dz))

    def second_hop(a, dz):
        net.recv((a, 1, dz))
        net.start((a, 3, dz))
        net.recv((a, 2, dz))
        net.start((a, 4, dz))

    def third_hop(a, dz):
        net.recv((a, 3, dz), (a, 4, dz))
        net.start((a, K_M, dz))

    project(0)
    net.recv(K_T1A)
    net.start(K_T3A)
    net.recv(K_T2B)
    net.start(K_T3B)
    net.recv(K_T1B)
    project(1)
    net.recv(K_T2A)
    project(2)
    keep_other(0)
    keep_other(1)
    keep_other(2)
    net.recv((K_IN, K_Z, 1))
    first_hop(K_IN, 1)
    line.start(K_BACK, K_OUT)
    net.recv(K_T3A, K_T3B)
    project(3)
    keep_other(3)
    loc.start(K_K_O, K_V_O, K_TOK_O, K_SMALL_O)

    query_tile, key_chunk = 2 * rows, 4 * rows
    tiles = 4 * rows // query_tile
    chunks = 8 * rows // key_chunk

    def attended_tile(which):
        for j in range(4):
            r = slice(j * rows, (j + 1) * rows)
            if which == 0:
                upper = pltpu.roll(o_s[1, r, :].astype(f32), 64, 1)
                value = jnp.where(lane < 64, o_s[0, r, :].astype(f32), upper)
            else:
                value = jnp.where(lane < 64, o_s[2, r, :].astype(f32), 0.0)
            place = slice(which * 128, (which + 1) * 128)
            if j == 0:
                att[chip, :, place] = value.astype(bf16)
            else:
                atts[j, :, place] = value.astype(bf16)
                net.start(((K_ATT0, K_ATT1)[which], j))

    def in_hop(dz):
        net.recv((K_IN, K_Z, dz))
        first_hop(K_IN, dz)

    stages = {
        0: lambda: (in_hop(2), in_hop(3)),
        1: lambda: line.step(1, K_BACK, K_OUT),
        2: lambda: (second_hop(K_IN, 1), first_hop(K_BACK, 1)),
        4: lambda: (second_hop(K_IN, 2), third_hop(K_IN, 1)),
        5: lambda: line.step(2, K_BACK, K_OUT),
        6: lambda: (second_hop(K_IN, 3), third_hop(K_IN, 2)),
        7: lambda: (attended_tile(0), second_hop(K_BACK, 1)),
        8: lambda: third_hop(K_IN, 3),
        9: lambda: (line.step(3, K_BACK, K_OUT), [net.start((K_OUT, K_M, dz)) for dz in (1, 2, 3)]),
        10: lambda: third_hop(K_BACK, 1),
        11: lambda: attended_tile(1),
    }

    def progress(n):
        for at, work in stages.items():
            pl.when(n == at)(lambda work=work: (work(), None)[1])

    def visit(t, carry):
        h, i = lax.div(t, tiles), lax.rem(t, tiles)
        qrows = pl.ds(pl.multiple_of(i * query_tile, query_tile), query_tile)
        q = q_s[h, qrows, :]
        top_score = jnp.full((query_tile, 1), -1e30, f32)
        acc = jnp.zeros((query_tile, 128), f32)
        for c in range(chunks):
            krows = slice(c * key_chunk, (c + 1) * key_chunk)
            scores = dot(q, k_s[h, krows, :], NT)
            new_top = jnp.maximum(top_score, jnp.max(scores, axis=1, keepdims=True))
            probs = jnp.exp2((scores - new_top) * LOG2E)
            fade = jnp.exp2((top_score - new_top) * LOG2E)
            acc = acc * fade + dot(probs.astype(bf16), v_s[h, krows, :])
            top_score = new_top
            if c < chunks - 1:
                progress(t * chunks + c)
        total = acc[:, 64:65]
        o_s[h, qrows, :] = (acc / total).astype(bf16)
        hi, mid, low = split3(-(top_score + jnp.log(total)))
        wide = q.astype(f32)
        wide = jnp.where(lane == 65, hi, jnp.where(lane == 66, mid, jnp.where(lane == 67, low, wide)))
        q_s[h, qrows, :] = wide.astype(bf16)
        progress(t * chunks + chunks - 1)
        return carry

    lax.fori_loop(0, GROUP_HEADS * tiles, visit, 0)
    loc.start(K_Q_O, K_O_O)
    for j in (1, 2, 3):
        net.recv((K_ATT0, j), (K_ATT1, j))
    loc.start(K_ATT_O)
    net.recv(*[(a, K_M, dz) for a, dz in mates])
    for name in net.specs:
        net.sent(name)
    line.sent()
    loc.wait(*[name for name, _, _ in outs])


def backward_kernel(
    do_ref, do1_ref, q_ref, k_ref, v_ref, o_ref, tok_ref, grads_ref, sums_ref, back_ref,
    dproj_out, gw_out, hw_out, fin_out, finb_out, sums_out,
    do_s, do1_s, q_s, k_s, v_s, o_s, doa, tok, tokt, dqs, dq_keep, kv_own, kvs, kvr, dall, fold,
    gw, gwr, gz, gzr, gwf, hw, hwr, hz, hzr, hwf, acc, rb, rx, ry, rx2, ry2, rz, rzb, backv, bx2, by2, fin, finb, sums, sums_r, sums_z, sums_f,
    send_sems, recv_sems, local_sems,
):
    s, z, core, chip = coordinates()
    other = 1 - core
    rows = do_ref.shape[1]
    peer = [None] + [(flip(chip, j) * 2 + core, z) for j in (1, 2, 3)]
    mate = (chip * 2 + other, z)
    plane = [None] + [(s, flip(z, dz)) for dz in (1, 2, 3)]
    zs = [z] + [flip(z, dz) for dz in (1, 2, 3)]
    ch = [chip] + [flip(chip, j) for j in (1, 2, 3)]
    net, loc = Net(send_sems, recv_sems), Local(local_sems)
    length = grads_ref.shape[3]
    cut = length // 32 * 16
    xs, ys = slice(0, cut), slice(cut, length)
    shard = tok.shape[2] // PLANES
    piece = shard // 2

    for h in range(GROUP_HEADS):
        net.add((K_KV, h), lambda h=h: kvs.at[h], lambda h=h: kvr.at[h], mate)
        kv_cols = slice(KV_TILE[h] * 128, KV_TILE[h] * 128 + 128)
        for j in (1, 2, 3):
            net.add((K_DP, h, j), lambda j=j, cols=kv_cols: dall.at[j, :, cols],
                    lambda cols=kv_cols: dproj_out.at[chip, :, cols], peer[j])
    for j in (1, 2, 3):
        net.add((K_DP, K_Q, j), lambda j=j: dall.at[j, :, 256:384], lambda: dproj_out.at[chip, :, 256:384], peer[j])
        net.add((K_DP, K_O, j), lambda j=j: fold.at[j], lambda: dproj_out.at[chip, 0 : rows // 2, 384:512], peer[j])
    loc.add((K_DP, 0), lambda: dall.at[0, :, 0:384], lambda: dproj_out.at[chip, :, 0:384])
    loc.add((K_DP, 1), lambda: dall.at[0, :, 512:640], lambda: dproj_out.at[chip, :, 512:640])
    loc.add((K_DP, 2), lambda: fold.at[0], lambda: dproj_out.at[chip, 0 : rows // 2, 384:512])
    for j in (1, 2, 3):
        net.add((K_DO, j), lambda j=j: do1_ref.at[ch[j]], lambda j=j: do1_s.at[j], peer[j])
    order = (3, 2, 1, 0)
    for dz in order:
        net.add((K_R1, dz), lambda dz=dz: grads_ref.at[other, zs[dz]], lambda dz=dz: rb.at[zs[dz]], mate)
        for n, j in enumerate((1, 3)):
            net.add((K_X1, n, dz), lambda dz=dz, j=j: acc.at[zs[dz], ch[j], xs], lambda dz=dz, n=n: rx.at[zs[dz], n], peer[1])
        net.add((K_X2, dz), lambda dz=dz: acc.at[zs[dz], ch[2], xs], lambda dz=dz: rx2.at[zs[dz]], peer[2])
        for n, j in enumerate((2, 3)):
            net.add((K_Y1, n, dz), lambda dz=dz, j=j: acc.at[zs[dz], ch[j], ys], lambda dz=dz, n=n: ry.at[zs[dz], n], peer[2])
        net.add((K_Y2, dz), lambda dz=dz: acc.at[zs[dz], ch[1], ys], lambda dz=dz: ry2.at[zs[dz]], peer[1])
        if dz:
            net.add((K_RZ, dz), lambda dz=dz: acc.at[zs[dz], chip], lambda dz=dz: rz.at[dz - 1], plane[dz])
    for dz in (1, 2, 3):
        net.add((K_RZB, dz), lambda dz=dz: backv.at[zs[dz]], lambda dz=dz: rzb.at[dz - 1], plane[dz])
    bh = finb.shape[2] // 2
    bx, by = slice(0, bh), slice(bh, 2 * bh)
    net.add((K_X2, K_BACK), lambda: back_ref.at[2, :, bx], lambda: bx2, peer[2])
    net.add((K_Y2, K_BACK), lambda: back_ref.at[1, :, by], lambda: by2, peer[1])
    net.add(K_B1, lambda: finb.at[core, chip], lambda: finb.at[core, chip], peer[1])
    net.add(K_B2, lambda: finb.at[core, chip], lambda: finb.at[core, chip], peer[2])
    net.add(K_B3X, lambda: finb.at[core, ch[1], bx], lambda: finb.at[core, ch[1], bx], peer[2])
    net.add(K_B3Y, lambda: finb.at[core, ch[2], by], lambda: finb.at[core, ch[2], by], peer[1])
    net.add(K_BM, lambda: finb.at[core], lambda: finb.at[core], mate)
    net.add(K_F1, lambda: fin.at[core, chip], lambda: fin.at[core, chip], peer[1])
    net.add(K_F2, lambda: fin.at[core, chip], lambda: fin.at[core, chip], peer[2])
    net.add(K_F3X, lambda: fin.at[core, ch[1], xs], lambda: fin.at[core, ch[1], xs], peer[2])
    net.add(K_F3Y, lambda: fin.at[core, ch[2], ys], lambda: fin.at[core, ch[2], ys], peer[1])
    net.add(K_FM, lambda: fin.at[core], lambda: fin.at[core], mate)
    net.add(K_S0, lambda: sums_ref, lambda: sums_r.at[0], mate)
    net.add(K_S1, lambda: sums.at[1], lambda: sums_r.at[1], peer[1])
    net.add(K_S2, lambda: sums.at[2], lambda: sums_r.at[2], peer[2])
    for dz in (1, 2, 3):
        net.add((K_SZ, dz), lambda dz=dz: sums.at[3, zs[dz]], lambda dz=dz: sums_z.at[dz - 1], plane[dz])
    for a, w, wr, g, gr, f in ((K_G, gw, gwr, gz, gzr, gwf), (K_H, hw, hwr, hz, hzr, hwf)):
        net.add((a, 0), lambda w=w: w.at[other], lambda wr=wr: wr, mate)
        for dz in (1, 2, 3):
            net.add((a, K_Z, dz), lambda g=g, dz=dz: g.at[zs[dz]], lambda gr=gr, dz=dz: gr.at[dz - 1], plane[dz])
        for j in (1, 2, 3):
            net.add((a, K_F, j), lambda f=f: f.at[core, chip], lambda f=f: f.at[core, chip], peer[j])
        net.add((a, K_M), lambda f=f: f.at[core], lambda f=f: f.at[core], mate)

    loads = ((K_DO, lambda: do_ref, lambda: do_s), (K_DO1, lambda: do1_ref.at[chip], lambda: do1_s.at[0]), (K_O, lambda: o_ref, lambda: o_s),
             (K_TOK, lambda: tok_ref, lambda: tok), (K_Q, lambda: q_ref, lambda: q_s),
             (K_K, lambda: k_ref, lambda: k_s), (K_V, lambda: v_ref, lambda: v_s),
             (K_SUMS, lambda: sums_ref, lambda: sums.at[0]), (K_BACK, lambda: back_ref.at[0], lambda: backv), (K_ACC, lambda: grads_ref.at[core], lambda: acc))
    for name, src, dst in loads:
        loc.add(name, src, dst)
    stores = ((K_GW_O, gwf, gw_out), (K_HW_O, hwf, hw_out), (K_FIN_O, fin, fin_out), (K_FINB_O, finb, finb_out))
    for name, src, dst in stores:
        loc.add(name, lambda src=src: src, lambda dst=dst: dst)
    loc.add(K_SUMS_O, lambda: sums_f, lambda: sums_out)

    loc.start(K_DO, K_O, K_Q, K_K, K_V)
    greet(peer[1:] + [mate] + plane[1:])
    net.start((K_X2, K_BACK), (K_Y2, K_BACK), K_S0, *[(K_R1, dz) for dz in order])
    loc.start(K_ACC, K_BACK, K_SUMS, K_TOK, K_DO1)
    lane = lanes_of()
    loc.wait(K_DO, K_O)

    def output_grad(h, tiles):
        for j in range(4):
            tile = tiles[j].astype(f32)
            if h == 1:
                tile = pltpu.roll(tile, 64, 1)
            tile = jnp.where(lane < 64, tile, 0.0)
            r = slice(j * rows, (j + 1) * rows)
            delta = jnp.sum(tile * o_s[h, r, :].astype(f32), axis=1, keepdims=True)
            hi, mid, low = split3(-delta)
            tile = jnp.where(lane == 64, hi, jnp.where(lane == 65, mid, jnp.where(lane == 66, low, tile)))
            doa[h, r, :] = tile.astype(bf16)

    output_grad(0, do_s)
    output_grad(1, do_s)
    loc.wait(K_Q, K_K, K_V)

    def late_loads():
        loc.wait(K_ACC, K_BACK, K_SUMS)
        net.start(*[(K_DO, j) for j in (1, 2, 3)])

    def transpose_tokens():
        loc.wait(K_TOK)
        for j in range(4):
            tokt[:, j * rows : (j + 1) * rows] = tok[j].T

    def last_head_grad():
        loc.wait(K_DO1)
        net.recv(*[(K_DO, j) for j in (1, 2, 3)])
        output_grad(2, do1_s)

    def add_into(ref, index, other_ref, other_index):
        ref[index] = (ref[index].astype(f32) + other_ref[other_index].astype(f32)).astype(bf16)

    def step_one(dz):
        net.recv((K_R1, dz))
        def body(c, carry):
            add_into(acc, (zs[dz], c), rb, (zs[dz], c))
            return carry
        lax.fori_loop(0, CHIPS, body, 0)
        net.start(*[(K_X1, n, dz) for n in (0, 1)], *[(K_Y1, n, dz) for n in (0, 1)])

    def step_two(dz):
        for n in range(2):
            net.recv((K_X1, 1 - n, dz), (K_Y1, 1 - n, dz))
            jx, jy = (2, 1) if n == 0 else (0, 0)
            add_into(acc, (zs[dz], ch[jx], xs), rx, (zs[dz], 1 - n))
            add_into(acc, (zs[dz], ch[jy], ys), ry, (zs[dz], 1 - n))
            if n == 0:
                net.start((K_X2, dz), (K_Y2, dz))

    def step_three(dz):
        net.recv((K_X2, dz), (K_Y2, dz))
        add_into(acc, (zs[dz], chip, xs), rx2, zs[dz])
        add_into(acc, (zs[dz], chip, ys), ry2, zs[dz])
        if dz:
            net.start((K_RZ, dz))

    def sums_step(n):
        net.recv((K_S0, K_S1, K_S2)[n])
        sums[n + 1] = (sums[n].astype(f32) + sums_r[n].astype(f32)).astype(bf16)
        if n < 2:
            net.start((K_S1, K_S2)[n])
        else:
            net.start(*[(K_SZ, dz) for dz in (1, 2, 3)])

    def back_plane():
        net.recv((K_X2, K_BACK), (K_Y2, K_BACK))
        for zz in range(PLANES):
            add_into(backv, (zz, bx), bx2, zz)
            add_into(backv, (zz, by), by2, zz)
        net.start(*[(K_RZB, dz) for dz in (1, 2, 3)])

    def back_total():
        net.recv(*[(K_RZB, dz) for dz in (1, 2, 3)])
        total = backv[z].astype(f32) + rzb[0].astype(f32) + rzb[1].astype(f32) + rzb[2].astype(f32)
        finb[core, chip] = total.astype(bf16)
        net.start(K_B1, K_B2)

    def back_forward():
        net.recv(K_B1)
        net.start(K_B3X)
        net.recv(K_B2)
        net.start(K_B3Y)

    def back_mate():
        net.recv(K_B3X, K_B3Y)
        net.start(K_BM)

    def fin_total():
        for dz in (1, 2, 3):
            net.recv((K_RZ, dz), (K_SZ, dz))
        total = acc[z, chip].astype(f32) + rz[0].astype(f32) + rz[1].astype(f32) + rz[2].astype(f32)
        fin[core, chip] = total.astype(bf16)
        net.start(K_F1, K_F2)
        total = sums[3, z].astype(f32)
        for n in range(3):
            total = total + sums_z[n].astype(f32)
        sums_f[...] = total.astype(bf16)
        loc.start(K_SUMS_O)

    def fin_forward():
        net.recv(K_F1)
        net.start(K_F3X)
        net.recv(K_F2)
        net.start(K_F3Y)

    def weight_part(a, w, first, last):
        cols = dall[:, :, first:last].reshape(4 * rows, last - first)
        column_sums = jnp.sum(cols.astype(f32), axis=0, keepdims=True)
        extra = jnp.where(lax.broadcasted_iota(jnp.int32, (16, 1), 0) == 0, column_sums, 0.0).astype(bf16)
        for zz in range(PLANES):
            part = dot(tokt[zz * shard : (zz + 1) * shard, :], cols)
            for m in range(2):
                w[m, zz, 0:piece, :] = part[m * piece : (m + 1) * piece, :].astype(bf16)
                w[m, zz, piece : piece + 16, :] = extra
        net.start((a, 0))

    def weight_pair(a, w, wr, g):
        net.recv((a, 0))
        for zz in range(PLANES):
            g[zz] = (w[core, zz].astype(f32) + wr[zz].astype(f32)).astype(bf16)
        net.start(*[(a, K_Z, dz) for dz in (1, 2, 3)])

    def weight_total(a, g, gr, f):
        total = g[z].astype(f32)
        for dz in (1, 2, 3):
            net.recv((a, K_Z, dz))
            total = total + gr[dz - 1].astype(f32)
        f[core, chip] = total.astype(bf16)
        net.start(*[(a, K_F, j) for j in (1, 2, 3)])

    def weight_mate(a):
        net.recv(*[(a, K_F, j) for j in (1, 2, 3)])
        net.start((a, K_M))

    key_chunk, query_tile = 2 * rows, 256
    per_head = 4

    def head_keys(h, slots):
        cols = slice(KV_TILE[h] * 128, KV_TILE[h] * 128 + 128)
        for j in slots:
            r = slice(j * rows, (j + 1) * rows)
            both = kv_own[r, :] + kvr[h, r, :].astype(f32)
            dall[j, :, cols] = both.astype(bf16)
            if j:
                net.start((K_DP, h, j))

    def head_queries(h):
        dq = dqs[...].T * 0.125
        for j in range(4):
            r = slice(j * rows, (j + 1) * rows)
            mine = dq[r, :]
            if h == 0:
                dq_keep[r, :] = mine
            elif h == 1:
                dall[j, :, 256:384] = jnp.where(lane < 64, dq_keep[r, :], pltpu.roll(mine, 64, 1)).astype(bf16)
                if j:
                    net.start((K_DP, K_Q, j))
            else:
                upper = pltpu.roll(mine[rows // 2 :, :], 64, 1)
                fold[j] = jnp.where(lane < 64, mine[: rows // 2, :], upper).astype(bf16)
                if j:
                    net.start((K_DP, K_O, j))
                dall[j, :, 384:512] = jnp.where(lane < 64, mine, 0.0).astype(bf16)

    stages = {
        0: lambda: (late_loads(), step_one(3), back_plane(), sums_step(0)),
        1: lambda: (step_one(2), sums_step(1)),
        2: lambda: (step_two(3), step_one(1), sums_step(2)),
        3: lambda: (step_three(3), step_two(2)),
        4: lambda: (step_one(0), back_total()),
        5: lambda: (step_three(2), step_two(1), transpose_tokens()),
        6: lambda: (step_two(0), back_forward(), last_head_grad()),
        7: lambda: (step_three(1), weight_part(K_G, gw, 0, 384)),
        8: lambda: (step_three(0), back_mate()),
        9: lambda: (fin_total(), weight_pair(K_G, gw, gwr, gz)),
        11: lambda: (fin_forward(), weight_total(K_G, gz, gzr, gwf)),
    }

    def visit(t, carry):
        h, part = lax.div(t, per_head), lax.rem(t, per_head)
        start = pl.multiple_of(jnp.where(part < 2, part + 2, 3 - part) * key_chunk, key_chunk)
        krows = pl.ds(start, key_chunk)
        k, v = k_s[h, krows, :], v_s[h, krows, :]
        kt = k.T

        @pl.when(part == 0)
        def _():
            dqs[...] = jnp.zeros_like(dqs)

        dk = jnp.zeros((key_chunk, 128), f32)
        dv = jnp.zeros((key_chunk, 128), f32)
        for i in range(4 * rows // query_tile):
            r = slice(i * query_tile, (i + 1) * query_tile)
            q, do = q_s[h, r, :], doa[h, r, :]
            probs = jnp.exp2(dot(k, q, NT) * LOG2E)
            dscores = (probs * dot(v, do, NT)).astype(bf16)
            dv = dv + dot(probs.astype(bf16), do)
            dk = dk + dot(dscores, q)
            dqs[:, r] += dot(kt, dscores)
        packed = jnp.where(lane < 64, dk, pltpu.roll(dv, 64, 1))

        @pl.when(part < 2)
        def _():
            kvs[h, pl.ds(pl.multiple_of(part * key_chunk, key_chunk), key_chunk), :] = packed.astype(bf16)

        @pl.when(part >= 2)
        def _():
            kv_own[pl.ds(pl.multiple_of((3 - part) * key_chunk, key_chunk), key_chunk), :] = packed

        for hh in range(GROUP_HEADS):
            @pl.when(t == hh * per_head + 1)
            def _(hh=hh):
                net.start((K_KV, hh))

            @pl.when(t == hh * per_head + 2)
            def _(hh=hh):
                net.recv((K_KV, hh))
                head_keys(hh, (2, 3))

            @pl.when(t == hh * per_head + 3)
            def _(hh=hh):
                head_keys(hh, (1, 0))
                head_queries(hh)
        for at, work in stages.items():
            pl.when(t == at)(lambda work=work: (work(), None)[1])
        return carry

    lax.fori_loop(0, GROUP_HEADS * per_head, visit, 0)

    weight_part(K_H, hw, 384, PACK)
    loc.start((K_DP, 0), (K_DP, 1), (K_DP, 2))
    weight_pair(K_H, hw, hwr, hz)
    weight_mate(K_G)
    net.recv(K_F3X, K_F3Y)
    net.start(K_FM)
    weight_total(K_H, hz, hzr, hwf)
    for h in (0, 1, 2, K_Q, K_O):
        for j in (1, 2, 3):
            net.recv((K_DP, h, j))
    net.recv(K_FM, K_BM, (K_G, K_M))
    loc.start(K_GW_O, K_FIN_O, K_FINB_O)
    weight_mate(K_H)
    net.recv((K_H, K_M))
    loc.start(K_HW_O)
    for name in net.specs:
        net.sent(name)
    loc.wait((K_DP, 0), (K_DP, 1), (K_DP, 2), K_GW_O, K_HW_O, K_FIN_O, K_FINB_O, K_SUMS_O)


def gelu_parts(u):
    x = jnp.abs(u) * (0.5 ** 0.5)
    d = 1.0 + 0.3275911 * x
    t = pl.reciprocal(d, approx=True)
    t = t * (2.0 - d * t)
    poly = t * (0.254829592 + t * (-0.284496736 + t * (1.421413741 + t * (-1.453152027 + t * 1.061405429))))
    bell = jnp.exp2(u * u * (-0.5 * LOG2E))
    tail = 0.5 * poly * bell
    phi = jnp.where(u >= 0, 1.0 - tail, tail)
    return u * phi, phi + u * bell * (1.0 / math.sqrt(2.0 * math.pi))


def row_mean(a):
    return jnp.mean(a, axis=1, keepdims=True)


def wide_vectors(small):
    step = small.shape[2] // PLANES
    lane = lax.broadcasted_iota(jnp.int32, (8, small.shape[2]), 1)
    total = 0.0
    for zz in range(PLANES):
        part = jnp.where(lane < step, small[zz].astype(f32)[0:8], 0.0)
        total = total + (pltpu.roll(part, zz * step, 1) if zz else part)
    return total


def ffn_kernel(
    length_ref, att_ref, tok_ref, cot_ref, win_ref, win_own, wout_ref, wout_own, small_ref, wback_ref, wback_own, wq_own,
    res_out, gh1_out, do_out, do1_out, grads_out, sums_ref, wq_full, back_out,
    winv, wbackv, woutv, act_s, gp_s, gi_s, acc, first_s, n1_s, low_s, lowt_s, gsec_s, gh2_s, isum,
    gb, rb, rx, ry, do_ref, do_in, out_ref, gh1_ref, grads_ref, send_sems, recv_sems, line_send, line_recv, local_sems,
):
    s, z, core, chip = coordinates()
    other = 1 - core
    rows, width = tok_ref.shape
    step = width // PLANES
    ch = winv.shape[1] // 8
    wide = 2 * ch
    back = wback_own.shape[0]
    shard = win_own.shape[0]
    piece = shard // 2
    peer = [None] + [(flip(chip, j) * 2 + core, z) for j in (1, 2, 3)]
    mate = (chip * 2 + other, z)
    plane = [(s, flip(z, dz)) for dz in (1, 2, 3)]
    ch_of = [chip] + [flip(chip, j) for j in (1, 2, 3)]
    net, loc = Net(send_sems, recv_sems), Local(local_sems)

    bpiece = back // 8
    line = Line(s, z, line_send, line_recv)
    lines = line.order
    line.add(K_QKV, lambda: wq_own.at[pl.ds(core * 2, 2)], lambda zz: wq_full.at[zz, pl.ds(core * 2, 2)])
    for dz in (1, 2, 3):
        net.add((K_QKV, dz), lambda dz=dz: wq_full.at[lines[dz], pl.ds(core * 2, 2)], lambda dz=dz: wq_full.at[lines[dz], pl.ds(core * 2, 2)], mate)

    def region(ref, zz, c):
        return ref.at[pl.ds(pl.multiple_of(zz * back + (core * 4 + c) * bpiece, 16), bpiece), :]

    def side(zz):
        return wbackv.at[pl.ds(pl.multiple_of(zz * back + core * 4 * bpiece, 16), 4 * bpiece), :]

    for dz in (2, 3):
        for j in (1, 2):
            net.add((j, dz), lambda dz=dz: region(wback_ref, lines[dz], chip), lambda dz=dz: region(wbackv, lines[dz], chip), peer[j])
        via, last = ((1, 2), (2, 1))[dz - 2]
        net.add((3, dz), lambda dz=dz, via=via: region(wbackv, lines[dz], ch_of[via]), lambda dz=dz, via=via: region(wbackv, lines[dz], ch_of[via]), peer[last])
        net.add((K_M, dz), lambda dz=dz: side(lines[dz]), lambda dz=dz: side(lines[dz]), mate)
        loc.add((K_M, dz), lambda dz=dz: region(wback_ref, lines[dz], chip), lambda dz=dz: region(wbackv, lines[dz], chip))
    half = gb.shape[3] // 2
    xs, ys = slice(0, half), slice(half, 2 * half)
    for zz in range(PLANES):
        net.add((K_R1, zz), lambda zz=zz: gb.at[other, zz], lambda zz=zz: rb.at[zz], mate)
        for n, j in enumerate((1, 3)):
            net.add((K_X1, n, zz), lambda zz=zz, j=j: gb.at[core, zz, ch_of[j], xs], lambda zz=zz, n=n: rx.at[zz, n], peer[1])
        for n, j in enumerate((2, 3)):
            net.add((K_Y1, n, zz), lambda zz=zz, j=j: gb.at[core, zz, ch_of[j], ys], lambda zz=zz, n=n: ry.at[zz, n], peer[2])
    for j in (1, 2, 3):
        net.add((K_DO, j), lambda j=j: do_ref.at[0, ch_of[j]], lambda j=j: do_in.at[j], peer[j])
    loc.add(K_DO_O, lambda: do_in, lambda: do_out)
    loc.add(K_DO1, lambda: do_ref.at[1], lambda: do1_out)
    loc.add(K_GH1, lambda: gh1_ref, lambda: gh1_out)
    loc.add(K_RES, lambda: out_ref, lambda: res_out)
    for n in range(PLANES):
        cut_of = lambda ref, n=n: ref.at[n // 2, :, pl.ds(n % 2 * 2, 2)]
        loc.add((K_GR, n), lambda cut_of=cut_of: cut_of(grads_ref), lambda cut_of=cut_of: cut_of(grads_out))
    for j in range(3):
        loc.add((K_BACK_O, j), lambda j=j: gb.at[core, :, ch_of[j]], lambda j=j: back_out.at[j])
    shards = {K_OUT: (wout_own, wout_ref, woutv), K_IN: (win_own, win_ref, winv), K_BACK: (wback_own, wback_ref, wbackv)}
    loads = [(name, i) for name in shards for i in range(4) if name != K_BACK or i < 2]
    for name, i in loads:
        own, full, dst = shards[name]
        n = own.shape[0]
        place = lambda i=i, n=n: pl.ds(pl.multiple_of(lines[i] * n, 16), n)
        loc.add((name, i), lambda own=own, full=full, i=i, place=place: full.at[place(), :] if i else own,
                lambda dst=dst, place=place: dst.at[place(), :])
    loc.start(*loads, (K_M, 2), (K_M, 3))
    greet(peer[1:] + [mate] + plane)
    net.start((1, 2), (2, 2), (1, 3), (2, 3))
    line.start(K_QKV)

    def hop_two(dz):
        net.recv((1, dz), (2, dz))
        net.start((3, dz))

    def hop_three(dz):
        net.recv((3, dz))
        loc.wait((K_M, dz))
        net.start((K_M, dz))

    def add_into(ref, index, other_ref, other_index):
        ref[index] = (ref[index].astype(f32) + other_ref[other_index].astype(f32)).astype(bf16)

    def step_one(zz):
        net.recv((K_R1, zz))
        for c in range(CHIPS):
            add_into(gb, (core, zz, c), rb, (zz, c))
        net.start(*[(K_X1, n, zz) for n in (0, 1)], *[(K_Y1, n, zz) for n in (0, 1)])

    def step_two(zz):
        net.recv((K_X1, 1, zz), (K_Y1, 1, zz))
        add_into(gb, (core, zz, ch_of[2], xs), rx, (zz, 1))
        add_into(gb, (core, zz, ch_of[1], ys), ry, (zz, 1))
        net.recv((K_X1, 0, zz), (K_Y1, 0, zz))
        add_into(gb, (core, zz, chip, xs), rx, (zz, 0))
        add_into(gb, (core, zz, chip, ys), ry, (zz, 0))

    def during(n, works):
        for at, work in works.items():
            pl.when(n == at)(lambda work=work: (work(), None)[1])

    vectors = wide_vectors(small_ref)
    vec = lambda i: vectors[i : i + 1, :]
    loc.wait(*[(K_OUT, dz) for dz in range(4)])
    branch = vec(0)
    for g in range(4):
        branch = branch + dot(att_ref[g, :, 0:step], woutv[g * step : (g + 1) * step, :])
    hidden = tok_ref[...].astype(f32) + branch
    centred = hidden - row_mean(hidden)
    inverse1 = lax.rsqrt(row_mean(centred * centred) + 1e-5)
    normed = centred * inverse1
    n1_s[...] = normed
    first = normed * vec(1) + vec(2)
    first_s[...] = first
    low_s[...] = first.astype(bf16)
    lowt_s[...] = first.astype(bf16).T
    loc.wait(*[(K_IN, i) for i in range(4)])

    def forward(n, carry):
        cols = pl.ds(pl.multiple_of(n * wide, 128), wide)
        inner = dot(low_s[...], winv[:, cols]) + small_ref[n, 6:7, :].astype(f32)
        value, slope = gelu_parts(inner)
        value = value.astype(bf16)
        act_s[n] = value
        gp_s[n] = slope
        during(n, {2: lambda: hop_two(2), 3: lambda: hop_two(3)})
        return carry

    lax.fori_loop(0, PLANES, forward, 0)

    def second_layer(i):
        zz = lines[i]
        return dot(act_s[zz], wbackv[pl.ds(pl.multiple_of(zz * back, 16), back), :])

    loc.wait((K_BACK, 0), (K_BACK, 1))
    acc[...] = second_layer(0)
    acc[...] += second_layer(1)
    hop_three(2)
    hop_three(3)
    line.step(1, K_QKV)
    net.recv((K_M, 2))
    acc[...] += second_layer(2)
    net.recv((K_M, 3))
    acc[...] += second_layer(3)
    position = s * rows + lax.broadcasted_iota(jnp.int32, (rows, 1), 0)
    valid = (position < length_ref[0]).astype(f32)
    hidden = first_s[...] + acc[...] + vec(3)
    centred = hidden - row_mean(hidden)
    inverse = lax.rsqrt(row_mean(centred * centred) + 1e-5)
    normed = centred * inverse
    out_ref[...] = ((normed * vec(4) + vec(5)) * valid).astype(bf16)
    loc.start(K_RES)
    grad = cot_ref[...].astype(f32) * valid
    sum_rows = lambda a: jnp.sum(a, axis=0, keepdims=True)
    g2_gain, g2_bias = sum_rows(grad * normed), sum_rows(grad)
    scaled = grad * vec(4)
    gh2 = inverse * (scaled - row_mean(scaled) - normed * row_mean(scaled * normed))
    gh2_s[...] = gh2
    second = gh2.astype(bf16)
    gsec_s[...] = second
    back_sum = sum_rows(second.astype(f32))
    acc[...] = jnp.zeros_like(acc)

    def back_weights(n, carry):
        gback = dot(act_s[n].T, gsec_s[...]).astype(bf16)
        part = wide // 8
        for m in range(2):
            for k in range(4):
                for x in range(2):
                    gb[m, n, k, x * part : (x + 1) * part, :] = gback[
                        (m * 4 + k) * part : (m * 4 + k + 1) * part, x * ch : (x + 1) * ch
                    ]
        during(n, {
            0: lambda: net.start((K_R1, 0)), 1: lambda: net.start((K_R1, 1)),
            2: lambda: net.start((K_R1, 2)), 3: lambda: net.start((K_R1, 3)),
        })
        return carry

    lax.fori_loop(0, PLANES, back_weights, 0)

    def backward(n, carry):
        cols = pl.ds(pl.multiple_of(n * wide, 128), wide)
        grad_inner = (dot(gsec_s[...], wbackv[cols, :], NT) * gp_s[n]).astype(bf16)
        gi_s[n] = grad_inner
        isum[n] = jnp.broadcast_to(sum_rows(grad_inner.astype(f32)), (8, wide))
        acc[...] += dot(grad_inner, winv[:, cols], NT)
        during(n, {
            0: lambda: step_one(0), 1: lambda: step_one(1),
            2: lambda: (step_one(2), step_two(0)), 3: lambda: step_one(3),
        })
        return carry

    lax.fori_loop(0, PLANES, backward, 0)
    grad = gh2_s[...] + acc[...]
    normed = n1_s[...]
    g1_gain, g1_bias = sum_rows(grad * normed), sum_rows(grad)
    scaled = grad * vec(1)
    gh1 = inverse1 * (scaled - row_mean(scaled) - normed * row_mean(scaled * normed))
    gh1_ref[...] = gh1
    loc.start(K_GH1)
    gbranch = gh1.astype(bf16)
    out_sum = sum_rows(gbranch.astype(f32))
    for g in range(4):
        w = woutv[g * step : (g + 1) * step, :]
        part = dot(gbranch, w, NT).astype(bf16)
        do_ref[0, g] = part[:, 0:128]
        do_ref[1, g, :, 0 : step - 128] = part[:, 128:step]
        do_ref[1, g, :, step - 128 :] = jnp.zeros((rows, 256 - step), bf16)
    net.start(*[(K_DO, j) for j in (1, 2, 3)])
    line.step(2, K_QKV)
    net.start((K_QKV, 1), (K_QKV, 2))
    do_in[0] = do_ref[0, chip]
    loc.start(K_DO1)
    for g in range(4):
        gw = dot(att_ref[g, :, 0:step].T, gbranch).astype(bf16)
        part = step // 4
        for c in range(4):
            for m in range(2):
                grads_ref[m, g, c, step:, :] = gw[c * part : (c + 1) * part, m * ch : (m + 1) * ch]

    def weights(n, carry):
        for zz in range(PLANES):
            gin = dot(lowt_s[zz * step : (zz + 1) * step, :], gi_s[n]).astype(bf16)
            for x in range(2):
                grads_ref[lax.div(n, 2), zz, lax.rem(n, 2) * 2 + x, 0:step, :] = gin[:, x * ch : (x + 1) * ch]
        during(n, {
            0: lambda: (loc.start((K_GR, 0)), step_two(1)), 1: lambda: (loc.start((K_GR, 1)), step_two(2)),
            2: lambda: (loc.start((K_GR, 2)), step_two(3)), 3: lambda: loc.start((K_GR, 3)),
        })
        return carry

    lax.fori_loop(0, PLANES, weights, 0)
    lane = lax.broadcasted_iota(jnp.int32, (8, width), 1)
    place = lax.broadcasted_iota(jnp.int32, (8, width), 0)
    total = jnp.zeros((8, width), f32)
    for i, v in enumerate((out_sum, g1_gain, g1_bias, back_sum, g2_gain, g2_bias)):
        total = jnp.where(place == i, v, total)
    for zz in range(PLANES):
        part = total if zz == 0 else pltpu.roll(total, width - zz * step, 1)
        part = jnp.where(lane < step, part, 0.0)
        part = jnp.where(place == 6, isum[zz], part)
        sums_ref[zz, 0:16, :] = jnp.concatenate([part, jnp.zeros((8, width), f32)], axis=0).astype(bf16)
    net.recv(*[(K_DO, j) for j in (1, 2, 3)])
    loc.start(*[(K_BACK_O, j) for j in range(3)], K_DO_O)
    line.step(3, K_QKV)
    net.start((K_QKV, 3))
    net.recv(*[(K_QKV, dz) for dz in (1, 2, 3)])
    for name in net.specs:
        net.sent(name)
    line.sent()
    loc.wait(*[(K_BACK_O, j) for j in range(3)], K_DO_O, K_DO1, K_GH1, K_RES, *[(K_GR, n) for n in range(PLANES)])


Q_PLACE, K_PLACE, V_PLACE = (4, 5, 6), (0, 2, 8), (1, 3, 9)


def half_tile(tile_of, block, upper):
    tile = tile_of(block // 2)
    return tile if block % 2 == upper else pltpu.roll(tile, 64, 1)


def final_kernel(
    dproj_ref, wq_ref, wq_own, gh1_ref, gw_ref, hw_ref, fin_ref, finb_ref, sums_ref,
    gt_ref, gqkv_ref, gin_ref, gback_ref, gout_ref, qb_ref, vb_ref, o0, o1, o2, o3, o4, o5, ib_ref,
    wv, row, last, local_sems,
):
    z = lax.axis_index("fsdp")
    loc = Local(local_sems)
    rows = gh1_ref.shape[0]
    shard = wq_ref.shape[2]
    for dz in range(PLANES):
        zz = flip(z, dz)
        loc.add(dz, lambda zz=zz, dz=dz: wq_own if dz == 0 else wq_ref.at[zz],
                lambda zz=zz: wv.at[:, pl.ds(pl.multiple_of(zz * shard, 16), shard), :])
    loc.start(*range(PLANES))
    lane = lanes_of()
    up = lambda a: a.astype(f32)
    ch = fin_ref.shape[3]
    for m in range(2):
        for c in range(4):
            n = m * 4 + c
            gin_ref[:, n * ch : (n + 1) * ch] = up(fin_ref[m, c, 0:shard, :])
            part = ch // 4
            for x in range(2):
                gback_ref[n * part : (n + 1) * part, x * ch : (x + 1) * ch] = up(
                    finb_ref[m, c, x * part : (x + 1) * part, :]
                )
            gout_ref[c * (shard // 4) : (c + 1) * (shard // 4), m * ch : (m + 1) * ch] = up(fin_ref[m, c, shard:, :])
    piece = shard // 2

    def packed_tile(m, g, r, t):
        if t < 3:
            return up(gw_ref[m, g, r, t * 128 : (t + 1) * 128])
        return up(hw_ref[m, g, r, (t - 3) * 128 : (t - 2) * 128])

    for m in range(2):
        r = slice(m * piece, (m + 1) * piece)
        for kind, places in enumerate((Q_PLACE, K_PLACE, V_PLACE)):
            for i in range(HEADS // 2):
                halves = []
                for upper in (0, 1):
                    g, h = divmod(2 * i + upper, GROUP_HEADS)
                    tile_of = lambda t, g=g: packed_tile(m, g, slice(0, piece), t)
                    halves.append(half_tile(tile_of, places[h], upper))
                at = kind * HEADS * 64 + i * 128
                gqkv_ref[r, at : at + 128] = jnp.where(lane < 64, halves[0], halves[1])
    tile_of = lambda t: packed_tile(0, z, slice(piece, piece + 16), t)
    for ref, places in ((qb_ref, Q_PLACE), (vb_ref, V_PLACE)):
        first = jnp.where(lane < 64, half_tile(tile_of, places[0], 0), half_tile(tile_of, places[1], 1))
        row[0:1, 0:128] = first[0:1]
        row[0:1, 128:256] = half_tile(tile_of, places[2], 0)[0:1]
        ref[...] = row[0:1, 0:shard].reshape(shard)
    for i, ref in enumerate((o0, o1, o2, o3, o4, o5)):
        ref[...] = up(sums_ref[...])[i : i + 1, 0:shard].reshape(shard)
    ib_ref[...] = up(sums_ref[...])[6:7, :].reshape(ib_ref.shape[0])
    loc.wait(*range(PLANES))
    total = gh1_ref[...]
    for g in range(4):
        total = total + dot(dproj_ref[g, :, 0:384], wv[g, :, 0:384], NT)
        folded = up(dproj_ref[g, 0 : rows // 2, 384:512])
        last[0 : rows // 2, 0:128] = jnp.where(lane < 64, folded, 0.0).astype(bf16)
        last[rows // 2 :, 0:128] = jnp.where(lane < 64, pltpu.roll(folded, 64, 1), 0.0).astype(bf16)
        last[:, 128:256] = dproj_ref[g, :, 512:640]
        total = total + dot(last[...], wv[g, :, 384:640], NT)
    gt_ref[...] = total.astype(bf16)


def vmem(shape, dtype=bf16):
    return pltpu.VMEM(shape, dtype)


ANY = pl.BlockSpec(memory_space=pl.ANY)
SMEM = pl.BlockSpec(memory_space=pltpu.SMEM)
VMEM = pl.BlockSpec(memory_space=pltpu.VMEM)
VMEM_BYTES = 60 * 2**20
SEMS = 112


def semaphores(line=False):
    counts = (SEMS, SEMS) + ((5 * 2, PLANES * 2) if line else ()) + (32,)
    return [pltpu.SemaphoreType.DMA((n,)) for n in counts]


def params(collective_id):
    return pltpu.CompilerParams(
        collective_id=collective_id, has_side_effects=True, vmem_limit_bytes=VMEM_BYTES
    )


def run_forward(lengths, tokens, w_qkv, w_in, w_back, w_out, *vectors):
    rows, width = tokens.shape
    shard = w_qkv.shape[0]
    hidden = w_in.shape[1]
    S = jax.ShapeDtypeStruct
    q_shape, kv_shape = (GROUP_HEADS, 4 * rows, 128), (GROUP_HEADS, 8 * rows, 128)
    return pl.pallas_call(
        forward_kernel,
        out_shape=(
            S(q_shape, bf16), S(kv_shape, bf16), S(kv_shape, bf16), S(q_shape, bf16),
            S((4, rows, width), bf16), S((4, rows, 256), bf16), S((PLANES, 16, width), bf16),
            S((PLANES * shard, hidden), bf16), S((width, width), bf16),
            S((CHIPS, shard, PACK), bf16), S((hidden, width), bf16),
        ),
        in_specs=[SMEM] + [ANY] * 5 + [VMEM] * 9,
        out_specs=[ANY] * 11,
        scratch_shapes=[
            vmem((4, rows, width)), vmem((width, PACK)), vmem(q_shape), vmem(kv_shape), vmem(kv_shape), vmem(q_shape),
            vmem((4, rows, 256)), vmem((4, rows, 256)), vmem((4, rows, 384)), vmem((4, rows, 384)),
            vmem((PLANES, 16, width)), vmem((shard, w_qkv.shape[1])), vmem((CHIPS, shard, PACK)),
            vmem((8, width), f32), vmem((8, 256), f32),
        ] + semaphores(line=True),
        compiler_params=params(1),
    )(lengths, tokens, w_qkv, w_in, w_back, w_out, *vectors)


def run_backward(do, do1, q, k, v, o, tok, grads, sums, back):
    rows = do.shape[1]
    width = tok.shape[2]
    shard = width // PLANES
    length, cols = grads.shape[3:]
    cut = length // 32 * 16
    S = jax.ShapeDtypeStruct
    ext = shard // 2 + 16
    return pl.pallas_call(
        backward_kernel,
        out_shape=(
            S((4, rows, PACK), bf16), S((2, 4, ext, 384), bf16), S((2, 4, ext, 256), bf16), S((2, 4, length, cols), bf16), S((2, 4) + back.shape[2:], bf16), S((16, width), bf16),
        ),
        in_specs=[ANY] * 10,
        out_specs=[ANY] * 6,
        scratch_shapes=[
            vmem((4, rows, 128)), vmem((4, rows, 128)), vmem(q.shape), vmem(k.shape), vmem(v.shape), vmem(o.shape), vmem(q.shape),
            vmem(tok.shape), vmem((width, 4 * rows)), vmem((128, 4 * rows), f32), vmem((4 * rows, 128), f32),
            vmem((4 * rows, 128), f32), vmem((3, 4 * rows, 128)), vmem((3, 4 * rows, 128)),
            vmem((4, rows, PACK)), vmem((4, rows // 2, 128)),
            *[vmem(lead + (ext, n)) for n in (384, 256) for lead in ((2, 4), (4,), (4,), (3,), (2, 4))],
            vmem((4, 4, length, cols)), vmem((4, 4, length, cols)),
            vmem((4, 2, cut, cols)), vmem((4, 2, length - cut, cols)), vmem((4, cut, cols)), vmem((4, length - cut, cols)),
            vmem((3, length, cols)), vmem((3,) + back.shape[2:]), vmem(back.shape[1:]),
            vmem((4, back.shape[2] // 2, cols)), vmem((4, back.shape[2] // 2, cols)), vmem((2, 4, length, cols)), vmem((2, 4) + back.shape[2:]),
            vmem((4, 4, 16, width)), vmem((3, 4, 16, width)), vmem((3, 16, width)), vmem((16, width)),
        ] + semaphores(),
        compiler_params=params(2),
    )(do, do1, q, k, v, o, tok, grads, sums, back)


def run_ffn(lengths, att, tokens, cotangent, full_in, w_in, full_out, w_out, small, full_back, w_back, wq):
    rows, width = tokens.shape
    hidden = w_in.shape[1]
    ch = hidden // 8
    S = jax.ShapeDtypeStruct
    one = S((rows, width), bf16)
    bp = w_back.shape[0] // 8
    return pl.pallas_call(
        ffn_kernel,
        out_shape=(
            one, S((rows, width), f32), S((4, rows, 128), bf16), S((4, rows, 128), bf16), S((2, 4, 4, width // 4 + 48, ch), bf16), S((4, 16, width), bf16),
            S((PLANES,) + wq.shape, bf16), S((3, 4, 2 * bp, ch), bf16),
        ),
        in_specs=[SMEM] + [VMEM] * 3 + [ANY] * 4 + [VMEM] + [ANY] * 3,
        out_specs=[ANY] * 5 + [VMEM] + [ANY] * 2,
        scratch_shapes=[
            vmem((width, hidden)), vmem((hidden, width)), vmem((width, width)),
            vmem((4, rows, 2 * ch)), vmem((4, rows, 2 * ch), f32), vmem((4, rows, 2 * ch)),
            vmem((rows, width), f32), vmem((rows, width), f32), vmem((rows, width), f32),
            vmem((rows, width)), vmem((width, rows)), vmem((rows, width)), vmem((rows, width), f32), vmem((4, 8, 2 * ch), f32),
            vmem((2, 4, 4, 2 * bp, ch)), vmem((4, 4, 2 * bp, ch)), vmem((4, 2, bp, ch)), vmem((4, 2, bp, ch)),
            vmem((2, 4, rows, 128)), vmem((4, rows, 128)),
            vmem((rows, width)), vmem((rows, width), f32), vmem((2, 4, 4, width // 4 + 48, ch)),
            pltpu.SemaphoreType.DMA((SEMS,)), pltpu.SemaphoreType.DMA((SEMS,)),
            pltpu.SemaphoreType.DMA((5,)), pltpu.SemaphoreType.DMA((PLANES,)), pltpu.SemaphoreType.DMA((32,)),
        ],
        compiler_params=params(3),
    )(lengths, att, tokens, cotangent, full_in, w_in, full_out, w_out, small, full_back, w_back, wq)


def run_final(dproj, wq_full, wq, gh1, gw, hw, fin, finb, sums):
    rows, width = gh1.shape
    shard = width // PLANES
    S = jax.ShapeDtypeStruct
    one = S((shard,), f32)
    return pl.pallas_call(
        final_kernel,
        out_shape=(
            S((rows, width), bf16), S((shard, 3 * width), f32), S((shard, 8 * fin.shape[3]), f32),
            S((2 * fin.shape[3], width), f32), S((shard, width), f32), one, one, one, one, one, one, one, one, S((width,), f32),
        ),
        in_specs=[VMEM, ANY, ANY] + [VMEM] * 6,
        out_specs=[VMEM] * 14,
        scratch_shapes=[vmem((4, width, PACK)), vmem((8, 256), f32), vmem((rows, 256)), pltpu.SemaphoreType.DMA((4,))],
        compiler_params=pltpu.CompilerParams(vmem_limit_bytes=VMEM_BYTES),
    )(dproj, wq_full, wq, gh1, gw, hw, fin, finb, sums)


def planned(
    tokens, lengths, w_qkv, q_bias, v_bias, w_out, out_bias, ln1_gain, ln1_bias,
    w_in, in_bias, w_back, back_bias, ln2_gain, ln2_bias, cotangent,
):
    vectors = (out_bias, ln1_gain, ln1_bias, back_bias, ln2_gain, ln2_bias, in_bias, q_bias, v_bias)
    q, k, v, o, tok_all, att, small_all, full_in, full_out, wq, full_back = run_forward(
        lengths, tokens[0], w_qkv, w_in, w_back, w_out, *vectors
    )
    output, gh1, do, do1, grads, sums, wq_full, back = run_ffn(
        lengths, att, tokens[0], cotangent[0], full_in, w_in, full_out, w_out, small_all, full_back, w_back, wq
    )
    dproj, gw, hw, fin, finb, sums_f = run_backward(do, do1, q, k, v, o, tok_all, grads, sums, back)
    gt, gqkv, gin, gback, gout, qb, vb, ob, g1, b1, bb, g2, b2, ib = run_final(dproj, wq_full, wq, gh1, gw, hw, fin, finb, sums_f)
    return (output[None], gt[None], gqkv, qb, vb, gout, ob, g1, b1, gin, ib, gback, bb, g2, b2)


masked_score = -1e30


def passed_along(block, axis, distance):
    devices = range(lax.axis_size(axis))
    route = [((i - distance) % len(devices), i) for i in devices]
    return lax.ppermute(block, axis, route)


def norm_forward(hidden, gain_vec, shift_vec):
    average = jnp.mean(hidden, axis=-1, keepdims=True)
    centred = hidden - average
    variance = jnp.mean(centred * centred, axis=-1, keepdims=True)
    inverse = lax.rsqrt(variance + 1e-05)
    normed = centred * inverse
    return (normed * gain_vec + shift_vec, normed, inverse)


def norm_backward(grad_norm, normed, inverse, gain_vec):
    scaled = grad_norm * gain_vec
    grad_input = inverse * (
        scaled
        - jnp.mean(scaled, axis=-1, keepdims=True)
        - normed * jnp.mean(scaled * normed, axis=-1, keepdims=True)
    )
    return (grad_input, jnp.sum(grad_norm * normed, axis=0), jnp.sum(grad_norm, axis=0))


def forward_tile(state_in, query_heads, key_pair, length):
    old_max, old_sum, old_acc = state_in
    key_rows = key_pair.shape[0]
    head_count = query_heads.shape[1]
    head_size = query_heads.shape[2]
    key_heads = key_pair[:, 0].reshape(key_rows, head_count, head_size)
    value_heads = key_pair[:, 1].reshape(key_rows, head_count, head_size)
    key_ok = jnp.arange(key_rows, dtype=jnp.int32) < length
    scores = jnp.einsum(
        "qhd,khd->hqk", query_heads, key_heads, preferred_element_type=jnp.float32
    ) * head_size ** (-0.5)
    scores = jnp.where(key_ok[None, None, :], scores, masked_score)
    new_max = jnp.maximum(old_max, jnp.max(scores, axis=2))
    prob_tile = jnp.where(key_ok[None, None, :], jnp.exp(scores - new_max[:, :, None]), 0.0)
    new_sum = jnp.sum(prob_tile, axis=2)
    new_acc = jnp.einsum(
        "hqk,khd->hqd",
        prob_tile.astype(jnp.bfloat16),
        value_heads,
        preferred_element_type=jnp.float32,
    )
    return (new_max, new_sum, new_acc)


def backward_tile(query_pair, log_total, delta, key_pair, key_start, length):
    query_rows = query_pair.shape[0]
    key_rows = key_pair.shape[0]
    model_width = query_pair.shape[2]
    head_count = log_total.shape[0]
    head_size = model_width // head_count
    score_scale = head_size ** (-0.5)
    query_heads = query_pair[:, 0].reshape(query_rows, head_count, head_size)
    grad_heads = query_pair[:, 1].reshape(query_rows, head_count, head_size)
    key_heads = key_pair[:, 0].reshape(key_rows, head_count, head_size)
    value_heads = key_pair[:, 1].reshape(key_rows, head_count, head_size)
    key_ok = key_start + jnp.arange(key_rows, dtype=jnp.int32) < length
    scores = (
        jnp.einsum("qhd,khd->hqk", query_heads, key_heads, preferred_element_type=jnp.float32)
        * score_scale
    )
    prob_tile = jnp.where(key_ok[None, None, :], jnp.exp(scores - log_total[:, :, None]), 0.0)
    grad_values = jnp.einsum(
        "hqk,qhd->khd",
        prob_tile.astype(jnp.bfloat16),
        grad_heads,
        preferred_element_type=jnp.float32,
    )
    grad_probs = jnp.einsum(
        "qhd,khd->hqk", grad_heads, value_heads, preferred_element_type=jnp.float32
    )
    grad_scores = (prob_tile * (grad_probs - delta[:, :, None])).astype(jnp.bfloat16)
    grad_queries = (
        jnp.einsum("hqk,khd->qhd", grad_scores, key_heads, preferred_element_type=jnp.float32)
        * score_scale
    )
    grad_keys = (
        jnp.einsum("hqk,qhd->khd", grad_scores, query_heads, preferred_element_type=jnp.float32)
        * score_scale
    )
    grad_pair = jnp.stack([grad_keys, grad_values], axis=1).reshape(key_rows, 2, model_width)
    return (grad_queries.reshape(query_rows, model_width), grad_pair)


def on_device(
    tokens,
    lengths,
    w_qkv,
    q_bias,
    v_bias,
    w_out,
    out_bias,
    ln1_gain,
    ln1_bias,
    w_in,
    in_bias,
    w_back,
    back_bias,
    ln2_gain,
    ln2_bias,
    cotangent,
):
    gathered = tuple(
        lax.all_gather(a, "fsdp", axis=0, tiled=True)
        for a in (
            w_qkv, q_bias, v_bias, w_out, out_bias, ln1_gain, ln1_bias, w_in, in_bias, w_back, back_bias, ln2_gain, ln2_bias
        )
    )
    (
        full_qkv,
        full_qbias,
        full_vbias,
        full_out,
        full_obias,
        full_g1,
        full_n1,
        full_in,
        full_ibias,
        full_back,
        full_bbias,
        full_g2,
        full_n2,
    ) = gathered
    f32 = jnp.float32
    seq_index = lax.axis_index("seq")
    seq_count = lax.axis_size("seq")
    token_rows = tokens.shape[1]
    model_width = tokens.shape[2]
    head_count = HEADS
    head_size = model_width // head_count
    length = lengths[0]
    my_start = seq_index * token_rows
    row_valid = (my_start + jnp.arange(token_rows, dtype=jnp.int32) < length).astype(f32)
    inputs_b = tokens[0]
    inputs_f = inputs_b.astype(f32)
    bias_all = jnp.concatenate(
        [full_qbias.astype(f32), jnp.zeros((model_width,), f32), full_vbias.astype(f32)]
    )
    projected = (jnp.dot(inputs_b, full_qkv, preferred_element_type=f32) + bias_all).astype(
        jnp.bfloat16
    )
    query_heads = projected[:, :model_width].reshape(token_rows, head_count, head_size)
    key_pair = projected[:, model_width:].reshape(token_rows, 2, model_width)
    init_state = (
        jnp.full((head_count, token_rows), masked_score, f32),
        jnp.zeros((head_count, token_rows), f32),
        jnp.zeros((head_count, token_rows, head_size), f32),
    )
    pieces = lax.all_gather(key_pair, "seq", axis=0, tiled=True)
    run_max, run_sum, run_acc = forward_tile(init_state, query_heads, pieces, length)
    positive = run_sum > 0.0
    safe_sum = jnp.where(positive, run_sum, 1.0)
    attended_heads = jnp.where(positive[:, :, None], run_acc / safe_sum[:, :, None], 0.0)
    log_total = jnp.where(positive, run_max + jnp.log(safe_sum), 0.0)
    attended_f = attended_heads.transpose(1, 0, 2).reshape(token_rows, model_width)
    attended_b = attended_f.astype(jnp.bfloat16)
    branch_f = jnp.dot(attended_b, full_out, preferred_element_type=f32) + full_obias.astype(f32)
    first_norm, normed_one, inverse_one = norm_forward(
        inputs_f + branch_f, full_g1.astype(f32), full_n1.astype(f32)
    )
    first_low = first_norm.astype(jnp.bfloat16)
    inner_act = jnp.dot(first_low, full_in, preferred_element_type=f32) + full_ibias.astype(f32)
    activated_b = jax.nn.gelu(inner_act, approximate=False).astype(jnp.bfloat16)
    second = jnp.dot(activated_b, full_back, preferred_element_type=f32) + full_bbias.astype(f32)
    result, normed_two, inverse_two = norm_forward(
        first_norm + second, full_g2.astype(f32), full_n2.astype(f32)
    )
    output = (result * row_valid[:, None]).astype(jnp.bfloat16)
    grad_result = cotangent[0].astype(f32) * row_valid[:, None]
    grad_h2, g_ln2_gain, g_ln2_bias = norm_backward(
        grad_result, normed_two, inverse_two, full_g2.astype(f32)
    )
    grad_second = grad_h2.astype(jnp.bfloat16)
    g_w_back = jnp.einsum("tf,td->fd", activated_b, grad_second, preferred_element_type=f32)
    g_back_bias = jnp.sum(grad_second.astype(f32), axis=0)
    grad_act = jnp.einsum("td,fd->tf", grad_second, full_back, preferred_element_type=f32)
    gelu_value, gelu_pull = jax.vjp(
        lambda values_in: jax.nn.gelu(values_in, approximate=False), inner_act
    )
    grad_inner = gelu_pull(grad_act)[0].astype(jnp.bfloat16)
    g_w_in = jnp.einsum("td,tf->df", first_low, grad_inner, preferred_element_type=f32)
    g_in_bias = jnp.sum(grad_inner.astype(f32), axis=0)
    grad_first = grad_h2 + jnp.einsum("tf,df->td", grad_inner, full_in, preferred_element_type=f32)
    grad_h1, g_ln1_gain, g_ln1_bias = norm_backward(
        grad_first, normed_one, inverse_one, full_g1.astype(f32)
    )
    grad_branch = grad_h1.astype(jnp.bfloat16)
    g_w_out = jnp.einsum("tc,td->cd", attended_b, grad_branch, preferred_element_type=f32)
    g_out_bias = jnp.sum(grad_branch.astype(f32), axis=0)
    grad_attended = jnp.einsum(
        "td,cd->tc", grad_branch, full_out, preferred_element_type=f32
    ).astype(jnp.bfloat16)
    delta = jnp.sum(
        (grad_attended.astype(f32) * attended_f).reshape(token_rows, head_count, head_size), axis=2
    ).T
    query_pair = jnp.stack([projected[:, :model_width], grad_attended], axis=1)
    zero_rows = jnp.zeros((token_rows, model_width), f32)
    zero_pair = jnp.zeros((token_rows, 2, model_width), f32)

    def visit_keys(hop_index, grad_q, moving_pair, grad_pair):
        anchor = (seq_index - hop_index) % seq_count
        add_q, add_pair = backward_tile(
            query_pair, log_total, delta, moving_pair, anchor * token_rows, length
        )
        return (grad_q + add_q, grad_pair + add_pair)

    def return_key_grads(grad_pair):
        return passed_along(grad_pair.astype(jnp.bfloat16), "seq", 1).astype(grad_pair.dtype)

    def key_hop(hop_index, loop_state):
        grad_q, moving_pair, grad_pair = loop_state
        grad_q, grad_pair = visit_keys(hop_index, grad_q, moving_pair, grad_pair)
        moved = passed_along(moving_pair, "seq", 1)
        return (grad_q, moved, return_key_grads(grad_pair))

    grad_q, moving_pair, grad_pair = lax.fori_loop(
        0, seq_count - 1, key_hop, (zero_rows, key_pair, zero_pair)
    )
    grad_q, grad_pair = visit_keys(seq_count - 1, grad_q, moving_pair, grad_pair)
    grad_pair = return_key_grads(grad_pair)
    grad_projected = jnp.concatenate(
        [grad_q, grad_pair.reshape(token_rows, 2 * model_width)], axis=1
    ).astype(jnp.bfloat16)
    g_w_qkv = jnp.einsum("td,te->de", inputs_b, grad_projected, preferred_element_type=f32)
    grad_proj_f = grad_projected.astype(f32)
    g_q_bias = jnp.sum(grad_proj_f[:, :model_width], axis=0)
    g_v_bias = jnp.sum(grad_proj_f[:, 2 * model_width :], axis=0)
    grad_input = grad_h1 + jnp.einsum(
        "te,de->td", grad_projected, full_qkv, preferred_element_type=f32
    )
    local_grads = (
        g_w_qkv,
        g_q_bias,
        g_v_bias,
        g_w_out,
        g_out_bias,
        g_ln1_gain,
        g_ln1_bias,
        g_w_in,
        g_in_bias,
        g_w_back,
        g_back_bias,
        g_ln2_gain,
        g_ln2_bias,
    )
    owned = [
        lax.psum_scatter(a.astype(jnp.bfloat16), "fsdp", scatter_dimension=0, tiled=True).astype(jnp.float32)
        for a in local_grads
    ]
    totals = [lax.psum(a.astype(jnp.bfloat16), "seq").astype(jnp.float32) for a in owned]
    return (output[None], grad_input.astype(jnp.bfloat16)[None]) + tuple(totals)


def solution(mesh):
    spread, vector, matrix = P("fsdp", "seq", None), P("fsdp"), P("fsdp", None)
    fits = mesh.shape["seq"] == 2 * CHIPS and mesh.shape["fsdp"] == PLANES
    return jax.shard_map(
        planned if fits else on_device,
        mesh=mesh,
        in_specs=(spread, vector, matrix, vector, vector, matrix) + (vector,) * 3
        + (matrix, vector, matrix) + (vector,) * 3 + (spread,),
        out_specs=(spread, spread, matrix, vector, vector, matrix) + (vector,) * 3
        + (matrix, vector, matrix) + (vector,) * 3,
        check_vma=False,
    )
```

```python
import functools
import math

import jax
import jax.numpy as jnp
from jax import lax
from jax.experimental import pallas as pl
from jax.experimental.pallas import tpu as pltpu
from jax.sharding import PartitionSpec as P

HEADS = 12
bf16 = jnp.bfloat16
f32 = jnp.float32
MESH = pl.DeviceIdType.MESH
LOG2E = math.log2(math.e)
NT = (((1,), (1,)), ((), ()))
NN = (((1,), (0,)), ((), ()))

PLANES = 4
CHIPS = 4
GROUP_HEADS = 3
PACKED = (12, 24, 13, 25, 0, 1, 2, None, 14, 26)
KV_TILE = (0, 1, 4)
PACK = 640


(
    K_ACC, K_ATT0, K_ATT1, K_ATT_O, K_B1, K_B2, K_B3X, K_B3Y, K_BACK, K_BACK_O, K_BM, K_DO, K_DO_O, K_DP,
    K_DP_O, K_F, K_F1, K_F2, K_F3X, K_F3Y, K_FINB_O, K_FIN_O, K_FM, K_G, K_GW_O, K_H, K_HW_O, K_IN, K_K, K_KV,
    K_K_O, K_M, K_O, K_OUT, K_O_O, K_Q, K_QKV, K_Q_O, K_R1, K_RAW, K_RZ, K_RZB, K_S0, K_S1, K_S2, K_SMALL,
    K_SMALL_O, K_SUMS, K_SUMS_O, K_SZ, K_T1A, K_T1B, K_T2A, K_T2B, K_T3A, K_T3B, K_TOK, K_TOK_O, K_V, K_V_O,
    K_WQ, K_WQM, K_WQ_O, K_X1, K_X2, K_Y1, K_Y2, K_Z,
    K_GH1, K_RES, K_GR, K_DO1,
) = range(100, 172)


def dot(a, b, dims=NN):
    return lax.dot_general(a, b, dims, preferred_element_type=f32)


class Net:
    def __init__(self, send_sems, recv_sems):
        self.send_sems, self.recv_sems = send_sems, recv_sems
        self.specs = {}

    def add(self, name, src, dst, device):
        self.specs[name] = (len(self.specs), src, dst, device)

    def get(self, name):
        k, src, dst, device = self.specs[name]
        return pltpu.make_async_remote_copy(
            src_ref=src(),
            dst_ref=dst(),
            send_sem=self.send_sems.at[k],
            recv_sem=self.recv_sems.at[k],
            device_id=device,
            device_id_type=MESH,
        )

    def start(self, *names):
        for name in names:
            self.get(name).start()

    def recv(self, *names):
        for name in names:
            self.get(name).wait_recv()

    def sent(self, *names):
        for name in names:
            self.get(name).wait_send()


class Local:
    def __init__(self, sems):
        self.sems = sems
        self.specs = {}

    def add(self, name, src, dst):
        self.specs[name] = (len(self.specs), src, dst)

    def get(self, name):
        k, src, dst = self.specs[name]
        return pltpu.make_async_copy(src(), dst(), self.sems.at[k])

    def start(self, *names):
        for name in names:
            self.get(name).start()

    def wait(self, *names):
        for name in names:
            self.get(name).wait()


class Line:
    def __init__(self, s, z, send_sems, recv_sems):
        high = lax.div(z, 2)
        self.s, self.z = s, z
        self.order = [z, 1 - z + 4 * high, 2 - high, 3 - 3 * high]
        self.has_right, self.has_left = z < PLANES - 1, z > 0
        self.right, self.left = jnp.minimum(z + 1, PLANES - 1), jnp.maximum(z - 1, 0)
        self.middle = jnp.logical_and(self.has_right, self.has_left)
        self.end = jnp.logical_not(self.middle)
        self.send_sems, self.recv_sems = send_sems, recv_sems
        self.specs = {}

    def add(self, name, own, place):
        self.specs[name] = (len(self.specs), own, place)

    def copy(self, name, i, to_right=False):
        n, own, place = self.specs[name]
        zz = self.order[i]
        if i:
            target = jnp.where(zz < self.z, self.right, self.left)
        else:
            target = self.right if to_right else self.left
        return pltpu.make_async_remote_copy(
            src_ref=place(zz) if i else own(),
            dst_ref=place(zz),
            send_sem=self.send_sems.at[n * 5 + (i + 1 if i else int(to_right))],
            recv_sem=self.recv_sems.at[n * PLANES + zz],
            device_id=(self.s, target),
            device_id_type=MESH,
        )

    def start(self, *names):
        for name in names:
            pl.when(self.has_right)(lambda: self.copy(name, 0, True).start())
            pl.when(self.has_left)(lambda: self.copy(name, 0).start())

    def pass_on(self, name, i):
        self.copy(name, i).wait_recv()
        self.copy(name, i).start()

    def step(self, n, *names):
        for name in names:
            if n == 1:
                @pl.when(self.middle)
                def _():
                    self.pass_on(name, 1)
                    self.pass_on(name, 2)

                pl.when(self.end)(lambda: self.copy(name, 1).wait_recv())
            elif n == 2:
                pl.when(self.middle)(lambda: self.pass_on(name, 3))
                pl.when(self.end)(lambda: self.copy(name, 2).wait_recv())
            else:
                pl.when(self.end)(lambda: self.copy(name, 3).wait_recv())

    def sent(self):
        for name in self.specs:
            pl.when(self.has_right)(lambda: self.copy(name, 0, True).wait_send())
            pl.when(self.has_left)(lambda: self.copy(name, 0).wait_send())

            @pl.when(self.middle)
            def _():
                for i in (1, 2, 3):
                    self.copy(name, i).wait_send()


def coordinates():
    s, z = lax.axis_index("seq"), lax.axis_index("fsdp")
    core = lax.rem(s, 2)
    chip = lax.div(s, 2)
    return s, z, core, chip


def flip(value, mask):
    low, high = lax.rem(value, 2), lax.div(value, 2)
    if mask & 1:
        low = 1 - low
    if mask & 2:
        high = 1 - high
    return high * 2 + low


def hello(devices):
    barrier = pltpu.get_barrier_semaphore()
    for device in devices:
        pl.semaphore_signal(barrier, inc=1, device_id=device, device_id_type=MESH)


def met(count):
    pl.semaphore_wait(pltpu.get_barrier_semaphore(), count)


def greet(devices):
    hello(devices)
    met(len(devices))


def lanes_of(rows=1):
    return lax.broadcasted_iota(jnp.int32, (rows, 128), 1)


def split3(column):
    hi = column.astype(bf16).astype(f32)
    mid = (column - hi).astype(bf16).astype(f32)
    return hi, mid, column - hi - mid


def forward_kernel(
    length_ref, tok_ref, wraw_ref, win_ref, wback_ref, wout_ref,
    ob_ref, g1_ref, n1_ref, bb_ref, g2_ref, n2_ref, ib_ref, qb_ref, vb_ref,
    q_out, k_out, v_out, o_out, tok_out, att_out, small_out, win_full, wout_full, wq_out, wback_full,
    tok, wqv, q_s, k_s, v_s, o_s, att, atts, kvs, kvr, small, wraw, wq_ref, vec_s, vec_v, send_sems, recv_sems, line_send, line_recv, local_sems,
):
    s, z, core, chip = coordinates()
    other = 1 - core
    rows = tok_ref.shape[0]
    half = rows // 2
    shard = wq_ref.shape[1]
    piece = shard // 2
    peer = [None] + [(flip(chip, j) * 2 + core, z) for j in (1, 2, 3)]
    mate = (chip * 2 + other, z)
    plane = [None] + [(s, flip(z, dz)) for dz in (1, 2, 3)]
    zs = [z] + [flip(z, dz) for dz in (1, 2, 3)]
    net, loc = Net(send_sems, recv_sems), Local(local_sems)
    width = win_full.shape[1] // 8
    back = wback_ref.shape[0]
    bpiece = back // 8
    hops = [(K_IN, 1), (K_IN, 2), (K_IN, 3), (K_BACK, 1)]
    at = lambda start, size, unit=16: pl.ds(pl.multiple_of(start, unit), size)

    def part(a, zz, m, c):
        if a == K_IN:
            return win_full.at[at(zz * shard, shard), at((m * 4 + c) * width, width, 128)]
        if a == K_BACK:
            return wback_full.at[at(zz * back + (m * 4 + c) * bpiece, bpiece), :]
        return wout_full.at[at(zz * shard + c * (shard // 4), shard // 4), at(m * width, width, 128)]

    def own_part(a, m, c):
        if a == K_IN:
            return win_ref.at[:, at((m * 4 + c) * width, width, 128)]
        if a == K_BACK:
            return wback_ref.at[at((m * 4 + c) * bpiece, bpiece), :]
        return wout_ref.at[at(c * (shard // 4), shard // 4), at(m * width, width, 128)]

    def side(a, zz, m):
        if a == K_IN:
            return win_full.at[at(zz * shard, shard), at(m * 4 * width, 4 * width, 128)]
        if a == K_BACK:
            return wback_full.at[at(zz * back + m * 4 * bpiece, 4 * bpiece), :]
        return wout_full.at[at(zz * shard, shard), at(m * width, width, 128)]

    line = Line(s, z, line_send, line_recv)
    lines = line.order
    line.add(K_BACK, lambda: own_part(K_BACK, core, chip), lambda zz: part(K_BACK, zz, core, chip))
    line.add(K_OUT, lambda: wout_ref.at[:, at(core * width, width, 128)], lambda zz: side(K_OUT, zz, core))

    for dz in (1, 2, 3):
        net.add((K_WQ, dz), lambda: wq_ref.at[chip, pl.ds(pl.multiple_of(core * piece, 16), piece), :],
                lambda: wqv.at[pl.ds(pl.multiple_of(z * shard + core * piece, 16), piece), :], plane[dz])
        net.add((K_WQM, dz), lambda dz=dz: wqv.at[pl.ds(pl.multiple_of(zs[dz] * shard + core * piece, 16), piece), :],
                lambda dz=dz: wqv.at[pl.ds(pl.multiple_of(zs[dz] * shard + core * piece, 16), piece), :], mate)
        net.add((K_SMALL, dz), lambda: small.at[z], lambda: small.at[z], plane[dz])
    top, bottom = slice(0, half), slice(half, rows)
    net.add(K_T1A, lambda: tok_ref.at[top], lambda: tok.at[1, top], peer[1])
    net.add(K_T1B, lambda: tok_ref.at[bottom], lambda: tok.at[1, bottom], peer[1])
    net.add(K_T2B, lambda: tok_ref.at[bottom], lambda: tok.at[2, bottom], peer[2])
    net.add(K_T2A, lambda: tok_ref.at[top], lambda: tok.at[2, top], peer[2])
    net.add(K_T3A, lambda: tok.at[1, top], lambda: tok.at[3, top], peer[2])
    net.add(K_T3B, lambda: tok.at[2, bottom], lambda: tok.at[3, bottom], peer[1])
    for j in range(4):
        net.add((K_KV, j), lambda j=j: kvs.at[j], lambda j=j: kvr.at[j], mate)
    for j in (1, 2, 3):
        net.add((K_ATT0, j), lambda j=j: atts.at[j, :, 0:128], lambda: att.at[chip, :, 0:128], peer[j])
        net.add((K_ATT1, j), lambda j=j: atts.at[j, :, 128:256], lambda: att.at[chip, :, 128:256], peer[j])
    where = {K_IN: zs, K_BACK: lines, K_OUT: lines}
    for a, dz in hops:
        place = lambda c, a=a, dz=dz: part(a, where[a][dz], core, c)

        def half_place(c, n, a=a, dz=dz):
            zz = where[a][dz]
            if a == K_IN:
                return win_full.at[at(zz * shard + n * piece, piece), at((core * 4 + c) * width, width, 128)]
            return wback_full.at[at(zz * back + (core * 4 + c) * bpiece + n * (bpiece // 2), bpiece // 2), :]

        for j in (1, 2):
            net.add((a, j, dz), lambda place=place: place(chip), lambda place=place: place(chip), peer[j])
        for n, via, last in ((0, 1, 2), (1, 2, 1)):
            there = lambda half_place=half_place, n=n, via=via: half_place(flip(chip, via), n)
            net.add((a, 3 + n, dz), there, there, peer[last])
    for dz in (1, 2, 3):
        net.add((K_IN, K_Z, dz), lambda: own_part(K_IN, core, chip), lambda: part(K_IN, z, core, chip), plane[dz])
    mates = hops + [(K_OUT, dz) for dz in (1, 2, 3)]
    for a, dz in mates:
        net.add((a, K_M, dz), lambda a=a, dz=dz: side(a, where[a][dz], core), lambda a=a, dz=dz: side(a, where[a][dz], core), mate)
    loc.add(K_RAW, lambda: wraw_ref, lambda: wraw)
    loc.add(K_TOK, lambda: tok_ref, lambda: tok.at[0])
    loc.add(K_WQ, lambda: wq_ref.at[chip], lambda: wqv.at[pl.ds(pl.multiple_of(z * shard, 16), shard), :])
    outs = ((K_WQ_O, wq_ref, wq_out), (K_K_O, k_s, k_out), (K_V_O, v_s, v_out), (K_Q_O, q_s, q_out), (K_O_O, o_s, o_out),
            (K_TOK_O, tok, tok_out), (K_ATT_O, att, att_out), (K_SMALL_O, small, small_out))
    for name, src, dst in outs:
        loc.add(name, lambda src=src: src, lambda dst=dst: dst)

    loc.start(K_RAW, K_TOK)
    greet(peer[1:] + [mate] + plane[1:])
    net.start(K_T1A, K_T2B, K_T1B, K_T2A)
    lane = lanes_of()
    loc.wait(K_RAW)
    for g in range(CHIPS):
        for t in range(PACK // 128):
            halves = []
            for upper in (0, 1):
                block = PACKED[2 * t + upper]
                if block is None:
                    halves.append(0.0)
                    continue
                block += GROUP_HEADS * g
                tile_of = lambda i: wraw[:, i * 128 : (i + 1) * 128].astype(f32)
                halves.append(half_tile(tile_of, block, upper))
            wq_ref[g, :, t * 128 : (t + 1) * 128] = jnp.where(lane < 64, halves[0], halves[1]).astype(bf16)
    loc.start(K_WQ, K_WQ_O)
    net.start(*[(K_WQ, dz) for dz in (1, 2, 3)])
    vec_s[...] = jnp.zeros_like(vec_s)
    vec_v[...] = jnp.zeros_like(vec_v)
    for i, ref in enumerate((ob_ref, g1_ref, n1_ref, bb_ref, g2_ref, n2_ref)):
        vec_s[i : i + 1, 0:shard] = ref[...].astype(f32).reshape(1, shard)
    vec_s[6:7, :] = ib_ref[...].astype(f32).reshape(1, ib_ref.shape[0])
    vec_s[7:8, 256 : 256 + shard] = qb_ref[...].astype(f32).reshape(1, shard)
    vec_v[0:1, 0:shard] = vb_ref[...].astype(f32).reshape(1, shard)
    first, last = vec_v[:, 0:128], vec_v[:, 128:256]
    for t, tile in ((0, pltpu.roll(first, 64, 1)), (1, first), (4, pltpu.roll(last, 64, 1))):
        vec_s[7:8, t * 128 : (t + 1) * 128] = jnp.where(lane < 64, 0.0, tile[0:1])
    small[z] = jnp.concatenate([vec_s[...], jnp.zeros_like(vec_s)], axis=0).astype(bf16)
    net.start(*[(K_SMALL, dz) for dz in (1, 2, 3)])
    for dz in (1, 2, 3):
        net.recv((K_WQ, dz))
        net.start((K_WQM, dz))
    net.start(*[(K_IN, K_Z, dz) for dz in (1, 2, 3)])
    loc.wait(K_TOK, K_WQ)
    for dz in (1, 2, 3):
        net.recv((K_SMALL, dz), (K_WQM, dz))

    length = length_ref[0]
    bias = small[chip, 7:8, 0:PACK].astype(f32)

    def keep(tile, h, slot, block):
        position = block * rows + lax.broadcasted_iota(jnp.int32, (rows, 1), 0)
        mask = jnp.where(position < length, 0.0, -1e30).astype(f32)
        ones = jnp.where((lane > 64) & (lane < 68), 1.0, 0.0)
        k_s[h, slot * rows : (slot + 1) * rows, :] = jnp.where(
            lane < 64, tile, jnp.where(lane == 64, mask, ones)
        ).astype(bf16)
        v_s[h, slot * rows : (slot + 1) * rows, :] = jnp.where(
            lane < 64, pltpu.roll(tile, 64, 1), jnp.where(lane < 67, 1.0, 0.0)
        ).astype(bf16)

    def project(j):
        proj = dot(tok[j], wqv[...]) + bias
        for h in range(GROUP_HEADS):
            tile = proj[:, KV_TILE[h] * 128 : (KV_TILE[h] + 1) * 128]
            keep(tile.astype(bf16).astype(f32), h, j, flip(chip, j) * 2 + core)
            kvs[j, :, h * 128 : (h + 1) * 128] = tile.astype(bf16)
            first = 256 + (h // 2) * 128
            tile = proj[:, first : first + 128].astype(bf16).astype(f32) * 0.125
            if h == 1:
                tile = pltpu.roll(tile, 64, 1)
            q_s[h, j * rows : (j + 1) * rows, :] = jnp.where(
                lane < 64, tile, jnp.where(lane == 64, 1.0, 0.0)
            ).astype(bf16)
        net.start((K_KV, j))

    def keep_other(j):
        net.recv((K_KV, j))
        for h in range(GROUP_HEADS):
            tile = kvr[j, :, h * 128 : (h + 1) * 128].astype(f32)
            keep(tile, h, 4 + j, flip(chip, j) * 2 + other)

    def first_hop(a, dz):
        net.start((a, 1, dz), (a, 2, dz))

    def second_hop(a, dz):
        net.recv((a, 1, dz))
        net.start((a, 3, dz))
        net.recv((a, 2, dz))
        net.start((a, 4, dz))

    def third_hop(a, dz):
        net.recv((a, 3, dz), (a, 4, dz))
        net.start((a, K_M, dz))

    project(0)
    net.recv(K_T1A)
    net.start(K_T3A)
    net.recv(K_T2B)
    net.start(K_T3B)
    net.recv(K_T1B)
    project(1)
    net.recv(K_T2A)
    project(2)
    keep_other(0)
    keep_other(1)
    keep_other(2)
    net.recv((K_IN, K_Z, 1))
    first_hop(K_IN, 1)
    line.start(K_BACK, K_OUT)
    net.recv(K_T3A, K_T3B)
    project(3)
    keep_other(3)
    loc.start(K_K_O, K_V_O, K_TOK_O, K_SMALL_O)

    query_tile, key_chunk = 2 * rows, 4 * rows
    tiles = 4 * rows // query_tile
    chunks = 8 * rows // key_chunk

    def attended_tile(which):
        for j in range(4):
            r = slice(j * rows, (j + 1) * rows)
            if which == 0:
                upper = pltpu.roll(o_s[1, r, :].astype(f32), 64, 1)
                value = jnp.where(lane < 64, o_s[0, r, :].astype(f32), upper)
            else:
                value = jnp.where(lane < 64, o_s[2, r, :].astype(f32), 0.0)
            place = slice(which * 128, (which + 1) * 128)
            if j == 0:
                att[chip, :, place] = value.astype(bf16)
            else:
                atts[j, :, place] = value.astype(bf16)
                net.start(((K_ATT0, K_ATT1)[which], j))

    def in_hop(dz):
        net.recv((K_IN, K_Z, dz))
        first_hop(K_IN, dz)

    stages = {
        0: lambda: (in_hop(2), in_hop(3)),
        1: lambda: line.step(1, K_BACK, K_OUT),
        2: lambda: (second_hop(K_IN, 1), first_hop(K_BACK, 1)),
        4: lambda: (second_hop(K_IN, 2), third_hop(K_IN, 1)),
        5: lambda: line.step(2, K_BACK, K_OUT),
        6: lambda: second_hop(K_IN, 3),
        7: lambda: (attended_tile(0), third_hop(K_IN, 2)),
        8: lambda: second_hop(K_BACK, 1),
        9: lambda: third_hop(K_IN, 3),
        10: lambda: (line.step(3, K_BACK, K_OUT), [net.start((K_OUT, K_M, dz)) for dz in (1, 2, 3)]),
        11: lambda: (attended_tile(1), third_hop(K_BACK, 1)),
    }

    def progress(n):
        for at, work in stages.items():
            pl.when(n == at)(lambda work=work: (work(), None)[1])

    def visit(t, carry):
        h, i = lax.div(t, tiles), lax.rem(t, tiles)
        qrows = pl.ds(pl.multiple_of(i * query_tile, query_tile), query_tile)
        q = q_s[h, qrows, :]
        top_score = jnp.full((query_tile, 1), -1e30, f32)
        acc = jnp.zeros((query_tile, 128), f32)
        for c in range(chunks):
            krows = slice(c * key_chunk, (c + 1) * key_chunk)
            scores = dot(q, k_s[h, krows, :], NT)
            new_top = jnp.maximum(top_score, jnp.max(scores, axis=1, keepdims=True))
            probs = jnp.exp2((scores - new_top) * LOG2E)
            fade = jnp.exp2((top_score - new_top) * LOG2E)
            acc = acc * fade + dot(probs.astype(bf16), v_s[h, krows, :])
            top_score = new_top
            if c < chunks - 1:
                progress(t * chunks + c)
        total = acc[:, 64:65]
        o_s[h, qrows, :] = (acc / total).astype(bf16)
        hi, mid, low = split3(-(top_score + jnp.log(total)))
        wide = q.astype(f32)
        wide = jnp.where(lane == 65, hi, jnp.where(lane == 66, mid, jnp.where(lane == 67, low, wide)))
        q_s[h, qrows, :] = wide.astype(bf16)
        progress(t * chunks + chunks - 1)
        return carry

    lax.fori_loop(0, GROUP_HEADS * tiles, visit, 0)
    loc.start(K_Q_O, K_O_O)
    for j in (1, 2, 3):
        net.recv((K_ATT0, j), (K_ATT1, j))
    loc.start(K_ATT_O)
    net.recv(*[(a, K_M, dz) for a, dz in mates])
    for name in net.specs:
        net.sent(name)
    line.sent()
    loc.wait(*[name for name, _, _ in outs])


def backward_kernel(
    do_ref, do1_ref, q_ref, k_ref, v_ref, o_ref, tok_ref, grads_ref, sums_ref, back_ref,
    dproj_out, gw_out, hw_out, fin_out, finb_out, sums_out,
    do_s, do1_s, q_s, k_s, v_s, o_s, doa, tok, tokt, dqs, dq_keep, kv_own, kvs, kvr, dall, fold,
    gw, gwr, gz, gzr, gwf, hw, hwr, hz, hzr, hwf, acc, rb, rx, ry, rx2, ry2, rz, rzb, backv, bx2, by2, fin, finb, sums, sums_r, sums_z, sums_f,
    send_sems, recv_sems, local_sems,
):
    s, z, core, chip = coordinates()
    other = 1 - core
    rows = do_ref.shape[1]
    peer = [None] + [(flip(chip, j) * 2 + core, z) for j in (1, 2, 3)]
    mate = (chip * 2 + other, z)
    plane = [None] + [(s, flip(z, dz)) for dz in (1, 2, 3)]
    zs = [z] + [flip(z, dz) for dz in (1, 2, 3)]
    ch = [chip] + [flip(chip, j) for j in (1, 2, 3)]
    net, loc = Net(send_sems, recv_sems), Local(local_sems)
    length = grads_ref.shape[3]
    cut = length // 32 * 16
    xs, ys = slice(0, cut), slice(cut, length)
    shard = tok.shape[2] // PLANES
    piece = shard // 2

    for h in range(GROUP_HEADS):
        net.add((K_KV, h), lambda h=h: kvs.at[h], lambda h=h: kvr.at[h], mate)
        kv_cols = slice(KV_TILE[h] * 128, KV_TILE[h] * 128 + 128)
        for j in (1, 2, 3):
            net.add((K_DP, h, j), lambda j=j, cols=kv_cols: dall.at[j, :, cols],
                    lambda cols=kv_cols: dproj_out.at[chip, :, cols], peer[j])
    for j in (1, 2, 3):
        net.add((K_DP, K_Q, j), lambda j=j: dall.at[j, :, 256:384], lambda: dproj_out.at[chip, :, 256:384], peer[j])
        net.add((K_DP, K_O, j), lambda j=j: fold.at[j], lambda: dproj_out.at[chip, 0 : rows // 2, 384:512], peer[j])
    loc.add((K_DP, 0), lambda: dall.at[0, :, 0:384], lambda: dproj_out.at[chip, :, 0:384])
    loc.add((K_DP, 1), lambda: dall.at[0, :, 512:640], lambda: dproj_out.at[chip, :, 512:640])
    loc.add((K_DP, 2), lambda: fold.at[0], lambda: dproj_out.at[chip, 0 : rows // 2, 384:512])
    for j in (1, 2, 3):
        net.add((K_DO, j), lambda j=j: do1_ref.at[ch[j]], lambda j=j: do1_s.at[j], peer[j])
    order = (3, 2, 1, 0)
    for dz in order:
        net.add((K_R1, dz), lambda dz=dz: grads_ref.at[other, zs[dz]], lambda dz=dz: rb.at[zs[dz]], mate)
        for n, j in enumerate((1, 3)):
            net.add((K_X1, n, dz), lambda dz=dz, j=j: acc.at[zs[dz], ch[j], xs], lambda dz=dz, n=n: rx.at[zs[dz], n], peer[1])
        net.add((K_X2, dz), lambda dz=dz: acc.at[zs[dz], ch[2], xs], lambda dz=dz: rx2.at[zs[dz]], peer[2])
        for n, j in enumerate((2, 3)):
            net.add((K_Y1, n, dz), lambda dz=dz, j=j: acc.at[zs[dz], ch[j], ys], lambda dz=dz, n=n: ry.at[zs[dz], n], peer[2])
        net.add((K_Y2, dz), lambda dz=dz: acc.at[zs[dz], ch[1], ys], lambda dz=dz: ry2.at[zs[dz]], peer[1])
        if dz:
            net.add((K_RZ, dz), lambda dz=dz: acc.at[zs[dz], chip], lambda dz=dz: rz.at[dz - 1], plane[dz])
    for dz in (1, 2, 3):
        net.add((K_RZB, dz), lambda dz=dz: backv.at[zs[dz]], lambda dz=dz: rzb.at[dz - 1], plane[dz])
    bh = finb.shape[2] // 2
    bx, by = slice(0, bh), slice(bh, 2 * bh)
    net.add((K_X2, K_BACK), lambda: back_ref.at[2, :, bx], lambda: bx2, peer[2])
    net.add((K_Y2, K_BACK), lambda: back_ref.at[1, :, by], lambda: by2, peer[1])
    net.add(K_B1, lambda: finb.at[core, chip], lambda: finb.at[core, chip], peer[1])
    net.add(K_B2, lambda: finb.at[core, chip], lambda: finb.at[core, chip], peer[2])
    net.add(K_B3X, lambda: finb.at[core, ch[1], bx], lambda: finb.at[core, ch[1], bx], peer[2])
    net.add(K_B3Y, lambda: finb.at[core, ch[2], by], lambda: finb.at[core, ch[2], by], peer[1])
    net.add(K_BM, lambda: finb.at[core], lambda: finb.at[core], mate)
    net.add(K_F1, lambda: fin.at[core, chip], lambda: fin.at[core, chip], peer[1])
    net.add(K_F2, lambda: fin.at[core, chip], lambda: fin.at[core, chip], peer[2])
    net.add(K_F3X, lambda: fin.at[core, ch[1], xs], lambda: fin.at[core, ch[1], xs], peer[2])
    net.add(K_F3Y, lambda: fin.at[core, ch[2], ys], lambda: fin.at[core, ch[2], ys], peer[1])
    net.add(K_FM, lambda: fin.at[core], lambda: fin.at[core], mate)
    net.add(K_S0, lambda: sums_ref, lambda: sums_r.at[0], mate)
    net.add(K_S1, lambda: sums.at[1], lambda: sums_r.at[1], peer[1])
    net.add(K_S2, lambda: sums.at[2], lambda: sums_r.at[2], peer[2])
    for dz in (1, 2, 3):
        net.add((K_SZ, dz), lambda dz=dz: sums.at[3, zs[dz]], lambda dz=dz: sums_z.at[dz - 1], plane[dz])
    for a, w, wr, g, gr, f in ((K_G, gw, gwr, gz, gzr, gwf), (K_H, hw, hwr, hz, hzr, hwf)):
        net.add((a, 0), lambda w=w: w.at[other], lambda wr=wr: wr, mate)
        for dz in (1, 2, 3):
            net.add((a, K_Z, dz), lambda g=g, dz=dz: g.at[zs[dz]], lambda gr=gr, dz=dz: gr.at[dz - 1], plane[dz])
        for j in (1, 2, 3):
            net.add((a, K_F, j), lambda f=f: f.at[core, chip], lambda f=f: f.at[core, chip], peer[j])
        net.add((a, K_M), lambda f=f: f.at[core], lambda f=f: f.at[core], mate)

    loads = ((K_DO, lambda: do_ref, lambda: do_s), (K_DO1, lambda: do1_ref.at[chip], lambda: do1_s.at[0]), (K_O, lambda: o_ref, lambda: o_s),
             (K_TOK, lambda: tok_ref, lambda: tok), (K_Q, lambda: q_ref, lambda: q_s),
             (K_K, lambda: k_ref, lambda: k_s), (K_V, lambda: v_ref, lambda: v_s),
             (K_SUMS, lambda: sums_ref, lambda: sums.at[0]), (K_BACK, lambda: back_ref.at[0], lambda: backv), (K_ACC, lambda: grads_ref.at[core], lambda: acc))
    for name, src, dst in loads:
        loc.add(name, src, dst)
    stores = ((K_GW_O, gwf, gw_out), (K_HW_O, hwf, hw_out), (K_FIN_O, fin, fin_out), (K_FINB_O, finb, finb_out))
    for name, src, dst in stores:
        loc.add(name, lambda src=src: src, lambda dst=dst: dst)
    loc.add(K_SUMS_O, lambda: sums_f, lambda: sums_out)

    loc.start(K_DO, K_O, K_Q, K_K, K_V)
    greet(peer[1:] + [mate] + plane[1:])
    net.start((K_X2, K_BACK), (K_Y2, K_BACK), K_S0, *[(K_R1, dz) for dz in order])
    loc.start(K_ACC, K_BACK, K_SUMS, K_TOK, K_DO1)
    lane = lanes_of()
    loc.wait(K_DO, K_O)

    def output_grad(h, tiles):
        for j in range(4):
            tile = tiles[j].astype(f32)
            if h == 1:
                tile = pltpu.roll(tile, 64, 1)
            tile = jnp.where(lane < 64, tile, 0.0)
            r = slice(j * rows, (j + 1) * rows)
            delta = jnp.sum(tile * o_s[h, r, :].astype(f32), axis=1, keepdims=True)
            hi, mid, low = split3(-delta)
            tile = jnp.where(lane == 64, hi, jnp.where(lane == 65, mid, jnp.where(lane == 66, low, tile)))
            doa[h, r, :] = tile.astype(bf16)

    output_grad(0, do_s)
    output_grad(1, do_s)
    loc.wait(K_Q, K_K, K_V)

    def late_loads():
        loc.wait(K_ACC, K_BACK, K_SUMS)
        net.start(*[(K_DO, j) for j in (1, 2, 3)])

    def transpose_tokens():
        loc.wait(K_TOK)
        for j in range(4):
            tokt[:, j * rows : (j + 1) * rows] = tok[j].T

    def last_head_grad():
        loc.wait(K_DO1)
        net.recv(*[(K_DO, j) for j in (1, 2, 3)])
        output_grad(2, do1_s)

    def add_into(ref, index, other_ref, other_index):
        ref[index] = (ref[index].astype(f32) + other_ref[other_index].astype(f32)).astype(bf16)

    def step_one(dz):
        net.recv((K_R1, dz))
        def body(c, carry):
            add_into(acc, (zs[dz], c), rb, (zs[dz], c))
            return carry
        lax.fori_loop(0, CHIPS, body, 0)
        net.start(*[(K_X1, n, dz) for n in (0, 1)], *[(K_Y1, n, dz) for n in (0, 1)])

    def step_two(dz):
        for n in range(2):
            net.recv((K_X1, 1 - n, dz), (K_Y1, 1 - n, dz))
            jx, jy = (2, 1) if n == 0 else (0, 0)
            add_into(acc, (zs[dz], ch[jx], xs), rx, (zs[dz], 1 - n))
            add_into(acc, (zs[dz], ch[jy], ys), ry, (zs[dz], 1 - n))
            if n == 0:
                net.start((K_X2, dz), (K_Y2, dz))

    def step_three(dz):
        net.recv((K_X2, dz), (K_Y2, dz))
        add_into(acc, (zs[dz], chip, xs), rx2, zs[dz])
        add_into(acc, (zs[dz], chip, ys), ry2, zs[dz])
        if dz:
            net.start((K_RZ, dz))

    def sums_step(n):
        net.recv((K_S0, K_S1, K_S2)[n])
        sums[n + 1] = (sums[n].astype(f32) + sums_r[n].astype(f32)).astype(bf16)
        if n < 2:
            net.start((K_S1, K_S2)[n])
        else:
            net.start(*[(K_SZ, dz) for dz in (1, 2, 3)])

    def back_plane():
        net.recv((K_X2, K_BACK), (K_Y2, K_BACK))
        for zz in range(PLANES):
            add_into(backv, (zz, bx), bx2, zz)
            add_into(backv, (zz, by), by2, zz)
        net.start(*[(K_RZB, dz) for dz in (1, 2, 3)])

    def back_total():
        net.recv(*[(K_RZB, dz) for dz in (1, 2, 3)])
        total = backv[z].astype(f32) + rzb[0].astype(f32) + rzb[1].astype(f32) + rzb[2].astype(f32)
        finb[core, chip] = total.astype(bf16)
        net.start(K_B1, K_B2)

    def back_forward():
        net.recv(K_B1)
        net.start(K_B3X)
        net.recv(K_B2)
        net.start(K_B3Y)

    def back_mate():
        net.recv(K_B3X, K_B3Y)
        net.start(K_BM)

    def fin_total():
        for dz in (1, 2, 3):
            net.recv((K_RZ, dz), (K_SZ, dz))
        total = acc[z, chip].astype(f32) + rz[0].astype(f32) + rz[1].astype(f32) + rz[2].astype(f32)
        fin[core, chip] = total.astype(bf16)
        net.start(K_F1, K_F2)
        total = sums[3, z].astype(f32)
        for n in range(3):
            total = total + sums_z[n].astype(f32)
        sums_f[...] = total.astype(bf16)
        loc.start(K_SUMS_O)

    def fin_forward():
        net.recv(K_F1)
        net.start(K_F3X)
        net.recv(K_F2)
        net.start(K_F3Y)

    def weight_part(a, w, first, last):
        cols = dall[:, :, first:last].reshape(4 * rows, last - first)
        column_sums = jnp.sum(cols.astype(f32), axis=0, keepdims=True)
        extra = jnp.where(lax.broadcasted_iota(jnp.int32, (16, 1), 0) == 0, column_sums, 0.0).astype(bf16)
        for zz in range(PLANES):
            part = dot(tokt[zz * shard : (zz + 1) * shard, :], cols)
            for m in range(2):
                w[m, zz, 0:piece, :] = part[m * piece : (m + 1) * piece, :].astype(bf16)
                w[m, zz, piece : piece + 16, :] = extra
        net.start((a, 0))

    def weight_pair(a, w, wr, g):
        net.recv((a, 0))
        for zz in range(PLANES):
            g[zz] = (w[core, zz].astype(f32) + wr[zz].astype(f32)).astype(bf16)
        net.start(*[(a, K_Z, dz) for dz in (1, 2, 3)])

    def weight_total(a, g, gr, f):
        total = g[z].astype(f32)
        for dz in (1, 2, 3):
            net.recv((a, K_Z, dz))
            total = total + gr[dz - 1].astype(f32)
        f[core, chip] = total.astype(bf16)
        net.start(*[(a, K_F, j) for j in (1, 2, 3)])

    def weight_mate(a):
        net.recv(*[(a, K_F, j) for j in (1, 2, 3)])
        net.start((a, K_M))

    key_chunk, query_tile = 2 * rows, 256
    per_head = 4

    def head_keys(h, slots):
        cols = slice(KV_TILE[h] * 128, KV_TILE[h] * 128 + 128)
        for j in slots:
            r = slice(j * rows, (j + 1) * rows)
            both = kv_own[r, :] + kvr[h, r, :].astype(f32)
            dall[j, :, cols] = both.astype(bf16)
            if j:
                net.start((K_DP, h, j))

    def head_queries(h):
        dq = dqs[...].T * 0.125
        for j in range(4):
            r = slice(j * rows, (j + 1) * rows)
            mine = dq[r, :]
            if h == 0:
                dq_keep[r, :] = mine
            elif h == 1:
                dall[j, :, 256:384] = jnp.where(lane < 64, dq_keep[r, :], pltpu.roll(mine, 64, 1)).astype(bf16)
                if j:
                    net.start((K_DP, K_Q, j))
            else:
                upper = pltpu.roll(mine[rows // 2 :, :], 64, 1)
                fold[j] = jnp.where(lane < 64, mine[: rows // 2, :], upper).astype(bf16)
                if j:
                    net.start((K_DP, K_O, j))
                dall[j, :, 384:512] = jnp.where(lane < 64, mine, 0.0).astype(bf16)

    stages = {
        0: lambda: (late_loads(), step_one(3), back_plane(), sums_step(0)),
        1: lambda: (step_one(2), sums_step(1)),
        2: lambda: (step_two(3), step_one(1), sums_step(2)),
        3: lambda: (step_three(3), step_two(2)),
        4: lambda: (step_one(0), back_total()),
        5: lambda: (step_three(2), step_two(1), transpose_tokens()),
        6: lambda: (step_two(0), back_forward(), last_head_grad()),
        7: lambda: (step_three(1), weight_part(K_G, gw, 0, 384)),
        8: lambda: (step_three(0), back_mate()),
        9: lambda: (fin_total(), weight_pair(K_G, gw, gwr, gz)),
        11: lambda: (fin_forward(), weight_total(K_G, gz, gzr, gwf)),
    }

    def visit(t, carry):
        h, part = lax.div(t, per_head), lax.rem(t, per_head)
        start = pl.multiple_of(jnp.where(part < 2, part + 2, 3 - part) * key_chunk, key_chunk)
        krows = pl.ds(start, key_chunk)
        k, v = k_s[h, krows, :], v_s[h, krows, :]
        kt = k.T

        @pl.when(part == 0)
        def _():
            dqs[...] = jnp.zeros_like(dqs)

        dk = jnp.zeros((key_chunk, 128), f32)
        dv = jnp.zeros((key_chunk, 128), f32)
        for i in range(4 * rows // query_tile):
            r = slice(i * query_tile, (i + 1) * query_tile)
            q, do = q_s[h, r, :], doa[h, r, :]
            probs = jnp.exp2(dot(k, q, NT) * LOG2E)
            dscores = (probs * dot(v, do, NT)).astype(bf16)
            dv = dv + dot(probs.astype(bf16), do)
            dk = dk + dot(dscores, q)
            dqs[:, r] += dot(kt, dscores)
        packed = jnp.where(lane < 64, dk, pltpu.roll(dv, 64, 1))

        @pl.when(part < 2)
        def _():
            kvs[h, pl.ds(pl.multiple_of(part * key_chunk, key_chunk), key_chunk), :] = packed.astype(bf16)

        @pl.when(part >= 2)
        def _():
            kv_own[pl.ds(pl.multiple_of((3 - part) * key_chunk, key_chunk), key_chunk), :] = packed

        for hh in range(GROUP_HEADS):
            @pl.when(t == hh * per_head + 1)
            def _(hh=hh):
                net.start((K_KV, hh))

            @pl.when(t == hh * per_head + 2)
            def _(hh=hh):
                net.recv((K_KV, hh))
                head_keys(hh, (2, 3))

            @pl.when(t == hh * per_head + 3)
            def _(hh=hh):
                head_keys(hh, (1, 0))
                head_queries(hh)
        for at, work in stages.items():
            pl.when(t == at)(lambda work=work: (work(), None)[1])
        return carry

    lax.fori_loop(0, GROUP_HEADS * per_head, visit, 0)

    weight_part(K_H, hw, 384, PACK)
    loc.start((K_DP, 0), (K_DP, 1), (K_DP, 2))
    weight_pair(K_H, hw, hwr, hz)
    weight_mate(K_G)
    net.recv(K_F3X, K_F3Y)
    net.start(K_FM)
    weight_total(K_H, hz, hzr, hwf)
    for h in (0, 1, 2, K_Q, K_O):
        for j in (1, 2, 3):
            net.recv((K_DP, h, j))
    net.recv(K_FM, K_BM, (K_G, K_M))
    loc.start(K_GW_O, K_FIN_O, K_FINB_O)
    weight_mate(K_H)
    net.recv((K_H, K_M))
    loc.start(K_HW_O)
    for name in net.specs:
        net.sent(name)
    loc.wait((K_DP, 0), (K_DP, 1), (K_DP, 2), K_GW_O, K_HW_O, K_FIN_O, K_FINB_O, K_SUMS_O)


def gelu_parts(u):
    x = jnp.abs(u) * (0.5 ** 0.5)
    d = 1.0 + 0.3275911 * x
    t = pl.reciprocal(d, approx=True)
    t = t * (2.0 - d * t)
    poly = t * (0.254829592 + t * (-0.284496736 + t * (1.421413741 + t * (-1.453152027 + t * 1.061405429))))
    bell = jnp.exp2(u * u * (-0.5 * LOG2E))
    tail = 0.5 * poly * bell
    phi = jnp.where(u >= 0, 1.0 - tail, tail)
    return u * phi, phi + u * bell * (1.0 / math.sqrt(2.0 * math.pi))


def row_mean(a):
    return jnp.mean(a, axis=1, keepdims=True)


def wide_vectors(small):
    step = small.shape[2] // PLANES
    lane = lax.broadcasted_iota(jnp.int32, (8, small.shape[2]), 1)
    total = 0.0
    for zz in range(PLANES):
        part = jnp.where(lane < step, small[zz].astype(f32)[0:8], 0.0)
        total = total + (pltpu.roll(part, zz * step, 1) if zz else part)
    return total


def ffn_kernel(
    length_ref, att_ref, tok_ref, cot_ref, win_ref, win_own, wout_ref, wout_own, small_ref, wback_ref, wback_own, wq_own,
    res_out, gh1_out, do_out, do1_out, grads_out, sums_ref, wq_full, back_out,
    winv, wbackv, woutv, act_s, gp_s, gi_s, acc, first_s, n1_s, low_s, lowt_s, gsec_s, gh2_s, isum,
    gb, rb, rx, ry, do_ref, do_in, out_ref, gh1_ref, grads_ref, send_sems, recv_sems, line_send, line_recv, local_sems,
):
    s, z, core, chip = coordinates()
    other = 1 - core
    rows, width = tok_ref.shape
    step = width // PLANES
    ch = winv.shape[1] // 8
    wide = 2 * ch
    back = wback_own.shape[0]
    shard = win_own.shape[0]
    piece = shard // 2
    peer = [None] + [(flip(chip, j) * 2 + core, z) for j in (1, 2, 3)]
    mate = (chip * 2 + other, z)
    plane = [(s, flip(z, dz)) for dz in (1, 2, 3)]
    ch_of = [chip] + [flip(chip, j) for j in (1, 2, 3)]
    net, loc = Net(send_sems, recv_sems), Local(local_sems)

    bpiece = back // 8
    line = Line(s, z, line_send, line_recv)
    lines = line.order
    line.add(K_QKV, lambda: wq_own.at[pl.ds(core * 2, 2)], lambda zz: wq_full.at[zz, pl.ds(core * 2, 2)])
    for dz in (1, 2, 3):
        net.add((K_QKV, dz), lambda dz=dz: wq_full.at[lines[dz], pl.ds(core * 2, 2)], lambda dz=dz: wq_full.at[lines[dz], pl.ds(core * 2, 2)], mate)

    def region(ref, zz, c):
        return ref.at[pl.ds(pl.multiple_of(zz * back + (core * 4 + c) * bpiece, 16), bpiece), :]

    def side(zz):
        return wbackv.at[pl.ds(pl.multiple_of(zz * back + core * 4 * bpiece, 16), 4 * bpiece), :]

    for dz in (2, 3):
        for j in (1, 2):
            net.add((j, dz), lambda dz=dz: region(wback_ref, lines[dz], chip), lambda dz=dz: region(wbackv, lines[dz], chip), peer[j])
        via, last = ((1, 2), (2, 1))[dz - 2]
        net.add((3, dz), lambda dz=dz, via=via: region(wbackv, lines[dz], ch_of[via]), lambda dz=dz, via=via: region(wbackv, lines[dz], ch_of[via]), peer[last])
        net.add((K_M, dz), lambda dz=dz: side(lines[dz]), lambda dz=dz: side(lines[dz]), mate)
        loc.add((K_M, dz), lambda dz=dz: region(wback_ref, lines[dz], chip), lambda dz=dz: region(wbackv, lines[dz], chip))
    half = gb.shape[3] // 2
    xs, ys = slice(0, half), slice(half, 2 * half)
    for zz in range(PLANES):
        net.add((K_R1, zz), lambda zz=zz: gb.at[other, zz], lambda zz=zz: rb.at[zz], mate)
        for n, j in enumerate((1, 3)):
            net.add((K_X1, n, zz), lambda zz=zz, j=j: gb.at[core, zz, ch_of[j], xs], lambda zz=zz, n=n: rx.at[zz, n], peer[1])
        for n, j in enumerate((2, 3)):
            net.add((K_Y1, n, zz), lambda zz=zz, j=j: gb.at[core, zz, ch_of[j], ys], lambda zz=zz, n=n: ry.at[zz, n], peer[2])
    for j in (1, 2, 3):
        net.add((K_DO, j), lambda j=j: do_ref.at[0, ch_of[j]], lambda j=j: do_in.at[j], peer[j])
    loc.add(K_DO_O, lambda: do_in, lambda: do_out)
    loc.add(K_DO1, lambda: do_ref.at[1], lambda: do1_out)
    loc.add(K_GH1, lambda: gh1_ref, lambda: gh1_out)
    loc.add(K_RES, lambda: out_ref, lambda: res_out)
    for n in range(PLANES):
        cut_of = lambda ref, n=n: ref.at[n // 2, :, pl.ds(n % 2 * 2, 2)]
        loc.add((K_GR, n), lambda cut_of=cut_of: cut_of(grads_ref), lambda cut_of=cut_of: cut_of(grads_out))
    for j in range(3):
        loc.add((K_BACK_O, j), lambda j=j: gb.at[core, :, ch_of[j]], lambda j=j: back_out.at[j])
    shards = {K_OUT: (wout_own, wout_ref, woutv), K_IN: (win_own, win_ref, winv), K_BACK: (wback_own, wback_ref, wbackv)}
    loads = [(name, i) for name in shards for i in range(4) if name != K_BACK or i < 2]
    for name, i in loads:
        own, full, dst = shards[name]
        n = own.shape[0]
        place = lambda i=i, n=n: pl.ds(pl.multiple_of(lines[i] * n, 16), n)
        loc.add((name, i), lambda own=own, full=full, i=i, place=place: full.at[place(), :] if i else own,
                lambda dst=dst, place=place: dst.at[place(), :])
    loc.start(*loads, (K_M, 2), (K_M, 3))
    greet(peer[1:] + [mate] + plane)
    net.start((1, 2), (2, 2), (1, 3), (2, 3))
    line.start(K_QKV)

    def hop_two(dz):
        net.recv((1, dz), (2, dz))
        net.start((3, dz))

    def hop_three(dz):
        net.recv((3, dz))
        loc.wait((K_M, dz))
        net.start((K_M, dz))

    def add_into(ref, index, other_ref, other_index):
        ref[index] = (ref[index].astype(f32) + other_ref[other_index].astype(f32)).astype(bf16)

    def step_one(zz):
        net.recv((K_R1, zz))
        for c in range(CHIPS):
            add_into(gb, (core, zz, c), rb, (zz, c))
        net.start(*[(K_X1, n, zz) for n in (0, 1)], *[(K_Y1, n, zz) for n in (0, 1)])

    def step_two(zz):
        net.recv((K_X1, 1, zz), (K_Y1, 1, zz))
        add_into(gb, (core, zz, ch_of[2], xs), rx, (zz, 1))
        add_into(gb, (core, zz, ch_of[1], ys), ry, (zz, 1))
        net.recv((K_X1, 0, zz), (K_Y1, 0, zz))
        add_into(gb, (core, zz, chip, xs), rx, (zz, 0))
        add_into(gb, (core, zz, chip, ys), ry, (zz, 0))

    def during(n, works):
        for at, work in works.items():
            pl.when(n == at)(lambda work=work: (work(), None)[1])

    vectors = wide_vectors(small_ref)
    vec = lambda i: vectors[i : i + 1, :]
    loc.wait(*[(K_OUT, dz) for dz in range(4)])
    branch = vec(0)
    for g in range(4):
        branch = branch + dot(att_ref[g, :, 0:step], woutv[g * step : (g + 1) * step, :])
    hidden = tok_ref[...].astype(f32) + branch
    centred = hidden - row_mean(hidden)
    inverse1 = lax.rsqrt(row_mean(centred * centred) + 1e-5)
    normed = centred * inverse1
    n1_s[...] = normed
    first = normed * vec(1) + vec(2)
    first_s[...] = first
    low_s[...] = first.astype(bf16)
    lowt_s[...] = first.astype(bf16).T
    loc.wait(*[(K_IN, i) for i in range(4)])

    def forward(n, carry):
        cols = pl.ds(pl.multiple_of(n * wide, 128), wide)
        inner = dot(low_s[...], winv[:, cols]) + small_ref[n, 6:7, :].astype(f32)
        value, slope = gelu_parts(inner)
        value = value.astype(bf16)
        act_s[n] = value
        gp_s[n] = slope
        during(n, {2: lambda: hop_two(2), 3: lambda: hop_two(3)})
        return carry

    lax.fori_loop(0, PLANES, forward, 0)

    def second_layer(i):
        zz = lines[i]
        return dot(act_s[zz], wbackv[pl.ds(pl.multiple_of(zz * back, 16), back), :])

    loc.wait((K_BACK, 0), (K_BACK, 1))
    acc[...] = second_layer(0)
    acc[...] += second_layer(1)
    hop_three(2)
    hop_three(3)
    line.step(1, K_QKV)
    net.recv((K_M, 2))
    acc[...] += second_layer(2)
    net.recv((K_M, 3))
    acc[...] += second_layer(3)
    position = s * rows + lax.broadcasted_iota(jnp.int32, (rows, 1), 0)
    valid = (position < length_ref[0]).astype(f32)
    hidden = first_s[...] + acc[...] + vec(3)
    centred = hidden - row_mean(hidden)
    inverse = lax.rsqrt(row_mean(centred * centred) + 1e-5)
    normed = centred * inverse
    out_ref[...] = ((normed * vec(4) + vec(5)) * valid).astype(bf16)
    loc.start(K_RES)
    grad = cot_ref[...].astype(f32) * valid
    sum_rows = lambda a: jnp.sum(a, axis=0, keepdims=True)
    g2_gain, g2_bias = sum_rows(grad * normed), sum_rows(grad)
    scaled = grad * vec(4)
    gh2 = inverse * (scaled - row_mean(scaled) - normed * row_mean(scaled * normed))
    gh2_s[...] = gh2
    second = gh2.astype(bf16)
    gsec_s[...] = second
    back_sum = sum_rows(second.astype(f32))
    acc[...] = jnp.zeros_like(acc)

    def back_weights(n, carry):
        gback = dot(act_s[n].T, gsec_s[...]).astype(bf16)
        part = wide // 8
        for m in range(2):
            for k in range(4):
                for x in range(2):
                    gb[m, n, k, x * part : (x + 1) * part, :] = gback[
                        (m * 4 + k) * part : (m * 4 + k + 1) * part, x * ch : (x + 1) * ch
                    ]
        during(n, {
            0: lambda: net.start((K_R1, 0)), 1: lambda: net.start((K_R1, 1)),
            2: lambda: net.start((K_R1, 2)), 3: lambda: net.start((K_R1, 3)),
        })
        return carry

    lax.fori_loop(0, PLANES, back_weights, 0)

    def backward(n, carry):
        cols = pl.ds(pl.multiple_of(n * wide, 128), wide)
        grad_inner = (dot(gsec_s[...], wbackv[cols, :], NT) * gp_s[n]).astype(bf16)
        gi_s[n] = grad_inner
        isum[n] = jnp.broadcast_to(sum_rows(grad_inner.astype(f32)), (8, wide))
        acc[...] += dot(grad_inner, winv[:, cols], NT)
        during(n, {
            0: lambda: step_one(0), 1: lambda: step_one(1),
            2: lambda: (step_one(2), step_two(0)),
            3: lambda: (step_one(3), line.step(2, K_QKV), net.start((K_QKV, 1), (K_QKV, 2))),
        })
        return carry

    lax.fori_loop(0, PLANES, backward, 0)
    grad = gh2_s[...] + acc[...]
    normed = n1_s[...]
    g1_gain, g1_bias = sum_rows(grad * normed), sum_rows(grad)
    scaled = grad * vec(1)
    gh1 = inverse1 * (scaled - row_mean(scaled) - normed * row_mean(scaled * normed))
    gh1_ref[...] = gh1
    loc.start(K_GH1)
    gbranch = gh1.astype(bf16)
    out_sum = sum_rows(gbranch.astype(f32))
    for g in range(4):
        w = woutv[g * step : (g + 1) * step, :]
        part = dot(gbranch, w, NT).astype(bf16)
        do_ref[0, g] = part[:, 0:128]
        do_ref[1, g, :, 0 : step - 128] = part[:, 128:step]
        do_ref[1, g, :, step - 128 :] = jnp.zeros((rows, 256 - step), bf16)
    net.start(*[(K_DO, j) for j in (1, 2, 3)])
    do_in[0] = do_ref[0, chip]
    loc.start(K_DO1)
    for g in range(4):
        gw = dot(att_ref[g, :, 0:step].T, gbranch).astype(bf16)
        part = step // 4
        for c in range(4):
            for m in range(2):
                grads_ref[m, g, c, step:, :] = gw[c * part : (c + 1) * part, m * ch : (m + 1) * ch]

    def weights(n, carry):
        for zz in range(PLANES):
            gin = dot(lowt_s[zz * step : (zz + 1) * step, :], gi_s[n]).astype(bf16)
            for x in range(2):
                grads_ref[lax.div(n, 2), zz, lax.rem(n, 2) * 2 + x, 0:step, :] = gin[:, x * ch : (x + 1) * ch]
        during(n, {
            0: lambda: (loc.start((K_GR, 0)), step_two(1)), 1: lambda: (loc.start((K_GR, 1)), step_two(2)),
            2: lambda: (loc.start((K_GR, 2)), step_two(3)), 3: lambda: loc.start((K_GR, 3)),
        })
        return carry

    lax.fori_loop(0, PLANES, weights, 0)
    lane = lax.broadcasted_iota(jnp.int32, (8, width), 1)
    place = lax.broadcasted_iota(jnp.int32, (8, width), 0)
    total = jnp.zeros((8, width), f32)
    for i, v in enumerate((out_sum, g1_gain, g1_bias, back_sum, g2_gain, g2_bias)):
        total = jnp.where(place == i, v, total)
    for zz in range(PLANES):
        part = total if zz == 0 else pltpu.roll(total, width - zz * step, 1)
        part = jnp.where(lane < step, part, 0.0)
        part = jnp.where(place == 6, isum[zz], part)
        sums_ref[zz, 0:16, :] = jnp.concatenate([part, jnp.zeros((8, width), f32)], axis=0).astype(bf16)
    net.recv(*[(K_DO, j) for j in (1, 2, 3)])
    loc.start(*[(K_BACK_O, j) for j in range(3)], K_DO_O)
    line.step(3, K_QKV)
    net.start((K_QKV, 3))
    net.recv(*[(K_QKV, dz) for dz in (1, 2, 3)])
    for name in net.specs:
        net.sent(name)
    line.sent()
    loc.wait(*[(K_BACK_O, j) for j in range(3)], K_DO_O, K_DO1, K_GH1, K_RES, *[(K_GR, n) for n in range(PLANES)])


Q_PLACE, K_PLACE, V_PLACE = (4, 5, 6), (0, 2, 8), (1, 3, 9)


def half_tile(tile_of, block, upper):
    tile = tile_of(block // 2)
    return tile if block % 2 == upper else pltpu.roll(tile, 64, 1)


def final_kernel(
    dproj_ref, wq_ref, wq_own, gh1_ref, gw_ref, hw_ref, fin_ref, finb_ref, sums_ref,
    gt_ref, gqkv_ref, gin_ref, gback_ref, gout_ref, qb_ref, vb_ref, o0, o1, o2, o3, o4, o5, ib_ref,
    wv, row, last, local_sems,
):
    z = lax.axis_index("fsdp")
    loc = Local(local_sems)
    rows = gh1_ref.shape[0]
    shard = wq_ref.shape[2]
    for dz in range(PLANES):
        zz = flip(z, dz)
        loc.add(dz, lambda zz=zz, dz=dz: wq_own if dz == 0 else wq_ref.at[zz],
                lambda zz=zz: wv.at[:, pl.ds(pl.multiple_of(zz * shard, 16), shard), :])
    loc.start(*range(PLANES))
    lane = lanes_of()
    up = lambda a: a.astype(f32)
    ch = fin_ref.shape[3]
    for m in range(2):
        for c in range(4):
            n = m * 4 + c
            gin_ref[:, n * ch : (n + 1) * ch] = up(fin_ref[m, c, 0:shard, :])
            part = ch // 4
            for x in range(2):
                gback_ref[n * part : (n + 1) * part, x * ch : (x + 1) * ch] = up(
                    finb_ref[m, c, x * part : (x + 1) * part, :]
                )
            gout_ref[c * (shard // 4) : (c + 1) * (shard // 4), m * ch : (m + 1) * ch] = up(fin_ref[m, c, shard:, :])
    piece = shard // 2

    def packed_tile(m, g, r, t):
        if t < 3:
            return up(gw_ref[m, g, r, t * 128 : (t + 1) * 128])
        return up(hw_ref[m, g, r, (t - 3) * 128 : (t - 2) * 128])

    for m in range(2):
        r = slice(m * piece, (m + 1) * piece)
        for kind, places in enumerate((Q_PLACE, K_PLACE, V_PLACE)):
            for i in range(HEADS // 2):
                halves = []
                for upper in (0, 1):
                    g, h = divmod(2 * i + upper, GROUP_HEADS)
                    tile_of = lambda t, g=g: packed_tile(m, g, slice(0, piece), t)
                    halves.append(half_tile(tile_of, places[h], upper))
                at = kind * HEADS * 64 + i * 128
                gqkv_ref[r, at : at + 128] = jnp.where(lane < 64, halves[0], halves[1])
    tile_of = lambda t: packed_tile(0, z, slice(piece, piece + 16), t)
    for ref, places in ((qb_ref, Q_PLACE), (vb_ref, V_PLACE)):
        first = jnp.where(lane < 64, half_tile(tile_of, places[0], 0), half_tile(tile_of, places[1], 1))
        row[0:1, 0:128] = first[0:1]
        row[0:1, 128:256] = half_tile(tile_of, places[2], 0)[0:1]
        ref[...] = row[0:1, 0:shard].reshape(shard)
    for i, ref in enumerate((o0, o1, o2, o3, o4, o5)):
        ref[...] = up(sums_ref[...])[i : i + 1, 0:shard].reshape(shard)
    ib_ref[...] = up(sums_ref[...])[6:7, :].reshape(ib_ref.shape[0])
    loc.wait(*range(PLANES))
    total = gh1_ref[...]
    for g in range(4):
        total = total + dot(dproj_ref[g, :, 0:384], wv[g, :, 0:384], NT)
        folded = up(dproj_ref[g, 0 : rows // 2, 384:512])
        last[0 : rows // 2, 0:128] = jnp.where(lane < 64, folded, 0.0).astype(bf16)
        last[rows // 2 :, 0:128] = jnp.where(lane < 64, pltpu.roll(folded, 64, 1), 0.0).astype(bf16)
        last[:, 128:256] = dproj_ref[g, :, 512:640]
        total = total + dot(last[...], wv[g, :, 384:640], NT)
    gt_ref[...] = total.astype(bf16)


def vmem(shape, dtype=bf16):
    return pltpu.VMEM(shape, dtype)


ANY = pl.BlockSpec(memory_space=pl.ANY)
SMEM = pl.BlockSpec(memory_space=pltpu.SMEM)
VMEM = pl.BlockSpec(memory_space=pltpu.VMEM)
VMEM_BYTES = 60 * 2**20
SEMS = 112


def semaphores(line=False):
    counts = (SEMS, SEMS) + ((5 * 2, PLANES * 2) if line else ()) + (32,)
    return [pltpu.SemaphoreType.DMA((n,)) for n in counts]


def params(collective_id):
    return pltpu.CompilerParams(
        collective_id=collective_id, has_side_effects=True, vmem_limit_bytes=VMEM_BYTES
    )


def run_forward(lengths, tokens, w_qkv, w_in, w_back, w_out, *vectors):
    rows, width = tokens.shape
    shard = w_qkv.shape[0]
    hidden = w_in.shape[1]
    S = jax.ShapeDtypeStruct
    q_shape, kv_shape = (GROUP_HEADS, 4 * rows, 128), (GROUP_HEADS, 8 * rows, 128)
    return pl.pallas_call(
        forward_kernel,
        out_shape=(
            S(q_shape, bf16), S(kv_shape, bf16), S(kv_shape, bf16), S(q_shape, bf16),
            S((4, rows, width), bf16), S((4, rows, 256), bf16), S((PLANES, 16, width), bf16),
            S((PLANES * shard, hidden), bf16), S((width, width), bf16),
            S((CHIPS, shard, PACK), bf16), S((hidden, width), bf16),
        ),
        in_specs=[SMEM] + [ANY] * 5 + [VMEM] * 9,
        out_specs=[ANY] * 11,
        scratch_shapes=[
            vmem((4, rows, width)), vmem((width, PACK)), vmem(q_shape), vmem(kv_shape), vmem(kv_shape), vmem(q_shape),
            vmem((4, rows, 256)), vmem((4, rows, 256)), vmem((4, rows, 384)), vmem((4, rows, 384)),
            vmem((PLANES, 16, width)), vmem((shard, w_qkv.shape[1])), vmem((CHIPS, shard, PACK)),
            vmem((8, width), f32), vmem((8, 256), f32),
        ] + semaphores(line=True),
        compiler_params=params(1),
    )(lengths, tokens, w_qkv, w_in, w_back, w_out, *vectors)


def run_backward(do, do1, q, k, v, o, tok, grads, sums, back):
    rows = do.shape[1]
    width = tok.shape[2]
    shard = width // PLANES
    length, cols = grads.shape[3:]
    cut = length // 32 * 16
    S = jax.ShapeDtypeStruct
    ext = shard // 2 + 16
    return pl.pallas_call(
        backward_kernel,
        out_shape=(
            S((4, rows, PACK), bf16), S((2, 4, ext, 384), bf16), S((2, 4, ext, 256), bf16), S((2, 4, length, cols), bf16), S((2, 4) + back.shape[2:], bf16), S((16, width), bf16),
        ),
        in_specs=[ANY] * 10,
        out_specs=[ANY] * 6,
        scratch_shapes=[
            vmem((4, rows, 128)), vmem((4, rows, 128)), vmem(q.shape), vmem(k.shape), vmem(v.shape), vmem(o.shape), vmem(q.shape),
            vmem(tok.shape), vmem((width, 4 * rows)), vmem((128, 4 * rows), f32), vmem((4 * rows, 128), f32),
            vmem((4 * rows, 128), f32), vmem((3, 4 * rows, 128)), vmem((3, 4 * rows, 128)),
            vmem((4, rows, PACK)), vmem((4, rows // 2, 128)),
            *[vmem(lead + (ext, n)) for n in (384, 256) for lead in ((2, 4), (4,), (4,), (3,), (2, 4))],
            vmem((4, 4, length, cols)), vmem((4, 4, length, cols)),
            vmem((4, 2, cut, cols)), vmem((4, 2, length - cut, cols)), vmem((4, cut, cols)), vmem((4, length - cut, cols)),
            vmem((3, length, cols)), vmem((3,) + back.shape[2:]), vmem(back.shape[1:]),
            vmem((4, back.shape[2] // 2, cols)), vmem((4, back.shape[2] // 2, cols)), vmem((2, 4, length, cols)), vmem((2, 4) + back.shape[2:]),
            vmem((4, 4, 16, width)), vmem((3, 4, 16, width)), vmem((3, 16, width)), vmem((16, width)),
        ] + semaphores(),
        compiler_params=params(2),
    )(do, do1, q, k, v, o, tok, grads, sums, back)


def run_ffn(lengths, att, tokens, cotangent, full_in, w_in, full_out, w_out, small, full_back, w_back, wq):
    rows, width = tokens.shape
    hidden = w_in.shape[1]
    ch = hidden // 8
    S = jax.ShapeDtypeStruct
    one = S((rows, width), bf16)
    bp = w_back.shape[0] // 8
    return pl.pallas_call(
        ffn_kernel,
        out_shape=(
            one, S((rows, width), f32), S((4, rows, 128), bf16), S((4, rows, 128), bf16), S((2, 4, 4, width // 4 + 48, ch), bf16), S((4, 16, width), bf16),
            S((PLANES,) + wq.shape, bf16), S((3, 4, 2 * bp, ch), bf16),
        ),
        in_specs=[SMEM] + [VMEM] * 3 + [ANY] * 4 + [VMEM] + [ANY] * 3,
        out_specs=[ANY] * 5 + [VMEM] + [ANY] * 2,
        scratch_shapes=[
            vmem((width, hidden)), vmem((hidden, width)), vmem((width, width)),
            vmem((4, rows, 2 * ch)), vmem((4, rows, 2 * ch), f32), vmem((4, rows, 2 * ch)),
            vmem((rows, width), f32), vmem((rows, width), f32), vmem((rows, width), f32),
            vmem((rows, width)), vmem((width, rows)), vmem((rows, width)), vmem((rows, width), f32), vmem((4, 8, 2 * ch), f32),
            vmem((2, 4, 4, 2 * bp, ch)), vmem((4, 4, 2 * bp, ch)), vmem((4, 2, bp, ch)), vmem((4, 2, bp, ch)),
            vmem((2, 4, rows, 128)), vmem((4, rows, 128)),
            vmem((rows, width)), vmem((rows, width), f32), vmem((2, 4, 4, width // 4 + 48, ch)),
            pltpu.SemaphoreType.DMA((SEMS,)), pltpu.SemaphoreType.DMA((SEMS,)),
            pltpu.SemaphoreType.DMA((5,)), pltpu.SemaphoreType.DMA((PLANES,)), pltpu.SemaphoreType.DMA((32,)),
        ],
        compiler_params=params(3),
    )(lengths, att, tokens, cotangent, full_in, w_in, full_out, w_out, small, full_back, w_back, wq)


def run_final(dproj, wq_full, wq, gh1, gw, hw, fin, finb, sums):
    rows, width = gh1.shape
    shard = width // PLANES
    S = jax.ShapeDtypeStruct
    one = S((shard,), f32)
    return pl.pallas_call(
        final_kernel,
        out_shape=(
            S((rows, width), bf16), S((shard, 3 * width), f32), S((shard, 8 * fin.shape[3]), f32),
            S((2 * fin.shape[3], width), f32), S((shard, width), f32), one, one, one, one, one, one, one, one, S((width,), f32),
        ),
        in_specs=[VMEM, ANY, ANY] + [VMEM] * 6,
        out_specs=[VMEM] * 14,
        scratch_shapes=[vmem((4, width, PACK)), vmem((8, 256), f32), vmem((rows, 256)), pltpu.SemaphoreType.DMA((4,))],
        compiler_params=pltpu.CompilerParams(vmem_limit_bytes=VMEM_BYTES),
    )(dproj, wq_full, wq, gh1, gw, hw, fin, finb, sums)


def planned(
    tokens, lengths, w_qkv, q_bias, v_bias, w_out, out_bias, ln1_gain, ln1_bias,
    w_in, in_bias, w_back, back_bias, ln2_gain, ln2_bias, cotangent,
):
    vectors = (out_bias, ln1_gain, ln1_bias, back_bias, ln2_gain, ln2_bias, in_bias, q_bias, v_bias)
    q, k, v, o, tok_all, att, small_all, full_in, full_out, wq, full_back = run_forward(
        lengths, tokens[0], w_qkv, w_in, w_back, w_out, *vectors
    )
    output, gh1, do, do1, grads, sums, wq_full, back = run_ffn(
        lengths, att, tokens[0], cotangent[0], full_in, w_in, full_out, w_out, small_all, full_back, w_back, wq
    )
    dproj, gw, hw, fin, finb, sums_f = run_backward(do, do1, q, k, v, o, tok_all, grads, sums, back)
    gt, gqkv, gin, gback, gout, qb, vb, ob, g1, b1, bb, g2, b2, ib = run_final(dproj, wq_full, wq, gh1, gw, hw, fin, finb, sums_f)
    return (output[None], gt[None], gqkv, qb, vb, gout, ob, g1, b1, gin, ib, gback, bb, g2, b2)


masked_score = -1e30


def passed_along(block, axis, distance):
    devices = range(lax.axis_size(axis))
    route = [((i - distance) % len(devices), i) for i in devices]
    return lax.ppermute(block, axis, route)


def norm_forward(hidden, gain_vec, shift_vec):
    average = jnp.mean(hidden, axis=-1, keepdims=True)
    centred = hidden - average
    variance = jnp.mean(centred * centred, axis=-1, keepdims=True)
    inverse = lax.rsqrt(variance + 1e-05)
    normed = centred * inverse
    return (normed * gain_vec + shift_vec, normed, inverse)


def norm_backward(grad_norm, normed, inverse, gain_vec):
    scaled = grad_norm * gain_vec
    grad_input = inverse * (
        scaled
        - jnp.mean(scaled, axis=-1, keepdims=True)
        - normed * jnp.mean(scaled * normed, axis=-1, keepdims=True)
    )
    return (grad_input, jnp.sum(grad_norm * normed, axis=0), jnp.sum(grad_norm, axis=0))


def forward_tile(state_in, query_heads, key_pair, length):
    old_max, old_sum, old_acc = state_in
    key_rows = key_pair.shape[0]
    head_count = query_heads.shape[1]
    head_size = query_heads.shape[2]
    key_heads = key_pair[:, 0].reshape(key_rows, head_count, head_size)
    value_heads = key_pair[:, 1].reshape(key_rows, head_count, head_size)
    key_ok = jnp.arange(key_rows, dtype=jnp.int32) < length
    scores = jnp.einsum(
        "qhd,khd->hqk", query_heads, key_heads, preferred_element_type=jnp.float32
    ) * head_size ** (-0.5)
    scores = jnp.where(key_ok[None, None, :], scores, masked_score)
    new_max = jnp.maximum(old_max, jnp.max(scores, axis=2))
    prob_tile = jnp.where(key_ok[None, None, :], jnp.exp(scores - new_max[:, :, None]), 0.0)
    new_sum = jnp.sum(prob_tile, axis=2)
    new_acc = jnp.einsum(
        "hqk,khd->hqd",
        prob_tile.astype(jnp.bfloat16),
        value_heads,
        preferred_element_type=jnp.float32,
    )
    return (new_max, new_sum, new_acc)


def backward_tile(query_pair, log_total, delta, key_pair, key_start, length):
    query_rows = query_pair.shape[0]
    key_rows = key_pair.shape[0]
    model_width = query_pair.shape[2]
    head_count = log_total.shape[0]
    head_size = model_width // head_count
    score_scale = head_size ** (-0.5)
    query_heads = query_pair[:, 0].reshape(query_rows, head_count, head_size)
    grad_heads = query_pair[:, 1].reshape(query_rows, head_count, head_size)
    key_heads = key_pair[:, 0].reshape(key_rows, head_count, head_size)
    value_heads = key_pair[:, 1].reshape(key_rows, head_count, head_size)
    key_ok = key_start + jnp.arange(key_rows, dtype=jnp.int32) < length
    scores = (
        jnp.einsum("qhd,khd->hqk", query_heads, key_heads, preferred_element_type=jnp.float32)
        * score_scale
    )
    prob_tile = jnp.where(key_ok[None, None, :], jnp.exp(scores - log_total[:, :, None]), 0.0)
    grad_values = jnp.einsum(
        "hqk,qhd->khd",
        prob_tile.astype(jnp.bfloat16),
        grad_heads,
        preferred_element_type=jnp.float32,
    )
    grad_probs = jnp.einsum(
        "qhd,khd->hqk", grad_heads, value_heads, preferred_element_type=jnp.float32
    )
    grad_scores = (prob_tile * (grad_probs - delta[:, :, None])).astype(jnp.bfloat16)
    grad_queries = (
        jnp.einsum("hqk,khd->qhd", grad_scores, key_heads, preferred_element_type=jnp.float32)
        * score_scale
    )
    grad_keys = (
        jnp.einsum("hqk,qhd->khd", grad_scores, query_heads, preferred_element_type=jnp.float32)
        * score_scale
    )
    grad_pair = jnp.stack([grad_keys, grad_values], axis=1).reshape(key_rows, 2, model_width)
    return (grad_queries.reshape(query_rows, model_width), grad_pair)


def on_device(
    tokens,
    lengths,
    w_qkv,
    q_bias,
    v_bias,
    w_out,
    out_bias,
    ln1_gain,
    ln1_bias,
    w_in,
    in_bias,
    w_back,
    back_bias,
    ln2_gain,
    ln2_bias,
    cotangent,
):
    gathered = tuple(
        lax.all_gather(a, "fsdp", axis=0, tiled=True)
        for a in (
            w_qkv, q_bias, v_bias, w_out, out_bias, ln1_gain, ln1_bias, w_in, in_bias, w_back, back_bias, ln2_gain, ln2_bias
        )
    )
    (
        full_qkv,
        full_qbias,
        full_vbias,
        full_out,
        full_obias,
        full_g1,
        full_n1,
        full_in,
        full_ibias,
        full_back,
        full_bbias,
        full_g2,
        full_n2,
    ) = gathered
    f32 = jnp.float32
    seq_index = lax.axis_index("seq")
    seq_count = lax.axis_size("seq")
    token_rows = tokens.shape[1]
    model_width = tokens.shape[2]
    head_count = HEADS
    head_size = model_width // head_count
    length = lengths[0]
    my_start = seq_index * token_rows
    row_valid = (my_start + jnp.arange(token_rows, dtype=jnp.int32) < length).astype(f32)
    inputs_b = tokens[0]
    inputs_f = inputs_b.astype(f32)
    bias_all = jnp.concatenate(
        [full_qbias.astype(f32), jnp.zeros((model_width,), f32), full_vbias.astype(f32)]
    )
    projected = (jnp.dot(inputs_b, full_qkv, preferred_element_type=f32) + bias_all).astype(
        jnp.bfloat16
    )
    query_heads = projected[:, :model_width].reshape(token_rows, head_count, head_size)
    key_pair = projected[:, model_width:].reshape(token_rows, 2, model_width)
    init_state = (
        jnp.full((head_count, token_rows), masked_score, f32),
        jnp.zeros((head_count, token_rows), f32),
        jnp.zeros((head_count, token_rows, head_size), f32),
    )
    pieces = lax.all_gather(key_pair, "seq", axis=0, tiled=True)
    run_max, run_sum, run_acc = forward_tile(init_state, query_heads, pieces, length)
    positive = run_sum > 0.0
    safe_sum = jnp.where(positive, run_sum, 1.0)
    attended_heads = jnp.where(positive[:, :, None], run_acc / safe_sum[:, :, None], 0.0)
    log_total = jnp.where(positive, run_max + jnp.log(safe_sum), 0.0)
    attended_f = attended_heads.transpose(1, 0, 2).reshape(token_rows, model_width)
    attended_b = attended_f.astype(jnp.bfloat16)
    branch_f = jnp.dot(attended_b, full_out, preferred_element_type=f32) + full_obias.astype(f32)
    first_norm, normed_one, inverse_one = norm_forward(
        inputs_f + branch_f, full_g1.astype(f32), full_n1.astype(f32)
    )
    first_low = first_norm.astype(jnp.bfloat16)
    inner_act = jnp.dot(first_low, full_in, preferred_element_type=f32) + full_ibias.astype(f32)
    activated_b = jax.nn.gelu(inner_act, approximate=False).astype(jnp.bfloat16)
    second = jnp.dot(activated_b, full_back, preferred_element_type=f32) + full_bbias.astype(f32)
    result, normed_two, inverse_two = norm_forward(
        first_norm + second, full_g2.astype(f32), full_n2.astype(f32)
    )
    output = (result * row_valid[:, None]).astype(jnp.bfloat16)
    grad_result = cotangent[0].astype(f32) * row_valid[:, None]
    grad_h2, g_ln2_gain, g_ln2_bias = norm_backward(
        grad_result, normed_two, inverse_two, full_g2.astype(f32)
    )
    grad_second = grad_h2.astype(jnp.bfloat16)
    g_w_back = jnp.einsum("tf,td->fd", activated_b, grad_second, preferred_element_type=f32)
    g_back_bias = jnp.sum(grad_second.astype(f32), axis=0)
    grad_act = jnp.einsum("td,fd->tf", grad_second, full_back, preferred_element_type=f32)
    gelu_value, gelu_pull = jax.vjp(
        lambda values_in: jax.nn.gelu(values_in, approximate=False), inner_act
    )
    grad_inner = gelu_pull(grad_act)[0].astype(jnp.bfloat16)
    g_w_in = jnp.einsum("td,tf->df", first_low, grad_inner, preferred_element_type=f32)
    g_in_bias = jnp.sum(grad_inner.astype(f32), axis=0)
    grad_first = grad_h2 + jnp.einsum("tf,df->td", grad_inner, full_in, preferred_element_type=f32)
    grad_h1, g_ln1_gain, g_ln1_bias = norm_backward(
        grad_first, normed_one, inverse_one, full_g1.astype(f32)
    )
    grad_branch = grad_h1.astype(jnp.bfloat16)
    g_w_out = jnp.einsum("tc,td->cd", attended_b, grad_branch, preferred_element_type=f32)
    g_out_bias = jnp.sum(grad_branch.astype(f32), axis=0)
    grad_attended = jnp.einsum(
        "td,cd->tc", grad_branch, full_out, preferred_element_type=f32
    ).astype(jnp.bfloat16)
    delta = jnp.sum(
        (grad_attended.astype(f32) * attended_f).reshape(token_rows, head_count, head_size), axis=2
    ).T
    query_pair = jnp.stack([projected[:, :model_width], grad_attended], axis=1)
    zero_rows = jnp.zeros((token_rows, model_width), f32)
    zero_pair = jnp.zeros((token_rows, 2, model_width), f32)

    def visit_keys(hop_index, grad_q, moving_pair, grad_pair):
        anchor = (seq_index - hop_index) % seq_count
        add_q, add_pair = backward_tile(
            query_pair, log_total, delta, moving_pair, anchor * token_rows, length
        )
        return (grad_q + add_q, grad_pair + add_pair)

    def return_key_grads(grad_pair):
        return passed_along(grad_pair.astype(jnp.bfloat16), "seq", 1).astype(grad_pair.dtype)

    def key_hop(hop_index, loop_state):
        grad_q, moving_pair, grad_pair = loop_state
        grad_q, grad_pair = visit_keys(hop_index, grad_q, moving_pair, grad_pair)
        moved = passed_along(moving_pair, "seq", 1)
        return (grad_q, moved, return_key_grads(grad_pair))

    grad_q, moving_pair, grad_pair = lax.fori_loop(
        0, seq_count - 1, key_hop, (zero_rows, key_pair, zero_pair)
    )
    grad_q, grad_pair = visit_keys(seq_count - 1, grad_q, moving_pair, grad_pair)
    grad_pair = return_key_grads(grad_pair)
    grad_projected = jnp.concatenate(
        [grad_q, grad_pair.reshape(token_rows, 2 * model_width)], axis=1
    ).astype(jnp.bfloat16)
    g_w_qkv = jnp.einsum("td,te->de", inputs_b, grad_projected, preferred_element_type=f32)
    grad_proj_f = grad_projected.astype(f32)
    g_q_bias = jnp.sum(grad_proj_f[:, :model_width], axis=0)
    g_v_bias = jnp.sum(grad_proj_f[:, 2 * model_width :], axis=0)
    grad_input = grad_h1 + jnp.einsum(
        "te,de->td", grad_projected, full_qkv, preferred_element_type=f32
    )
    local_grads = (
        g_w_qkv,
        g_q_bias,
        g_v_bias,
        g_w_out,
        g_out_bias,
        g_ln1_gain,
        g_ln1_bias,
        g_w_in,
        g_in_bias,
        g_w_back,
        g_back_bias,
        g_ln2_gain,
        g_ln2_bias,
    )
    owned = [
        lax.psum_scatter(a.astype(jnp.bfloat16), "fsdp", scatter_dimension=0, tiled=True).astype(jnp.float32)
        for a in local_grads
    ]
    totals = [lax.psum(a.astype(jnp.bfloat16), "seq").astype(jnp.float32) for a in owned]
    return (output[None], grad_input.astype(jnp.bfloat16)[None]) + tuple(totals)


def solution(mesh):
    spread, vector, matrix = P("fsdp", "seq", None), P("fsdp"), P("fsdp", None)
    fits = mesh.shape["seq"] == 2 * CHIPS and mesh.shape["fsdp"] == PLANES
    return jax.shard_map(
        planned if fits else on_device,
        mesh=mesh,
        in_specs=(spread, vector, matrix, vector, vector, matrix) + (vector,) * 3
        + (matrix, vector, matrix) + (vector,) * 3 + (spread,),
        out_specs=(spread, spread, matrix, vector, vector, matrix) + (vector,) * 3
        + (matrix, vector, matrix) + (vector,) * 3,
        check_vma=False,
    )
```

```python
import functools
import math

import jax
import jax.numpy as jnp
from jax import lax
from jax.experimental import pallas as pl
from jax.experimental.pallas import tpu as pltpu
from jax.sharding import PartitionSpec as P

HEADS = 12
bf16 = jnp.bfloat16
f32 = jnp.float32
MESH = pl.DeviceIdType.MESH
LOG2E = math.log2(math.e)
NT = (((1,), (1,)), ((), ()))
NN = (((1,), (0,)), ((), ()))

PLANES = 4
CHIPS = 4
GROUP_HEADS = 3
PACKED = (12, 24, 13, 25, 0, 1, 2, None, 14, 26)
KV_TILE = (0, 1, 4)
PACK = 640


(
    K_ACC, K_ATT0, K_ATT1, K_ATT_O, K_B1, K_B2, K_B3X, K_B3Y, K_BACK, K_BACK_O, K_BM, K_DO, K_DO_O, K_DP,
    K_DP_O, K_F, K_F1, K_F2, K_F3X, K_F3Y, K_FINB_O, K_FIN_O, K_FM, K_G, K_GW_O, K_H, K_HW_O, K_IN, K_K, K_KV,
    K_K_O, K_M, K_O, K_OUT, K_O_O, K_Q, K_QKV, K_Q_O, K_R1, K_RAW, K_RZ, K_RZB, K_S0, K_S1, K_S2, K_SMALL,
    K_SMALL_O, K_SUMS, K_SUMS_O, K_SZ, K_T1A, K_T1B, K_T2A, K_T2B, K_T3A, K_T3B, K_TOK, K_TOK_O, K_V, K_V_O,
    K_WQ, K_WQM, K_WQ_O, K_X1, K_X2, K_Y1, K_Y2, K_Z,
    K_GH1, K_RES, K_GR, K_DO1,
) = range(100, 172)


def dot(a, b, dims=NN):
    return lax.dot_general(a, b, dims, preferred_element_type=f32)


class Net:
    def __init__(self, send_sems, recv_sems):
        self.send_sems, self.recv_sems = send_sems, recv_sems
        self.specs = {}

    def add(self, name, src, dst, device):
        self.specs[name] = (len(self.specs), src, dst, device)

    def get(self, name):
        k, src, dst, device = self.specs[name]
        return pltpu.make_async_remote_copy(
            src_ref=src(),
            dst_ref=dst(),
            send_sem=self.send_sems.at[k],
            recv_sem=self.recv_sems.at[k],
            device_id=device,
            device_id_type=MESH,
        )

    def start(self, *names):
        for name in names:
            self.get(name).start()

    def recv(self, *names):
        for name in names:
            self.get(name).wait_recv()

    def sent(self, *names):
        for name in names:
            self.get(name).wait_send()


class Local:
    def __init__(self, sems):
        self.sems = sems
        self.specs = {}

    def add(self, name, src, dst):
        self.specs[name] = (len(self.specs), src, dst)

    def get(self, name):
        k, src, dst = self.specs[name]
        return pltpu.make_async_copy(src(), dst(), self.sems.at[k])

    def start(self, *names):
        for name in names:
            self.get(name).start()

    def wait(self, *names):
        for name in names:
            self.get(name).wait()


class Line:
    def __init__(self, s, z, send_sems, recv_sems):
        high = lax.div(z, 2)
        self.s, self.z = s, z
        self.order = [z, 1 - z + 4 * high, 2 - high, 3 - 3 * high]
        self.has_right, self.has_left = z < PLANES - 1, z > 0
        self.right, self.left = jnp.minimum(z + 1, PLANES - 1), jnp.maximum(z - 1, 0)
        self.middle = jnp.logical_and(self.has_right, self.has_left)
        self.end = jnp.logical_not(self.middle)
        self.send_sems, self.recv_sems = send_sems, recv_sems
        self.specs = {}

    def add(self, name, own, place):
        self.specs[name] = (len(self.specs), own, place)

    def copy(self, name, i, to_right=False):
        n, own, place = self.specs[name]
        zz = self.order[i]
        if i:
            target = jnp.where(zz < self.z, self.right, self.left)
        else:
            target = self.right if to_right else self.left
        return pltpu.make_async_remote_copy(
            src_ref=place(zz) if i else own(),
            dst_ref=place(zz),
            send_sem=self.send_sems.at[n * 5 + (i + 1 if i else int(to_right))],
            recv_sem=self.recv_sems.at[n * PLANES + zz],
            device_id=(self.s, target),
            device_id_type=MESH,
        )

    def start(self, *names):
        for name in names:
            pl.when(self.has_right)(lambda: self.copy(name, 0, True).start())
            pl.when(self.has_left)(lambda: self.copy(name, 0).start())

    def pass_on(self, name, i):
        self.copy(name, i).wait_recv()
        self.copy(name, i).start()

    def step(self, n, *names):
        for name in names:
            if n == 1:
                @pl.when(self.middle)
                def _():
                    self.pass_on(name, 1)
                    self.pass_on(name, 2)

                pl.when(self.end)(lambda: self.copy(name, 1).wait_recv())
            elif n == 2:
                pl.when(self.middle)(lambda: self.pass_on(name, 3))
                pl.when(self.end)(lambda: self.copy(name, 2).wait_recv())
            else:
                pl.when(self.end)(lambda: self.copy(name, 3).wait_recv())

    def sent(self):
        for name in self.specs:
            pl.when(self.has_right)(lambda: self.copy(name, 0, True).wait_send())
            pl.when(self.has_left)(lambda: self.copy(name, 0).wait_send())

            @pl.when(self.middle)
            def _():
                for i in (1, 2, 3):
                    self.copy(name, i).wait_send()


def coordinates():
    s, z = lax.axis_index("seq"), lax.axis_index("fsdp")
    core = lax.rem(s, 2)
    chip = lax.div(s, 2)
    return s, z, core, chip


def flip(value, mask):
    low, high = lax.rem(value, 2), lax.div(value, 2)
    if mask & 1:
        low = 1 - low
    if mask & 2:
        high = 1 - high
    return high * 2 + low


def hello(devices):
    barrier = pltpu.get_barrier_semaphore()
    for device in devices:
        pl.semaphore_signal(barrier, inc=1, device_id=device, device_id_type=MESH)


def met(count):
    pl.semaphore_wait(pltpu.get_barrier_semaphore(), count)


def greet(devices):
    hello(devices)
    met(len(devices))


def lanes_of(rows=1):
    return lax.broadcasted_iota(jnp.int32, (rows, 128), 1)


def split3(column):
    hi = column.astype(bf16).astype(f32)
    mid = (column - hi).astype(bf16).astype(f32)
    return hi, mid, column - hi - mid


def forward_kernel(
    length_ref, tok_ref, wraw_ref, win_ref, wback_ref, wout_ref,
    ob_ref, g1_ref, n1_ref, bb_ref, g2_ref, n2_ref, ib_ref, qb_ref, vb_ref,
    q_out, k_out, v_out, o_out, tok_out, att_out, small_out, win_full, wout_full, wq_out, wback_full,
    tok, wqv, q_s, k_s, v_s, o_s, att, atts, kvs, kvr, small, wraw, wq_ref, vec_s, vec_v, send_sems, recv_sems, line_send, line_recv, local_sems,
):
    s, z, core, chip = coordinates()
    other = 1 - core
    rows = tok_ref.shape[0]
    half = rows // 2
    shard = wq_ref.shape[1]
    piece = shard // 2
    peer = [None] + [(flip(chip, j) * 2 + core, z) for j in (1, 2, 3)]
    mate = (chip * 2 + other, z)
    plane = [None] + [(s, flip(z, dz)) for dz in (1, 2, 3)]
    zs = [z] + [flip(z, dz) for dz in (1, 2, 3)]
    net, loc = Net(send_sems, recv_sems), Local(local_sems)
    width = win_full.shape[1] // 8
    back = wback_ref.shape[0]
    bpiece = back // 8
    hops = [(K_IN, 1), (K_IN, 2), (K_IN, 3), (K_BACK, 1)]
    at = lambda start, size, unit=16: pl.ds(pl.multiple_of(start, unit), size)

    def part(a, zz, m, c):
        if a == K_IN:
            return win_full.at[at(zz * shard, shard), at((m * 4 + c) * width, width, 128)]
        if a == K_BACK:
            return wback_full.at[at(zz * back + (m * 4 + c) * bpiece, bpiece), :]
        return wout_full.at[at(zz * shard + c * (shard // 4), shard // 4), at(m * width, width, 128)]

    def own_part(a, m, c):
        if a == K_IN:
            return win_ref.at[:, at((m * 4 + c) * width, width, 128)]
        if a == K_BACK:
            return wback_ref.at[at((m * 4 + c) * bpiece, bpiece), :]
        return wout_ref.at[at(c * (shard // 4), shard // 4), at(m * width, width, 128)]

    def side(a, zz, m):
        if a == K_IN:
            return win_full.at[at(zz * shard, shard), at(m * 4 * width, 4 * width, 128)]
        if a == K_BACK:
            return wback_full.at[at(zz * back + m * 4 * bpiece, 4 * bpiece), :]
        return wout_full.at[at(zz * shard, shard), at(m * width, width, 128)]

    line = Line(s, z, line_send, line_recv)
    lines = line.order
    line.add(K_BACK, lambda: own_part(K_BACK, core, chip), lambda zz: part(K_BACK, zz, core, chip))
    line.add(K_OUT, lambda: wout_ref.at[:, at(core * width, width, 128)], lambda zz: side(K_OUT, zz, core))

    for dz in (1, 2, 3):
        net.add((K_WQ, dz), lambda: wq_ref.at[chip, pl.ds(pl.multiple_of(core * piece, 16), piece), :],
                lambda: wqv.at[pl.ds(pl.multiple_of(z * shard + core * piece, 16), piece), :], plane[dz])
        net.add((K_WQM, dz), lambda dz=dz: wqv.at[pl.ds(pl.multiple_of(zs[dz] * shard + core * piece, 16), piece), :],
                lambda dz=dz: wqv.at[pl.ds(pl.multiple_of(zs[dz] * shard + core * piece, 16), piece), :], mate)
        net.add((K_SMALL, dz), lambda: small.at[z], lambda: small.at[z], plane[dz])
    top, bottom = slice(0, half), slice(half, rows)
    net.add(K_T1A, lambda: tok_ref.at[top], lambda: tok.at[1, top], peer[1])
    net.add(K_T1B, lambda: tok_ref.at[bottom], lambda: tok.at[1, bottom], peer[1])
    net.add(K_T2B, lambda: tok_ref.at[bottom], lambda: tok.at[2, bottom], peer[2])
    net.add(K_T2A, lambda: tok_ref.at[top], lambda: tok.at[2, top], peer[2])
    net.add(K_T3A, lambda: tok.at[1, top], lambda: tok.at[3, top], peer[2])
    net.add(K_T3B, lambda: tok.at[2, bottom], lambda: tok.at[3, bottom], peer[1])
    for j in range(4):
        net.add((K_KV, j), lambda j=j: kvs.at[j], lambda j=j: kvr.at[j], mate)
    for j in (1, 2, 3):
        net.add((K_ATT0, j), lambda j=j: atts.at[j, :, 0:128], lambda: att.at[chip, :, 0:128], peer[j])
        net.add((K_ATT1, j), lambda j=j: atts.at[j, :, 128:256], lambda: att.at[chip, :, 128:256], peer[j])
    where = {K_IN: zs, K_BACK: lines, K_OUT: lines}
    for a, dz in hops:
        place = lambda c, a=a, dz=dz: part(a, where[a][dz], core, c)

        def half_place(c, n, a=a, dz=dz):
            zz = where[a][dz]
            if a == K_IN:
                return win_full.at[at(zz * shard + n * piece, piece), at((core * 4 + c) * width, width, 128)]
            return wback_full.at[at(zz * back + (core * 4 + c) * bpiece + n * (bpiece // 2), bpiece // 2), :]

        for j in (1, 2):
            net.add((a, j, dz), lambda place=place: place(chip), lambda place=place: place(chip), peer[j])
        for n, via, last in ((0, 1, 2), (1, 2, 1)):
            there = lambda half_place=half_place, n=n, via=via: half_place(flip(chip, via), n)
            net.add((a, 3 + n, dz), there, there, peer[last])
    for dz in (1, 2, 3):
        net.add((K_IN, K_Z, dz), lambda: own_part(K_IN, core, chip), lambda: part(K_IN, z, core, chip), plane[dz])
    mates = hops + [(K_OUT, dz) for dz in (1, 2, 3)]
    for a, dz in mates:
        net.add((a, K_M, dz), lambda a=a, dz=dz: side(a, where[a][dz], core), lambda a=a, dz=dz: side(a, where[a][dz], core), mate)
    loc.add(K_RAW, lambda: wraw_ref, lambda: wraw)
    loc.add(K_TOK, lambda: tok_ref, lambda: tok.at[0])
    loc.add(K_WQ, lambda: wq_ref.at[chip], lambda: wqv.at[pl.ds(pl.multiple_of(z * shard, 16), shard), :])
    outs = ((K_WQ_O, wq_ref, wq_out), (K_K_O, k_s, k_out), (K_V_O, v_s, v_out), (K_Q_O, q_s, q_out), (K_O_O, o_s, o_out),
            (K_TOK_O, tok, tok_out), (K_ATT_O, att, att_out), (K_SMALL_O, small, small_out))
    for name, src, dst in outs:
        loc.add(name, lambda src=src: src, lambda dst=dst: dst)

    loc.start(K_RAW, K_TOK)
    greet(peer[1:] + [mate] + plane[1:])
    net.start(K_T1A, K_T2B, K_T1B, K_T2A)
    lane = lanes_of()
    loc.wait(K_RAW)
    for g in range(CHIPS):
        for t in range(PACK // 128):
            halves = []
            for upper in (0, 1):
                block = PACKED[2 * t + upper]
                if block is None:
                    halves.append(0.0)
                    continue
                block += GROUP_HEADS * g
                tile_of = lambda i: wraw[:, i * 128 : (i + 1) * 128].astype(f32)
                halves.append(half_tile(tile_of, block, upper))
            wq_ref[g, :, t * 128 : (t + 1) * 128] = jnp.where(lane < 64, halves[0], halves[1]).astype(bf16)
    loc.start(K_WQ, K_WQ_O)
    net.start(*[(K_WQ, dz) for dz in (1, 2, 3)])
    vec_s[...] = jnp.zeros_like(vec_s)
    vec_v[...] = jnp.zeros_like(vec_v)
    for i, ref in enumerate((ob_ref, g1_ref, n1_ref, bb_ref, g2_ref, n2_ref)):
        vec_s[i : i + 1, 0:shard] = ref[...].astype(f32).reshape(1, shard)
    vec_s[6:7, :] = ib_ref[...].astype(f32).reshape(1, ib_ref.shape[0])
    vec_s[7:8, 256 : 256 + shard] = qb_ref[...].astype(f32).reshape(1, shard)
    vec_v[0:1, 0:shard] = vb_ref[...].astype(f32).reshape(1, shard)
    first, last = vec_v[:, 0:128], vec_v[:, 128:256]
    for t, tile in ((0, pltpu.roll(first, 64, 1)), (1, first), (4, pltpu.roll(last, 64, 1))):
        vec_s[7:8, t * 128 : (t + 1) * 128] = jnp.where(lane < 64, 0.0, tile[0:1])
    small[z] = jnp.concatenate([vec_s[...], jnp.zeros_like(vec_s)], axis=0).astype(bf16)
    net.start(*[(K_SMALL, dz) for dz in (1, 2, 3)])
    for dz in (1, 2, 3):
        net.recv((K_WQ, dz))
        net.start((K_WQM, dz))
    net.start(*[(K_IN, K_Z, dz) for dz in (1, 2, 3)])
    loc.wait(K_TOK, K_WQ)
    for dz in (1, 2, 3):
        net.recv((K_SMALL, dz), (K_WQM, dz))

    length = length_ref[0]
    bias = small[chip, 7:8, 0:PACK].astype(f32)

    def keep(tile, h, slot, block):
        position = block * rows + lax.broadcasted_iota(jnp.int32, (rows, 1), 0)
        mask = jnp.where(position < length, 0.0, -1e30).astype(f32)
        ones = jnp.where((lane > 64) & (lane < 68), 1.0, 0.0)
        k_s[h, slot * rows : (slot + 1) * rows, :] = jnp.where(
            lane < 64, tile, jnp.where(lane == 64, mask, ones)
        ).astype(bf16)
        v_s[h, slot * rows : (slot + 1) * rows, :] = jnp.where(
            lane < 64, pltpu.roll(tile, 64, 1), jnp.where(lane < 67, 1.0, 0.0)
        ).astype(bf16)

    def project(j):
        proj = dot(tok[j], wqv[...]) + bias
        for h in range(GROUP_HEADS):
            tile = proj[:, KV_TILE[h] * 128 : (KV_TILE[h] + 1) * 128]
            keep(tile.astype(bf16).astype(f32), h, j, flip(chip, j) * 2 + core)
            kvs[j, :, h * 128 : (h + 1) * 128] = tile.astype(bf16)
            first = 256 + (h // 2) * 128
            tile = proj[:, first : first + 128].astype(bf16).astype(f32) * 0.125
            if h == 1:
                tile = pltpu.roll(tile, 64, 1)
            q_s[h, j * rows : (j + 1) * rows, :] = jnp.where(
                lane < 64, tile, jnp.where(lane == 64, 1.0, 0.0)
            ).astype(bf16)
        net.start((K_KV, j))

    def keep_other(j):
        net.recv((K_KV, j))
        for h in range(GROUP_HEADS):
            tile = kvr[j, :, h * 128 : (h + 1) * 128].astype(f32)
            keep(tile, h, 4 + j, flip(chip, j) * 2 + other)

    def first_hop(a, dz):
        net.start((a, 1, dz), (a, 2, dz))

    def second_hop(a, dz):
        net.recv((a, 1, dz))
        net.start((a, 3, dz))
        net.recv((a, 2, dz))
        net.start((a, 4, dz))

    def third_hop(a, dz):
        net.recv((a, 3, dz), (a, 4, dz))
        net.start((a, K_M, dz))

    project(0)
    net.recv(K_T1A)
    net.start(K_T3A)
    net.recv(K_T2B)
    net.start(K_T3B)
    net.recv(K_T1B)
    project(1)
    net.recv(K_T2A)
    project(2)
    keep_other(0)
    keep_other(1)
    keep_other(2)
    net.recv((K_IN, K_Z, 1))
    first_hop(K_IN, 1)
    line.start(K_BACK, K_OUT)
    net.recv(K_T3A, K_T3B)
    project(3)
    keep_other(3)
    loc.start(K_K_O, K_V_O, K_TOK_O, K_SMALL_O)

    query_tile, key_chunk = 2 * rows, 4 * rows
    tiles = 4 * rows // query_tile
    chunks = 8 * rows // key_chunk

    def attended_tile(which):
        for j in range(4):
            r = slice(j * rows, (j + 1) * rows)
            if which == 0:
                upper = pltpu.roll(o_s[1, r, :].astype(f32), 64, 1)
                value = jnp.where(lane < 64, o_s[0, r, :].astype(f32), upper)
            else:
                value = jnp.where(lane < 64, o_s[2, r, :].astype(f32), 0.0)
            place = slice(which * 128, (which + 1) * 128)
            if j == 0:
                att[chip, :, place] = value.astype(bf16)
            else:
                atts[j, :, place] = value.astype(bf16)
                net.start(((K_ATT0, K_ATT1)[which], j))

    def in_hop(dz):
        net.recv((K_IN, K_Z, dz))
        first_hop(K_IN, dz)

    stages = {
        0: lambda: (in_hop(2), in_hop(3)),
        1: lambda: line.step(1, K_BACK, K_OUT),
        2: lambda: (second_hop(K_IN, 1), first_hop(K_BACK, 1)),
        4: lambda: second_hop(K_IN, 2),
        5: lambda: (third_hop(K_IN, 1), line.step(2, K_BACK, K_OUT)),
        6: lambda: second_hop(K_IN, 3),
        7: lambda: (attended_tile(0), third_hop(K_IN, 2)),
        8: lambda: second_hop(K_BACK, 1),
        9: lambda: third_hop(K_IN, 3),
        10: lambda: (line.step(3, K_BACK, K_OUT), [net.start((K_OUT, K_M, dz)) for dz in (1, 2, 3)]),
        11: lambda: (attended_tile(1), third_hop(K_BACK, 1)),
    }

    def progress(n):
        for at, work in stages.items():
            pl.when(n == at)(lambda work=work: (work(), None)[1])

    def visit(t, carry):
        h, i = lax.div(t, tiles), lax.rem(t, tiles)
        qrows = pl.ds(pl.multiple_of(i * query_tile, query_tile), query_tile)
        q = q_s[h, qrows, :]
        top_score = jnp.full((query_tile, 1), -1e30, f32)
        acc = jnp.zeros((query_tile, 128), f32)
        for c in range(chunks):
            krows = slice(c * key_chunk, (c + 1) * key_chunk)
            scores = dot(q, k_s[h, krows, :], NT)
            new_top = jnp.maximum(top_score, jnp.max(scores, axis=1, keepdims=True))
            probs = jnp.exp2((scores - new_top) * LOG2E)
            fade = jnp.exp2((top_score - new_top) * LOG2E)
            acc = acc * fade + dot(probs.astype(bf16), v_s[h, krows, :])
            top_score = new_top
            if c < chunks - 1:
                progress(t * chunks + c)
        total = acc[:, 64:65]
        o_s[h, qrows, :] = (acc / total).astype(bf16)
        hi, mid, low = split3(-(top_score + jnp.log(total)))
        wide = q.astype(f32)
        wide = jnp.where(lane == 65, hi, jnp.where(lane == 66, mid, jnp.where(lane == 67, low, wide)))
        q_s[h, qrows, :] = wide.astype(bf16)
        progress(t * chunks + chunks - 1)
        return carry

    lax.fori_loop(0, GROUP_HEADS * tiles, visit, 0)
    loc.start(K_Q_O, K_O_O)
    for j in (1, 2, 3):
        net.recv((K_ATT0, j), (K_ATT1, j))
    loc.start(K_ATT_O)
    net.recv(*[(a, K_M, dz) for a, dz in mates])
    for name in net.specs:
        net.sent(name)
    line.sent()
    loc.wait(*[name for name, _, _ in outs])


def backward_kernel(
    do_ref, do1_ref, q_ref, k_ref, v_ref, o_ref, tok_ref, grads_ref, sums_ref, back_ref,
    dproj_out, gw_out, hw_out, fin_out, finb_out, sums_out,
    do_s, do1_s, q_s, k_s, v_s, o_s, doa, tok, tokt, dqs, dq_keep, kv_own, kvs, kvr, dall, fold,
    gw, gwr, gz, gzr, gwf, hw, hwr, hz, hzr, hwf, acc, rb, rx, ry, rx2, ry2, rz, rzb, backv, bx2, by2, fin, finb, sums, sums_r, sums_z, sums_f,
    send_sems, recv_sems, local_sems,
):
    s, z, core, chip = coordinates()
    other = 1 - core
    rows = do_ref.shape[1]
    peer = [None] + [(flip(chip, j) * 2 + core, z) for j in (1, 2, 3)]
    mate = (chip * 2 + other, z)
    plane = [None] + [(s, flip(z, dz)) for dz in (1, 2, 3)]
    zs = [z] + [flip(z, dz) for dz in (1, 2, 3)]
    ch = [chip] + [flip(chip, j) for j in (1, 2, 3)]
    net, loc = Net(send_sems, recv_sems), Local(local_sems)
    length = grads_ref.shape[3]
    cut = length // 32 * 16
    xs, ys = slice(0, cut), slice(cut, length)
    shard = tok.shape[2] // PLANES
    piece = shard // 2

    for h in range(GROUP_HEADS):
        net.add((K_KV, h), lambda h=h: kvs.at[h], lambda h=h: kvr.at[h], mate)
        kv_cols = slice(KV_TILE[h] * 128, KV_TILE[h] * 128 + 128)
        for j in (1, 2, 3):
            net.add((K_DP, h, j), lambda j=j, cols=kv_cols: dall.at[j, :, cols],
                    lambda cols=kv_cols: dproj_out.at[chip, :, cols], peer[j])
    for j in (1, 2, 3):
        net.add((K_DP, K_Q, j), lambda j=j: dall.at[j, :, 256:384], lambda: dproj_out.at[chip, :, 256:384], peer[j])
        net.add((K_DP, K_O, j), lambda j=j: fold.at[j], lambda: dproj_out.at[chip, 0 : rows // 2, 384:512], peer[j])
    loc.add((K_DP, 0), lambda: dall.at[0, :, 0:384], lambda: dproj_out.at[chip, :, 0:384])
    loc.add((K_DP, 1), lambda: dall.at[0, :, 512:640], lambda: dproj_out.at[chip, :, 512:640])
    loc.add((K_DP, 2), lambda: fold.at[0], lambda: dproj_out.at[chip, 0 : rows // 2, 384:512])
    for j in (1, 2, 3):
        net.add((K_DO, j), lambda j=j: do1_ref.at[ch[j]], lambda j=j: do1_s.at[j], peer[j])
    order = (3, 2, 1, 0)
    for dz in order:
        net.add((K_R1, dz), lambda dz=dz: grads_ref.at[other, zs[dz]], lambda dz=dz: rb.at[zs[dz]], mate)
        for n, j in enumerate((1, 3)):
            net.add((K_X1, n, dz), lambda dz=dz, j=j: acc.at[zs[dz], ch[j], xs], lambda dz=dz, n=n: rx.at[zs[dz], n], peer[1])
        net.add((K_X2, dz), lambda dz=dz: acc.at[zs[dz], ch[2], xs], lambda dz=dz: rx2.at[zs[dz]], peer[2])
        for n, j in enumerate((2, 3)):
            net.add((K_Y1, n, dz), lambda dz=dz, j=j: acc.at[zs[dz], ch[j], ys], lambda dz=dz, n=n: ry.at[zs[dz], n], peer[2])
        net.add((K_Y2, dz), lambda dz=dz: acc.at[zs[dz], ch[1], ys], lambda dz=dz: ry2.at[zs[dz]], peer[1])
        if dz:
            net.add((K_RZ, dz), lambda dz=dz: acc.at[zs[dz], chip], lambda dz=dz: rz.at[dz - 1], plane[dz])
    for dz in (1, 2, 3):
        net.add((K_RZB, dz), lambda dz=dz: backv.at[zs[dz]], lambda dz=dz: rzb.at[dz - 1], plane[dz])
    bh = finb.shape[2] // 2
    bx, by = slice(0, bh), slice(bh, 2 * bh)
    net.add((K_X2, K_BACK), lambda: back_ref.at[2, :, bx], lambda: bx2, peer[2])
    net.add((K_Y2, K_BACK), lambda: back_ref.at[1, :, by], lambda: by2, peer[1])
    net.add(K_B1, lambda: finb.at[core, chip], lambda: finb.at[core, chip], peer[1])
    net.add(K_B2, lambda: finb.at[core, chip], lambda: finb.at[core, chip], peer[2])
    net.add(K_B3X, lambda: finb.at[core, ch[1], bx], lambda: finb.at[core, ch[1], bx], peer[2])
    net.add(K_B3Y, lambda: finb.at[core, ch[2], by], lambda: finb.at[core, ch[2], by], peer[1])
    net.add(K_BM, lambda: finb.at[core], lambda: finb.at[core], mate)
    net.add(K_F1, lambda: fin.at[core, chip], lambda: fin.at[core, chip], peer[1])
    net.add(K_F2, lambda: fin.at[core, chip], lambda: fin.at[core, chip], peer[2])
    net.add(K_F3X, lambda: fin.at[core, ch[1], xs], lambda: fin.at[core, ch[1], xs], peer[2])
    net.add(K_F3Y, lambda: fin.at[core, ch[2], ys], lambda: fin.at[core, ch[2], ys], peer[1])
    net.add(K_FM, lambda: fin.at[core], lambda: fin.at[core], mate)
    net.add(K_S0, lambda: sums_ref, lambda: sums_r.at[0], mate)
    net.add(K_S1, lambda: sums.at[1], lambda: sums_r.at[1], peer[1])
    net.add(K_S2, lambda: sums.at[2], lambda: sums_r.at[2], peer[2])
    for dz in (1, 2, 3):
        net.add((K_SZ, dz), lambda dz=dz: sums.at[3, zs[dz]], lambda dz=dz: sums_z.at[dz - 1], plane[dz])
    for a, w, wr, g, gr, f in ((K_G, gw, gwr, gz, gzr, gwf), (K_H, hw, hwr, hz, hzr, hwf)):
        net.add((a, 0), lambda w=w: w.at[other], lambda wr=wr: wr, mate)
        for dz in (1, 2, 3):
            net.add((a, K_Z, dz), lambda g=g, dz=dz: g.at[zs[dz]], lambda gr=gr, dz=dz: gr.at[dz - 1], plane[dz])
        for j in (1, 2, 3):
            net.add((a, K_F, j), lambda f=f: f.at[core, chip], lambda f=f: f.at[core, chip], peer[j])
        net.add((a, K_M), lambda f=f: f.at[core], lambda f=f: f.at[core], mate)

    loads = ((K_DO, lambda: do_ref, lambda: do_s), (K_DO1, lambda: do1_ref.at[chip], lambda: do1_s.at[0]), (K_O, lambda: o_ref, lambda: o_s),
             (K_TOK, lambda: tok_ref, lambda: tok), (K_Q, lambda: q_ref, lambda: q_s),
             (K_K, lambda: k_ref, lambda: k_s), (K_V, lambda: v_ref, lambda: v_s),
             (K_SUMS, lambda: sums_ref, lambda: sums.at[0]), (K_BACK, lambda: back_ref.at[0], lambda: backv), (K_ACC, lambda: grads_ref.at[core], lambda: acc))
    for name, src, dst in loads:
        loc.add(name, src, dst)
    stores = ((K_GW_O, gwf, gw_out), (K_HW_O, hwf, hw_out), (K_FIN_O, fin, fin_out), (K_FINB_O, finb, finb_out))
    for name, src, dst in stores:
        loc.add(name, lambda src=src: src, lambda dst=dst: dst)
    loc.add(K_SUMS_O, lambda: sums_f, lambda: sums_out)

    loc.start(K_DO, K_O, K_Q, K_K, K_V)
    greet(peer[1:] + [mate] + plane[1:])
    net.start((K_X2, K_BACK), (K_Y2, K_BACK), K_S0, *[(K_R1, dz) for dz in order])
    loc.start(K_ACC, K_BACK, K_SUMS, K_TOK, K_DO1)
    lane = lanes_of()
    loc.wait(K_DO, K_O)

    def output_grad(h, tiles):
        for j in range(4):
            tile = tiles[j].astype(f32)
            if h == 1:
                tile = pltpu.roll(tile, 64, 1)
            tile = jnp.where(lane < 64, tile, 0.0)
            r = slice(j * rows, (j + 1) * rows)
            delta = jnp.sum(tile * o_s[h, r, :].astype(f32), axis=1, keepdims=True)
            hi, mid, low = split3(-delta)
            tile = jnp.where(lane == 64, hi, jnp.where(lane == 65, mid, jnp.where(lane == 66, low, tile)))
            doa[h, r, :] = tile.astype(bf16)

    output_grad(0, do_s)
    output_grad(1, do_s)
    loc.wait(K_Q, K_K, K_V)

    def late_loads():
        loc.wait(K_ACC, K_BACK, K_SUMS)
        net.start(*[(K_DO, j) for j in (1, 2, 3)])

    def transpose_tokens():
        loc.wait(K_TOK)
        for j in range(4):
            tokt[:, j * rows : (j + 1) * rows] = tok[j].T

    def last_head_grad():
        loc.wait(K_DO1)
        net.recv(*[(K_DO, j) for j in (1, 2, 3)])
        output_grad(2, do1_s)

    def add_into(ref, index, other_ref, other_index):
        ref[index] = (ref[index].astype(f32) + other_ref[other_index].astype(f32)).astype(bf16)

    def step_one(dz):
        net.recv((K_R1, dz))
        def body(c, carry):
            add_into(acc, (zs[dz], c), rb, (zs[dz], c))
            return carry
        lax.fori_loop(0, CHIPS, body, 0)
        net.start(*[(K_X1, n, dz) for n in (0, 1)], *[(K_Y1, n, dz) for n in (0, 1)])

    def step_two(dz):
        for n in range(2):
            net.recv((K_X1, 1 - n, dz), (K_Y1, 1 - n, dz))
            jx, jy = (2, 1) if n == 0 else (0, 0)
            add_into(acc, (zs[dz], ch[jx], xs), rx, (zs[dz], 1 - n))
            add_into(acc, (zs[dz], ch[jy], ys), ry, (zs[dz], 1 - n))
            if n == 0:
                net.start((K_X2, dz), (K_Y2, dz))

    def step_three(dz):
        net.recv((K_X2, dz), (K_Y2, dz))
        add_into(acc, (zs[dz], chip, xs), rx2, zs[dz])
        add_into(acc, (zs[dz], chip, ys), ry2, zs[dz])
        if dz:
            net.start((K_RZ, dz))

    def sums_step(n):
        net.recv((K_S0, K_S1, K_S2)[n])
        sums[n + 1] = (sums[n].astype(f32) + sums_r[n].astype(f32)).astype(bf16)
        if n < 2:
            net.start((K_S1, K_S2)[n])
        else:
            net.start(*[(K_SZ, dz) for dz in (1, 2, 3)])

    def back_plane():
        net.recv((K_X2, K_BACK), (K_Y2, K_BACK))
        for zz in range(PLANES):
            add_into(backv, (zz, bx), bx2, zz)
            add_into(backv, (zz, by), by2, zz)
        net.start(*[(K_RZB, dz) for dz in (1, 2, 3)])

    def back_total():
        net.recv(*[(K_RZB, dz) for dz in (1, 2, 3)])
        total = backv[z].astype(f32) + rzb[0].astype(f32) + rzb[1].astype(f32) + rzb[2].astype(f32)
        finb[core, chip] = total.astype(bf16)
        net.start(K_B1, K_B2)

    def back_forward():
        net.recv(K_B1)
        net.start(K_B3X)
        net.recv(K_B2)
        net.start(K_B3Y)

    def back_mate():
        net.recv(K_B3X, K_B3Y)
        net.start(K_BM)

    def fin_total():
        for dz in (1, 2, 3):
            net.recv((K_RZ, dz), (K_SZ, dz))
        total = acc[z, chip].astype(f32) + rz[0].astype(f32) + rz[1].astype(f32) + rz[2].astype(f32)
        fin[core, chip] = total.astype(bf16)
        net.start(K_F1, K_F2)
        total = sums[3, z].astype(f32)
        for n in range(3):
            total = total + sums_z[n].astype(f32)
        sums_f[...] = total.astype(bf16)
        loc.start(K_SUMS_O)

    def fin_forward():
        net.recv(K_F1)
        net.start(K_F3X)
        net.recv(K_F2)
        net.start(K_F3Y)

    def weight_part(a, w, first, last):
        cols = dall[:, :, first:last].reshape(4 * rows, last - first)
        column_sums = jnp.sum(cols.astype(f32), axis=0, keepdims=True)
        extra = jnp.where(lax.broadcasted_iota(jnp.int32, (16, 1), 0) == 0, column_sums, 0.0).astype(bf16)
        for zz in range(PLANES):
            part = dot(tokt[zz * shard : (zz + 1) * shard, :], cols)
            for m in range(2):
                w[m, zz, 0:piece, :] = part[m * piece : (m + 1) * piece, :].astype(bf16)
                w[m, zz, piece : piece + 16, :] = extra
        net.start((a, 0))

    def weight_pair(a, w, wr, g):
        net.recv((a, 0))
        for zz in range(PLANES):
            g[zz] = (w[core, zz].astype(f32) + wr[zz].astype(f32)).astype(bf16)
        net.start(*[(a, K_Z, dz) for dz in (1, 2, 3)])

    def weight_total(a, g, gr, f):
        total = g[z].astype(f32)
        for dz in (1, 2, 3):
            net.recv((a, K_Z, dz))
            total = total + gr[dz - 1].astype(f32)
        f[core, chip] = total.astype(bf16)
        net.start(*[(a, K_F, j) for j in (1, 2, 3)])

    def weight_mate(a):
        net.recv(*[(a, K_F, j) for j in (1, 2, 3)])
        net.start((a, K_M))

    key_chunk, query_tile = 2 * rows, 256
    per_head = 4

    def head_keys(h, slots):
        cols = slice(KV_TILE[h] * 128, KV_TILE[h] * 128 + 128)
        for j in slots:
            r = slice(j * rows, (j + 1) * rows)
            both = kv_own[r, :] + kvr[h, r, :].astype(f32)
            dall[j, :, cols] = both.astype(bf16)
            if j:
                net.start((K_DP, h, j))

    def head_queries(h):
        dq = dqs[...].T * 0.125
        for j in range(4):
            r = slice(j * rows, (j + 1) * rows)
            mine = dq[r, :]
            if h == 0:
                dq_keep[r, :] = mine
            elif h == 1:
                dall[j, :, 256:384] = jnp.where(lane < 64, dq_keep[r, :], pltpu.roll(mine, 64, 1)).astype(bf16)
                if j:
                    net.start((K_DP, K_Q, j))
            else:
                upper = pltpu.roll(mine[rows // 2 :, :], 64, 1)
                fold[j] = jnp.where(lane < 64, mine[: rows // 2, :], upper).astype(bf16)
                if j:
                    net.start((K_DP, K_O, j))
                dall[j, :, 384:512] = jnp.where(lane < 64, mine, 0.0).astype(bf16)

    stages = {
        0: lambda: (late_loads(), step_one(3), back_plane(), sums_step(0)),
        1: lambda: (step_one(2), sums_step(1)),
        2: lambda: (step_two(3), step_one(1), sums_step(2)),
        3: lambda: (step_three(3), step_two(2)),
        4: lambda: (step_one(0), back_total()),
        5: lambda: (step_three(2), step_two(1), transpose_tokens()),
        6: lambda: (step_two(0), back_forward(), last_head_grad()),
        7: lambda: (step_three(1), weight_part(K_G, gw, 0, 384)),
        8: lambda: (step_three(0), back_mate()),
        9: lambda: (fin_total(), weight_pair(K_G, gw, gwr, gz)),
        11: lambda: (fin_forward(), weight_total(K_G, gz, gzr, gwf)),
    }

    def visit(t, carry):
        h, part = lax.div(t, per_head), lax.rem(t, per_head)
        start = pl.multiple_of(jnp.where(part < 2, part + 2, 3 - part) * key_chunk, key_chunk)
        krows = pl.ds(start, key_chunk)
        k, v = k_s[h, krows, :], v_s[h, krows, :]
        kt = k.T

        @pl.when(part == 0)
        def _():
            dqs[...] = jnp.zeros_like(dqs)

        dk = jnp.zeros((key_chunk, 128), f32)
        dv = jnp.zeros((key_chunk, 128), f32)
        for i in range(4 * rows // query_tile):
            r = slice(i * query_tile, (i + 1) * query_tile)
            q, do = q_s[h, r, :], doa[h, r, :]
            probs = jnp.exp2(dot(k, q, NT) * LOG2E)
            dscores = (probs * dot(v, do, NT)).astype(bf16)
            dv = dv + dot(probs.astype(bf16), do)
            dk = dk + dot(dscores, q)
            dqs[:, r] += dot(kt, dscores)
        packed = jnp.where(lane < 64, dk, pltpu.roll(dv, 64, 1))

        @pl.when(part < 2)
        def _():
            kvs[h, pl.ds(pl.multiple_of(part * key_chunk, key_chunk), key_chunk), :] = packed.astype(bf16)

        @pl.when(part >= 2)
        def _():
            kv_own[pl.ds(pl.multiple_of((3 - part) * key_chunk, key_chunk), key_chunk), :] = packed

        for hh in range(GROUP_HEADS):
            @pl.when(t == hh * per_head + 1)
            def _(hh=hh):
                net.start((K_KV, hh))

            @pl.when(t == hh * per_head + 2)
            def _(hh=hh):
                net.recv((K_KV, hh))
                head_keys(hh, (2, 3))

            @pl.when(t == hh * per_head + 3)
            def _(hh=hh):
                head_keys(hh, (1, 0))
                head_queries(hh)
        for at, work in stages.items():
            pl.when(t == at)(lambda work=work: (work(), None)[1])
        return carry

    lax.fori_loop(0, GROUP_HEADS * per_head, visit, 0)

    weight_part(K_H, hw, 384, PACK)
    loc.start((K_DP, 0), (K_DP, 1), (K_DP, 2))
    weight_pair(K_H, hw, hwr, hz)
    weight_mate(K_G)
    net.recv(K_F3X, K_F3Y)
    net.start(K_FM)
    weight_total(K_H, hz, hzr, hwf)
    for h in (0, 1, 2, K_Q, K_O):
        for j in (1, 2, 3):
            net.recv((K_DP, h, j))
    net.recv(K_FM, K_BM, (K_G, K_M))
    loc.start(K_GW_O, K_FIN_O, K_FINB_O)
    weight_mate(K_H)
    net.recv((K_H, K_M))
    loc.start(K_HW_O)
    for name in net.specs:
        net.sent(name)
    loc.wait((K_DP, 0), (K_DP, 1), (K_DP, 2), K_GW_O, K_HW_O, K_FIN_O, K_FINB_O, K_SUMS_O)


def gelu_parts(u):
    x = jnp.abs(u) * (0.5 ** 0.5)
    d = 1.0 + 0.3275911 * x
    t = pl.reciprocal(d, approx=True)
    t = t * (2.0 - d * t)
    poly = t * (0.254829592 + t * (-0.284496736 + t * (1.421413741 + t * (-1.453152027 + t * 1.061405429))))
    bell = jnp.exp2(u * u * (-0.5 * LOG2E))
    tail = 0.5 * poly * bell
    phi = jnp.where(u >= 0, 1.0 - tail, tail)
    return u * phi, phi + u * bell * (1.0 / math.sqrt(2.0 * math.pi))


def row_mean(a):
    return jnp.mean(a, axis=1, keepdims=True)


def wide_vectors(small):
    step = small.shape[2] // PLANES
    lane = lax.broadcasted_iota(jnp.int32, (8, small.shape[2]), 1)
    total = 0.0
    for zz in range(PLANES):
        part = jnp.where(lane < step, small[zz].astype(f32)[0:8], 0.0)
        total = total + (pltpu.roll(part, zz * step, 1) if zz else part)
    return total


def ffn_kernel(
    length_ref, att_ref, tok_ref, cot_ref, win_ref, win_own, wout_ref, wout_own, small_ref, wback_ref, wback_own, wq_own,
    res_out, gh1_out, do_out, do1_out, grads_out, sums_ref, wq_full, back_out,
    winv, wbackv, woutv, act_s, gp_s, gi_s, acc, first_s, n1_s, low_s, lowt_s, gsec_s, gh2_s, isum,
    gb, rb, rx, ry, do_ref, do_in, out_ref, gh1_ref, grads_ref, send_sems, recv_sems, line_send, line_recv, local_sems,
):
    s, z, core, chip = coordinates()
    other = 1 - core
    rows, width = tok_ref.shape
    step = width // PLANES
    ch = winv.shape[1] // 8
    wide = 2 * ch
    back = wback_own.shape[0]
    shard = win_own.shape[0]
    piece = shard // 2
    peer = [None] + [(flip(chip, j) * 2 + core, z) for j in (1, 2, 3)]
    mate = (chip * 2 + other, z)
    plane = [(s, flip(z, dz)) for dz in (1, 2, 3)]
    ch_of = [chip] + [flip(chip, j) for j in (1, 2, 3)]
    net, loc = Net(send_sems, recv_sems), Local(local_sems)

    bpiece = back // 8
    line = Line(s, z, line_send, line_recv)
    lines = line.order
    line.add(K_QKV, lambda: wq_own.at[pl.ds(core * 2, 2)], lambda zz: wq_full.at[zz, pl.ds(core * 2, 2)])
    for dz in (1, 2, 3):
        net.add((K_QKV, dz), lambda dz=dz: wq_full.at[lines[dz], pl.ds(core * 2, 2)], lambda dz=dz: wq_full.at[lines[dz], pl.ds(core * 2, 2)], mate)

    def region(ref, zz, c):
        return ref.at[pl.ds(pl.multiple_of(zz * back + (core * 4 + c) * bpiece, 16), bpiece), :]

    def side(zz):
        return wbackv.at[pl.ds(pl.multiple_of(zz * back + core * 4 * bpiece, 16), 4 * bpiece), :]

    for dz in (2, 3):
        for j in (1, 2):
            net.add((j, dz), lambda dz=dz: region(wback_ref, lines[dz], chip), lambda dz=dz: region(wbackv, lines[dz], chip), peer[j])
        via, last = ((1, 2), (2, 1))[dz - 2]
        net.add((3, dz), lambda dz=dz, via=via: region(wbackv, lines[dz], ch_of[via]), lambda dz=dz, via=via: region(wbackv, lines[dz], ch_of[via]), peer[last])
        net.add((K_M, dz), lambda dz=dz: side(lines[dz]), lambda dz=dz: side(lines[dz]), mate)
        loc.add((K_M, dz), lambda dz=dz: region(wback_ref, lines[dz], chip), lambda dz=dz: region(wbackv, lines[dz], chip))
    half = gb.shape[3] // 2
    xs, ys = slice(0, half), slice(half, 2 * half)
    for zz in range(PLANES):
        net.add((K_R1, zz), lambda zz=zz: gb.at[other, zz], lambda zz=zz: rb.at[zz], mate)
        for n, j in enumerate((1, 3)):
            net.add((K_X1, n, zz), lambda zz=zz, j=j: gb.at[core, zz, ch_of[j], xs], lambda zz=zz, n=n: rx.at[zz, n], peer[1])
        for n, j in enumerate((2, 3)):
            net.add((K_Y1, n, zz), lambda zz=zz, j=j: gb.at[core, zz, ch_of[j], ys], lambda zz=zz, n=n: ry.at[zz, n], peer[2])
    for j in (1, 2, 3):
        net.add((K_DO, j), lambda j=j: do_ref.at[0, ch_of[j]], lambda j=j: do_in.at[j], peer[j])
    loc.add(K_DO_O, lambda: do_in, lambda: do_out)
    loc.add(K_DO1, lambda: do_ref.at[1], lambda: do1_out)
    loc.add(K_GH1, lambda: gh1_ref, lambda: gh1_out)
    loc.add(K_RES, lambda: out_ref, lambda: res_out)
    for n in range(PLANES):
        cut_of = lambda ref, n=n: ref.at[n // 2, :, pl.ds(n % 2 * 2, 2)]
        loc.add((K_GR, n), lambda cut_of=cut_of: cut_of(grads_ref), lambda cut_of=cut_of: cut_of(grads_out))
    for j in range(3):
        loc.add((K_BACK_O, j), lambda j=j: gb.at[core, :, ch_of[j]], lambda j=j: back_out.at[j])
    shards = {K_OUT: (wout_own, wout_ref, woutv), K_IN: (win_own, win_ref, winv), K_BACK: (wback_own, wback_ref, wbackv)}
    loads = [(name, i) for name in shards for i in range(4) if name != K_BACK or i < 2]
    for name, i in loads:
        own, full, dst = shards[name]
        n = own.shape[0]
        place = lambda i=i, n=n: pl.ds(pl.multiple_of(lines[i] * n, 16), n)
        loc.add((name, i), lambda own=own, full=full, i=i, place=place: full.at[place(), :] if i else own,
                lambda dst=dst, place=place: dst.at[place(), :])
    loc.start(*loads, (K_M, 2), (K_M, 3))
    greet(peer[1:] + [mate] + plane)
    net.start((1, 2), (2, 2), (1, 3), (2, 3))
    line.start(K_QKV)

    def hop_two(dz):
        net.recv((1, dz), (2, dz))
        net.start((3, dz))

    def hop_three(dz):
        net.recv((3, dz))
        loc.wait((K_M, dz))
        net.start((K_M, dz))

    def add_into(ref, index, other_ref, other_index):
        ref[index] = (ref[index].astype(f32) + other_ref[other_index].astype(f32)).astype(bf16)

    def step_one(zz):
        net.recv((K_R1, zz))
        for c in range(CHIPS):
            add_into(gb, (core, zz, c), rb, (zz, c))
        net.start(*[(K_X1, n, zz) for n in (0, 1)], *[(K_Y1, n, zz) for n in (0, 1)])

    def step_two(zz):
        net.recv((K_X1, 1, zz), (K_Y1, 1, zz))
        add_into(gb, (core, zz, ch_of[2], xs), rx, (zz, 1))
        add_into(gb, (core, zz, ch_of[1], ys), ry, (zz, 1))
        net.recv((K_X1, 0, zz), (K_Y1, 0, zz))
        add_into(gb, (core, zz, chip, xs), rx, (zz, 0))
        add_into(gb, (core, zz, chip, ys), ry, (zz, 0))

    def during(n, works):
        for at, work in works.items():
            pl.when(n == at)(lambda work=work: (work(), None)[1])

    vectors = wide_vectors(small_ref)
    vec = lambda i: vectors[i : i + 1, :]
    loc.wait(*[(K_OUT, dz) for dz in range(4)])
    branch = vec(0)
    for g in range(4):
        branch = branch + dot(att_ref[g, :, 0:step], woutv[g * step : (g + 1) * step, :])
    hidden = tok_ref[...].astype(f32) + branch
    centred = hidden - row_mean(hidden)
    inverse1 = lax.rsqrt(row_mean(centred * centred) + 1e-5)
    normed = centred * inverse1
    n1_s[...] = normed
    first = normed * vec(1) + vec(2)
    first_s[...] = first
    low_s[...] = first.astype(bf16)
    lowt_s[...] = first.astype(bf16).T
    loc.wait(*[(K_IN, i) for i in range(4)])

    def forward(n, carry):
        cols = pl.ds(pl.multiple_of(n * wide, 128), wide)
        inner = dot(low_s[...], winv[:, cols]) + small_ref[n, 6:7, :].astype(f32)
        value, slope = gelu_parts(inner)
        value = value.astype(bf16)
        act_s[n] = value
        gp_s[n] = slope
        during(n, {2: lambda: hop_two(2), 3: lambda: hop_two(3)})
        return carry

    lax.fori_loop(0, PLANES, forward, 0)

    def second_layer(i):
        zz = lines[i]
        return dot(act_s[zz], wbackv[pl.ds(pl.multiple_of(zz * back, 16), back), :])

    loc.wait((K_BACK, 0), (K_BACK, 1))
    acc[...] = second_layer(0)
    acc[...] += second_layer(1)
    hop_three(2)
    hop_three(3)
    line.step(1, K_QKV)
    net.recv((K_M, 2))
    acc[...] += second_layer(2)
    net.recv((K_M, 3))
    acc[...] += second_layer(3)
    position = s * rows + lax.broadcasted_iota(jnp.int32, (rows, 1), 0)
    valid = (position < length_ref[0]).astype(f32)
    hidden = first_s[...] + acc[...] + vec(3)
    centred = hidden - row_mean(hidden)
    inverse = lax.rsqrt(row_mean(centred * centred) + 1e-5)
    normed = centred * inverse
    out_ref[...] = ((normed * vec(4) + vec(5)) * valid).astype(bf16)
    loc.start(K_RES)
    grad = cot_ref[...].astype(f32) * valid
    sum_rows = lambda a: jnp.sum(a, axis=0, keepdims=True)
    g2_gain, g2_bias = sum_rows(grad * normed), sum_rows(grad)
    scaled = grad * vec(4)
    gh2 = inverse * (scaled - row_mean(scaled) - normed * row_mean(scaled * normed))
    gh2_s[...] = gh2
    second = gh2.astype(bf16)
    gsec_s[...] = second
    back_sum = sum_rows(second.astype(f32))
    acc[...] = jnp.zeros_like(acc)

    def back_weights(n, carry):
        gback = dot(act_s[n].T, gsec_s[...]).astype(bf16)
        part = wide // 8
        for m in range(2):
            for k in range(4):
                for x in range(2):
                    gb[m, n, k, x * part : (x + 1) * part, :] = gback[
                        (m * 4 + k) * part : (m * 4 + k + 1) * part, x * ch : (x + 1) * ch
                    ]
        during(n, {
            0: lambda: net.start((K_R1, 0)), 1: lambda: net.start((K_R1, 1)),
            2: lambda: net.start((K_R1, 2)), 3: lambda: net.start((K_R1, 3)),
        })
        return carry

    lax.fori_loop(0, PLANES, back_weights, 0)

    def backward(n, carry):
        cols = pl.ds(pl.multiple_of(n * wide, 128), wide)
        grad_inner = (dot(gsec_s[...], wbackv[cols, :], NT) * gp_s[n]).astype(bf16)
        gi_s[n] = grad_inner
        isum[n] = jnp.broadcast_to(sum_rows(grad_inner.astype(f32)), (8, wide))
        acc[...] += dot(grad_inner, winv[:, cols], NT)
        during(n, {
            0: lambda: step_one(0), 1: lambda: step_one(1),
            2: lambda: (step_one(2), step_two(0)),
            3: lambda: (step_one(3), line.step(2, K_QKV), net.start((K_QKV, 1), (K_QKV, 2))),
        })
        return carry

    lax.fori_loop(0, PLANES, backward, 0)
    grad = gh2_s[...] + acc[...]
    normed = n1_s[...]
    g1_gain, g1_bias = sum_rows(grad * normed), sum_rows(grad)
    scaled = grad * vec(1)
    gh1 = inverse1 * (scaled - row_mean(scaled) - normed * row_mean(scaled * normed))
    gh1_ref[...] = gh1
    loc.start(K_GH1)
    gbranch = gh1.astype(bf16)
    out_sum = sum_rows(gbranch.astype(f32))
    for g in range(4):
        w = woutv[g * step : (g + 1) * step, :]
        part = dot(gbranch, w, NT).astype(bf16)
        do_ref[0, g] = part[:, 0:128]
        do_ref[1, g, :, 0 : step - 128] = part[:, 128:step]
        do_ref[1, g, :, step - 128 :] = jnp.zeros((rows, 256 - step), bf16)
    net.start(*[(K_DO, j) for j in (1, 2, 3)])
    do_in[0] = do_ref[0, chip]
    loc.start(K_DO1)
    for g in range(4):
        gw = dot(att_ref[g, :, 0:step].T, gbranch).astype(bf16)
        part = step // 4
        for c in range(4):
            for m in range(2):
                grads_ref[m, g, c, step:, :] = gw[c * part : (c + 1) * part, m * ch : (m + 1) * ch]

    def weights(n, carry):
        for zz in range(PLANES):
            gin = dot(lowt_s[zz * step : (zz + 1) * step, :], gi_s[n]).astype(bf16)
            for x in range(2):
                grads_ref[lax.div(n, 2), zz, lax.rem(n, 2) * 2 + x, 0:step, :] = gin[:, x * ch : (x + 1) * ch]
        during(n, {
            0: lambda: (loc.start((K_GR, 0)), step_two(1)), 1: lambda: (loc.start((K_GR, 1)), step_two(2)),
            2: lambda: (loc.start((K_GR, 2)), step_two(3)), 3: lambda: loc.start((K_GR, 3)),
        })
        return carry

    lax.fori_loop(0, PLANES, weights, 0)
    lane = lax.broadcasted_iota(jnp.int32, (8, width), 1)
    place = lax.broadcasted_iota(jnp.int32, (8, width), 0)
    total = jnp.zeros((8, width), f32)
    for i, v in enumerate((out_sum, g1_gain, g1_bias, back_sum, g2_gain, g2_bias)):
        total = jnp.where(place == i, v, total)
    for zz in range(PLANES):
        part = total if zz == 0 else pltpu.roll(total, width - zz * step, 1)
        part = jnp.where(lane < step, part, 0.0)
        part = jnp.where(place == 6, isum[zz], part)
        sums_ref[zz, 0:16, :] = jnp.concatenate([part, jnp.zeros((8, width), f32)], axis=0).astype(bf16)
    net.recv(*[(K_DO, j) for j in (1, 2, 3)])
    loc.start(*[(K_BACK_O, j) for j in range(3)], K_DO_O)
    line.step(3, K_QKV)
    net.start((K_QKV, 3))
    net.recv(*[(K_QKV, dz) for dz in (1, 2, 3)])
    for name in net.specs:
        net.sent(name)
    line.sent()
    loc.wait(*[(K_BACK_O, j) for j in range(3)], K_DO_O, K_DO1, K_GH1, K_RES, *[(K_GR, n) for n in range(PLANES)])


Q_PLACE, K_PLACE, V_PLACE = (4, 5, 6), (0, 2, 8), (1, 3, 9)


def half_tile(tile_of, block, upper):
    tile = tile_of(block // 2)
    return tile if block % 2 == upper else pltpu.roll(tile, 64, 1)


def final_kernel(
    dproj_ref, wq_ref, wq_own, gh1_ref, gw_ref, hw_ref, fin_ref, finb_ref, sums_ref,
    gt_ref, gqkv_ref, gin_ref, gback_ref, gout_ref, qb_ref, vb_ref, o0, o1, o2, o3, o4, o5, ib_ref,
    wv, row, last, local_sems,
):
    z = lax.axis_index("fsdp")
    loc = Local(local_sems)
    rows = gh1_ref.shape[0]
    shard = wq_ref.shape[2]
    for dz in range(PLANES):
        zz = flip(z, dz)
        loc.add(dz, lambda zz=zz, dz=dz: wq_own if dz == 0 else wq_ref.at[zz],
                lambda zz=zz: wv.at[:, pl.ds(pl.multiple_of(zz * shard, 16), shard), :])
    loc.start(*range(PLANES))
    lane = lanes_of()
    up = lambda a: a.astype(f32)
    ch = fin_ref.shape[3]
    for m in range(2):
        for c in range(4):
            n = m * 4 + c
            gin_ref[:, n * ch : (n + 1) * ch] = up(fin_ref[m, c, 0:shard, :])
            part = ch // 4
            for x in range(2):
                gback_ref[n * part : (n + 1) * part, x * ch : (x + 1) * ch] = up(
                    finb_ref[m, c, x * part : (x + 1) * part, :]
                )
            gout_ref[c * (shard // 4) : (c + 1) * (shard // 4), m * ch : (m + 1) * ch] = up(fin_ref[m, c, shard:, :])
    piece = shard // 2

    def packed_tile(m, g, r, t):
        if t < 3:
            return up(gw_ref[m, g, r, t * 128 : (t + 1) * 128])
        return up(hw_ref[m, g, r, (t - 3) * 128 : (t - 2) * 128])

    for m in range(2):
        r = slice(m * piece, (m + 1) * piece)
        for kind, places in enumerate((Q_PLACE, K_PLACE, V_PLACE)):
            for i in range(HEADS // 2):
                halves = []
                for upper in (0, 1):
                    g, h = divmod(2 * i + upper, GROUP_HEADS)
                    tile_of = lambda t, g=g: packed_tile(m, g, slice(0, piece), t)
                    halves.append(half_tile(tile_of, places[h], upper))
                at = kind * HEADS * 64 + i * 128
                gqkv_ref[r, at : at + 128] = jnp.where(lane < 64, halves[0], halves[1])
    tile_of = lambda t: packed_tile(0, z, slice(piece, piece + 16), t)
    for ref, places in ((qb_ref, Q_PLACE), (vb_ref, V_PLACE)):
        first = jnp.where(lane < 64, half_tile(tile_of, places[0], 0), half_tile(tile_of, places[1], 1))
        row[0:1, 0:128] = first[0:1]
        row[0:1, 128:256] = half_tile(tile_of, places[2], 0)[0:1]
        ref[...] = row[0:1, 0:shard].reshape(shard)
    for i, ref in enumerate((o0, o1, o2, o3, o4, o5)):
        ref[...] = up(sums_ref[...])[i : i + 1, 0:shard].reshape(shard)
    ib_ref[...] = up(sums_ref[...])[6:7, :].reshape(ib_ref.shape[0])
    loc.wait(*range(PLANES))
    total = gh1_ref[...]
    for g in range(4):
        total = total + dot(dproj_ref[g, :, 0:384], wv[g, :, 0:384], NT)
        folded = up(dproj_ref[g, 0 : rows // 2, 384:512])
        last[0 : rows // 2, 0:128] = jnp.where(lane < 64, folded, 0.0).astype(bf16)
        last[rows // 2 :, 0:128] = jnp.where(lane < 64, pltpu.roll(folded, 64, 1), 0.0).astype(bf16)
        last[:, 128:256] = dproj_ref[g, :, 512:640]
        total = total + dot(last[...], wv[g, :, 384:640], NT)
    gt_ref[...] = total.astype(bf16)


def vmem(shape, dtype=bf16):
    return pltpu.VMEM(shape, dtype)


ANY = pl.BlockSpec(memory_space=pl.ANY)
SMEM = pl.BlockSpec(memory_space=pltpu.SMEM)
VMEM = pl.BlockSpec(memory_space=pltpu.VMEM)
VMEM_BYTES = 60 * 2**20
SEMS = 112


def semaphores(line=False):
    counts = (SEMS, SEMS) + ((5 * 2, PLANES * 2) if line else ()) + (32,)
    return [pltpu.SemaphoreType.DMA((n,)) for n in counts]


def params(collective_id):
    return pltpu.CompilerParams(
        collective_id=collective_id, has_side_effects=True, vmem_limit_bytes=VMEM_BYTES
    )


def run_forward(lengths, tokens, w_qkv, w_in, w_back, w_out, *vectors):
    rows, width = tokens.shape
    shard = w_qkv.shape[0]
    hidden = w_in.shape[1]
    S = jax.ShapeDtypeStruct
    q_shape, kv_shape = (GROUP_HEADS, 4 * rows, 128), (GROUP_HEADS, 8 * rows, 128)
    return pl.pallas_call(
        forward_kernel,
        out_shape=(
            S(q_shape, bf16), S(kv_shape, bf16), S(kv_shape, bf16), S(q_shape, bf16),
            S((4, rows, width), bf16), S((4, rows, 256), bf16), S((PLANES, 16, width), bf16),
            S((PLANES * shard, hidden), bf16), S((width, width), bf16),
            S((CHIPS, shard, PACK), bf16), S((hidden, width), bf16),
        ),
        in_specs=[SMEM] + [ANY] * 5 + [VMEM] * 9,
        out_specs=[ANY] * 11,
        scratch_shapes=[
            vmem((4, rows, width)), vmem((width, PACK)), vmem(q_shape), vmem(kv_shape), vmem(kv_shape), vmem(q_shape),
            vmem((4, rows, 256)), vmem((4, rows, 256)), vmem((4, rows, 384)), vmem((4, rows, 384)),
            vmem((PLANES, 16, width)), vmem((shard, w_qkv.shape[1])), vmem((CHIPS, shard, PACK)),
            vmem((8, width), f32), vmem((8, 256), f32),
        ] + semaphores(line=True),
        compiler_params=params(1),
    )(lengths, tokens, w_qkv, w_in, w_back, w_out, *vectors)


def run_backward(do, do1, q, k, v, o, tok, grads, sums, back):
    rows = do.shape[1]
    width = tok.shape[2]
    shard = width // PLANES
    length, cols = grads.shape[3:]
    cut = length // 32 * 16
    S = jax.ShapeDtypeStruct
    ext = shard // 2 + 16
    return pl.pallas_call(
        backward_kernel,
        out_shape=(
            S((4, rows, PACK), bf16), S((2, 4, ext, 384), bf16), S((2, 4, ext, 256), bf16), S((2, 4, length, cols), bf16), S((2, 4) + back.shape[2:], bf16), S((16, width), bf16),
        ),
        in_specs=[ANY] * 10,
        out_specs=[ANY] * 6,
        scratch_shapes=[
            vmem((4, rows, 128)), vmem((4, rows, 128)), vmem(q.shape), vmem(k.shape), vmem(v.shape), vmem(o.shape), vmem(q.shape),
            vmem(tok.shape), vmem((width, 4 * rows)), vmem((128, 4 * rows), f32), vmem((4 * rows, 128), f32),
            vmem((4 * rows, 128), f32), vmem((3, 4 * rows, 128)), vmem((3, 4 * rows, 128)),
            vmem((4, rows, PACK)), vmem((4, rows // 2, 128)),
            *[vmem(lead + (ext, n)) for n in (384, 256) for lead in ((2, 4), (4,), (4,), (3,), (2, 4))],
            vmem((4, 4, length, cols)), vmem((4, 4, length, cols)),
            vmem((4, 2, cut, cols)), vmem((4, 2, length - cut, cols)), vmem((4, cut, cols)), vmem((4, length - cut, cols)),
            vmem((3, length, cols)), vmem((3,) + back.shape[2:]), vmem(back.shape[1:]),
            vmem((4, back.shape[2] // 2, cols)), vmem((4, back.shape[2] // 2, cols)), vmem((2, 4, length, cols)), vmem((2, 4) + back.shape[2:]),
            vmem((4, 4, 16, width)), vmem((3, 4, 16, width)), vmem((3, 16, width)), vmem((16, width)),
        ] + semaphores(),
        compiler_params=params(2),
    )(do, do1, q, k, v, o, tok, grads, sums, back)


def run_ffn(lengths, att, tokens, cotangent, full_in, w_in, full_out, w_out, small, full_back, w_back, wq):
    rows, width = tokens.shape
    hidden = w_in.shape[1]
    ch = hidden // 8
    S = jax.ShapeDtypeStruct
    one = S((rows, width), bf16)
    bp = w_back.shape[0] // 8
    return pl.pallas_call(
        ffn_kernel,
        out_shape=(
            one, S((rows, width), f32), S((4, rows, 128), bf16), S((4, rows, 128), bf16), S((2, 4, 4, width // 4 + 48, ch), bf16), S((4, 16, width), bf16),
            S((PLANES,) + wq.shape, bf16), S((3, 4, 2 * bp, ch), bf16),
        ),
        in_specs=[SMEM] + [VMEM] * 3 + [ANY] * 4 + [VMEM] + [ANY] * 3,
        out_specs=[ANY] * 5 + [VMEM] + [ANY] * 2,
        scratch_shapes=[
            vmem((width, hidden)), vmem((hidden, width)), vmem((width, width)),
            vmem((4, rows, 2 * ch)), vmem((4, rows, 2 * ch), f32), vmem((4, rows, 2 * ch)),
            vmem((rows, width), f32), vmem((rows, width), f32), vmem((rows, width), f32),
            vmem((rows, width)), vmem((width, rows)), vmem((rows, width)), vmem((rows, width), f32), vmem((4, 8, 2 * ch), f32),
            vmem((2, 4, 4, 2 * bp, ch)), vmem((4, 4, 2 * bp, ch)), vmem((4, 2, bp, ch)), vmem((4, 2, bp, ch)),
            vmem((2, 4, rows, 128)), vmem((4, rows, 128)),
            vmem((rows, width)), vmem((rows, width), f32), vmem((2, 4, 4, width // 4 + 48, ch)),
            pltpu.SemaphoreType.DMA((SEMS,)), pltpu.SemaphoreType.DMA((SEMS,)),
            pltpu.SemaphoreType.DMA((5,)), pltpu.SemaphoreType.DMA((PLANES,)), pltpu.SemaphoreType.DMA((32,)),
        ],
        compiler_params=params(3),
    )(lengths, att, tokens, cotangent, full_in, w_in, full_out, w_out, small, full_back, w_back, wq)


def run_final(dproj, wq_full, wq, gh1, gw, hw, fin, finb, sums):
    rows, width = gh1.shape
    shard = width // PLANES
    S = jax.ShapeDtypeStruct
    one = S((shard,), f32)
    return pl.pallas_call(
        final_kernel,
        out_shape=(
            S((rows, width), bf16), S((shard, 3 * width), f32), S((shard, 8 * fin.shape[3]), f32),
            S((2 * fin.shape[3], width), f32), S((shard, width), f32), one, one, one, one, one, one, one, one, S((width,), f32),
        ),
        in_specs=[VMEM, ANY, ANY] + [VMEM] * 6,
        out_specs=[VMEM] * 14,
        scratch_shapes=[vmem((4, width, PACK)), vmem((8, 256), f32), vmem((rows, 256)), pltpu.SemaphoreType.DMA((4,))],
        compiler_params=pltpu.CompilerParams(vmem_limit_bytes=VMEM_BYTES),
    )(dproj, wq_full, wq, gh1, gw, hw, fin, finb, sums)


def planned(
    tokens, lengths, w_qkv, q_bias, v_bias, w_out, out_bias, ln1_gain, ln1_bias,
    w_in, in_bias, w_back, back_bias, ln2_gain, ln2_bias, cotangent,
):
    vectors = (out_bias, ln1_gain, ln1_bias, back_bias, ln2_gain, ln2_bias, in_bias, q_bias, v_bias)
    q, k, v, o, tok_all, att, small_all, full_in, full_out, wq, full_back = run_forward(
        lengths, tokens[0], w_qkv, w_in, w_back, w_out, *vectors
    )
    output, gh1, do, do1, grads, sums, wq_full, back = run_ffn(
        lengths, att, tokens[0], cotangent[0], full_in, w_in, full_out, w_out, small_all, full_back, w_back, wq
    )
    dproj, gw, hw, fin, finb, sums_f = run_backward(do, do1, q, k, v, o, tok_all, grads, sums, back)
    gt, gqkv, gin, gback, gout, qb, vb, ob, g1, b1, bb, g2, b2, ib = run_final(dproj, wq_full, wq, gh1, gw, hw, fin, finb, sums_f)
    return (output[None], gt[None], gqkv, qb, vb, gout, ob, g1, b1, gin, ib, gback, bb, g2, b2)


masked_score = -1e30


def passed_along(block, axis, distance):
    devices = range(lax.axis_size(axis))
    route = [((i - distance) % len(devices), i) for i in devices]
    return lax.ppermute(block, axis, route)


def norm_forward(hidden, gain_vec, shift_vec):
    average = jnp.mean(hidden, axis=-1, keepdims=True)
    centred = hidden - average
    variance = jnp.mean(centred * centred, axis=-1, keepdims=True)
    inverse = lax.rsqrt(variance + 1e-05)
    normed = centred * inverse
    return (normed * gain_vec + shift_vec, normed, inverse)


def norm_backward(grad_norm, normed, inverse, gain_vec):
    scaled = grad_norm * gain_vec
    grad_input = inverse * (
        scaled
        - jnp.mean(scaled, axis=-1, keepdims=True)
        - normed * jnp.mean(scaled * normed, axis=-1, keepdims=True)
    )
    return (grad_input, jnp.sum(grad_norm * normed, axis=0), jnp.sum(grad_norm, axis=0))


def forward_tile(state_in, query_heads, key_pair, length):
    old_max, old_sum, old_acc = state_in
    key_rows = key_pair.shape[0]
    head_count = query_heads.shape[1]
    head_size = query_heads.shape[2]
    key_heads = key_pair[:, 0].reshape(key_rows, head_count, head_size)
    value_heads = key_pair[:, 1].reshape(key_rows, head_count, head_size)
    key_ok = jnp.arange(key_rows, dtype=jnp.int32) < length
    scores = jnp.einsum(
        "qhd,khd->hqk", query_heads, key_heads, preferred_element_type=jnp.float32
    ) * head_size ** (-0.5)
    scores = jnp.where(key_ok[None, None, :], scores, masked_score)
    new_max = jnp.maximum(old_max, jnp.max(scores, axis=2))
    prob_tile = jnp.where(key_ok[None, None, :], jnp.exp(scores - new_max[:, :, None]), 0.0)
    new_sum = jnp.sum(prob_tile, axis=2)
    new_acc = jnp.einsum(
        "hqk,khd->hqd",
        prob_tile.astype(jnp.bfloat16),
        value_heads,
        preferred_element_type=jnp.float32,
    )
    return (new_max, new_sum, new_acc)


def backward_tile(query_pair, log_total, delta, key_pair, key_start, length):
    query_rows = query_pair.shape[0]
    key_rows = key_pair.shape[0]
    model_width = query_pair.shape[2]
    head_count = log_total.shape[0]
    head_size = model_width // head_count
    score_scale = head_size ** (-0.5)
    query_heads = query_pair[:, 0].reshape(query_rows, head_count, head_size)
    grad_heads = query_pair[:, 1].reshape(query_rows, head_count, head_size)
    key_heads = key_pair[:, 0].reshape(key_rows, head_count, head_size)
    value_heads = key_pair[:, 1].reshape(key_rows, head_count, head_size)
    key_ok = key_start + jnp.arange(key_rows, dtype=jnp.int32) < length
    scores = (
        jnp.einsum("qhd,khd->hqk", query_heads, key_heads, preferred_element_type=jnp.float32)
        * score_scale
    )
    prob_tile = jnp.where(key_ok[None, None, :], jnp.exp(scores - log_total[:, :, None]), 0.0)
    grad_values = jnp.einsum(
        "hqk,qhd->khd",
        prob_tile.astype(jnp.bfloat16),
        grad_heads,
        preferred_element_type=jnp.float32,
    )
    grad_probs = jnp.einsum(
        "qhd,khd->hqk", grad_heads, value_heads, preferred_element_type=jnp.float32
    )
    grad_scores = (prob_tile * (grad_probs - delta[:, :, None])).astype(jnp.bfloat16)
    grad_queries = (
        jnp.einsum("hqk,khd->qhd", grad_scores, key_heads, preferred_element_type=jnp.float32)
        * score_scale
    )
    grad_keys = (
        jnp.einsum("hqk,qhd->khd", grad_scores, query_heads, preferred_element_type=jnp.float32)
        * score_scale
    )
    grad_pair = jnp.stack([grad_keys, grad_values], axis=1).reshape(key_rows, 2, model_width)
    return (grad_queries.reshape(query_rows, model_width), grad_pair)


def on_device(
    tokens,
    lengths,
    w_qkv,
    q_bias,
    v_bias,
    w_out,
    out_bias,
    ln1_gain,
    ln1_bias,
    w_in,
    in_bias,
    w_back,
    back_bias,
    ln2_gain,
    ln2_bias,
    cotangent,
):
    gathered = tuple(
        lax.all_gather(a, "fsdp", axis=0, tiled=True)
        for a in (
            w_qkv, q_bias, v_bias, w_out, out_bias, ln1_gain, ln1_bias, w_in, in_bias, w_back, back_bias, ln2_gain, ln2_bias
        )
    )
    (
        full_qkv,
        full_qbias,
        full_vbias,
        full_out,
        full_obias,
        full_g1,
        full_n1,
        full_in,
        full_ibias,
        full_back,
        full_bbias,
        full_g2,
        full_n2,
    ) = gathered
    f32 = jnp.float32
    seq_index = lax.axis_index("seq")
    seq_count = lax.axis_size("seq")
    token_rows = tokens.shape[1]
    model_width = tokens.shape[2]
    head_count = HEADS
    head_size = model_width // head_count
    length = lengths[0]
    my_start = seq_index * token_rows
    row_valid = (my_start + jnp.arange(token_rows, dtype=jnp.int32) < length).astype(f32)
    inputs_b = tokens[0]
    inputs_f = inputs_b.astype(f32)
    bias_all = jnp.concatenate(
        [full_qbias.astype(f32), jnp.zeros((model_width,), f32), full_vbias.astype(f32)]
    )
    projected = (jnp.dot(inputs_b, full_qkv, preferred_element_type=f32) + bias_all).astype(
        jnp.bfloat16
    )
    query_heads = projected[:, :model_width].reshape(token_rows, head_count, head_size)
    key_pair = projected[:, model_width:].reshape(token_rows, 2, model_width)
    init_state = (
        jnp.full((head_count, token_rows), masked_score, f32),
        jnp.zeros((head_count, token_rows), f32),
        jnp.zeros((head_count, token_rows, head_size), f32),
    )
    pieces = lax.all_gather(key_pair, "seq", axis=0, tiled=True)
    run_max, run_sum, run_acc = forward_tile(init_state, query_heads, pieces, length)
    positive = run_sum > 0.0
    safe_sum = jnp.where(positive, run_sum, 1.0)
    attended_heads = jnp.where(positive[:, :, None], run_acc / safe_sum[:, :, None], 0.0)
    log_total = jnp.where(positive, run_max + jnp.log(safe_sum), 0.0)
    attended_f = attended_heads.transpose(1, 0, 2).reshape(token_rows, model_width)
    attended_b = attended_f.astype(jnp.bfloat16)
    branch_f = jnp.dot(attended_b, full_out, preferred_element_type=f32) + full_obias.astype(f32)
    first_norm, normed_one, inverse_one = norm_forward(
        inputs_f + branch_f, full_g1.astype(f32), full_n1.astype(f32)
    )
    first_low = first_norm.astype(jnp.bfloat16)
    inner_act = jnp.dot(first_low, full_in, preferred_element_type=f32) + full_ibias.astype(f32)
    activated_b = jax.nn.gelu(inner_act, approximate=False).astype(jnp.bfloat16)
    second = jnp.dot(activated_b, full_back, preferred_element_type=f32) + full_bbias.astype(f32)
    result, normed_two, inverse_two = norm_forward(
        first_norm + second, full_g2.astype(f32), full_n2.astype(f32)
    )
    output = (result * row_valid[:, None]).astype(jnp.bfloat16)
    grad_result = cotangent[0].astype(f32) * row_valid[:, None]
    grad_h2, g_ln2_gain, g_ln2_bias = norm_backward(
        grad_result, normed_two, inverse_two, full_g2.astype(f32)
    )
    grad_second = grad_h2.astype(jnp.bfloat16)
    g_w_back = jnp.einsum("tf,td->fd", activated_b, grad_second, preferred_element_type=f32)
    g_back_bias = jnp.sum(grad_second.astype(f32), axis=0)
    grad_act = jnp.einsum("td,fd->tf", grad_second, full_back, preferred_element_type=f32)
    gelu_value, gelu_pull = jax.vjp(
        lambda values_in: jax.nn.gelu(values_in, approximate=False), inner_act
    )
    grad_inner = gelu_pull(grad_act)[0].astype(jnp.bfloat16)
    g_w_in = jnp.einsum("td,tf->df", first_low, grad_inner, preferred_element_type=f32)
    g_in_bias = jnp.sum(grad_inner.astype(f32), axis=0)
    grad_first = grad_h2 + jnp.einsum("tf,df->td", grad_inner, full_in, preferred_element_type=f32)
    grad_h1, g_ln1_gain, g_ln1_bias = norm_backward(
        grad_first, normed_one, inverse_one, full_g1.astype(f32)
    )
    grad_branch = grad_h1.astype(jnp.bfloat16)
    g_w_out = jnp.einsum("tc,td->cd", attended_b, grad_branch, preferred_element_type=f32)
    g_out_bias = jnp.sum(grad_branch.astype(f32), axis=0)
    grad_attended = jnp.einsum(
        "td,cd->tc", grad_branch, full_out, preferred_element_type=f32
    ).astype(jnp.bfloat16)
    delta = jnp.sum(
        (grad_attended.astype(f32) * attended_f).reshape(token_rows, head_count, head_size), axis=2
    ).T
    query_pair = jnp.stack([projected[:, :model_width], grad_attended], axis=1)
    zero_rows = jnp.zeros((token_rows, model_width), f32)
    zero_pair = jnp.zeros((token_rows, 2, model_width), f32)

    def visit_keys(hop_index, grad_q, moving_pair, grad_pair):
        anchor = (seq_index - hop_index) % seq_count
        add_q, add_pair = backward_tile(
            query_pair, log_total, delta, moving_pair, anchor * token_rows, length
        )
        return (grad_q + add_q, grad_pair + add_pair)

    def return_key_grads(grad_pair):
        return passed_along(grad_pair.astype(jnp.bfloat16), "seq", 1).astype(grad_pair.dtype)

    def key_hop(hop_index, loop_state):
        grad_q, moving_pair, grad_pair = loop_state
        grad_q, grad_pair = visit_keys(hop_index, grad_q, moving_pair, grad_pair)
        moved = passed_along(moving_pair, "seq", 1)
        return (grad_q, moved, return_key_grads(grad_pair))

    grad_q, moving_pair, grad_pair = lax.fori_loop(
        0, seq_count - 1, key_hop, (zero_rows, key_pair, zero_pair)
    )
    grad_q, grad_pair = visit_keys(seq_count - 1, grad_q, moving_pair, grad_pair)
    grad_pair = return_key_grads(grad_pair)
    grad_projected = jnp.concatenate(
        [grad_q, grad_pair.reshape(token_rows, 2 * model_width)], axis=1
    ).astype(jnp.bfloat16)
    g_w_qkv = jnp.einsum("td,te->de", inputs_b, grad_projected, preferred_element_type=f32)
    grad_proj_f = grad_projected.astype(f32)
    g_q_bias = jnp.sum(grad_proj_f[:, :model_width], axis=0)
    g_v_bias = jnp.sum(grad_proj_f[:, 2 * model_width :], axis=0)
    grad_input = grad_h1 + jnp.einsum(
        "te,de->td", grad_projected, full_qkv, preferred_element_type=f32
    )
    local_grads = (
        g_w_qkv,
        g_q_bias,
        g_v_bias,
        g_w_out,
        g_out_bias,
        g_ln1_gain,
        g_ln1_bias,
        g_w_in,
        g_in_bias,
        g_w_back,
        g_back_bias,
        g_ln2_gain,
        g_ln2_bias,
    )
    owned = [
        lax.psum_scatter(a.astype(jnp.bfloat16), "fsdp", scatter_dimension=0, tiled=True).astype(jnp.float32)
        for a in local_grads
    ]
    totals = [lax.psum(a.astype(jnp.bfloat16), "seq").astype(jnp.float32) for a in owned]
    return (output[None], grad_input.astype(jnp.bfloat16)[None]) + tuple(totals)


def solution(mesh):
    spread, vector, matrix = P("fsdp", "seq", None), P("fsdp"), P("fsdp", None)
    fits = mesh.shape["seq"] == 2 * CHIPS and mesh.shape["fsdp"] == PLANES
    return jax.shard_map(
        planned if fits else on_device,
        mesh=mesh,
        in_specs=(spread, vector, matrix, vector, vector, matrix) + (vector,) * 3
        + (matrix, vector, matrix) + (vector,) * 3 + (spread,),
        out_specs=(spread, spread, matrix, vector, vector, matrix) + (vector,) * 3
        + (matrix, vector, matrix) + (vector,) * 3,
        check_vma=False,
    )
```
